32 devices in a mesh: grp: 4 (over y, x), seq: 8 (over z, core).
Axes of the slice: x: 2, y: 2, z: 4, core: 2. Of those that a mesh axis runs over, the one named last changes fastest.
Arguments:
- points: bfloat16 [16384, 512], P(('grp', 'seq')), may hold values from -6 to 6
- pattern_first: int32 [256, 3], P(('grp', 'seq')), may hold values from 0 to 63, as said below
- pattern_second: int32 [256, 3], P(('grp', 'seq')), may hold values from 0 to 7
- destination: int32 [16384], P(('grp', 'seq')), may hold values from 0 to 16383, as said below
- norm_gains: float32 [4, 512], replicated, may hold values from 0.1 to 1.9
- w_qkv: bfloat16 [2, 512, 1536], replicated
- w_proj: bfloat16 [2, 512, 512], replicated, may hold values from -0.25 to 0.25
- w_up: bfloat16 [2, 512, 2048], replicated, may hold values from -0.25 to 0.25
- w_down: bfloat16 [2, 2048, 512], replicated, may hold values from -0.125 to 0.125
- w_head: bfloat16 [3, 512], replicated, may hold values from -0.25 to 0.25
Outputs:
- features: bfloat16 [16384, 512], P(('grp', 'seq'))
- normals: float32 [3, 16384], P(None, ('grp', 'seq'))
The draws below stay inside these ranges and needn't reach their ends.
Inputs may be any that keep to these rules, and one draw needn't show every extreme that they name: `pattern_first`: the 24 entries of the patches of one device name at most 4 patches (repeats counted) lying on any one device of the group, and exactly 4 on some device. `destination`: a permutation of the positions; the 512 points of one device place at most 32 points in any one block of 512 consecutive positions of the second order, and exactly 32 in some block for every device.
All inputs are finite; a program needn't handle non-finite values.
Results may differ from the reference program's by a relative error of at most 0.024.
Values may be sent and summed in bfloat16 or wider, within the bound.
No kernel may reach another device: no remote copies, remote signals or barrier semaphores. Data moves between devices by JAX's collectives and lax.ppermute only.
A program may use at most 128 MiB of HBM per device.

```python
import math
import jax
import jax.numpy as jnp
from jax import lax

C = 512
HEADS = 8
FF = 2048
PATCH = 64
K_SEL = 3
ROWS_DEV = 512
PATCH_DEV = 8
N_PATCHES = 256
N_POINTS = 16384
REQ = 4
N_GRP = 4
N_SEQ = 8


def draw_w_qkv(key, part):
    parts_keys = jax.random.split(key, 3)
    spread_qk = 2.0 / math.sqrt(C)
    queries = jax.random.normal(parts_keys[0], (2, C, C), jnp.float32) * spread_qk
    values = jax.random.normal(parts_keys[2], (2, C, C), jnp.float32) / math.sqrt(C)
    key_part = jax.random.normal(parts_keys[1], (2, C, C), jnp.float32) * spread_qk
    return jnp.concatenate([queries, key_part, values], axis=-1).astype(jnp.bfloat16)


def draw_pattern_first(key, part):
    devices = N_GRP * N_SEQ
    wanted = PATCH_DEV * K_SEL
    slots = N_SEQ * REQ
    device_keys = jax.random.split(key, devices)

    def one_device(sub):
        pieces = jax.random.split(sub, 4)
        favored = jax.random.randint(pieces[0], (), 0, N_SEQ)
        ranking = jax.random.permutation(pieces[1], slots).astype(jnp.int32)
        source = (jnp.arange(slots, dtype=jnp.int32) // REQ).astype(jnp.int32)
        scored = jnp.where(source == favored, ranking - slots, ranking)
        order = jnp.argsort(scored, stable=True)
        picked = source[order[:wanted]]
        picked = jax.random.permutation(pieces[2], picked)
        local = jax.random.randint(pieces[3], (wanted,), 0, PATCH_DEV)
        return (picked * PATCH_DEV + local).astype(jnp.int32)
    return jax.vmap(one_device)(device_keys).reshape(N_PATCHES, K_SEL).astype(jnp.int32)


def draw_destination(key, part):
    devices = N_GRP * N_SEQ
    per_peer = ROWS_DEV // devices
    parts_keys = jax.random.split(key, 5)
    levels = jnp.concatenate([jnp.full((devices // 4,), 2 * per_peer, jnp.int32), jnp.full((devices // 2,), per_peer, jnp.int32), jnp.zeros((devices - devices // 4 - devices // 2,), jnp.int32)])
    weights = jax.random.permutation(parts_keys[0], levels)
    ending = jnp.cumsum(weights)
    shifting = jax.random.permutation(parts_keys[1], devices)
    relabel = jax.random.permutation(parts_keys[2], devices)
    slots_src = jax.vmap(lambda sub: jax.random.permutation(sub, ROWS_DEV))(jax.random.split(parts_keys[3], devices))
    classes = jnp.sum((ending[None, None, :] <= slots_src[:, :, None]).astype(jnp.int32), axis=-1)
    target = relabel[(shifting[:, None] + classes) % devices]
    places = jax.vmap(lambda sub: jax.random.permutation(sub, ROWS_DEV))(jax.random.split(parts_keys[4], devices))
    return (target * ROWS_DEV + places[target, slots_src]).reshape(-1).astype(jnp.int32)


def with_ends(values, rng, smallest, high):
    index_at = [jax.random.randint(jax.random.fold_in(rng, axis), (), 0, length) for axis, length in enumerate(values.shape)]
    main_axis = values.shape.index(max(values.shape))
    beside = index_at[:main_axis] + [(index_at[main_axis] + 1) % values.shape[main_axis]] + index_at[main_axis + 1:]
    return values.at[tuple(index_at)].set(smallest).at[tuple(beside)].set(high)


def steps_of(stream_key, extent, cuts, smallest, high):
    def one(dim, parts):
        heights = jax.random.uniform(jax.random.fold_in(jax.random.fold_in(stream_key, 6), dim), (parts,), jnp.float32, smallest / len(cuts), high / len(cuts))
        return jnp.repeat(jnp.exp(heights), extent[dim] // parts).reshape((-1,) + (1,) * (len(extent) - dim - 1))

    level = one(*cuts[0])
    for cut in cuts[1:]:
        level = level * one(*cut)
    return level


def scatter_about(stream_key, shape, deviation, bound, cuts=(), held_as=jnp.bfloat16):
    values = jax.random.normal(stream_key, shape, jnp.float32) * deviation
    if len(cuts) > 0:
        values = steps_of(stream_key, shape, cuts, -0.22, 0.18) * values
    return jnp.clip(values, min=-bound, max=bound).astype(held_as)


def setup_inputs(seed: int = 0) -> dict:
    key_list = jax.random.split(jax.random.key(seed), 11)
    return {
        "points": scatter_about(key_list[0], (N_POINTS, C), 1.0, 6.0, ((0, 32),)),
        "pattern_first": draw_pattern_first(jax.random.fold_in(key_list[10], 71), 0),
        "pattern_second": with_ends(jax.random.randint(key_list[2], (N_PATCHES, K_SEL), 0, PATCH_DEV), jax.random.fold_in(key_list[2], 1), 0, PATCH_DEV - 1).astype(jnp.int32),
        "destination": draw_destination(jax.random.fold_in(key_list[10], 71), 0),
        "norm_gains": jnp.clip(1.0 + 0.18 * jax.random.normal(key_list[4], (4, C), jnp.float32), 0.1, 1.9),
        "w_qkv": draw_w_qkv(jax.random.fold_in(key_list[10], 71), 0),
        "w_proj": scatter_about(key_list[6], (2, C, C), C ** -0.5, 0.25),
        "w_up": scatter_about(key_list[7], (2, C, FF), C ** -0.5, 0.25),
        "w_down": scatter_about(key_list[8], (2, FF, C), FF ** -0.5, 0.125),
        "w_head": scatter_about(key_list[9], (3, C), C ** -0.5, 0.25),
    }


def layer_norm(rows, gains):
    values = rows.astype(jnp.float32)
    average = lax.optimization_barrier(jnp.mean(values, axis=-1, keepdims=True))
    spread = lax.optimization_barrier(jnp.mean((values - average) ** 2, axis=-1, keepdims=True))
    return (values - average) * lax.rsqrt(spread + 1e-05) * gains

def attend(queries, key_rows, value_rows):
    count = queries.shape[0]
    head_dim = C // HEADS
    qh = queries.reshape(count, PATCH, HEADS, head_dim).astype(jnp.float32)
    kh = key_rows.reshape(count, -1, HEADS, head_dim).astype(jnp.float32)
    vh = value_rows.reshape(count, -1, HEADS, head_dim).astype(jnp.float32)
    scores = jnp.einsum('nqhd,nkhd->nhqk', qh, kh) * head_dim ** (-0.5)
    probs = jax.nn.softmax(scores, axis=-1).astype(jnp.bfloat16)
    probs = lax.optimization_barrier(probs).astype(jnp.float32)
    mixed = jnp.einsum('nhqk,nkhd->nqhd', probs, vh)
    return mixed.reshape(count * PATCH, C).astype(jnp.bfloat16)

def block(rows, pattern, groups, section, norm_gains, w_qkv, w_proj, w_up, w_down):
    normed = layer_norm(rows, norm_gains[2 * section]).astype(jnp.bfloat16)
    proj = jnp.dot(normed, w_qkv[section], preferred_element_type=jnp.float32)
    queries = proj[:, :C].astype(jnp.bfloat16)
    key_rows = proj[:, C:2 * C].astype(jnp.bfloat16)
    value_rows = proj[:, 2 * C:].astype(jnp.bfloat16)
    per_group = rows.shape[0] // (groups * PATCH)
    qg = queries.reshape(groups, per_group, PATCH, C)
    kg = key_rows.reshape(groups, per_group, PATCH, C)
    vg = value_rows.reshape(groups, per_group, PATCH, C)
    pg = pattern.reshape(groups, per_group, K_SEL)

    def one_group(items):
        qq, kk, vv, chosen = items
        keys_all = jnp.concatenate([kk[:, None], kk[chosen]], axis=1).reshape(per_group, -1, C)
        vals_all = jnp.concatenate([vv[:, None], vv[chosen]], axis=1).reshape(per_group, -1, C)
        return attend(qq, keys_all, vals_all)
    attended = lax.map(one_group, (qg, kg, vg, pg)).reshape(-1, C)
    first = (rows.astype(jnp.float32) + jnp.dot(attended, w_proj[section], preferred_element_type=jnp.float32)).astype(jnp.bfloat16)
    hidden = layer_norm(first, norm_gains[2 * section + 1]).astype(jnp.bfloat16)
    upper = jnp.dot(hidden, w_up[section], preferred_element_type=jnp.float32)
    act = jax.nn.gelu(upper, approximate=False).astype(jnp.bfloat16)
    return (first.astype(jnp.float32) + jnp.dot(act, w_down[section], preferred_element_type=jnp.float32)).astype(jnp.bfloat16)

def reference(points, pattern_first, pattern_second, destination, norm_gains, w_qkv, w_proj, w_up, w_down, w_head):
    first = block(points, pattern_first, N_GRP, 0, norm_gains, w_qkv, w_proj, w_up, w_down)
    second = jnp.zeros_like(first).at[destination].set(first)
    features = block(second, pattern_second, N_GRP * N_SEQ, 1, norm_gains, w_qkv, w_proj, w_up, w_down)
    normals = lax.dot_general(w_head, features, (((1,), (1,)), ((), ())), preferred_element_type=jnp.float32)
    return (features, normals)
```

```python
import functools

import jax
import jax.numpy as jnp
from jax import lax
from jax.experimental import pallas as pl
from jax.experimental.pallas import tpu as pltpu
from jax.sharding import PartitionSpec as P

HEADS = 8
PATCH = 64
HEADS_TOGETHER = 4
VMEM_BYTES = 48 * 1024 * 1024
F32 = jnp.float32
BF16 = jnp.bfloat16


def layer_norm(rows, gains):
    values = rows.astype(F32)
    average = jnp.mean(values, axis=-1, keepdims=True)
    spread = jnp.mean((values - average) ** 2, axis=-1, keepdims=True)
    return ((values - average) * lax.rsqrt(spread + 1e-05) * gains).astype(BF16)


def head_masks(head_dim):
    lane = lax.broadcasted_iota(jnp.int32, (PATCH, HEADS_TOGETHER * head_dim), 1)
    return [
        jnp.where((lane >= h * head_dim) & (lane < (h + 1) * head_dim), 1.0, 0.0).astype(F32)
        for h in range(HEADS_TOGETHER)
    ]


def attend_patch(queries, key_rows, value_rows, masks):
    channels = queries.shape[1]
    width = HEADS_TOGETHER * (channels // HEADS)
    sides = []
    for at in range(0, channels, width):
        q = queries[:, at : at + width]
        stacked = jnp.concatenate([q * mask.astype(BF16) for mask in masks], axis=0)
        scores = lax.dot_general(
            stacked,
            key_rows[:, at : at + width],
            (((1,), (1,)), ((), ())),
            preferred_element_type=F32,
        )
        top = jnp.max(scores, axis=-1, keepdims=True)
        grown = jnp.exp(scores - top)
        total = jnp.sum(grown, axis=-1, keepdims=True)
        weights = (grown * (1.0 / total)).astype(BF16)
        mixed = jnp.dot(weights, value_rows[:, at : at + width], preferred_element_type=F32)
        side = mixed[:PATCH] * masks[0]
        for h in range(1, HEADS_TOGETHER):
            side = side + mixed[h * PATCH : (h + 1) * PATCH] * masks[h]
        sides.append(side.astype(BF16))
    return jnp.concatenate(sides, axis=1)


def weight_copies(section, sources, held, sems):
    return [
        pltpu.make_async_copy(source.at[section], kept, sems.at[at])
        for at, (source, kept) in enumerate(zip(sources, held))
    ]


def finish(rows, attended, gain, held, copies):
    w_proj, w_up, w_down = held
    copies[0].wait()
    first = (
        rows.astype(F32) + jnp.dot(attended, w_proj[...], preferred_element_type=F32)
    ).astype(BF16)
    hidden = layer_norm(first, gain)
    total = first.astype(F32)
    copies[1].wait()
    copies[2].wait()
    piece = 512
    for at in range(0, w_up.shape[1], piece):
        upper = jnp.dot(hidden, w_up[:, at : at + piece], preferred_element_type=F32)
        act = (upper * (0.5 + 0.5 * lax.erf(upper * 0.5**0.5))).astype(BF16)
        total = total + jnp.dot(act, w_down[at : at + piece, :], preferred_element_type=F32)
    return total.astype(BF16)


def first_kernel(
    pattern,
    points,
    normed,
    gathered,
    gains,
    w_qkv,
    w_proj,
    w_up,
    w_down,
    send,
    outgoing,
    keyed,
    kv,
    attended,
    qkv_held,
    proj_held,
    up_held,
    down_held,
    sems,
    weight_sems,
):
    rows, channels = points.shape
    patches, chosen = pattern.shape
    span = (1 + chosen) * PATCH
    copies = []
    for p in range(patches):
        for j in range(chosen):
            start = pl.multiple_of(pattern[p, j] * PATCH, PATCH)
            copies.append(
                pltpu.make_async_copy(
                    gathered.at[pl.ds(start, PATCH), :],
                    keyed.at[pl.ds(p * span + (1 + j) * PATCH, PATCH), :],
                    sems.at[p, j],
                )
            )
    fetches = weight_copies(
        0, (w_qkv, w_proj, w_up, w_down), (qkv_held, proj_held, up_held, down_held), weight_sems
    )
    fetches[0].start()
    for copy in copies:
        copy.start()
    for fetch in fetches[1:]:
        fetch.start()
    for p in range(patches):
        keyed[p * span : p * span + PATCH, :] = normed[p * PATCH : (p + 1) * PATCH, :]
    scale = (channels // HEADS) ** (-0.5)
    fetches[0].wait()
    queries = (
        jnp.dot(normed[...], qkv_held[:, :channels], preferred_element_type=F32).astype(BF16)
        * BF16(scale)
    ).astype(BF16)
    masks = head_masks(channels // HEADS)
    for copy in copies:
        copy.wait()
    for p in range(patches):
        kv[p * span : (p + 1) * span, :] = jnp.dot(
            keyed[p * span : (p + 1) * span, :], qkv_held[:, channels:], preferred_element_type=F32
        ).astype(BF16)
    for p in range(patches):
        attended[p * PATCH : (p + 1) * PATCH, :] = attend_patch(
            queries[p * PATCH : (p + 1) * PATCH, :],
            kv[p * span : (p + 1) * span, :channels],
            kv[p * span : (p + 1) * span, channels:],
            masks,
        )
    first = finish(
        points[...], attended[...], gains[1:2, :], (proj_held, up_held, down_held), fetches[1:]
    )
    outgoing[...] = jnp.dot(send[...], first, preferred_element_type=F32).astype(BF16)


def second_kernel(
    pattern,
    incoming,
    place,
    gains,
    w_qkv,
    w_proj,
    w_up,
    w_down,
    w_head,
    features,
    normals,
    kv,
    attended,
    qkv_held,
    proj_held,
    up_held,
    down_held,
    weight_sems,
):
    rows, channels = features.shape
    patches, chosen = pattern.shape
    fetches = weight_copies(
        1, (w_qkv, w_proj, w_up, w_down), (qkv_held, proj_held, up_held, down_held), weight_sems
    )
    for fetch in fetches:
        fetch.start()
    second = jnp.dot(place[...], incoming[...], preferred_element_type=F32).astype(BF16)
    normed = layer_norm(second, gains[2:3, :])
    scale = (channels // HEADS) ** (-0.5)
    fetches[0].wait()
    queries = (
        jnp.dot(normed, qkv_held[:, :channels], preferred_element_type=F32).astype(BF16)
        * BF16(scale)
    ).astype(BF16)
    kv[...] = jnp.dot(normed, qkv_held[:, channels:], preferred_element_type=F32).astype(BF16)
    masks = head_masks(channels // HEADS)
    for p in range(patches):
        pieces = [kv[p * PATCH : (p + 1) * PATCH, :]]
        for j in range(chosen):
            start = pl.multiple_of(pattern[p, j] * PATCH, PATCH)
            pieces.append(kv[pl.ds(start, PATCH), :])
        both = jnp.concatenate(pieces, axis=0)
        attended[p * PATCH : (p + 1) * PATCH, :] = attend_patch(
            queries[p * PATCH : (p + 1) * PATCH, :], both[:, :channels], both[:, channels:], masks
        )
    done = finish(
        second, attended[...], gains[3:4, :], (proj_held, up_held, down_held), fetches[1:]
    )
    features[...] = done
    normals[...] = lax.dot_general(
        w_head[...], done, (((1,), (1,)), ((), ())), preferred_element_type=F32
    )


def held_weights(weights):
    return [pltpu.VMEM(w.shape[1:], BF16) for w in weights]


VMEM_SPEC = pl.BlockSpec(memory_space=pltpu.VMEM)
SMEM_SPEC = pl.BlockSpec(memory_space=pltpu.SMEM)
ANY_SPEC = pl.BlockSpec(memory_space=pl.ANY)


def shards(
    points,
    pattern_first,
    pattern_second,
    destination,
    norm_gains,
    w_qkv,
    w_proj,
    w_up,
    w_down,
    w_head,
):
    rows_here, channels = points.shape
    patches, chosen = pattern_first.shape
    devices = lax.axis_size("grp") * lax.axis_size("seq")
    capacity = 2 * rows_here // devices
    slot_total = devices * capacity

    normed = layer_norm(points, norm_gains[0])
    gathered = lax.all_gather(normed, "seq", axis=0, tiled=True)

    target = destination // rows_here
    place_at = destination % rows_here
    onehot_dev = (target[:, None] == jnp.arange(devices, dtype=jnp.int32)[None, :]).astype(
        jnp.int32
    )
    earlier = jnp.cumsum(onehot_dev, axis=0) - onehot_dev
    send_rank = jnp.sum(earlier * onehot_dev, axis=1)
    slot_index = target * capacity + send_rank
    row_ids = jnp.arange(rows_here, dtype=jnp.int32)
    slot_ids = jnp.arange(slot_total, dtype=jnp.int32)
    match_send = slot_index[None, :] == slot_ids[:, None]
    send = match_send.astype(BF16)
    out_places = jnp.sum(jnp.where(match_send, place_at[None, :] + 1, 0), axis=1) - 1
    in_places = lax.all_to_all(
        out_places.reshape(devices, capacity),
        ("grp", "seq"),
        split_axis=0,
        concat_axis=0,
        tiled=True,
    ).reshape(-1)
    place = (in_places[None, :] == row_ids[:, None]).astype(BF16)

    weights = (w_qkv, w_proj, w_up, w_down)
    keyed_rows = patches * (1 + chosen) * PATCH
    outgoing = pl.pallas_call(
        first_kernel,
        out_shape=jax.ShapeDtypeStruct((slot_total, channels), BF16),
        in_specs=[SMEM_SPEC, VMEM_SPEC, VMEM_SPEC, ANY_SPEC, VMEM_SPEC]
        + [ANY_SPEC] * len(weights)
        + [VMEM_SPEC],
        out_specs=VMEM_SPEC,
        scratch_shapes=[
            pltpu.VMEM((keyed_rows, channels), BF16),
            pltpu.VMEM((keyed_rows, 2 * channels), BF16),
            pltpu.VMEM((rows_here, channels), BF16),
            *held_weights(weights),
            pltpu.SemaphoreType.DMA((patches, chosen)),
            pltpu.SemaphoreType.DMA((len(weights),)),
        ],
        compiler_params=pltpu.CompilerParams(vmem_limit_bytes=VMEM_BYTES),
        name="block_first",
    )(pattern_first, points, normed, gathered, norm_gains, *weights, send)

    incoming = lax.all_to_all(
        outgoing.reshape(devices, capacity, channels),
        ("grp", "seq"),
        split_axis=0,
        concat_axis=0,
        tiled=True,
    ).reshape(slot_total, channels)

    return pl.pallas_call(
        second_kernel,
        out_shape=(
            jax.ShapeDtypeStruct((rows_here, channels), BF16),
            jax.ShapeDtypeStruct((w_head.shape[0], rows_here), F32),
        ),
        in_specs=[SMEM_SPEC, VMEM_SPEC, VMEM_SPEC, VMEM_SPEC]
        + [ANY_SPEC] * len(weights)
        + [VMEM_SPEC],
        out_specs=(VMEM_SPEC, VMEM_SPEC),
        scratch_shapes=[
            pltpu.VMEM((rows_here, 2 * channels), BF16),
            pltpu.VMEM((rows_here, channels), BF16),
            *held_weights(weights),
            pltpu.SemaphoreType.DMA((len(weights),)),
        ],
        compiler_params=pltpu.CompilerParams(vmem_limit_bytes=VMEM_BYTES),
        name="block_second",
    )(pattern_second, incoming, place, norm_gains, *weights, w_head)


def solution(mesh):
    placed = (
        P(("grp", "seq"), None),
        P(("grp", "seq"), None),
        P(("grp", "seq"), None),
        P(("grp", "seq")),
        P(),
        P(),
        P(),
        P(),
        P(),
        P(),
    )
    return jax.shard_map(
        shards,
        mesh=mesh,
        in_specs=placed,
        out_specs=(P(("grp", "seq"), None), P(None, ("grp", "seq"))),
        check_vma=False,
    )
```

```python
import functools

import jax
import jax.numpy as jnp
from jax import lax
from jax.experimental import pallas as pl
from jax.experimental.pallas import tpu as pltpu
from jax.sharding import PartitionSpec as P

HEADS = 8
PATCH = 64
HEADS_TOGETHER = 4
RING_PARTS = 2
VMEM_BYTES = 48 * 1024 * 1024
ERF_TOP = 30.0
ERF_TERMS = (
    1.81392502e-09,
    -1.33783099e-07,
    3.97406914e-06,
    -5.52733748e-05,
    -3.30267412e-05,
    3.63341492e-02,
    7.97884268e-01,
)
F32 = jnp.float32
BF16 = jnp.bfloat16


def layer_norm(rows, gains):
    values = rows.astype(F32)
    average = jnp.mean(values, axis=-1, keepdims=True)
    spread = jnp.mean((values - average) ** 2, axis=-1, keepdims=True)
    return ((values - average) * lax.rsqrt(spread + 1e-05) * gains).astype(BF16)


def gelu(x):
    square = jnp.minimum(x * x, ERF_TOP)
    inner = jnp.full_like(square, ERF_TERMS[0])
    for term in ERF_TERMS[1:]:
        inner = inner * square + term
    half = 0.5 * x
    return half + half * jnp.tanh(x * inner)


def head_masks(head_dim):
    lane = lax.broadcasted_iota(jnp.int32, (PATCH, HEADS_TOGETHER * head_dim), 1)
    return [
        jnp.where((lane >= h * head_dim) & (lane < (h + 1) * head_dim), 1.0, 0.0).astype(F32)
        for h in range(HEADS_TOGETHER)
    ]


def attend_patch(queries, key_rows, value_rows, masks):
    channels = queries.shape[1]
    width = HEADS_TOGETHER * (channels // HEADS)
    sides = []
    for at in range(0, channels, width):
        q = queries[:, at : at + width]
        stacked = jnp.concatenate([q * mask.astype(BF16) for mask in masks], axis=0)
        scores = lax.dot_general(
            stacked,
            key_rows[:, at : at + width],
            (((1,), (1,)), ((), ())),
            preferred_element_type=F32,
        )
        top = jnp.max(scores, axis=-1, keepdims=True)
        grown = jnp.exp(scores - top)
        total = jnp.sum(grown, axis=-1, keepdims=True)
        weights = (grown * (1.0 / total)).astype(BF16)
        mixed = jnp.dot(weights, value_rows[:, at : at + width], preferred_element_type=F32)
        side = mixed[:PATCH] * masks[0]
        for h in range(1, HEADS_TOGETHER):
            side = side + mixed[h * PATCH : (h + 1) * PATCH] * masks[h]
        sides.append(side.astype(BF16))
    return jnp.concatenate(sides, axis=1)


def weight_copies(section, sources, held, sems):
    return [
        pltpu.make_async_copy(source.at[section], kept, sems.at[at])
        for at, (source, kept) in enumerate(zip(sources, held))
    ]


def finish(rows, attended, gain, held, copies):
    w_proj, w_up, w_down = held
    copies[0].wait()
    first = (
        rows.astype(F32) + jnp.dot(attended, w_proj[...], preferred_element_type=F32)
    ).astype(BF16)
    hidden = layer_norm(first, gain)
    total = first.astype(F32)
    copies[1].wait()
    copies[2].wait()
    piece = 512
    for at in range(0, w_up.shape[1], piece):
        upper = jnp.dot(hidden, w_up[:, at : at + piece], preferred_element_type=F32)
        act = gelu(upper).astype(BF16)
        total = total + jnp.dot(act, w_down[at : at + piece, :], preferred_element_type=F32)
    return total.astype(BF16)


def project_kernel(slot, *refs):
    *parts, gains, w_qkv, _, whole, kv, sems = refs
    channels = w_qkv.shape[1]
    rows = parts[0].shape[0]
    copies = []
    for i, part in enumerate(parts):
        here = pl.ds(i * rows, rows)
        normed = layer_norm(part[...], gains[0:1, :])
        kv[here, :] = jnp.dot(
            normed, w_qkv[0, :, channels:], preferred_element_type=F32
        ).astype(BF16)
        copies.append(
            pltpu.make_async_copy(
                kv.at[here, :],
                whole.at[pl.ds(slot * len(parts) * rows + i * rows, rows), :],
                sems.at[i],
            )
        )
        copies[-1].start()
    for copy in copies:
        copy.wait()


def own_kernel(*refs):
    *parts, gains, w_qkv, whole, queries, kv, sems = refs
    channels = w_qkv.shape[1]
    rows = parts[0].shape[0]
    scale = (channels // HEADS) ** (-0.5)
    copies = []
    for i, part in enumerate(parts):
        here = pl.ds(i * rows, rows)
        normed = layer_norm(part[...], gains[0:1, :])
        kv[here, :] = jnp.dot(
            normed, w_qkv[0, :, channels:], preferred_element_type=F32
        ).astype(BF16)
        copies.append(
            pltpu.make_async_copy(
                kv.at[here, :], whole.at[pl.ds(i * rows, rows), :], sems.at[i]
            )
        )
        copies[-1].start()
        own = jnp.dot(normed, w_qkv[0, :, :channels], preferred_element_type=F32).astype(BF16)
        queries[here, :] = (own * BF16(scale)).astype(BF16)
    for copy in copies:
        copy.wait()


def first_kernel(
    pattern,
    points,
    queries,
    keyed,
    gains,
    w_proj,
    w_up,
    w_down,
    send,
    outgoing,
    kv,
    attended,
    proj_held,
    up_held,
    down_held,
    sems,
    weight_sems,
):
    rows, channels = points.shape
    patches, chosen = pattern.shape
    span = (1 + chosen) * PATCH
    copies = []
    for p in range(patches):
        for j in range(1 + chosen):
            start = p * PATCH if j == 0 else pl.multiple_of(pattern[p, j - 1] * PATCH, PATCH)
            copies.append(
                pltpu.make_async_copy(
                    keyed.at[pl.ds(start, PATCH), :],
                    kv.at[pl.ds(p * span + j * PATCH, PATCH), :],
                    sems.at[p, j],
                )
            )
    for copy in copies:
        copy.start()
    fetches = weight_copies(
        0, (w_proj, w_up, w_down), (proj_held, up_held, down_held), weight_sems
    )
    for fetch in fetches:
        fetch.start()
    masks = head_masks(channels // HEADS)
    for p in range(patches):
        for j in range(1 + chosen):
            copies[p * (1 + chosen) + j].wait()
        attended[p * PATCH : (p + 1) * PATCH, :] = attend_patch(
            queries[p * PATCH : (p + 1) * PATCH, :],
            kv[p * span : (p + 1) * span, :channels],
            kv[p * span : (p + 1) * span, channels:],
            masks,
        )
    first = finish(
        points[...], attended[...], gains[1:2, :], (proj_held, up_held, down_held), fetches
    )
    outgoing[...] = jnp.dot(send[...], first, preferred_element_type=F32).astype(BF16)


def second_kernel(
    pattern,
    incoming,
    place,
    gains,
    w_qkv,
    w_proj,
    w_up,
    w_down,
    w_head,
    features,
    normals,
    kv,
    attended,
    qkv_held,
    proj_held,
    up_held,
    down_held,
    weight_sems,
):
    rows, channels = features.shape
    patches, chosen = pattern.shape
    fetches = weight_copies(
        1, (w_qkv, w_proj, w_up, w_down), (qkv_held, proj_held, up_held, down_held), weight_sems
    )
    for fetch in fetches:
        fetch.start()
    second = jnp.dot(place[...], incoming[...], preferred_element_type=F32).astype(BF16)
    normed = layer_norm(second, gains[2:3, :])
    scale = (channels // HEADS) ** (-0.5)
    fetches[0].wait()
    queries = (
        jnp.dot(normed, qkv_held[:, :channels], preferred_element_type=F32).astype(BF16)
        * BF16(scale)
    ).astype(BF16)
    kv[...] = jnp.dot(normed, qkv_held[:, channels:], preferred_element_type=F32).astype(BF16)
    masks = head_masks(channels // HEADS)
    for p in range(patches):
        pieces = [kv[p * PATCH : (p + 1) * PATCH, :]]
        for j in range(chosen):
            start = pl.multiple_of(pattern[p, j] * PATCH, PATCH)
            pieces.append(kv[pl.ds(start, PATCH), :])
        both = jnp.concatenate(pieces, axis=0)
        attended[p * PATCH : (p + 1) * PATCH, :] = attend_patch(
            queries[p * PATCH : (p + 1) * PATCH, :], both[:, :channels], both[:, channels:], masks
        )
    done = finish(
        second, attended[...], gains[3:4, :], (proj_held, up_held, down_held), fetches[1:]
    )
    features[...] = done
    normals[...] = lax.dot_general(
        w_head[...], done, (((1,), (1,)), ((), ())), preferred_element_type=F32
    )


def held_weights(weights):
    return [pltpu.VMEM(w.shape[1:], BF16) for w in weights]


VMEM_SPEC = pl.BlockSpec(memory_space=pltpu.VMEM)
SMEM_SPEC = pl.BlockSpec(memory_space=pltpu.SMEM)
ANY_SPEC = pl.BlockSpec(memory_space=pl.ANY)


def shards(
    points,
    pattern_first,
    pattern_second,
    destination,
    norm_gains,
    w_qkv,
    w_proj,
    w_up,
    w_down,
    w_head,
):
    rows_here, channels = points.shape
    patches, chosen = pattern_first.shape
    devices = lax.axis_size("grp") * lax.axis_size("seq")
    capacity = 2 * rows_here // devices
    slot_total = devices * capacity

    shards_in_group = lax.axis_size("seq")
    chips = shards_in_group // 2
    onward = [(i, (i + 2) % shards_in_group) for i in range(shards_in_group)]
    swap = [(i, i ^ 1) for i in range(shards_in_group)]
    part = rows_here // RING_PARTS
    column = [points[i * part : (i + 1) * part] for i in range(RING_PARTS)]
    blocks = [column, [lax.ppermute(rows, "seq", swap) for rows in column]]
    for _ in range(1, chips):
        column = [lax.ppermute(rows, "seq", onward) for rows in column]
        blocks += [column, [lax.ppermute(rows, "seq", swap) for rows in column]]

    block_bytes = rows_here * channels * 2
    kv_shape = jax.ShapeDtypeStruct((shards_in_group * rows_here, 2 * channels), BF16)
    kv_scratch = [
        pltpu.VMEM((rows_here, 2 * channels), BF16),
        pltpu.SemaphoreType.DMA((RING_PARTS,)),
    ]
    keyed, queries = pl.pallas_call(
        own_kernel,
        out_shape=(kv_shape, jax.ShapeDtypeStruct((rows_here, channels), BF16)),
        in_specs=[VMEM_SPEC] * (RING_PARTS + 2),
        out_specs=(ANY_SPEC, VMEM_SPEC),
        scratch_shapes=kv_scratch,
        cost_estimate=pl.CostEstimate(
            flops=6 * rows_here * channels**2, bytes_accessed=6 * block_bytes, transcendentals=0
        ),
        compiler_params=pltpu.CompilerParams(vmem_limit_bytes=VMEM_BYTES),
        name="project_own",
    )(*blocks[0], norm_gains, w_qkv)
    for slot in range(1, 2 * chips):
        keyed = pl.pallas_call(
            functools.partial(project_kernel, slot),
            out_shape=kv_shape,
            in_specs=[VMEM_SPEC] * (RING_PARTS + 2) + [ANY_SPEC],
            out_specs=ANY_SPEC,
            scratch_shapes=kv_scratch,
            input_output_aliases={RING_PARTS + 2: 0},
            cost_estimate=pl.CostEstimate(
                flops=4 * rows_here * channels**2, bytes_accessed=5 * block_bytes, transcendentals=0
            ),
            compiler_params=pltpu.CompilerParams(vmem_limit_bytes=VMEM_BYTES),
            name="project",
        )(*blocks[slot], norm_gains, w_qkv, keyed)

    me = lax.axis_index("seq")
    owner = pattern_first // patches
    slot_of = 2 * ((me // 2 - owner // 2) % chips) + (me % 2 != owner % 2).astype(jnp.int32)
    pattern_slots = slot_of * patches + pattern_first % patches

    target = destination // rows_here
    place_at = destination % rows_here
    onehot_dev = (target[:, None] == jnp.arange(devices, dtype=jnp.int32)[None, :]).astype(
        jnp.int32
    )
    earlier = jnp.cumsum(onehot_dev, axis=0) - onehot_dev
    send_rank = jnp.sum(earlier * onehot_dev, axis=1)
    slot_index = target * capacity + send_rank
    row_ids = jnp.arange(rows_here, dtype=jnp.int32)
    slot_ids = jnp.arange(slot_total, dtype=jnp.int32)
    match_send = slot_index[None, :] == slot_ids[:, None]
    send = match_send.astype(BF16)
    out_places = jnp.sum(jnp.where(match_send, place_at[None, :] + 1, 0), axis=1) - 1
    in_places = lax.all_to_all(
        out_places.reshape(devices, capacity),
        ("grp", "seq"),
        split_axis=0,
        concat_axis=0,
        tiled=True,
    ).reshape(-1)
    place = (in_places[None, :] == row_ids[:, None]).astype(BF16)

    weights = (w_qkv, w_proj, w_up, w_down)
    keyed_rows = patches * (1 + chosen) * PATCH
    outgoing = pl.pallas_call(
        first_kernel,
        out_shape=jax.ShapeDtypeStruct((slot_total, channels), BF16),
        in_specs=[SMEM_SPEC, VMEM_SPEC, VMEM_SPEC, ANY_SPEC, VMEM_SPEC]
        + [ANY_SPEC] * 3
        + [VMEM_SPEC],
        out_specs=VMEM_SPEC,
        scratch_shapes=[
            pltpu.VMEM((keyed_rows, 2 * channels), BF16),
            pltpu.VMEM((rows_here, channels), BF16),
            *held_weights(weights[1:]),
            pltpu.SemaphoreType.DMA((patches, 1 + chosen)),
            pltpu.SemaphoreType.DMA((3,)),
        ],
        compiler_params=pltpu.CompilerParams(vmem_limit_bytes=VMEM_BYTES),
        name="block_first",
    )(pattern_slots, points, queries, keyed, norm_gains, *weights[1:], send)

    incoming = lax.all_to_all(
        outgoing.reshape(devices, capacity, channels),
        ("grp", "seq"),
        split_axis=0,
        concat_axis=0,
        tiled=True,
    ).reshape(slot_total, channels)

    return pl.pallas_call(
        second_kernel,
        out_shape=(
            jax.ShapeDtypeStruct((rows_here, channels), BF16),
            jax.ShapeDtypeStruct((w_head.shape[0], rows_here), F32),
        ),
        in_specs=[SMEM_SPEC, VMEM_SPEC, VMEM_SPEC, VMEM_SPEC]
        + [ANY_SPEC] * len(weights)
        + [VMEM_SPEC],
        out_specs=(VMEM_SPEC, VMEM_SPEC),
        scratch_shapes=[
            pltpu.VMEM((rows_here, 2 * channels), BF16),
            pltpu.VMEM((rows_here, channels), BF16),
            *held_weights(weights),
            pltpu.SemaphoreType.DMA((len(weights),)),
        ],
        compiler_params=pltpu.CompilerParams(vmem_limit_bytes=VMEM_BYTES),
        name="block_second",
    )(pattern_second, incoming, place, norm_gains, *weights, w_head)


def solution(mesh):
    placed = (
        P(("grp", "seq"), None),
        P(("grp", "seq"), None),
        P(("grp", "seq"), None),
        P(("grp", "seq")),
        P(),
        P(),
        P(),
        P(),
        P(),
        P(),
    )
    return jax.shard_map(
        shards,
        mesh=mesh,
        in_specs=placed,
        out_specs=(P(("grp", "seq"), None), P(None, ("grp", "seq"))),
        check_vma=False,
    )
```

```python
import functools

import jax
import jax.numpy as jnp
from jax import lax
from jax.experimental import pallas as pl
from jax.experimental.pallas import tpu as pltpu
from jax.sharding import PartitionSpec as P

HEADS = 8
PATCH = 64
HEADS_TOGETHER = 4
RING_PARTS = 2
VMEM_BYTES = 32 * 1024 * 1024
RING_BYTES = 16 * 1024 * 1024
F32 = jnp.float32
BF16 = jnp.bfloat16


def layer_norm(rows, gains):
    values = rows.astype(F32)
    average = jnp.mean(values, axis=-1, keepdims=True)
    spread = jnp.mean((values - average) ** 2, axis=-1, keepdims=True)
    return ((values - average) * lax.rsqrt(spread + 1e-05) * gains).astype(BF16)


def gelu(x):
    half = 0.5 * x
    return half + half * lax.erf(x * 0.5**0.5)


def head_masks(head_dim):
    lane = lax.broadcasted_iota(jnp.int32, (PATCH, HEADS_TOGETHER * head_dim), 1)
    return [
        jnp.where((lane >= h * head_dim) & (lane < (h + 1) * head_dim), 1.0, 0.0).astype(F32)
        for h in range(HEADS_TOGETHER)
    ]


def attend_patch(queries, key_rows, value_rows, masks):
    channels = queries.shape[1]
    width = HEADS_TOGETHER * (channels // HEADS)
    sides = []
    for at in range(0, channels, width):
        q = queries[:, at : at + width]
        stacked = jnp.concatenate([q * mask.astype(BF16) for mask in masks], axis=0)
        scores = lax.dot_general(
            stacked,
            key_rows[:, at : at + width],
            (((1,), (1,)), ((), ())),
            preferred_element_type=F32,
        )
        top = jnp.max(scores, axis=-1, keepdims=True)
        grown = jnp.exp(scores - top)
        total = jnp.sum(grown, axis=-1, keepdims=True)
        weights = (grown * (1.0 / total)).astype(BF16)
        mixed = jnp.dot(weights, value_rows[:, at : at + width], preferred_element_type=F32)
        side = mixed[:PATCH] * masks[0]
        for h in range(1, HEADS_TOGETHER):
            side = side + mixed[h * PATCH : (h + 1) * PATCH] * masks[h]
        sides.append(side.astype(BF16))
    return jnp.concatenate(sides, axis=1)


def finish(rows, attended, gain, w_proj, w_up, w_down):
    first = (
        rows.astype(F32) + jnp.dot(attended, w_proj[...], preferred_element_type=F32)
    ).astype(BF16)
    hidden = layer_norm(first, gain)
    total = first.astype(F32)
    piece = 512
    for at in range(0, w_up.shape[1], piece):
        upper = jnp.dot(hidden, w_up[:, at : at + piece], preferred_element_type=F32)
        act = gelu(upper).astype(BF16)
        total = total + jnp.dot(act, w_down[at : at + piece, :], preferred_element_type=F32)
    return total.astype(BF16)


def project_rows(parts, first_row, gains, w_qkv, whole):
    channels = w_qkv.shape[1]
    rows = parts[0].shape[0]
    all_normed = []
    for i, part in enumerate(parts):
        normed = layer_norm(part[...], gains[0:1, :])
        whole[first_row + i * rows : first_row + (i + 1) * rows, :] = jnp.dot(
            normed, w_qkv[0, :, channels:], preferred_element_type=F32
        ).astype(BF16)
        all_normed.append(normed)
    return all_normed


def project_kernel(first_row, *refs):
    *parts, gains, w_qkv, _, whole = refs
    project_rows(parts, first_row, gains, w_qkv, whole)


def own_kernel(*refs):
    *parts, gains, w_qkv, whole, queries = refs
    channels = w_qkv.shape[1]
    rows = parts[0].shape[0]
    scale = (channels // HEADS) ** (-0.5)
    for i, normed in enumerate(project_rows(parts, 0, gains, w_qkv, whole)):
        own = jnp.dot(normed, w_qkv[0, :, :channels], preferred_element_type=F32).astype(BF16)
        queries[i * rows : (i + 1) * rows, :] = (own * BF16(scale)).astype(BF16)


def first_kernel(
    pattern,
    points,
    queries,
    keyed,
    gains,
    w_proj,
    w_up,
    w_down,
    send,
    outgoing,
    attended,
):
    channels = points.shape[1]
    patches, chosen = pattern.shape
    masks = head_masks(channels // HEADS)
    for p in range(patches):
        pieces = [keyed[p * PATCH : (p + 1) * PATCH, :]]
        for j in range(chosen):
            start = pl.multiple_of(pattern[p, j] * PATCH, PATCH)
            pieces.append(keyed[pl.ds(start, PATCH), :])
        both = jnp.concatenate(pieces, axis=0)
        attended[p * PATCH : (p + 1) * PATCH, :] = attend_patch(
            queries[p * PATCH : (p + 1) * PATCH, :], both[:, :channels], both[:, channels:], masks
        )
    first = finish(
        points[...], attended[...], gains[1:2, :], w_proj.at[0], w_up.at[0], w_down.at[0]
    )
    outgoing[...] = jnp.dot(send[...], first, preferred_element_type=F32).astype(BF16)


def second_kernel(
    pattern,
    incoming,
    place,
    gains,
    w_qkv,
    w_proj,
    w_up,
    w_down,
    w_head,
    features,
    normals,
    kv,
    attended,
):
    channels = features.shape[1]
    patches, chosen = pattern.shape
    second = jnp.dot(place[...], incoming[...], preferred_element_type=F32).astype(BF16)
    normed = layer_norm(second, gains[2:3, :])
    scale = (channels // HEADS) ** (-0.5)
    queries = (
        jnp.dot(normed, w_qkv[1, :, :channels], preferred_element_type=F32).astype(BF16)
        * BF16(scale)
    ).astype(BF16)
    kv[...] = jnp.dot(normed, w_qkv[1, :, channels:], preferred_element_type=F32).astype(BF16)
    masks = head_masks(channels // HEADS)
    for p in range(patches):
        pieces = [kv[p * PATCH : (p + 1) * PATCH, :]]
        for j in range(chosen):
            start = pl.multiple_of(pattern[p, j] * PATCH, PATCH)
            pieces.append(kv[pl.ds(start, PATCH), :])
        both = jnp.concatenate(pieces, axis=0)
        attended[p * PATCH : (p + 1) * PATCH, :] = attend_patch(
            queries[p * PATCH : (p + 1) * PATCH, :], both[:, :channels], both[:, channels:], masks
        )
    done = finish(
        second, attended[...], gains[3:4, :], w_proj.at[1], w_up.at[1], w_down.at[1]
    )
    features[...] = done
    normals[...] = lax.dot_general(
        w_head[...], done, (((1,), (1,)), ((), ())), preferred_element_type=F32
    )


VMEM_SPEC = pl.BlockSpec(memory_space=pltpu.VMEM)
SMEM_SPEC = pl.BlockSpec(memory_space=pltpu.SMEM)


def shards(
    points,
    pattern_first,
    pattern_second,
    destination,
    norm_gains,
    w_qkv,
    w_proj,
    w_up,
    w_down,
    w_head,
):
    rows_here, channels = points.shape
    patches, chosen = pattern_first.shape
    devices = lax.axis_size("grp") * lax.axis_size("seq")
    capacity = 2 * rows_here // devices
    slot_total = devices * capacity

    shards_in_group = lax.axis_size("seq")
    chips = shards_in_group // 2
    onward = [(i, (i + 2) % shards_in_group) for i in range(shards_in_group)]
    swap = [(i, i ^ 1) for i in range(shards_in_group)]
    ring = shards_in_group * rows_here * 2 * channels * 2 <= RING_BYTES
    kept_rows = shards_in_group * rows_here if ring else patches * (1 + chosen) * PATCH
    part = rows_here // RING_PARTS
    column = [points[i * part : (i + 1) * part] for i in range(RING_PARTS)]

    block_bytes = rows_here * channels * 2
    kv_shape = jax.ShapeDtypeStruct((kept_rows, 2 * channels), BF16)

    def project(keyed, slot, parts):
        return pl.pallas_call(
            functools.partial(project_kernel, slot * rows_here),
            out_shape=kv_shape,
            in_specs=[VMEM_SPEC] * (len(parts) + 3),
            out_specs=VMEM_SPEC,
            input_output_aliases={len(parts) + 2: 0},
            cost_estimate=pl.CostEstimate(
                flops=4 * rows_here * channels**2 * len(parts) // RING_PARTS,
                bytes_accessed=5 * block_bytes * len(parts) // RING_PARTS,
                transcendentals=0,
            ),
            compiler_params=pltpu.CompilerParams(vmem_limit_bytes=VMEM_BYTES),
            name="project",
        )(*parts, norm_gains, w_qkv, keyed)

    keyed, queries = pl.pallas_call(
        own_kernel,
        out_shape=(kv_shape, jax.ShapeDtypeStruct((rows_here, channels), BF16)),
        in_specs=[VMEM_SPEC] * (RING_PARTS + 2),
        out_specs=(VMEM_SPEC, VMEM_SPEC),
        cost_estimate=pl.CostEstimate(
            flops=6 * rows_here * channels**2, bytes_accessed=6 * block_bytes, transcendentals=0
        ),
        compiler_params=pltpu.CompilerParams(vmem_limit_bytes=VMEM_BYTES),
        name="project_own",
    )(*column, norm_gains, w_qkv)
    me = lax.axis_index("seq")
    if ring:
        beside = [lax.ppermute(rows, "seq", swap) for rows in column]
        waiting = [(1, beside)]
        for step in range(1, chips):
            column = [lax.ppermute(rows, "seq", onward) for rows in column]
            for slot, parts in waiting:
                keyed = project(keyed, slot, parts)
            column, keyed = lax.optimization_barrier((column, keyed))
            beside = [lax.ppermute(rows, "seq", swap) for rows in column]
            waiting = [(2 * step, column), (2 * step + 1, beside)]
        for slot, parts in waiting:
            keyed = project(keyed, slot, parts)
        owner = pattern_first // patches
        slot_of = 2 * ((me // 2 - owner // 2) % chips) + (me % 2 != owner % 2).astype(jnp.int32)
        pattern_slots = slot_of * patches + pattern_first % patches
    else:
        group = lax.all_gather(points, "seq", axis=0, tiled=True)
        picked = group.reshape(-1, PATCH, channels)[pattern_first].reshape(-1, channels)
        keyed = project(keyed, 1, [picked])
        pattern_slots = patches + jnp.arange(patches * chosen, dtype=jnp.int32).reshape(
            patches, chosen
        )

    target = destination // rows_here
    place_at = destination % rows_here
    onehot_dev = (target[:, None] == jnp.arange(devices, dtype=jnp.int32)[None, :]).astype(
        jnp.int32
    )
    earlier = jnp.cumsum(onehot_dev, axis=0) - onehot_dev
    send_rank = jnp.sum(earlier * onehot_dev, axis=1)
    slot_index = target * capacity + send_rank
    row_ids = jnp.arange(rows_here, dtype=jnp.int32)
    slot_ids = jnp.arange(slot_total, dtype=jnp.int32)
    match_send = slot_index[None, :] == slot_ids[:, None]
    send = match_send.astype(BF16)
    out_places = jnp.sum(jnp.where(match_send, place_at[None, :] + 1, 0), axis=1) - 1
    in_places = lax.all_to_all(
        out_places.reshape(devices, capacity),
        ("grp", "seq"),
        split_axis=0,
        concat_axis=0,
        tiled=True,
    ).reshape(-1)
    place = (in_places[None, :] == row_ids[:, None]).astype(BF16)

    weights = (w_proj, w_up, w_down)
    outgoing = pl.pallas_call(
        first_kernel,
        out_shape=jax.ShapeDtypeStruct((slot_total, channels), BF16),
        in_specs=[SMEM_SPEC] + [VMEM_SPEC] * 8,
        out_specs=VMEM_SPEC,
        scratch_shapes=[pltpu.VMEM((rows_here, channels), BF16)],
        compiler_params=pltpu.CompilerParams(vmem_limit_bytes=VMEM_BYTES),
        name="block_first",
    )(pattern_slots, points, queries, keyed, norm_gains, *weights, send)

    incoming = lax.all_to_all(
        outgoing.reshape(devices, capacity, channels),
        ("grp", "seq"),
        split_axis=0,
        concat_axis=0,
        tiled=True,
    ).reshape(slot_total, channels)

    return pl.pallas_call(
        second_kernel,
        out_shape=(
            jax.ShapeDtypeStruct((rows_here, channels), BF16),
            jax.ShapeDtypeStruct((w_head.shape[0], rows_here), F32),
        ),
        in_specs=[SMEM_SPEC] + [VMEM_SPEC] * 8,
        out_specs=(VMEM_SPEC, VMEM_SPEC),
        scratch_shapes=[
            pltpu.VMEM((rows_here, 2 * channels), BF16),
            pltpu.VMEM((rows_here, channels), BF16),
        ],
        compiler_params=pltpu.CompilerParams(vmem_limit_bytes=VMEM_BYTES),
        name="block_second",
    )(pattern_second, incoming, place, norm_gains, w_qkv, *weights, w_head)


def solution(mesh):
    placed = (
        P(("grp", "seq"), None),
        P(("grp", "seq"), None),
        P(("grp", "seq"), None),
        P(("grp", "seq")),
        P(),
        P(),
        P(),
        P(),
        P(),
        P(),
    )
    return jax.shard_map(
        shards,
        mesh=mesh,
        in_specs=placed,
        out_specs=(P(("grp", "seq"), None), P(None, ("grp", "seq"))),
        check_vma=False,
    )
```

```python
import functools

import jax
import jax.numpy as jnp
from jax import lax
from jax.experimental import pallas as pl
from jax.experimental.pallas import tpu as pltpu
from jax.sharding import PartitionSpec as P

HEADS = 8
PATCH = 64
HEADS_TOGETHER = 4
RING_PARTS = 2
SEND_PARTS = 4
FIRST_BYTES = 28 * 1024 * 1024
SECOND_BYTES = 50 * 1024 * 1024
PROJECT_BYTES = 16 * 1024 * 1024
OWN_BYTES = 16 * 1024 * 1024
NORMALIZE_BYTES = 60 * 1024 * 1024
RING_BYTES = 16 * 1024 * 1024
F32 = jnp.float32
BF16 = jnp.bfloat16


def layer_norm(rows, gains):
    values = rows.astype(F32)
    average = jnp.mean(values, axis=-1, keepdims=True)
    spread = jnp.mean((values - average) ** 2, axis=-1, keepdims=True)
    return ((values - average) * lax.rsqrt(spread + 1e-05) * gains).astype(BF16)


def gelu(x):
    half = 0.5 * x
    return half + half * lax.erf(x * 0.5**0.5)


def head_masks(head_dim):
    lane = lax.broadcasted_iota(jnp.int32, (PATCH, HEADS_TOGETHER * head_dim), 1)
    return [
        jnp.where((lane >= h * head_dim) & (lane < (h + 1) * head_dim), 1.0, 0.0).astype(F32)
        for h in range(HEADS_TOGETHER)
    ]


def attend_patch(queries, key_rows, value_rows, masks):
    channels = queries.shape[1]
    width = HEADS_TOGETHER * (channels // HEADS)
    sides = []
    for at in range(0, channels, width):
        q = queries[:, at : at + width]
        stacked = jnp.concatenate([q * mask.astype(BF16) for mask in masks], axis=0)
        scores = lax.dot_general(
            stacked,
            key_rows[:, at : at + width],
            (((1,), (1,)), ((), ())),
            preferred_element_type=F32,
        )
        top = jnp.max(scores, axis=-1, keepdims=True)
        grown = jnp.exp(scores - top)
        total = jnp.sum(grown, axis=-1, keepdims=True)
        weights = (grown * (1.0 / total)).astype(BF16)
        mixed = jnp.dot(weights, value_rows[:, at : at + width], preferred_element_type=F32)
        side = mixed[:PATCH] * masks[0]
        for h in range(1, HEADS_TOGETHER):
            side = side + mixed[h * PATCH : (h + 1) * PATCH] * masks[h]
        sides.append(side.astype(BF16))
    return jnp.concatenate(sides, axis=1)


def one_hot_rows(places, rows):
    row = lax.broadcasted_iota(jnp.int32, (rows, places.shape[1]), 0)
    return jnp.where(row == places, 1.0, 0.0).astype(BF16)


def started(pairs, sems):
    copies = [
        pltpu.make_async_copy(source, place, sems.at[at])
        for at, (source, place) in enumerate(pairs)
    ]
    for copy in copies:
        copy.start()
    return copies


def finish(rows, attended, gain, held, copies=()):
    w_proj, w_up, w_down = held
    for copy in copies[:1]:
        copy.wait()
    first = (
        rows.astype(F32) + jnp.dot(attended, w_proj[...], preferred_element_type=F32)
    ).astype(BF16)
    hidden = layer_norm(first, gain)
    total = first.astype(F32)
    for copy in copies[1:]:
        copy.wait()
    piece = 512
    for at in range(0, w_up.shape[1], piece):
        upper = jnp.dot(hidden, w_up[:, at : at + piece], preferred_element_type=F32)
        act = gelu(upper).astype(BF16)
        total = total + jnp.dot(act, w_down[at : at + piece, :], preferred_element_type=F32)
    return total.astype(BF16)


def normalize_kernel(points, gains, *refs):
    *parts, held, gains_held, sems = refs
    rows = parts[0].shape[0]
    fetch, *copies = started(
        [(gains, gains_held)]
        + [(points.at[pl.ds(i * rows, rows), :], held.at[i]) for i in range(len(parts))],
        sems,
    )
    fetch.wait()
    for i, part in enumerate(parts):
        copies[i].wait()
        part[...] = layer_norm(held[i], gains_held[0:1, :])


def project_kernel(first_rows, *refs):
    count = len(first_rows)
    parts, w_qkv, whole = refs[:count], refs[count], refs[count + 2]
    held, held_w, sems = refs[count + 3 :]
    channels = w_qkv.shape[1]
    rows = held.shape[1]
    fetch, *copies = started(
        [(w_qkv.at[0, :, pl.ds(channels, 2 * channels)], held_w)]
        + [(part, held.at[i]) for i, part in enumerate(parts)],
        sems,
    )
    fetch.wait()
    for i, first in enumerate(first_rows):
        copies[i].wait()
        whole[first : first + rows, :] = jnp.dot(
            held[i], held_w[...], preferred_element_type=F32
        ).astype(BF16)


def own_kernel(first_rows, *refs):
    count = len(first_rows)
    parts, w_qkv, others = refs[:count], refs[count], refs[count + 1 : count + 4]
    whole, queries, *kept = refs[count + 4 : count + 9]
    held, held_w, sems, kept_sems = refs[count + 9 :]
    channels = w_qkv.shape[1]
    rows = held.shape[1]
    scale = (channels // HEADS) ** (-0.5)
    fetch, *copies = started(
        [(w_qkv.at[0], held_w)] + [(part, held.at[i]) for i, part in enumerate(parts)], sems
    )
    keeping = started([(w.at[0], place) for w, place in zip(others, kept)], kept_sems)
    fetch.wait()
    for i, first in enumerate(first_rows):
        copies[i].wait()
        whole[first : first + rows, :] = jnp.dot(
            held[i], held_w[:, channels:], preferred_element_type=F32
        ).astype(BF16)
        if i * rows < queries.shape[0]:
            own = jnp.dot(held[i], held_w[:, :channels], preferred_element_type=F32).astype(BF16)
            queries[i * rows : (i + 1) * rows, :] = (own * BF16(scale)).astype(BF16)
    for copy in keeping:
        copy.wait()


def first_kernel(
    pattern,
    slot_of_row,
    gains,
    keyed,
    queries,
    points,
    w_proj,
    w_up,
    w_down,
    outgoing,
    attended,
    points_held,
    gains_held,
    slots_held,
    outgoing_held,
    sems,
):
    rows, channels = points.shape
    patches = rows // PATCH
    chosen = pattern.shape[0] // patches
    copies = started(
        [
            (points, points_held),
            (gains, gains_held),
            (slot_of_row, slots_held),
        ],
        sems,
    )
    masks = head_masks(channels // HEADS)
    for p in range(patches):
        pieces = [keyed[p * PATCH : (p + 1) * PATCH, :]]
        for j in range(chosen):
            start = pl.multiple_of(pattern[p * chosen + j] * PATCH, PATCH)
            pieces.append(keyed[pl.ds(start, PATCH), :])
        both = jnp.concatenate(pieces, axis=0)
        attended[p * PATCH : (p + 1) * PATCH, :] = attend_patch(
            queries[p * PATCH : (p + 1) * PATCH, :],
            both[:, :channels],
            both[:, channels:],
            masks,
        )
    for copy in copies:
        copy.wait()
    first = finish(
        points_held[...], attended[...], gains_held[1:2, :], (w_proj, w_up, w_down)
    )
    slots = slots_held[...]
    piece = outgoing.shape[0] // SEND_PARTS
    leaving = []
    for i in range(SEND_PARTS):
        here = pl.ds(i * piece, piece)
        send = one_hot_rows(slots - i * piece, piece)
        outgoing_held[here, :] = jnp.dot(send, first, preferred_element_type=F32).astype(BF16)
        leaving.append(
            pltpu.make_async_copy(
                outgoing_held.at[here, :], outgoing.at[here, :], sems.at[len(copies) + i]
            )
        )
        leaving[-1].start()
    for copy in leaving:
        copy.wait()


def second_kernel(
    pattern,
    slot_places,
    gains,
    incoming,
    w_qkv,
    w_proj,
    w_up,
    w_down,
    w_head,
    features,
    normals,
    kv,
    attended,
    incoming_held,
    qkv_held,
    proj_held,
    up_held,
    down_held,
    gains_held,
    places_held,
    head_held,
    sems,
):
    rows, channels = features.shape
    patches = rows // PATCH
    chosen = pattern.shape[0] // patches
    small = started(
        [(slot_places, places_held), (gains, gains_held), (w_head, head_held)], sems.at[1]
    )
    copies = started(
        [
            (incoming, incoming_held),
            (w_qkv.at[1], qkv_held),
            (w_proj.at[1], proj_held),
            (w_up.at[1], up_held),
            (w_down.at[1], down_held),
        ],
        sems.at[0],
    )
    for copy in small:
        copy.wait()
    place = one_hot_rows(places_held[...], rows)
    copies[0].wait()
    second = jnp.dot(place, incoming_held[...], preferred_element_type=F32).astype(BF16)
    normed = layer_norm(second, gains_held[2:3, :])
    scale = (channels // HEADS) ** (-0.5)
    copies[1].wait()
    queries = (
        jnp.dot(normed, qkv_held[:, :channels], preferred_element_type=F32).astype(BF16)
        * BF16(scale)
    ).astype(BF16)
    kv[...] = jnp.dot(normed, qkv_held[:, channels:], preferred_element_type=F32).astype(BF16)
    masks = head_masks(channels // HEADS)
    for p in range(patches):
        pieces = [kv[p * PATCH : (p + 1) * PATCH, :]]
        for j in range(chosen):
            start = pl.multiple_of(pattern[p * chosen + j] * PATCH, PATCH)
            pieces.append(kv[pl.ds(start, PATCH), :])
        both = jnp.concatenate(pieces, axis=0)
        attended[p * PATCH : (p + 1) * PATCH, :] = attend_patch(
            queries[p * PATCH : (p + 1) * PATCH, :], both[:, :channels], both[:, channels:], masks
        )
    done = finish(
        second, attended[...], gains_held[3:4, :], (proj_held, up_held, down_held), copies[2:]
    )
    features[...] = done
    normals[...] = lax.dot_general(
        head_held[...], done, (((1,), (1,)), ((), ())), preferred_element_type=F32
    )


VMEM_SPEC = pl.BlockSpec(memory_space=pltpu.VMEM)
SMEM_SPEC = pl.BlockSpec(memory_space=pltpu.SMEM)
ANY_SPEC = pl.BlockSpec(memory_space=pl.ANY)


def shards(
    points,
    pattern_first,
    pattern_second,
    destination,
    norm_gains,
    w_qkv,
    w_proj,
    w_up,
    w_down,
    w_head,
):
    rows_here, channels = points.shape
    patches, chosen = pattern_first.shape
    devices = lax.axis_size("grp") * lax.axis_size("seq")
    capacity = 2 * rows_here // devices
    slot_total = devices * capacity

    shards_in_group = lax.axis_size("seq")
    chips = shards_in_group // 2
    onward = [(i, (i + 2) % shards_in_group) for i in range(shards_in_group)]
    swap = [(i, i ^ 1) for i in range(shards_in_group)]
    ring = shards_in_group * rows_here * 2 * channels * 2 <= RING_BYTES
    kept_rows = shards_in_group * rows_here if ring else patches * (1 + chosen) * PATCH
    part = rows_here // RING_PARTS
    part_bytes = part * channels * 2

    column = pl.pallas_call(
        normalize_kernel,
        out_shape=[jax.ShapeDtypeStruct((part, channels), BF16)] * RING_PARTS,
        in_specs=[ANY_SPEC, ANY_SPEC],
        out_specs=[VMEM_SPEC] * RING_PARTS,
        scratch_shapes=[
            pltpu.VMEM((RING_PARTS, part, channels), BF16),
            pltpu.VMEM(norm_gains.shape, F32),
            pltpu.SemaphoreType.DMA((1 + RING_PARTS,)),
        ],
        compiler_params=pltpu.CompilerParams(vmem_limit_bytes=NORMALIZE_BYTES),
        name="normalize",
    )(points, norm_gains)

    weights = (w_proj, w_up, w_down)
    kv_shape = jax.ShapeDtypeStruct((kept_rows, 2 * channels), BF16)

    def project(keyed, blocks):
        parts = [rows for _, block in blocks for rows in block]
        count = len(parts)
        rows = parts[0].shape[0]
        first_rows = [
            slot * rows_here + i * rows for slot, block in blocks for i in range(len(block))
        ]
        own = keyed is None
        own_shapes = [jax.ShapeDtypeStruct((rows_here, channels), BF16)]
        own_shapes += [jax.ShapeDtypeStruct(w.shape[1:], BF16) for w in weights]
        return pl.pallas_call(
            functools.partial(own_kernel if own else project_kernel, first_rows),
            out_shape=[kv_shape] + own_shapes if own else kv_shape,
            in_specs=[ANY_SPEC] * (count + 1) + ([ANY_SPEC] * 3 if own else [VMEM_SPEC]),
            out_specs=[VMEM_SPEC] * 5 if own else VMEM_SPEC,
            scratch_shapes=[
                pltpu.VMEM((count, rows, channels), BF16),
                pltpu.VMEM((channels, (3 if own else 2) * channels), BF16),
                pltpu.SemaphoreType.DMA((count + 1,)),
            ]
            + ([pltpu.SemaphoreType.DMA((3,))] if own else []),
            input_output_aliases={} if own else {count + 1: 0},
            cost_estimate=pl.CostEstimate(
                flops=4 * count * rows * channels**2,
                bytes_accessed=3 * count * rows * channels * 2 + 3 * channels**2 * 2,
                transcendentals=0,
            ),
            compiler_params=pltpu.CompilerParams(
                vmem_limit_bytes=OWN_BYTES if own else PROJECT_BYTES
            ),
            name="project_own" if own else "project",
        )(*parts, w_qkv, *(weights if own else [keyed]))

    target = destination // rows_here
    place_at = destination % rows_here
    onehot_dev = (target[:, None] == jnp.arange(devices, dtype=jnp.int32)[None, :]).astype(
        jnp.int32
    )
    earlier = jnp.cumsum(onehot_dev, axis=0) - onehot_dev
    send_rank = jnp.sum(earlier * onehot_dev, axis=1)
    slot_index = target * capacity + send_rank
    slot_ids = jnp.arange(slot_total, dtype=jnp.int32)
    match_send = slot_index[None, :] == slot_ids[:, None]
    out_places = jnp.sum(jnp.where(match_send, place_at[None, :] + 1, 0), axis=1) - 1
    in_places = lax.all_to_all(
        out_places.reshape(devices, capacity),
        ("grp", "seq"),
        split_axis=0,
        concat_axis=0,
        tiled=True,
    ).reshape(1, slot_total)
    slot_index = slot_index.reshape(1, rows_here)

    pattern_second = pattern_second.reshape(-1)
    me = lax.axis_index("seq")
    if ring:
        owner = pattern_first // patches
        slot_of = 2 * ((me // 2 - owner // 2) % chips) + (me % 2 != owner % 2).astype(jnp.int32)
        pattern_slots = (slot_of * patches + pattern_first % patches).reshape(-1)
    else:
        pattern_slots = patches + jnp.arange(patches * chosen, dtype=jnp.int32)

    if ring:
        beside = [lax.ppermute(rows, "seq", swap) for rows in column]
        waiting = [(0, column), (1, beside)]
        keyed = None
        for step in range(1, chips):
            column = [lax.ppermute(rows, "seq", onward) for rows in column]
            if step == 1:
                tied = (column, waiting[0][1], beside, pattern_slots, pattern_second, slot_index)
                tied, in_places = lax.optimization_barrier((tied, in_places))
                column, own, beside, pattern_slots, pattern_second, slot_index = tied
                waiting = [(0, own), (1, beside)]
            elif step == 2:
                keyed, queries, *kept = project(None, waiting)
                waiting = []
            else:
                keyed = project(keyed, waiting)
                waiting = []
            if step > 1:
                column, keyed = lax.optimization_barrier((column, keyed))
            beside = [lax.ppermute(rows, "seq", swap) for rows in column]
            waiting = waiting + [(2 * step, column), (2 * step + 1, beside)]
        for block in waiting:
            keyed = project(keyed, [block])
    else:
        group = lax.all_gather(jnp.concatenate(column), "seq", axis=0, tiled=True)
        picked = group.reshape(-1, PATCH, channels)[pattern_first].reshape(-1, channels)
        keyed, queries, *kept = project(None, [(0, column)])
        keyed = project(keyed, [(1, [picked])])

    held_weights = [pltpu.VMEM(w.shape[1:], BF16) for w in weights]
    held_rows = pltpu.VMEM((rows_here, channels), BF16)
    outgoing = pl.pallas_call(
        first_kernel,
        out_shape=jax.ShapeDtypeStruct((slot_total, channels), BF16),
        in_specs=[SMEM_SPEC, ANY_SPEC, ANY_SPEC, VMEM_SPEC, VMEM_SPEC, ANY_SPEC]
        + [VMEM_SPEC] * 3,
        out_specs=ANY_SPEC,
        scratch_shapes=[
            held_rows,
            held_rows,
            pltpu.VMEM(norm_gains.shape, F32),
            pltpu.VMEM(slot_index.shape, jnp.int32),
            pltpu.VMEM((slot_total, channels), BF16),
            pltpu.SemaphoreType.DMA((3 + SEND_PARTS,)),
        ],
        compiler_params=pltpu.CompilerParams(vmem_limit_bytes=FIRST_BYTES),
        name="block_first",
    )(pattern_slots, slot_index, norm_gains, keyed, queries, points, *kept)

    incoming = lax.all_to_all(
        outgoing.reshape(devices, capacity, channels),
        ("grp", "seq"),
        split_axis=0,
        concat_axis=0,
        tiled=True,
    ).reshape(slot_total, channels)

    return pl.pallas_call(
        second_kernel,
        out_shape=(
            jax.ShapeDtypeStruct((rows_here, channels), BF16),
            jax.ShapeDtypeStruct((w_head.shape[0], rows_here), F32),
        ),
        in_specs=[SMEM_SPEC] + [ANY_SPEC] * 8,
        out_specs=(VMEM_SPEC, VMEM_SPEC),
        scratch_shapes=[
            pltpu.VMEM((rows_here, 2 * channels), BF16),
            held_rows,
            pltpu.VMEM((slot_total, channels), BF16),
            pltpu.VMEM(w_qkv.shape[1:], BF16),
            *held_weights,
            pltpu.VMEM(norm_gains.shape, F32),
            pltpu.VMEM(in_places.shape, jnp.int32),
            pltpu.VMEM(w_head.shape, BF16),
            pltpu.SemaphoreType.DMA((2, 5)),
        ],
        compiler_params=pltpu.CompilerParams(vmem_limit_bytes=SECOND_BYTES),
        name="block_second",
    )(pattern_second, in_places, norm_gains, incoming, w_qkv, *weights, w_head)


def solution(mesh):
    placed = (
        P(("grp", "seq"), None),
        P(("grp", "seq"), None),
        P(("grp", "seq"), None),
        P(("grp", "seq")),
        P(),
        P(),
        P(),
        P(),
        P(),
        P(),
    )
    return jax.shard_map(
        shards,
        mesh=mesh,
        in_specs=placed,
        out_specs=(P(("grp", "seq"), None), P(None, ("grp", "seq"))),
        check_vma=False,
    )
```

```python
import functools

import jax
import jax.numpy as jnp
from jax import lax
from jax.experimental import pallas as pl
from jax.experimental.pallas import tpu as pltpu
from jax.sharding import PartitionSpec as P

HEADS = 8
PATCH = 64
HEADS_TOGETHER = 4
RING_PARTS = 2
SEND_PARTS = 4
LANES = 128
TAIL = 8
DIGIT = 256
FIRST_BYTES = 28 * 1024 * 1024
SECOND_BYTES = 50 * 1024 * 1024
PROJECT_BYTES = 16 * 1024 * 1024
NORMALIZE_BYTES = 60 * 1024 * 1024
RING_BYTES = 16 * 1024 * 1024
F32 = jnp.float32
BF16 = jnp.bfloat16


def layer_norm(rows, gains):
    values = rows.astype(F32)
    average = jnp.mean(values, axis=-1, keepdims=True)
    spread = jnp.mean((values - average) ** 2, axis=-1, keepdims=True)
    return ((values - average) * lax.rsqrt(spread + 1e-05) * gains).astype(BF16)


def gelu(x):
    half = 0.5 * x
    return half + half * lax.erf(x * 0.5**0.5)


def head_masks(head_dim):
    lane = lax.broadcasted_iota(jnp.int32, (PATCH, HEADS_TOGETHER * head_dim), 1)
    return [
        jnp.where((lane >= h * head_dim) & (lane < (h + 1) * head_dim), 1.0, 0.0).astype(F32)
        for h in range(HEADS_TOGETHER)
    ]


def attend_patch(queries, key_rows, value_rows, masks):
    channels = queries.shape[1]
    width = HEADS_TOGETHER * (channels // HEADS)
    sides = []
    for at in range(0, channels, width):
        q = queries[:, at : at + width]
        stacked = jnp.concatenate([q * mask.astype(BF16) for mask in masks], axis=0)
        scores = lax.dot_general(
            stacked,
            key_rows[:, at : at + width],
            (((1,), (1,)), ((), ())),
            preferred_element_type=F32,
        )
        top = jnp.max(scores, axis=-1, keepdims=True)
        grown = jnp.exp(scores - top)
        total = jnp.sum(grown, axis=-1, keepdims=True)
        weights = (grown * (1.0 / total)).astype(BF16)
        mixed = jnp.dot(weights, value_rows[:, at : at + width], preferred_element_type=F32)
        side = mixed[:PATCH] * masks[0]
        for h in range(1, HEADS_TOGETHER):
            side = side + mixed[h * PATCH : (h + 1) * PATCH] * masks[h]
        sides.append(side.astype(BF16))
    return jnp.concatenate(sides, axis=1)


def one_hot_rows(places, rows):
    row = lax.broadcasted_iota(jnp.int32, (rows, places.shape[1]), 0)
    return jnp.where(row == places, 1.0, 0.0).astype(BF16)


def started(pairs, sems):
    copies = [
        pltpu.make_async_copy(source, place, sems.at[at])
        for at, (source, place) in enumerate(pairs)
    ]
    for copy in copies:
        copy.start()
    return copies


def finish(rows, attended, gain, held, copies=()):
    w_proj, w_up, w_down = held
    for copy in copies[:1]:
        copy.wait()
    first = (
        rows.astype(F32) + jnp.dot(attended, w_proj[...], preferred_element_type=F32)
    ).astype(BF16)
    hidden = layer_norm(first, gain)
    total = first.astype(F32)
    for copy in copies[1:]:
        copy.wait()
    piece = 512
    for at in range(0, w_up.shape[1], piece):
        upper = jnp.dot(hidden, w_up[:, at : at + piece], preferred_element_type=F32)
        act = gelu(upper).astype(BF16)
        total = total + jnp.dot(act, w_down[at : at + piece, :], preferred_element_type=F32)
    return total.astype(BF16)


def normalize_kernel(points, gains, *refs):
    *parts, held, gains_held, sems = refs
    rows = parts[0].shape[0]
    fetch, *copies = started(
        [(gains, gains_held)]
        + [(points.at[pl.ds(i * rows, rows), :], held.at[i]) for i in range(len(parts))],
        sems,
    )
    fetch.wait()
    for i, part in enumerate(parts):
        copies[i].wait()
        part[...] = layer_norm(held[i], gains_held[0:1, :])


def project_kernel(first_rows, own, keep, *refs):
    refs = list(refs)

    def take(count):
        taken = refs[:count]
        del refs[:count]
        return taken

    count = len(first_rows)
    parts = take(count)
    (w_qkv,) = take(1)
    others = take(3 * keep)
    take(not own)
    (whole,) = take(1)
    queries = take(own)
    kept = take(3 * keep)
    held, held_w, sems, kept_sems = refs
    channels = w_qkv.shape[1]
    rows = held.shape[1]
    first_column = 0 if own else channels
    fetch, *copies = started(
        [(w_qkv.at[0, :, pl.ds(first_column, held_w.shape[1])], held_w)]
        + [(part, held.at[i]) for i, part in enumerate(parts)],
        sems,
    )
    keeping = started([(w.at[0], place) for w, place in zip(others, kept)], kept_sems)
    fetch.wait()
    for i, first in enumerate(first_rows):
        copies[i].wait()
        whole[first : first + rows, :] = jnp.dot(
            held[i], held_w[:, channels - first_column :], preferred_element_type=F32
        ).astype(BF16)
        if own and i * rows < queries[0].shape[0]:
            scale = BF16((channels // HEADS) ** (-0.5))
            query = jnp.dot(held[i], held_w[:, :channels], preferred_element_type=F32).astype(BF16)
            queries[0][i * rows : (i + 1) * rows, :] = (query * scale).astype(BF16)
    for copy in keeping:
        copy.wait()


def lane_tiles(packed, rows):
    capacity, channels = rows.shape[1:]
    return [
        (
            packed.at[:, pl.ds(j * capacity, capacity), :],
            rows.at[:, :, pl.ds(j * LANES, LANES)],
        )
        for j in range(channels // LANES)
    ]


def first_kernel(
    pattern,
    slot_of_row,
    gains,
    keyed,
    queries,
    points,
    w_proj,
    w_up,
    w_down,
    tail,
    outgoing,
    attended,
    points_held,
    gains_held,
    slots_held,
    outgoing_held,
    sems,
):
    rows, channels = points.shape
    devices, capacity, _ = outgoing_held.shape
    packed = outgoing.shape[2] == LANES
    row_tiles = channels // LANES * capacity
    patches = rows // PATCH
    chosen = pattern.shape[0] // patches
    copies = started(
        [
            (points, points_held),
            (gains, gains_held),
            (slot_of_row, slots_held),
        ]
        + ([(tail, outgoing.at[:, pl.ds(row_tiles, TAIL), :])] if packed else []),
        sems.at[0],
    )
    masks = head_masks(channels // HEADS)
    for p in range(patches):
        pieces = [keyed[p * PATCH : (p + 1) * PATCH, :]]
        for j in range(chosen):
            start = pl.multiple_of(pattern[p * chosen + j] * PATCH, PATCH)
            pieces.append(keyed[pl.ds(start, PATCH), :])
        both = jnp.concatenate(pieces, axis=0)
        attended[p * PATCH : (p + 1) * PATCH, :] = attend_patch(
            queries[p * PATCH : (p + 1) * PATCH, :],
            both[:, :channels],
            both[:, channels:],
            masks,
        )
    for copy in copies:
        copy.wait()
    first = finish(
        points_held[...], attended[...], gains_held[1:2, :], (w_proj, w_up, w_down)
    )
    slots = slots_held[...]
    targets = devices // SEND_PARTS
    piece = targets * capacity
    leaving = []
    for i in range(SEND_PARTS):
        here = pl.ds(i * targets, targets)
        send = one_hot_rows(slots - i * piece, piece)
        moved = jnp.dot(send, first, preferred_element_type=F32).astype(BF16)
        outgoing_held[here] = moved.reshape(targets, capacity, channels)
        there = outgoing.at[here]
        pairs = [(there, outgoing_held.at[here])]
        if packed:
            pairs = lane_tiles(there, outgoing_held.at[here])
        leaving += started([(source, place) for place, source in pairs], sems.at[1 + i])
    for copy in leaving:
        copy.wait()


def second_kernel(
    pattern,
    gains,
    tail,
    incoming,
    w_qkv,
    w_proj,
    w_up,
    w_down,
    w_head,
    features,
    normals,
    kv,
    attended,
    incoming_held,
    qkv_held,
    proj_held,
    up_held,
    down_held,
    gains_held,
    tail_held,
    head_held,
    sems,
):
    rows, channels = features.shape
    devices, capacity, _ = incoming_held.shape
    packed = incoming.shape[2] == LANES
    arriving = [(incoming, incoming_held)]
    if packed:
        arriving = lane_tiles(incoming, incoming_held)
        tail = incoming.at[:, pl.ds(channels // LANES * capacity, TAIL), :]
    patches = rows // PATCH
    chosen = pattern.shape[0] // patches
    small = started(
        [(tail, tail_held), (gains, gains_held), (w_head, head_held)], sems.at[0]
    )
    landing = started(arriving, sems.at[1])
    copies = started(
        [
            (w_qkv.at[1], qkv_held),
            (w_proj.at[1], proj_held),
            (w_up.at[1], up_held),
            (w_down.at[1], down_held),
        ],
        sems.at[2],
    )
    for copy in small:
        copy.wait()
    per_row = LANES // capacity
    digits = tail_held[...].astype(F32)
    codes = digits[:, 0:1, :] + DIGIT * digits[:, 1:2, :]
    pieces = []
    for at in range(0, devices, per_row):
        code = codes[at]
        for i in range(1, per_row):
            code = code + codes[at + i]
        pieces.append(code)
    places = jnp.concatenate(pieces, axis=1).astype(jnp.int32) - 1
    place = one_hot_rows(places, rows)
    for copy in landing:
        copy.wait()
    moved = incoming_held[...].reshape(devices * capacity, channels)
    second = jnp.dot(place, moved, preferred_element_type=F32).astype(BF16)
    normed = layer_norm(second, gains_held[2:3, :])
    scale = (channels // HEADS) ** (-0.5)
    copies[0].wait()
    queries = (
        jnp.dot(normed, qkv_held[:, :channels], preferred_element_type=F32).astype(BF16)
        * BF16(scale)
    ).astype(BF16)
    kv[...] = jnp.dot(normed, qkv_held[:, channels:], preferred_element_type=F32).astype(BF16)
    masks = head_masks(channels // HEADS)
    for p in range(patches):
        pieces = [kv[p * PATCH : (p + 1) * PATCH, :]]
        for j in range(chosen):
            start = pl.multiple_of(pattern[p * chosen + j] * PATCH, PATCH)
            pieces.append(kv[pl.ds(start, PATCH), :])
        both = jnp.concatenate(pieces, axis=0)
        attended[p * PATCH : (p + 1) * PATCH, :] = attend_patch(
            queries[p * PATCH : (p + 1) * PATCH, :], both[:, :channels], both[:, channels:], masks
        )
    done = finish(
        second, attended[...], gains_held[3:4, :], (proj_held, up_held, down_held), copies[1:]
    )
    features[...] = done
    normals[...] = lax.dot_general(
        head_held[...], done, (((1,), (1,)), ((), ())), preferred_element_type=F32
    )


VMEM_SPEC = pl.BlockSpec(memory_space=pltpu.VMEM)
SMEM_SPEC = pl.BlockSpec(memory_space=pltpu.SMEM)
ANY_SPEC = pl.BlockSpec(memory_space=pl.ANY)


def shards(
    points,
    pattern_first,
    pattern_second,
    destination,
    norm_gains,
    w_qkv,
    w_proj,
    w_up,
    w_down,
    w_head,
):
    rows_here, channels = points.shape
    patches, chosen = pattern_first.shape
    devices = lax.axis_size("grp") * lax.axis_size("seq")
    capacity = 2 * rows_here // devices
    slot_total = devices * capacity

    shards_in_group = lax.axis_size("seq")
    chips = shards_in_group // 2
    onward = [(i, (i + 2) % shards_in_group) for i in range(shards_in_group)]
    swap = [(i, i ^ 1) for i in range(shards_in_group)]
    ring = shards_in_group * rows_here * 2 * channels * 2 <= RING_BYTES
    kept_rows = shards_in_group * rows_here if ring else patches * (1 + chosen) * PATCH
    part = rows_here // RING_PARTS
    part_bytes = part * channels * 2

    column = pl.pallas_call(
        normalize_kernel,
        out_shape=[jax.ShapeDtypeStruct((part, channels), BF16)] * RING_PARTS,
        in_specs=[ANY_SPEC, ANY_SPEC],
        out_specs=[VMEM_SPEC] * RING_PARTS,
        scratch_shapes=[
            pltpu.VMEM((RING_PARTS, part, channels), BF16),
            pltpu.VMEM(norm_gains.shape, F32),
            pltpu.SemaphoreType.DMA((1 + RING_PARTS,)),
        ],
        compiler_params=pltpu.CompilerParams(vmem_limit_bytes=NORMALIZE_BYTES),
        name="normalize",
    )(points, norm_gains)

    weights = (w_proj, w_up, w_down)
    kv_shape = jax.ShapeDtypeStruct((kept_rows, 2 * channels), BF16)

    def project(keyed, blocks, keep=False):
        parts = [rows for _, block in blocks for rows in block]
        count = len(parts)
        rows = parts[0].shape[0]
        first_rows = [
            slot * rows_here + i * rows for slot, block in blocks for i in range(len(block))
        ]
        own = keyed is None
        shapes = [kv_shape]
        shapes += [jax.ShapeDtypeStruct((rows_here, channels), BF16)] * own
        shapes += [jax.ShapeDtypeStruct(w.shape[1:], BF16) for w in weights] * keep
        return pl.pallas_call(
            functools.partial(project_kernel, first_rows, own, keep),
            out_shape=shapes,
            in_specs=[ANY_SPEC] * (count + 1 + 3 * keep) + [VMEM_SPEC] * (not own),
            out_specs=[VMEM_SPEC] * len(shapes),
            scratch_shapes=[
                pltpu.VMEM((count, rows, channels), BF16),
                pltpu.VMEM((channels, (3 if own else 2) * channels), BF16),
                pltpu.SemaphoreType.DMA((count + 1,)),
                pltpu.SemaphoreType.DMA((3,)),
            ],
            input_output_aliases={} if own else {count + 1 + 3 * keep: 0},
            cost_estimate=pl.CostEstimate(
                flops=4 * count * rows * channels**2,
                bytes_accessed=3 * count * rows * channels * 2 + 3 * channels**2 * 2,
                transcendentals=0,
            ),
            compiler_params=pltpu.CompilerParams(vmem_limit_bytes=PROJECT_BYTES),
            name="project_own" if own else "project",
        )(*parts, w_qkv, *(weights * keep), *([] if own else [keyed]))

    target = destination // rows_here
    place_at = destination % rows_here
    onehot_dev = (target[:, None] == jnp.arange(devices, dtype=jnp.int32)[None, :]).astype(
        jnp.int32
    )
    earlier = jnp.cumsum(onehot_dev, axis=0) - onehot_dev
    send_rank = jnp.sum(earlier * onehot_dev, axis=1)
    slot_index = target * capacity + send_rank
    slot_ids = jnp.arange(slot_total, dtype=jnp.int32)
    match_send = slot_index[None, :] == slot_ids[:, None]
    codes = jnp.sum(jnp.where(match_send, place_at[None, :] + 1, 0), axis=1)
    index = lax.axis_index("grp") * lax.axis_size("seq") + lax.axis_index("seq")
    per_row = LANES // capacity
    lane = jnp.arange(LANES, dtype=jnp.int32)
    codes = jnp.where(
        lane // capacity == index % per_row, jnp.tile(codes.reshape(devices, capacity), per_row), 0
    )
    digits = jnp.stack([codes % DIGIT, codes // DIGIT], axis=1).astype(BF16)
    tail = jnp.concatenate([digits, jnp.zeros((devices, TAIL - 2, LANES), BF16)], axis=1)
    slot_index = slot_index.reshape(1, rows_here)
    packed = capacity % 16 == 0

    pattern_second = pattern_second.reshape(-1)
    me = lax.axis_index("seq")
    if ring:
        owner = pattern_first // patches
        slot_of = 2 * ((me // 2 - owner // 2) % chips) + (me % 2 != owner % 2).astype(jnp.int32)
        pattern_slots = (slot_of * patches + pattern_first % patches).reshape(-1)
    else:
        pattern_slots = patches + jnp.arange(patches * chosen, dtype=jnp.int32)

    if ring:
        beside = [lax.ppermute(rows, "seq", swap) for rows in column]
        waiting = [(0, column), (1, beside)]
        for step in range(1, chips):
            column = [lax.ppermute(rows, "seq", onward) for rows in column]
            if step == 1:
                own = [rows for _, block in waiting for rows in block]
                own, tail, slot_index, pattern_slots, pattern_second = lax.optimization_barrier(
                    (own, tail, slot_index, pattern_slots, pattern_second)
                )
                waiting = [(0, own[:RING_PARTS]), (1, own[RING_PARTS:])]
            else:
                if step == 2:
                    keyed, queries = project(None, waiting)
                else:
                    keyed, *kept = project(keyed, waiting, keep=step == 3)
                column, keyed = lax.optimization_barrier((column, keyed))
                waiting = []
            beside = [lax.ppermute(rows, "seq", swap) for rows in column]
            waiting = waiting + [(2 * step, column), (2 * step + 1, beside)]
        for block in waiting:
            (keyed,) = project(keyed, [block])
    else:
        group = lax.all_gather(jnp.concatenate(column), "seq", axis=0, tiled=True)
        picked = group.reshape(-1, PATCH, channels)[pattern_first].reshape(-1, channels)
        keyed, queries = project(None, [(0, column)])
        keyed, *kept = project(keyed, [(1, [picked])], keep=True)

    held_weights = [pltpu.VMEM(w.shape[1:], BF16) for w in weights]
    held_rows = pltpu.VMEM((rows_here, channels), BF16)
    pair_shape = (capacity, channels)
    if packed:
        pair_shape = (channels // LANES * capacity + TAIL, LANES)
    held_slots = pltpu.VMEM((devices, capacity, channels), BF16)
    outgoing = pl.pallas_call(
        first_kernel,
        out_shape=jax.ShapeDtypeStruct((devices,) + pair_shape, BF16),
        in_specs=[SMEM_SPEC, ANY_SPEC, ANY_SPEC, VMEM_SPEC, VMEM_SPEC, ANY_SPEC]
        + [VMEM_SPEC] * 3
        + [ANY_SPEC],
        out_specs=ANY_SPEC,
        scratch_shapes=[
            held_rows,
            held_rows,
            pltpu.VMEM(norm_gains.shape, F32),
            pltpu.VMEM(slot_index.shape, jnp.int32),
            held_slots,
            pltpu.SemaphoreType.DMA((1 + SEND_PARTS, 4)),
        ],
        compiler_params=pltpu.CompilerParams(vmem_limit_bytes=FIRST_BYTES),
        name="block_first",
    )(pattern_slots, slot_index, norm_gains, keyed, queries, points, *kept, tail)

    def exchange(array):
        return lax.all_to_all(array, ("grp", "seq"), split_axis=0, concat_axis=0, tiled=True)

    incoming = exchange(outgoing)
    tail = tail if packed else exchange(tail)

    return pl.pallas_call(
        second_kernel,
        out_shape=(
            jax.ShapeDtypeStruct((rows_here, channels), BF16),
            jax.ShapeDtypeStruct((w_head.shape[0], rows_here), F32),
        ),
        in_specs=[SMEM_SPEC] + [ANY_SPEC] * 8,
        out_specs=(VMEM_SPEC, VMEM_SPEC),
        scratch_shapes=[
            pltpu.VMEM((rows_here, 2 * channels), BF16),
            held_rows,
            held_slots,
            pltpu.VMEM(w_qkv.shape[1:], BF16),
            *held_weights,
            pltpu.VMEM(norm_gains.shape, F32),
            pltpu.VMEM(tail.shape, BF16),
            pltpu.VMEM(w_head.shape, BF16),
            pltpu.SemaphoreType.DMA((3, 5)),
        ],
        compiler_params=pltpu.CompilerParams(vmem_limit_bytes=SECOND_BYTES),
        name="block_second",
    )(pattern_second, norm_gains, tail, incoming, w_qkv, *weights, w_head)


def solution(mesh):
    placed = (
        P(("grp", "seq"), None),
        P(("grp", "seq"), None),
        P(("grp", "seq"), None),
        P(("grp", "seq")),
        P(),
        P(),
        P(),
        P(),
        P(),
        P(),
    )
    return jax.shard_map(
        shards,
        mesh=mesh,
        in_specs=placed,
        out_specs=(P(("grp", "seq"), None), P(None, ("grp", "seq"))),
        check_vma=False,
    )
```

```python
import functools

import jax
import jax.numpy as jnp
from jax import lax
from jax.experimental import pallas as pl
from jax.experimental.pallas import tpu as pltpu
from jax.sharding import PartitionSpec as P

HEADS = 8
PATCH = 64
HEADS_TOGETHER = 4
RING_PARTS = 2
SEND_PARTS = 4
LANES = 128
TAIL = 8
DIGIT = 256
FIRST_BYTES = 28 * 1024 * 1024
SECOND_BYTES = 50 * 1024 * 1024
PROJECT_BYTES = 16 * 1024 * 1024
NORMALIZE_BYTES = 60 * 1024 * 1024
PREPARE_BYTES = 46 * 1024 * 1024
RING_BYTES = 16 * 1024 * 1024
F32 = jnp.float32
BF16 = jnp.bfloat16


def layer_norm(rows, gains):
    values = rows.astype(F32)
    average = jnp.mean(values, axis=-1, keepdims=True)
    spread = jnp.mean((values - average) ** 2, axis=-1, keepdims=True)
    return ((values - average) * lax.rsqrt(spread + 1e-05) * gains).astype(BF16)


def gelu(x):
    half = 0.5 * x
    return half + half * lax.erf(x * 0.5**0.5)


def head_masks(head_dim):
    lane = lax.broadcasted_iota(jnp.int32, (PATCH, HEADS_TOGETHER * head_dim), 1)
    return [
        jnp.where((lane >= h * head_dim) & (lane < (h + 1) * head_dim), 1.0, 0.0).astype(F32)
        for h in range(HEADS_TOGETHER)
    ]


def attend_patch(queries, key_rows, value_rows, masks):
    channels = queries.shape[1]
    width = HEADS_TOGETHER * (channels // HEADS)
    sides = []
    for at in range(0, channels, width):
        q = queries[:, at : at + width]
        stacked = jnp.concatenate([q * mask.astype(BF16) for mask in masks], axis=0)
        scores = lax.dot_general(
            stacked,
            key_rows[:, at : at + width],
            (((1,), (1,)), ((), ())),
            preferred_element_type=F32,
        )
        top = jnp.max(scores, axis=-1, keepdims=True)
        grown = jnp.exp(scores - top)
        total = jnp.sum(grown, axis=-1, keepdims=True)
        weights = (grown * (1.0 / total)).astype(BF16)
        mixed = jnp.dot(weights, value_rows[:, at : at + width], preferred_element_type=F32)
        side = mixed[:PATCH] * masks[0]
        for h in range(1, HEADS_TOGETHER):
            side = side + mixed[h * PATCH : (h + 1) * PATCH] * masks[h]
        sides.append(side.astype(BF16))
    return jnp.concatenate(sides, axis=1)


def one_hot_rows(places, rows):
    row = lax.broadcasted_iota(jnp.int32, (rows, places.shape[1]), 0)
    return jnp.where(row == places, 1.0, 0.0).astype(BF16)


def started(pairs, sems):
    copies = [
        pltpu.make_async_copy(source, place, sems.at[at])
        for at, (source, place) in enumerate(pairs)
    ]
    for copy in copies:
        copy.start()
    return copies


def finish(rows, attended, gain, held, copies=()):
    w_proj, w_up, w_down = held
    for copy in copies[:1]:
        copy.wait()
    first = (
        rows.astype(F32) + jnp.dot(attended, w_proj[...], preferred_element_type=F32)
    ).astype(BF16)
    hidden = layer_norm(first, gain)
    total = first.astype(F32)
    for copy in copies[1:]:
        copy.wait()
    piece = 512
    for at in range(0, w_up.shape[1], piece):
        upper = jnp.dot(hidden, w_up[:, at : at + piece], preferred_element_type=F32)
        act = gelu(upper).astype(BF16)
        total = total + jnp.dot(act, w_down[at : at + piece, :], preferred_element_type=F32)
    return total.astype(BF16)


def normalize_kernel(points, gains, *refs):
    *parts, held, gains_held, sems = refs
    rows = parts[0].shape[0]
    fetch, *copies = started(
        [(gains, gains_held)]
        + [(points.at[pl.ds(i * rows, rows), :], held.at[i]) for i in range(len(parts))],
        sems,
    )
    fetch.wait()
    for i, part in enumerate(parts):
        copies[i].wait()
        part[...] = layer_norm(held[i], gains_held[0:1, :])


def prepare_kernel(capacity, destination, *refs):
    count = (len(refs) - 4) // 2
    weights, (slots, tail), kept = refs[:count], refs[count : count + 2], refs[count + 2 : -2]
    held, sems = refs[-2:]
    fetch, *copies = started(
        [(destination, held)] + [(w.at[0], place) for w, place in zip(weights, kept)], sems
    )
    fetch.wait()
    rows = held.shape[1]
    devices = tail.shape[0]
    shift = rows.bit_length() - 1
    target = lax.shift_right_logical(held[...], shift)
    place = held[...] & (rows - 1)
    mine = lax.broadcasted_iota(jnp.int32, (devices, rows), 0) == target
    mine = jnp.where(mine, 1.0, 0.0).astype(F32)
    before = lax.broadcasted_iota(jnp.int32, (rows, rows), 0)
    before = before < lax.broadcasted_iota(jnp.int32, (rows, rows), 1)
    earlier = jnp.dot(
        mine.astype(BF16),
        jnp.where(before, 1.0, 0.0).astype(BF16),
        preferred_element_type=F32,
    )
    rank = jnp.sum(mine * earlier, axis=0, keepdims=True).astype(jnp.int32)
    slots[...] = target * capacity + rank

    index = lax.axis_index("grp") * lax.axis_size("seq") + lax.axis_index("seq")
    lane = rank + lax.rem(index, LANES // capacity) * capacity
    by_lane = lax.broadcasted_iota(jnp.int32, (LANES, rows), 0) == lane
    by_lane = jnp.where(by_lane, 1.0, 0.0).astype(BF16)
    line = lax.broadcasted_iota(jnp.int32, (devices * TAIL, rows), 0)
    code = place + 1
    low = (code & (DIGIT - 1)).astype(F32)
    high = lax.shift_right_logical(code, DIGIT.bit_length() - 1).astype(F32)
    digit = line & (TAIL - 1)
    digits = jnp.where(digit == 0, low, jnp.where(digit == 1, high, 0.0))
    digits = jnp.where(lax.shift_right_logical(line, TAIL.bit_length() - 1) == target, digits, 0.0)
    lines = lax.dot_general(
        digits.astype(BF16), by_lane, (((1,), (1,)), ((), ())), preferred_element_type=F32
    )
    tail[...] = lines.reshape(devices, TAIL, LANES).astype(BF16)
    for copy in copies:
        copy.wait()


def project_kernel(first_rows, own, *refs):
    count = len(first_rows)
    parts, w_qkv = refs[:count], refs[count]
    refs = refs[count + 1 if own else count + 2 :]
    whole, (held, sems) = refs[0], refs[-2:]
    channels = w_qkv.shape[0]
    rows = held.shape[1]
    copies = started([(part, held.at[i]) for i, part in enumerate(parts)], sems)
    for i, first in enumerate(first_rows):
        copies[i].wait()
        whole[first : first + rows, :] = jnp.dot(
            held[i], w_qkv[:, channels:], preferred_element_type=F32
        ).astype(BF16)
        if own and i * rows < refs[1].shape[0]:
            scale = BF16((channels // HEADS) ** (-0.5))
            query = jnp.dot(held[i], w_qkv[:, :channels], preferred_element_type=F32).astype(BF16)
            refs[1][i * rows : (i + 1) * rows, :] = (query * scale).astype(BF16)


def lane_tiles(packed, rows):
    capacity, channels = rows.shape[1:]
    return [
        (
            packed.at[:, pl.ds(j * capacity, capacity), :],
            rows.at[:, :, pl.ds(j * LANES, LANES)],
        )
        for j in range(channels // LANES)
    ]


def first_kernel(
    ring_chips,
    pattern,
    slot_of_row,
    gains,
    keyed,
    queries,
    points,
    w_proj,
    w_up,
    w_down,
    tail,
    outgoing,
    attended,
    points_held,
    gains_held,
    outgoing_held,
    sems,
):
    rows, channels = points.shape
    me = lax.axis_index("seq")
    devices, capacity, _ = outgoing_held.shape
    packed = outgoing.shape[2] == LANES
    row_tiles = channels // LANES * capacity
    patches = rows // PATCH
    chosen = pattern.shape[0]
    copies = started(
        [
            (points, points_held),
            (gains, gains_held),
        ]
        + ([(tail, outgoing.at[:, pl.ds(row_tiles, TAIL), :])] if packed else []),
        sems.at[0],
    )
    masks = head_masks(channels // HEADS)
    for p in range(patches):
        pieces = [keyed[p * PATCH : (p + 1) * PATCH, :]]
        for j in range(chosen):
            patch = pattern[j, p]
            if ring_chips:
                owner, local = lax.div(patch, patches), lax.rem(patch, patches)
                chip = lax.rem(lax.div(me, 2) - lax.div(owner, 2) + ring_chips, ring_chips)
                slot = 2 * chip + jnp.where(lax.rem(me, 2) == lax.rem(owner, 2), 0, 1)
                patch = slot * patches + local
            else:
                patch = patches + p * chosen + j
            start = pl.multiple_of(patch * PATCH, PATCH)
            pieces.append(keyed[pl.ds(start, PATCH), :])
        both = jnp.concatenate(pieces, axis=0)
        attended[p * PATCH : (p + 1) * PATCH, :] = attend_patch(
            queries[p * PATCH : (p + 1) * PATCH, :],
            both[:, :channels],
            both[:, channels:],
            masks,
        )
    for copy in copies:
        copy.wait()
    first = finish(
        points_held[...], attended[...], gains_held[1:2, :], (w_proj, w_up, w_down)
    )
    slots = slot_of_row[...]
    targets = devices // SEND_PARTS
    piece = targets * capacity
    leaving = []
    for i in range(SEND_PARTS):
        here = pl.ds(i * targets, targets)
        send = one_hot_rows(slots - i * piece, piece)
        moved = jnp.dot(send, first, preferred_element_type=F32).astype(BF16)
        outgoing_held[here] = moved.reshape(targets, capacity, channels)
        there = outgoing.at[here]
        pairs = [(there, outgoing_held.at[here])]
        if packed:
            pairs = lane_tiles(there, outgoing_held.at[here])
        leaving += started([(source, place) for place, source in pairs], sems.at[1 + i])
    for copy in leaving:
        copy.wait()


def second_kernel(
    pattern,
    gains,
    tail,
    incoming,
    w_qkv,
    w_proj,
    w_up,
    w_down,
    w_head,
    features,
    normals,
    kv,
    attended,
    incoming_held,
    qkv_held,
    proj_held,
    up_held,
    down_held,
    gains_held,
    tail_held,
    head_held,
    sems,
):
    rows, channels = features.shape
    devices, capacity, _ = incoming_held.shape
    packed = incoming.shape[2] == LANES
    arriving = [(incoming, incoming_held)]
    if packed:
        arriving = lane_tiles(incoming, incoming_held)
        tail = incoming.at[:, pl.ds(channels // LANES * capacity, TAIL), :]
    patches = rows // PATCH
    chosen = pattern.shape[0]
    small = started(
        [(tail, tail_held), (gains, gains_held), (w_head, head_held)], sems.at[0]
    )
    landing = started(arriving, sems.at[1])
    copies = started(
        [
            (w_qkv.at[1], qkv_held),
            (w_proj.at[1], proj_held),
            (w_up.at[1], up_held),
            (w_down.at[1], down_held),
        ],
        sems.at[2],
    )
    for copy in small:
        copy.wait()
    per_row = LANES // capacity
    digits = tail_held[...].astype(F32)
    codes = digits[:, 0:1, :] + DIGIT * digits[:, 1:2, :]
    pieces = []
    for at in range(0, devices, per_row):
        code = codes[at]
        for i in range(1, per_row):
            code = code + codes[at + i]
        pieces.append(code)
    places = jnp.concatenate(pieces, axis=1).astype(jnp.int32) - 1
    place = one_hot_rows(places, rows)
    for copy in landing:
        copy.wait()
    moved = incoming_held[...].reshape(devices * capacity, channels)
    second = jnp.dot(place, moved, preferred_element_type=F32).astype(BF16)
    normed = layer_norm(second, gains_held[2:3, :])
    scale = (channels // HEADS) ** (-0.5)
    copies[0].wait()
    queries = (
        jnp.dot(normed, qkv_held[:, :channels], preferred_element_type=F32).astype(BF16)
        * BF16(scale)
    ).astype(BF16)
    kv[...] = jnp.dot(normed, qkv_held[:, channels:], preferred_element_type=F32).astype(BF16)
    masks = head_masks(channels // HEADS)
    for p in range(patches):
        pieces = [kv[p * PATCH : (p + 1) * PATCH, :]]
        for j in range(chosen):
            start = pl.multiple_of(pattern[j, p] * PATCH, PATCH)
            pieces.append(kv[pl.ds(start, PATCH), :])
        both = jnp.concatenate(pieces, axis=0)
        attended[p * PATCH : (p + 1) * PATCH, :] = attend_patch(
            queries[p * PATCH : (p + 1) * PATCH, :], both[:, :channels], both[:, channels:], masks
        )
    done = finish(
        second, attended[...], gains_held[3:4, :], (proj_held, up_held, down_held), copies[1:]
    )
    features[...] = done
    normals[...] = lax.dot_general(
        head_held[...], done, (((1,), (1,)), ((), ())), preferred_element_type=F32
    )


VMEM_SPEC = pl.BlockSpec(memory_space=pltpu.VMEM)
SMEM_SPEC = pl.BlockSpec(memory_space=pltpu.SMEM)
ANY_SPEC = pl.BlockSpec(memory_space=pl.ANY)


def shards(
    points,
    pattern_first,
    pattern_second,
    destination,
    norm_gains,
    w_qkv,
    w_proj,
    w_up,
    w_down,
    w_head,
):
    rows_here, channels = points.shape
    patches, chosen = pattern_first.shape
    devices = lax.axis_size("grp") * lax.axis_size("seq")
    capacity = 2 * rows_here // devices
    slot_total = devices * capacity

    shards_in_group = lax.axis_size("seq")
    chips = shards_in_group // 2
    onward = [(i, (i + 2) % shards_in_group) for i in range(shards_in_group)]
    swap = [(i, i ^ 1) for i in range(shards_in_group)]
    ring = shards_in_group * rows_here * 2 * channels * 2 <= RING_BYTES
    kept_rows = shards_in_group * rows_here if ring else patches * (1 + chosen) * PATCH
    part = rows_here // RING_PARTS
    part_bytes = part * channels * 2

    column = pl.pallas_call(
        normalize_kernel,
        out_shape=[jax.ShapeDtypeStruct((part, channels), BF16)] * RING_PARTS,
        in_specs=[ANY_SPEC, ANY_SPEC],
        out_specs=[VMEM_SPEC] * RING_PARTS,
        scratch_shapes=[
            pltpu.VMEM((RING_PARTS, part, channels), BF16),
            pltpu.VMEM(norm_gains.shape, F32),
            pltpu.SemaphoreType.DMA((1 + RING_PARTS,)),
        ],
        compiler_params=pltpu.CompilerParams(vmem_limit_bytes=NORMALIZE_BYTES),
        name="normalize",
    )(points, norm_gains)

    weights = (w_proj, w_up, w_down)
    kv_shape = jax.ShapeDtypeStruct((kept_rows, 2 * channels), BF16)
    own_shape = jax.ShapeDtypeStruct((rows_here, channels), BF16)

    slot_index, tail, qkv_kept, *kept = pl.pallas_call(
        functools.partial(prepare_kernel, capacity),
        out_shape=[
            jax.ShapeDtypeStruct((1, rows_here), jnp.int32),
            jax.ShapeDtypeStruct((devices, TAIL, LANES), BF16),
            *[jax.ShapeDtypeStruct(w.shape[1:], BF16) for w in (w_qkv,) + weights],
        ],
        in_specs=[ANY_SPEC] * 5,
        out_specs=[VMEM_SPEC] * 6,
        scratch_shapes=[
            pltpu.VMEM((1, rows_here), jnp.int32),
            pltpu.SemaphoreType.DMA((5,)),
        ],
        compiler_params=pltpu.CompilerParams(vmem_limit_bytes=PREPARE_BYTES),
        name="prepare",
    )(destination.reshape(1, rows_here), w_qkv, *weights)

    def project(keyed, blocks):
        parts = [rows for _, block in blocks for rows in block]
        count = len(parts)
        rows = parts[0].shape[0]
        first_rows = [
            slot * rows_here + i * rows for slot, block in blocks for i in range(len(block))
        ]
        own = keyed is None
        return pl.pallas_call(
            functools.partial(project_kernel, first_rows, own),
            out_shape=[kv_shape, own_shape] if own else kv_shape,
            in_specs=[ANY_SPEC] * count + [VMEM_SPEC] * (1 if own else 2),
            out_specs=[VMEM_SPEC] * 2 if own else VMEM_SPEC,
            scratch_shapes=[
                pltpu.VMEM((count, rows, channels), BF16),
                pltpu.SemaphoreType.DMA((count,)),
            ],
            input_output_aliases={} if own else {count + 1: 0},
            cost_estimate=pl.CostEstimate(
                flops=4 * count * rows * channels**2,
                bytes_accessed=3 * count * rows * channels * 2 + 3 * channels**2 * 2,
                transcendentals=0,
            ),
            compiler_params=pltpu.CompilerParams(vmem_limit_bytes=PROJECT_BYTES),
            name="project_own" if own else "project",
        )(*parts, qkv_kept, *([] if own else [keyed]))

    packed = capacity % 16 == 0
    if ring:
        beside = [lax.ppermute(rows, "seq", swap) for rows in column]
        waiting = [(0, column), (1, beside)]
        for step in range(1, chips):
            column = [lax.ppermute(rows, "seq", onward) for rows in column]
            if step == 1:
                column[0], slot_index = lax.optimization_barrier((column[0], slot_index))
                keyed, queries = project(None, waiting)
                column[1], keyed = lax.optimization_barrier((column[1], keyed))
            else:
                for i, block in enumerate(waiting):
                    keyed = project(keyed, [block])
                    column[i], keyed = lax.optimization_barrier((column[i], keyed))
            beside = [lax.ppermute(rows, "seq", swap) for rows in column]
            waiting = [(2 * step, column), (2 * step + 1, beside)]
        for block in waiting:
            keyed = project(keyed, [block])
    else:
        group = lax.all_gather(jnp.concatenate(column), "seq", axis=0, tiled=True)
        picked = group.reshape(-1, PATCH, channels)[pattern_first].reshape(-1, channels)
        keyed, queries = project(None, [(0, column)])
        keyed = project(keyed, [(1, [picked])])

    held_weights = [pltpu.VMEM(w.shape[1:], BF16) for w in weights]
    held_rows = pltpu.VMEM((rows_here, channels), BF16)
    pair_shape = (capacity, channels)
    if packed:
        pair_shape = (channels // LANES * capacity + TAIL, LANES)
    held_slots = pltpu.VMEM((devices, capacity, channels), BF16)
    outgoing = pl.pallas_call(
        functools.partial(first_kernel, chips if ring else 0),
        out_shape=jax.ShapeDtypeStruct((devices,) + pair_shape, BF16),
        in_specs=[SMEM_SPEC, VMEM_SPEC, ANY_SPEC, VMEM_SPEC, VMEM_SPEC, ANY_SPEC]
        + [VMEM_SPEC] * 3
        + [ANY_SPEC],
        out_specs=ANY_SPEC,
        scratch_shapes=[
            held_rows,
            held_rows,
            pltpu.VMEM(norm_gains.shape, F32),
            held_slots,
            pltpu.SemaphoreType.DMA((1 + SEND_PARTS, 4)),
        ],
        compiler_params=pltpu.CompilerParams(vmem_limit_bytes=FIRST_BYTES),
        name="block_first",
    )(pattern_first.T, slot_index, norm_gains, keyed, queries, points, *kept, tail)

    def exchange(array):
        return lax.all_to_all(array, ("grp", "seq"), split_axis=0, concat_axis=0, tiled=True)

    incoming = exchange(outgoing)
    tail = tail if packed else exchange(tail)

    return pl.pallas_call(
        second_kernel,
        out_shape=(
            jax.ShapeDtypeStruct((rows_here, channels), BF16),
            jax.ShapeDtypeStruct((w_head.shape[0], rows_here), F32),
        ),
        in_specs=[SMEM_SPEC] + [ANY_SPEC] * 8,
        out_specs=(VMEM_SPEC, VMEM_SPEC),
        scratch_shapes=[
            pltpu.VMEM((rows_here, 2 * channels), BF16),
            held_rows,
            held_slots,
            pltpu.VMEM(w_qkv.shape[1:], BF16),
            *held_weights,
            pltpu.VMEM(norm_gains.shape, F32),
            pltpu.VMEM(tail.shape, BF16),
            pltpu.VMEM(w_head.shape, BF16),
            pltpu.SemaphoreType.DMA((3, 5)),
        ],
        compiler_params=pltpu.CompilerParams(vmem_limit_bytes=SECOND_BYTES),
        name="block_second",
    )(pattern_second.T, norm_gains, tail, incoming, w_qkv, *weights, w_head)


def solution(mesh):
    placed = (
        P(("grp", "seq"), None),
        P(("grp", "seq"), None),
        P(("grp", "seq"), None),
        P(("grp", "seq")),
        P(),
        P(),
        P(),
        P(),
        P(),
        P(),
    )
    return jax.shard_map(
        shards,
        mesh=mesh,
        in_specs=placed,
        out_specs=(P(("grp", "seq"), None), P(None, ("grp", "seq"))),
        check_vma=False,
    )
```

```python
import functools

import jax
import jax.numpy as jnp
from jax import lax
from jax.experimental import pallas as pl
from jax.experimental.pallas import tpu as pltpu
from jax.sharding import Mesh, PartitionSpec as P

HEADS = 8
PATCH = 64
HEADS_TOGETHER = 4
GROUP = ("half", "seq")
RING_PARTS = 2
SEND_PARTS = 4
LANES = 128
TAIL = 8
DIGIT = 256
FIRST_BYTES = 28 * 1024 * 1024
SECOND_BYTES = 50 * 1024 * 1024
PROJECT_BYTES = 16 * 1024 * 1024
SPLIT_BYTES = 60 * 1024 * 1024
PREPARE_BYTES = 46 * 1024 * 1024
RING_BYTES = 16 * 1024 * 1024
F32 = jnp.float32
BF16 = jnp.bfloat16


def layer_norm(rows, gains):
    values = rows.astype(F32)
    average = jnp.mean(values, axis=-1, keepdims=True)
    spread = jnp.mean((values - average) ** 2, axis=-1, keepdims=True)
    return ((values - average) * lax.rsqrt(spread + 1e-05) * gains).astype(BF16)


def gelu(x):
    half = 0.5 * x
    return half + half * lax.erf(x * 0.5**0.5)


def head_masks(head_dim):
    lane = lax.broadcasted_iota(jnp.int32, (PATCH, HEADS_TOGETHER * head_dim), 1)
    return [
        jnp.where((lane >= h * head_dim) & (lane < (h + 1) * head_dim), 1.0, 0.0).astype(F32)
        for h in range(HEADS_TOGETHER)
    ]


def attend_patch(queries, key_rows, value_rows, masks):
    channels = queries.shape[1]
    width = HEADS_TOGETHER * (channels // HEADS)
    sides = []
    for at in range(0, channels, width):
        q = queries[:, at : at + width]
        stacked = jnp.concatenate([q * mask.astype(BF16) for mask in masks], axis=0)
        scores = lax.dot_general(
            stacked,
            key_rows[:, at : at + width],
            (((1,), (1,)), ((), ())),
            preferred_element_type=F32,
        )
        top = jnp.max(scores, axis=-1, keepdims=True)
        grown = jnp.exp(scores - top)
        total = jnp.sum(grown, axis=-1, keepdims=True)
        weights = (grown * (1.0 / total)).astype(BF16)
        mixed = jnp.dot(weights, value_rows[:, at : at + width], preferred_element_type=F32)
        side = mixed[:PATCH] * masks[0]
        for h in range(1, HEADS_TOGETHER):
            side = side + mixed[h * PATCH : (h + 1) * PATCH] * masks[h]
        sides.append(side.astype(BF16))
    return jnp.concatenate(sides, axis=1)


def one_hot_rows(places, rows):
    row = lax.broadcasted_iota(jnp.int32, (rows, places.shape[1]), 0)
    return jnp.where(row == places, 1.0, 0.0).astype(BF16)


def started(pairs, sems):
    copies = [
        pltpu.make_async_copy(source, place, sems.at[at])
        for at, (source, place) in enumerate(pairs)
    ]
    for copy in copies:
        copy.start()
    return copies


def finish(rows, attended, gain, held, copies=()):
    w_proj, w_up, w_down = held
    for copy in copies[:1]:
        copy.wait()
    first = (
        rows.astype(F32) + jnp.dot(attended, w_proj[...], preferred_element_type=F32)
    ).astype(BF16)
    hidden = layer_norm(first, gain)
    total = first.astype(F32)
    for copy in copies[1:]:
        copy.wait()
    piece = 512
    for at in range(0, w_up.shape[1], piece):
        upper = jnp.dot(hidden, w_up[:, at : at + piece], preferred_element_type=F32)
        act = gelu(upper).astype(BF16)
        total = total + jnp.dot(act, w_down[at : at + piece, :], preferred_element_type=F32)
    return total.astype(BF16)


def split_kernel(points, *refs):
    *parts, sems = refs
    rows = parts[0].shape[0]
    for copy in started(
        [(points.at[pl.ds(i * rows, rows), :], part) for i, part in enumerate(parts)], sems
    ):
        copy.wait()


def prepare_kernel(capacity, destination, beyond, *refs):
    count = (len(refs) - 4) // 2
    sources, (slots, tail), kept = refs[:count], refs[count : count + 2], refs[count + 2 : -2]
    held, sems = refs[-2:]
    fetches = started([(destination, held.at[0]), (beyond, held.at[1])], sems.at[0])
    copies = started(
        [
            (source.at[0] if len(source.shape) == 3 else source, place)
            for source, place in zip(sources, kept)
        ],
        sems.at[1],
    )
    for fetch in fetches:
        fetch.wait()
    rows = held.shape[2]
    devices = tail.shape[0]
    in_half = lax.axis_size("seq")
    seq_bits = in_half.bit_length() - 1
    index = lax.axis_index(("grp", "seq"))
    offset = lax.rem(index, LANES // (2 * capacity)) * 2 * capacity
    before = lax.broadcasted_iota(jnp.int32, (rows, rows), 0)
    before = before < lax.broadcasted_iota(jnp.int32, (rows, rows), 1)
    before = jnp.where(before, 1.0, 0.0).astype(BF16)
    lines = jnp.zeros((devices * TAIL, LANES), F32)
    for b in range(2):
        target = lax.shift_right_logical(held[b], rows.bit_length() - 1)
        place = held[b] & (rows - 1)
        half = lax.shift_right_logical(target, seq_bits) & 1
        group = lax.shift_right_logical(target, seq_bits + 1)
        target = group * in_half + (target & (in_half - 1))
        target = jnp.where(half == lax.axis_index("half"), target, -1)
        mine = lax.broadcasted_iota(jnp.int32, (devices, rows), 0) == target
        mine = jnp.where(mine, 1.0, 0.0).astype(F32)
        earlier = jnp.dot(mine.astype(BF16), before, preferred_element_type=F32)
        rank = jnp.sum(mine * earlier, axis=0, keepdims=True).astype(jnp.int32) + b * capacity
        slots[:, b * rows : (b + 1) * rows] = jnp.where(
            target >= 0, target * 2 * capacity + rank, -1
        )
        by_lane = lax.broadcasted_iota(jnp.int32, (LANES, rows), 0) == rank + offset
        by_lane = jnp.where(by_lane, 1.0, 0.0).astype(BF16)
        line = lax.broadcasted_iota(jnp.int32, (devices * TAIL, rows), 0)
        code = place + 1
        low = (code & (DIGIT - 1)).astype(F32)
        high = lax.shift_right_logical(code, DIGIT.bit_length() - 1).astype(F32)
        digit = line & (TAIL - 1)
        digits = jnp.where(digit == 0, low, jnp.where(digit == 1, high, 0.0))
        line = lax.shift_right_logical(line, TAIL.bit_length() - 1)
        digits = jnp.where(line == target, digits, 0.0)
        lines = lines + lax.dot_general(
            digits.astype(BF16), by_lane, (((1,), (1,)), ((), ())), preferred_element_type=F32
        )
    tail[...] = lines.reshape(devices, TAIL, LANES).astype(BF16)
    for copy in copies:
        copy.wait()


def project_kernel(first_rows, new, ask, *refs):
    count = len(first_rows)
    parts, gains, w_qkv = refs[:count], refs[count], refs[count + 1]
    refs = refs[count + 2 if new else count + 3 :]
    whole, (held, sems) = refs[0], refs[-2:]
    channels = w_qkv.shape[0]
    rows = held.shape[1]
    copies = started([(part, held.at[i]) for i, part in enumerate(parts)], sems)
    for i, first in enumerate(first_rows):
        copies[i].wait()
        normed = layer_norm(held[i], gains[0:1, :])
        whole[first : first + rows, :] = jnp.dot(
            normed, w_qkv[:, channels:], preferred_element_type=F32
        ).astype(BF16)
        if ask and i * rows < refs[1].shape[0]:
            scale = BF16((channels // HEADS) ** (-0.5))
            query = jnp.dot(normed, w_qkv[:, :channels], preferred_element_type=F32).astype(BF16)
            refs[1][i * rows : (i + 1) * rows, :] = (query * scale).astype(BF16)


def lane_tiles(packed, rows):
    capacity, channels = rows.shape[1:]
    return [
        (
            packed.at[:, pl.ds(j * capacity, capacity), :],
            rows.at[:, :, pl.ds(j * LANES, LANES)],
        )
        for j in range(channels // LANES)
    ]


def first_kernel(
    ring_chips,
    pattern,
    pattern_beyond,
    slot_of_row,
    gains,
    keyed,
    queries,
    queries_beyond,
    w_proj,
    w_up,
    w_down,
    tail,
    points,
    *refs,
):
    *points_beyond, outgoing, attended, points_held, first_held, outgoing_held, sems = refs
    rows, channels = points.shape
    devices, capacity, _ = outgoing_held.shape
    row_tiles = channels // LANES * capacity
    patches = rows // PATCH
    chosen = pattern.shape[0]
    me = lax.axis_index(GROUP)
    part = rows // len(points_beyond)
    copies = started(
        [(tail, outgoing.at[:, pl.ds(row_tiles, TAIL), :]), (points, points_held.at[:rows])]
        + [
            (piece, points_held.at[pl.ds(rows + i * part, part), :])
            for i, piece in enumerate(points_beyond)
        ],
        sems.at[0],
    )
    masks = head_masks(channels // HEADS)
    blocks = ((pattern, queries, 0), (pattern_beyond, queries_beyond, ring_chips or 1))
    for b, (picked, asking, own_slot) in enumerate(blocks):
        for p in range(patches):
            start = own_slot * rows + p * PATCH
            pieces = [keyed[start : start + PATCH, :]]
            for j in range(chosen):
                if ring_chips:
                    patch = picked[j, p]
                    owner, local = lax.div(patch, patches), lax.rem(patch, patches)
                    chip = lax.rem(lax.div(me, 2) - lax.div(owner, 2) + ring_chips, ring_chips)
                    slot = 2 * chip + jnp.where(lax.rem(me, 2) == lax.rem(owner, 2), 0, 1)
                    patch = slot * patches + local
                else:
                    patch = 2 * patches + (b * patches + p) * chosen + j
                start = patch * PATCH
                if ring_chips:
                    start = pl.multiple_of(start, PATCH)
                pieces.append(keyed[pl.ds(start, PATCH), :])
            both = jnp.concatenate(pieces, axis=0)
            attended[b * rows + p * PATCH : b * rows + (p + 1) * PATCH, :] = attend_patch(
                asking[p * PATCH : (p + 1) * PATCH, :], both[:, :channels], both[:, channels:], masks
            )
    for copy in copies[1:]:
        copy.wait()

    @pl.loop(0, 2)
    def _(b):
        here = pl.ds(pl.multiple_of(b * rows, rows), rows)
        first_held[here, :] = finish(
            points_held[here, :], attended[here, :], gains[1:2, :], (w_proj, w_up, w_down)
        )

    copies[0].wait()
    slots = slot_of_row[...]
    targets = devices // SEND_PARTS
    piece = targets * capacity
    leaving = []
    for i in range(SEND_PARTS):
        here = pl.ds(i * targets, targets)
        send = one_hot_rows(slots - i * piece, piece)
        moved = jnp.dot(send, first_held[...], preferred_element_type=F32).astype(BF16)
        outgoing_held[here] = moved.reshape(targets, capacity, channels)
        pairs = lane_tiles(outgoing.at[here], outgoing_held.at[here])
        leaving += started([(source, place) for place, source in pairs], sems.at[1 + i])
    for copy in leaving:
        copy.wait()


def second_kernel(
    pattern,
    gains,
    incoming,
    w_qkv,
    w_proj,
    w_up,
    w_down,
    w_head,
    features,
    normals,
    kv,
    attended,
    incoming_held,
    qkv_held,
    proj_held,
    up_held,
    down_held,
    gains_held,
    tail_held,
    head_held,
    sems,
):
    rows, channels = features.shape
    devices, capacity, _ = incoming_held.shape
    patches = rows // PATCH
    chosen = pattern.shape[0]
    tail = incoming.at[:, pl.ds(channels // LANES * capacity, TAIL), :]
    small = started(
        [(tail, tail_held), (gains, gains_held), (w_head, head_held)], sems.at[0]
    )
    landing = started(lane_tiles(incoming, incoming_held), sems.at[1])
    copies = started(
        [
            (w_qkv.at[1], qkv_held),
            (w_proj.at[1], proj_held),
            (w_up.at[1], up_held),
            (w_down.at[1], down_held),
        ],
        sems.at[2],
    )
    for copy in small:
        copy.wait()
    per_row = LANES // capacity
    digits = tail_held[...].astype(F32)
    codes = digits[:, 0:1, :] + DIGIT * digits[:, 1:2, :]
    pieces = []
    for at in range(0, devices, per_row):
        code = codes[at]
        for i in range(1, per_row):
            code = code + codes[at + i]
        pieces.append(code)
    places = jnp.concatenate(pieces, axis=1).astype(jnp.int32) - 1
    place = one_hot_rows(places, rows)
    for copy in landing:
        copy.wait()
    moved = incoming_held[...].reshape(devices * capacity, channels)
    second = jnp.dot(place, moved, preferred_element_type=F32).astype(BF16)
    normed = layer_norm(second, gains_held[2:3, :])
    scale = (channels // HEADS) ** (-0.5)
    copies[0].wait()
    queries = (
        jnp.dot(normed, qkv_held[:, :channels], preferred_element_type=F32).astype(BF16)
        * BF16(scale)
    ).astype(BF16)
    kv[...] = jnp.dot(normed, qkv_held[:, channels:], preferred_element_type=F32).astype(BF16)
    masks = head_masks(channels // HEADS)
    for p in range(patches):
        pieces = [kv[p * PATCH : (p + 1) * PATCH, :]]
        for j in range(chosen):
            start = pl.multiple_of(pattern[j, p] * PATCH, PATCH)
            pieces.append(kv[pl.ds(start, PATCH), :])
        both = jnp.concatenate(pieces, axis=0)
        attended[p * PATCH : (p + 1) * PATCH, :] = attend_patch(
            queries[p * PATCH : (p + 1) * PATCH, :], both[:, :channels], both[:, channels:], masks
        )
    done = finish(
        second, attended[...], gains_held[3:4, :], (proj_held, up_held, down_held), copies[1:]
    )
    features[...] = done
    normals[...] = lax.dot_general(
        head_held[...], done, (((1,), (1,)), ((), ())), preferred_element_type=F32
    )


VMEM_SPEC = pl.BlockSpec(memory_space=pltpu.VMEM)
SMEM_SPEC = pl.BlockSpec(memory_space=pltpu.SMEM)
ANY_SPEC = pl.BlockSpec(memory_space=pl.ANY)


def shards(
    points,
    pattern_first,
    pattern_second,
    destination,
    norm_gains,
    w_qkv,
    w_proj,
    w_up,
    w_down,
    w_head,
):
    rows_here, channels = points.shape
    patches, chosen = pattern_first.shape
    devices = lax.axis_size("grp") * lax.axis_size("seq")
    capacity = 2 * rows_here // (2 * devices)
    pair_slots = 2 * capacity

    shards_in_group = lax.axis_size(GROUP)
    chips = shards_in_group // 2
    onward = [(i, (i + 2) % shards_in_group) for i in range(shards_in_group)]
    swap = [(i, i ^ 1) for i in range(shards_in_group)]
    across = [(i, (i + chips) % shards_in_group) for i in range(shards_in_group)]
    ring = shards_in_group * rows_here * 2 * channels * 2 <= RING_BYTES
    kept_rows = shards_in_group * rows_here if ring else 2 * patches * (1 + chosen) * PATCH
    part = rows_here // RING_PARTS

    column = pl.pallas_call(
        split_kernel,
        out_shape=[jax.ShapeDtypeStruct((part, channels), BF16)] * RING_PARTS,
        in_specs=[ANY_SPEC],
        out_specs=[ANY_SPEC] * RING_PARTS,
        scratch_shapes=[pltpu.SemaphoreType.DMA((RING_PARTS,))],
        compiler_params=pltpu.CompilerParams(vmem_limit_bytes=SPLIT_BYTES),
        name="split",
    )(points)

    weights = (w_proj, w_up, w_down)
    kv_shape = jax.ShapeDtypeStruct((kept_rows, 2 * channels), BF16)
    own_shape = jax.ShapeDtypeStruct((rows_here, channels), BF16)

    destination = destination.reshape(1, rows_here)
    pattern_first = pattern_first.T
    pattern_beyond = lax.ppermute(pattern_first, GROUP, across)
    slot_index, tail, qkv_kept, *kept, gains_kept = pl.pallas_call(
        functools.partial(prepare_kernel, capacity),
        out_shape=[
            jax.ShapeDtypeStruct((1, 2 * rows_here), jnp.int32),
            jax.ShapeDtypeStruct((devices, TAIL, LANES), BF16),
            *[jax.ShapeDtypeStruct(w.shape[1:], BF16) for w in (w_qkv,) + weights],
            jax.ShapeDtypeStruct(norm_gains.shape, F32),
        ],
        in_specs=[ANY_SPEC] * 7,
        out_specs=[VMEM_SPEC] * 7,
        scratch_shapes=[
            pltpu.VMEM((2, 1, rows_here), jnp.int32),
            pltpu.SemaphoreType.DMA((2, 5)),
        ],
        compiler_params=pltpu.CompilerParams(vmem_limit_bytes=PREPARE_BYTES),
        name="prepare",
    )(destination, lax.ppermute(destination, GROUP, across), w_qkv, *weights, norm_gains)

    def project(keyed, blocks, ask=False):
        parts = [rows for _, block in blocks for rows in block]
        count = len(parts)
        rows = parts[0].shape[0]
        first_rows = [
            slot * rows_here + i * rows for slot, block in blocks for i in range(len(block))
        ]
        new = keyed is None
        return pl.pallas_call(
            functools.partial(project_kernel, first_rows, new, ask),
            out_shape=[kv_shape] + [own_shape] * ask,
            in_specs=[ANY_SPEC] * count + [VMEM_SPEC] * (2 if new else 3),
            out_specs=[VMEM_SPEC] * (1 + ask),
            scratch_shapes=[
                pltpu.VMEM((count, rows, channels), BF16),
                pltpu.SemaphoreType.DMA((count,)),
            ],
            input_output_aliases={} if new else {count + 2: 0},
            cost_estimate=pl.CostEstimate(
                flops=4 * count * rows * channels**2,
                bytes_accessed=3 * count * rows * channels * 2 + 3 * channels**2 * 2,
                transcendentals=0,
            ),
            compiler_params=pltpu.CompilerParams(vmem_limit_bytes=PROJECT_BYTES),
            name="project_own" if new else "project",
        )(*parts, gains_kept, qkv_kept, *([] if new else [keyed]))

    if ring:
        beside = [lax.ppermute(rows, GROUP, swap) for rows in column]
        waiting = [(0, column), (1, beside)]
        for step in range(1, chips):
            column = [lax.ppermute(rows, GROUP, onward) for rows in column]
            if step == 1:
                column[0], slot_index = lax.optimization_barrier((column[0], slot_index))
                keyed, queries = project(None, waiting, ask=True)
                column[1], keyed = lax.optimization_barrier((column[1], keyed))
            else:
                for i, block in enumerate(waiting):
                    if block[0] == chips:
                        keyed, queries_beyond = project(keyed, [block], ask=True)
                    else:
                        (keyed,) = project(keyed, [block])
                    column[i], keyed = lax.optimization_barrier((column[i], keyed))
            if step == chips // 2:
                points_beyond = column
            beside = [lax.ppermute(rows, GROUP, swap) for rows in column]
            waiting = [(2 * step, column), (2 * step + 1, beside)]
        for block in waiting:
            (keyed,) = project(keyed, [block])
    else:
        group = lax.all_gather(points, GROUP, axis=0, tiled=True)
        partner = lax.rem(lax.axis_index(GROUP) + chips, shards_in_group)
        points_beyond = [lax.dynamic_slice_in_dim(group, partner * rows_here, rows_here)]
        group = group.reshape(-1, PATCH, channels)
        picked = [
            group[pattern.T].reshape(-1, channels) for pattern in (pattern_first, pattern_beyond)
        ]
        keyed, queries = project(None, [(0, column)], ask=True)
        keyed, queries_beyond = project(keyed, [(1, points_beyond)], ask=True)
        (keyed,) = project(keyed, [(2, [picked[0]])])
        (keyed,) = project(keyed, [(2 + chosen, [picked[1]])])

    held_weights = [pltpu.VMEM(w.shape[1:], BF16) for w in weights]
    held_rows = pltpu.VMEM((rows_here, channels), BF16)
    held_slots = pltpu.VMEM((devices, pair_slots, channels), BF16)
    held_both = pltpu.VMEM((2 * rows_here, channels), BF16)
    pair_rows = channels // LANES * pair_slots + TAIL
    outgoing = pl.pallas_call(
        functools.partial(first_kernel, chips if ring else 0),
        out_shape=jax.ShapeDtypeStruct((devices, pair_rows, LANES), BF16),
        in_specs=[SMEM_SPEC] * 2 + [VMEM_SPEC] * 8 + [ANY_SPEC] * (2 + len(points_beyond)),
        out_specs=ANY_SPEC,
        scratch_shapes=[
            held_both,
            held_both,
            held_both,
            held_slots,
            pltpu.SemaphoreType.DMA((1 + SEND_PARTS, 4)),
        ],
        compiler_params=pltpu.CompilerParams(vmem_limit_bytes=FIRST_BYTES),
        name="block_first",
    )(
        pattern_first,
        pattern_beyond,
        slot_index,
        gains_kept,
        keyed,
        queries,
        queries_beyond,
        *kept,
        tail,
        points,
        *points_beyond,
    )
    incoming = lax.all_to_all(outgoing, ("grp", "seq"), split_axis=0, concat_axis=0, tiled=True)

    return pl.pallas_call(
        second_kernel,
        out_shape=(
            jax.ShapeDtypeStruct((rows_here, channels), BF16),
            jax.ShapeDtypeStruct((w_head.shape[0], rows_here), F32),
        ),
        in_specs=[SMEM_SPEC] + [ANY_SPEC] * 7,
        out_specs=(VMEM_SPEC, VMEM_SPEC),
        scratch_shapes=[
            pltpu.VMEM((rows_here, 2 * channels), BF16),
            held_rows,
            held_slots,
            pltpu.VMEM(w_qkv.shape[1:], BF16),
            *held_weights,
            pltpu.VMEM(norm_gains.shape, F32),
            pltpu.VMEM(tail.shape, BF16),
            pltpu.VMEM(w_head.shape, BF16),
            pltpu.SemaphoreType.DMA((3, 5)),
        ],
        compiler_params=pltpu.CompilerParams(vmem_limit_bytes=SECOND_BYTES),
        name="block_second",
    )(pattern_second.T, norm_gains, incoming, w_qkv, *weights, w_head)


def solution(mesh):
    groups, shards_in_group = mesh.devices.shape
    halves = Mesh(
        mesh.devices.reshape(groups, 2, shards_in_group // 2), ("grp",) + GROUP
    )
    everywhere = ("grp",) + GROUP
    placed = (
        P(everywhere, None),
        P(everywhere, None),
        P(everywhere, None),
        P(everywhere),
        P(),
        P(),
        P(),
        P(),
        P(),
        P(),
    )
    return jax.shard_map(
        shards,
        mesh=halves,
        in_specs=placed,
        out_specs=(P(everywhere, None), P(None, everywhere)),
        check_vma=False,
    )
```

```python
import functools

import jax
import jax.numpy as jnp
from jax import lax
from jax.experimental import pallas as pl
from jax.experimental.pallas import tpu as pltpu
from jax.sharding import Mesh, PartitionSpec as P

HEADS = 8
PATCH = 64
HEADS_TOGETHER = 4
GROUP = ("half", "seq")
RING_PARTS = 2
SEND_PARTS = 4
LANES = 128
TAIL = 8
DIGIT = 256
FIRST_BYTES = 28 * 1024 * 1024
SECOND_BYTES = 50 * 1024 * 1024
PROJECT_BYTES = 16 * 1024 * 1024
SPLIT_BYTES = 60 * 1024 * 1024
PREPARE_BYTES = 46 * 1024 * 1024
RING_BYTES = 16 * 1024 * 1024
F32 = jnp.float32
BF16 = jnp.bfloat16


def layer_norm(rows, gains):
    values = rows.astype(F32)
    average = jnp.mean(values, axis=-1, keepdims=True)
    spread = jnp.mean((values - average) ** 2, axis=-1, keepdims=True)
    return ((values - average) * lax.rsqrt(spread + 1e-05) * gains).astype(BF16)


def gelu(x):
    half = 0.5 * x
    return half + half * lax.erf(x * 0.5**0.5)


def head_masks(head_dim):
    lane = lax.broadcasted_iota(jnp.int32, (PATCH, HEADS_TOGETHER * head_dim), 1)
    return [
        jnp.where((lane >= h * head_dim) & (lane < (h + 1) * head_dim), 1.0, 0.0).astype(F32)
        for h in range(HEADS_TOGETHER)
    ]


def attend_patch(queries, key_rows, value_rows, masks):
    channels = queries.shape[1]
    width = HEADS_TOGETHER * (channels // HEADS)
    sides = []
    for at in range(0, channels, width):
        q = queries[:, at : at + width]
        stacked = jnp.concatenate([q * mask.astype(BF16) for mask in masks], axis=0)
        scores = lax.dot_general(
            stacked,
            key_rows[:, at : at + width],
            (((1,), (1,)), ((), ())),
            preferred_element_type=F32,
        )
        top = jnp.max(scores, axis=-1, keepdims=True)
        grown = jnp.exp(scores - top)
        total = jnp.sum(grown, axis=-1, keepdims=True)
        weights = (grown * (1.0 / total)).astype(BF16)
        mixed = jnp.dot(weights, value_rows[:, at : at + width], preferred_element_type=F32)
        side = mixed[:PATCH] * masks[0]
        for h in range(1, HEADS_TOGETHER):
            side = side + mixed[h * PATCH : (h + 1) * PATCH] * masks[h]
        sides.append(side.astype(BF16))
    return jnp.concatenate(sides, axis=1)


def one_hot_rows(places, rows):
    row = lax.broadcasted_iota(jnp.int32, (rows, places.shape[1]), 0)
    return jnp.where(row == places, 1.0, 0.0).astype(BF16)


def started(pairs, sems):
    copies = [
        pltpu.make_async_copy(source, place, sems.at[at])
        for at, (source, place) in enumerate(pairs)
    ]
    for copy in copies:
        copy.start()
    return copies


def finish(rows, attended, gain, held, copies=()):
    w_proj, w_up, w_down = held
    for copy in copies[:1]:
        copy.wait()
    first = (
        rows.astype(F32) + jnp.dot(attended, w_proj[...], preferred_element_type=F32)
    ).astype(BF16)
    hidden = layer_norm(first, gain)
    total = first.astype(F32)
    for copy in copies[1:]:
        copy.wait()
    piece = 512
    for at in range(0, w_up.shape[1], piece):
        upper = jnp.dot(hidden, w_up[:, at : at + piece], preferred_element_type=F32)
        act = gelu(upper).astype(BF16)
        total = total + jnp.dot(act, w_down[at : at + piece, :], preferred_element_type=F32)
    return total.astype(BF16)


def split_kernel(points, destination, pattern, *refs):
    *parts, destination_held, pattern_held, notes, sems = refs
    rows = points.shape[0] // len(parts)
    fetches = started([(destination, destination_held), (pattern, pattern_held)], sems.at[0])
    copies = started(
        [
            (points.at[pl.ds(i * rows, rows), :], part.at[pl.ds(0, rows), :])
            for i, part in enumerate(parts)
        ],
        sems.at[1],
    )
    for fetch in fetches:
        fetch.wait()
    chosen, patches = pattern.shape
    row = lax.broadcasted_iota(jnp.int32, notes.shape, 0)
    low = destination_held[...] & (DIGIT - 1)
    high = lax.shift_right_logical(destination_held[...], DIGIT.bit_length() - 1)
    values = jnp.where(row == chosen, low, jnp.where(row == chosen + 1, high, 0))
    notes[...] = values.astype(F32)
    notes[0:chosen, 0:patches] = pattern_held[...].astype(F32)
    parts[0][rows : rows + TAIL, :] = notes[...].astype(BF16)
    for copy in copies:
        copy.wait()


def keep_kernel(*refs):
    *refs, sems = refs
    count = len(refs) // 2
    for copy in started(
        [
            (source.at[0] if len(source.shape) == 3 else source, place)
            for source, place in zip(refs[:count], refs[count:])
        ],
        sems,
    ):
        copy.wait()


def index_kernel(capacity, destination, beyond, slots, tail, pattern, held, notes, sems):
    added = beyond.at[pl.ds(beyond.shape[0] - TAIL, TAIL), :]
    for fetch in started([(destination, held.at[0]), (added, notes)], sems):
        fetch.wait()
    chosen, patches = pattern.shape
    noted = notes[...].astype(F32)
    pattern[...] = noted[0:chosen, 0:patches].astype(jnp.int32)
    low, high = noted[chosen : chosen + 1, :], noted[chosen + 1 : chosen + 2, :]
    held[1] = (low + DIGIT * high).astype(jnp.int32)
    rows = held.shape[2]
    devices = tail.shape[0]
    in_half = lax.axis_size("seq")
    seq_bits = in_half.bit_length() - 1
    index = lax.axis_index(("grp", "seq"))
    offset = lax.rem(index, LANES // (2 * capacity)) * 2 * capacity
    before = lax.broadcasted_iota(jnp.int32, (rows, rows), 0)
    before = before < lax.broadcasted_iota(jnp.int32, (rows, rows), 1)
    before = jnp.where(before, 1.0, 0.0).astype(BF16)
    lines = jnp.zeros((devices * TAIL, LANES), F32)
    for b in range(2):
        target = lax.shift_right_logical(held[b], rows.bit_length() - 1)
        place = held[b] & (rows - 1)
        half = lax.shift_right_logical(target, seq_bits) & 1
        group = lax.shift_right_logical(target, seq_bits + 1)
        target = group * in_half + (target & (in_half - 1))
        target = jnp.where(half == lax.axis_index("half"), target, -1)
        mine = lax.broadcasted_iota(jnp.int32, (devices, rows), 0) == target
        mine = jnp.where(mine, 1.0, 0.0).astype(F32)
        earlier = jnp.dot(mine.astype(BF16), before, preferred_element_type=F32)
        rank = jnp.sum(mine * earlier, axis=0, keepdims=True).astype(jnp.int32) + b * capacity
        slots[:, b * rows : (b + 1) * rows] = jnp.where(
            target >= 0, target * 2 * capacity + rank, -1
        )
        by_lane = lax.broadcasted_iota(jnp.int32, (LANES, rows), 0) == rank + offset
        by_lane = jnp.where(by_lane, 1.0, 0.0).astype(BF16)
        line = lax.broadcasted_iota(jnp.int32, (devices * TAIL, rows), 0)
        code = place + 1
        low = (code & (DIGIT - 1)).astype(F32)
        high = lax.shift_right_logical(code, DIGIT.bit_length() - 1).astype(F32)
        digit = line & (TAIL - 1)
        digits = jnp.where(digit == 0, low, jnp.where(digit == 1, high, 0.0))
        line = lax.shift_right_logical(line, TAIL.bit_length() - 1)
        digits = jnp.where(line == target, digits, 0.0)
        lines = lines + lax.dot_general(
            digits.astype(BF16), by_lane, (((1,), (1,)), ((), ())), preferred_element_type=F32
        )
    tail[...] = lines.reshape(devices, TAIL, LANES).astype(BF16)


def project_kernel(first_rows, new, ask, *refs):
    count = len(first_rows)
    parts, gains, w_qkv = refs[:count], refs[count], refs[count + 1]
    refs = refs[count + 2 if new else count + 3 :]
    whole, (held, sems) = refs[0], refs[-2:]
    channels = w_qkv.shape[0]
    rows = held.shape[1]
    copies = started(
        [(part.at[pl.ds(0, rows), :], held.at[i]) for i, part in enumerate(parts)], sems
    )
    for i, first in enumerate(first_rows):
        copies[i].wait()
        normed = layer_norm(held[i], gains[0:1, :])
        whole[first : first + rows, :] = jnp.dot(
            normed, w_qkv[:, channels:], preferred_element_type=F32
        ).astype(BF16)
        if ask and i * rows < refs[1].shape[0]:
            scale = BF16((channels // HEADS) ** (-0.5))
            query = jnp.dot(normed, w_qkv[:, :channels], preferred_element_type=F32).astype(BF16)
            refs[1][i * rows : (i + 1) * rows, :] = (query * scale).astype(BF16)


def lane_tiles(packed, rows):
    capacity, channels = rows.shape[1:]
    return [
        (
            packed.at[:, pl.ds(j * capacity, capacity), :],
            rows.at[:, :, pl.ds(j * LANES, LANES)],
        )
        for j in range(channels // LANES)
    ]


def first_kernel(
    ring_chips,
    pattern,
    pattern_beyond,
    slot_of_row,
    gains,
    keyed,
    queries,
    queries_beyond,
    w_proj,
    w_up,
    w_down,
    tail,
    points,
    *refs,
):
    *points_beyond, outgoing, attended, points_held, first_held, outgoing_held, sems = refs
    rows, channels = points.shape
    devices, capacity, _ = outgoing_held.shape
    row_tiles = channels // LANES * capacity
    patches = rows // PATCH
    chosen = pattern.shape[0]
    me = lax.axis_index(GROUP)
    part = rows // len(points_beyond)
    copies = started(
        [(tail, outgoing.at[:, pl.ds(row_tiles, TAIL), :]), (points, points_held.at[:rows])]
        + [
            (piece.at[pl.ds(0, part), :], points_held.at[pl.ds(rows + i * part, part), :])
            for i, piece in enumerate(points_beyond)
        ],
        sems.at[0],
    )
    masks = head_masks(channels // HEADS)
    blocks = ((pattern, queries, 0), (pattern_beyond, queries_beyond, ring_chips or 1))
    for b, (picked, asking, own_slot) in enumerate(blocks):
        for p in range(patches):
            start = own_slot * rows + p * PATCH
            pieces = [keyed[start : start + PATCH, :]]
            for j in range(chosen):
                if ring_chips:
                    patch = picked[j, p]
                    owner, local = lax.div(patch, patches), lax.rem(patch, patches)
                    chip = lax.rem(lax.div(me, 2) - lax.div(owner, 2) + ring_chips, ring_chips)
                    slot = 2 * chip + jnp.where(lax.rem(me, 2) == lax.rem(owner, 2), 0, 1)
                    patch = slot * patches + local
                else:
                    patch = 2 * patches + (b * patches + p) * chosen + j
                start = patch * PATCH
                if ring_chips:
                    start = pl.multiple_of(start, PATCH)
                pieces.append(keyed[pl.ds(start, PATCH), :])
            both = jnp.concatenate(pieces, axis=0)
            attended[b * rows + p * PATCH : b * rows + (p + 1) * PATCH, :] = attend_patch(
                asking[p * PATCH : (p + 1) * PATCH, :], both[:, :channels], both[:, channels:], masks
            )
    for copy in copies[1:]:
        copy.wait()

    @pl.loop(0, 2)
    def _(b):
        here = pl.ds(pl.multiple_of(b * rows, rows), rows)
        first_held[here, :] = finish(
            points_held[here, :], attended[here, :], gains[1:2, :], (w_proj, w_up, w_down)
        )

    copies[0].wait()
    slots = slot_of_row[...]
    targets = devices // SEND_PARTS
    piece = targets * capacity
    leaving = []
    for i in range(SEND_PARTS):
        here = pl.ds(i * targets, targets)
        send = one_hot_rows(slots - i * piece, piece)
        moved = jnp.dot(send, first_held[...], preferred_element_type=F32).astype(BF16)
        outgoing_held[here] = moved.reshape(targets, capacity, channels)
        pairs = lane_tiles(outgoing.at[here], outgoing_held.at[here])
        leaving += started([(source, place) for place, source in pairs], sems.at[1 + i])
    for copy in leaving:
        copy.wait()


def second_kernel(
    pattern,
    gains,
    incoming,
    w_qkv,
    w_proj,
    w_up,
    w_down,
    w_head,
    features,
    normals,
    kv,
    attended,
    incoming_held,
    qkv_held,
    proj_held,
    up_held,
    down_held,
    gains_held,
    tail_held,
    head_held,
    sems,
):
    rows, channels = features.shape
    devices, capacity, _ = incoming_held.shape
    patches = rows // PATCH
    chosen = pattern.shape[0]
    tail = incoming.at[:, pl.ds(channels // LANES * capacity, TAIL), :]
    small = started(
        [(tail, tail_held), (gains, gains_held), (w_head, head_held)], sems.at[0]
    )
    landing = started(lane_tiles(incoming, incoming_held), sems.at[1])
    copies = started(
        [
            (w_qkv.at[1], qkv_held),
            (w_proj.at[1], proj_held),
            (w_up.at[1], up_held),
            (w_down.at[1], down_held),
        ],
        sems.at[2],
    )
    for copy in small:
        copy.wait()
    per_row = LANES // capacity
    digits = tail_held[...].astype(F32)
    codes = digits[:, 0:1, :] + DIGIT * digits[:, 1:2, :]
    pieces = []
    for at in range(0, devices, per_row):
        code = codes[at]
        for i in range(1, per_row):
            code = code + codes[at + i]
        pieces.append(code)
    places = jnp.concatenate(pieces, axis=1).astype(jnp.int32) - 1
    place = one_hot_rows(places, rows)
    for copy in landing:
        copy.wait()
    moved = incoming_held[...].reshape(devices * capacity, channels)
    second = jnp.dot(place, moved, preferred_element_type=F32).astype(BF16)
    normed = layer_norm(second, gains_held[2:3, :])
    scale = (channels // HEADS) ** (-0.5)
    copies[0].wait()
    queries = (
        jnp.dot(normed, qkv_held[:, :channels], preferred_element_type=F32).astype(BF16)
        * BF16(scale)
    ).astype(BF16)
    kv[...] = jnp.dot(normed, qkv_held[:, channels:], preferred_element_type=F32).astype(BF16)
    masks = head_masks(channels // HEADS)
    for p in range(patches):
        pieces = [kv[p * PATCH : (p + 1) * PATCH, :]]
        for j in range(chosen):
            start = pl.multiple_of(pattern[j, p] * PATCH, PATCH)
            pieces.append(kv[pl.ds(start, PATCH), :])
        both = jnp.concatenate(pieces, axis=0)
        attended[p * PATCH : (p + 1) * PATCH, :] = attend_patch(
            queries[p * PATCH : (p + 1) * PATCH, :], both[:, :channels], both[:, channels:], masks
        )
    done = finish(
        second, attended[...], gains_held[3:4, :], (proj_held, up_held, down_held), copies[1:]
    )
    features[...] = done
    normals[...] = lax.dot_general(
        head_held[...], done, (((1,), (1,)), ((), ())), preferred_element_type=F32
    )


VMEM_SPEC = pl.BlockSpec(memory_space=pltpu.VMEM)
SMEM_SPEC = pl.BlockSpec(memory_space=pltpu.SMEM)
ANY_SPEC = pl.BlockSpec(memory_space=pl.ANY)


def shards(
    points,
    pattern_first,
    pattern_second,
    destination,
    norm_gains,
    w_qkv,
    w_proj,
    w_up,
    w_down,
    w_head,
):
    rows_here, channels = points.shape
    patches, chosen = pattern_first.shape
    devices = lax.axis_size("grp") * lax.axis_size("seq")
    capacity = 2 * rows_here // (2 * devices)
    pair_slots = 2 * capacity

    shards_in_group = lax.axis_size(GROUP)
    chips = shards_in_group // 2
    onward = [(i, (i + 2) % shards_in_group) for i in range(shards_in_group)]
    swap = [(i, i ^ 1) for i in range(shards_in_group)]
    across = [(i, (i + chips) % shards_in_group) for i in range(shards_in_group)]
    ring = shards_in_group * rows_here * 2 * channels * 2 <= RING_BYTES
    kept_rows = shards_in_group * rows_here if ring else 2 * patches * (1 + chosen) * PATCH
    part = rows_here // RING_PARTS

    destination = destination.reshape(1, rows_here)
    pattern_first = pattern_first.T
    part_rows = [part + TAIL] + [part] * (RING_PARTS - 1)
    column = pl.pallas_call(
        split_kernel,
        out_shape=[jax.ShapeDtypeStruct((rows, channels), BF16) for rows in part_rows],
        in_specs=[ANY_SPEC] * 3,
        out_specs=[VMEM_SPEC] * RING_PARTS,
        scratch_shapes=[
            pltpu.VMEM((1, rows_here), jnp.int32),
            pltpu.VMEM(pattern_first.shape, jnp.int32),
            pltpu.VMEM((TAIL, channels), F32),
            pltpu.SemaphoreType.DMA((2, RING_PARTS)),
        ],
        compiler_params=pltpu.CompilerParams(vmem_limit_bytes=SPLIT_BYTES),
        name="split",
    )(points, destination, pattern_first)

    weights = (w_proj, w_up, w_down)
    kv_shape = jax.ShapeDtypeStruct((kept_rows, 2 * channels), BF16)
    own_shape = jax.ShapeDtypeStruct((rows_here, channels), BF16)

    qkv_kept, *kept, gains_kept = pl.pallas_call(
        keep_kernel,
        out_shape=[
            *[jax.ShapeDtypeStruct(w.shape[1:], BF16) for w in (w_qkv,) + weights],
            jax.ShapeDtypeStruct(norm_gains.shape, F32),
        ],
        in_specs=[ANY_SPEC] * 5,
        out_specs=[VMEM_SPEC] * 5,
        scratch_shapes=[pltpu.SemaphoreType.DMA((5,))],
        compiler_params=pltpu.CompilerParams(vmem_limit_bytes=PREPARE_BYTES),
        name="keep",
    )(w_qkv, *weights, norm_gains)
    def index(beyond):
        return pl.pallas_call(
            functools.partial(index_kernel, capacity),
            out_shape=[
                jax.ShapeDtypeStruct((1, 2 * rows_here), jnp.int32),
                jax.ShapeDtypeStruct((devices, TAIL, LANES), BF16),
                jax.ShapeDtypeStruct(pattern_first.shape, jnp.int32),
            ],
            in_specs=[ANY_SPEC] * 2,
            out_specs=[VMEM_SPEC] * 3,
            scratch_shapes=[
                pltpu.VMEM((2, 1, rows_here), jnp.int32),
                pltpu.VMEM((TAIL, channels), BF16),
                pltpu.SemaphoreType.DMA((2,)),
            ],
            compiler_params=pltpu.CompilerParams(vmem_limit_bytes=PROJECT_BYTES),
            name="index",
        )(destination, beyond)

    def project(keyed, blocks, ask=False, rows=part):
        parts = [piece for _, block in blocks for piece in block]
        count = len(parts)
        first_rows = [
            slot * rows_here + i * rows for slot, block in blocks for i in range(len(block))
        ]
        new = keyed is None
        return pl.pallas_call(
            functools.partial(project_kernel, first_rows, new, ask),
            out_shape=[kv_shape] + [own_shape] * ask,
            in_specs=[ANY_SPEC] * count + [VMEM_SPEC] * (2 if new else 3),
            out_specs=[VMEM_SPEC] * (1 + ask),
            scratch_shapes=[
                pltpu.VMEM((count, rows, channels), BF16),
                pltpu.SemaphoreType.DMA((count,)),
            ],
            input_output_aliases={} if new else {count + 2: 0},
            cost_estimate=pl.CostEstimate(
                flops=4 * count * rows * channels**2,
                bytes_accessed=3 * count * rows * channels * 2 + 3 * channels**2 * 2,
                transcendentals=0,
            ),
            compiler_params=pltpu.CompilerParams(vmem_limit_bytes=PROJECT_BYTES),
            name="project_own" if new else "project",
        )(*parts, gains_kept, qkv_kept, *([] if new else [keyed]))

    if ring:
        beside = [lax.ppermute(rows, GROUP, swap) for rows in column]
        waiting = [(0, column), (1, beside)]
        for step in range(1, chips):
            column = [lax.ppermute(rows, GROUP, onward) for rows in column]
            if step == 1:
                column[0], gains_kept = lax.optimization_barrier((column[0], gains_kept))
                keyed, queries = project(None, waiting, ask=True)
                column[1], keyed = lax.optimization_barrier((column[1], keyed))
            else:
                for i, block in enumerate(waiting):
                    if block[0] == chips:
                        keyed, queries_beyond = project(keyed, [block], ask=True)
                    else:
                        (keyed,) = project(keyed, [block])
                    column[i], keyed = lax.optimization_barrier((column[i], keyed))
            if step == chips // 2:
                points_beyond = column
                slot_index, tail, pattern_beyond = index(column[0])
            if step == chips - 1:
                column[0], slot_index = lax.optimization_barrier((column[0], slot_index))
            beside = [lax.ppermute(rows, GROUP, swap) for rows in column]
            waiting = [(2 * step, column), (2 * step + 1, beside)]
        for block in waiting:
            (keyed,) = project(keyed, [block])
    else:
        group = lax.all_gather(points, GROUP, axis=0, tiled=True)
        partner = lax.rem(lax.axis_index(GROUP) + chips, shards_in_group)
        points_beyond = [lax.dynamic_slice_in_dim(group, partner * rows_here, rows_here)]
        group = group.reshape(-1, PATCH, channels)
        slot_index, tail, pattern_beyond = index(lax.ppermute(column[0], GROUP, across))
        picked = [
            group[pattern.T].reshape(-1, channels) for pattern in (pattern_first, pattern_beyond)
        ]
        wide = picked[0].shape[0]
        keyed, queries = project(None, [(0, column)], ask=True)
        keyed, queries_beyond = project(keyed, [(1, points_beyond)], ask=True, rows=rows_here)
        (keyed,) = project(keyed, [(2, [picked[0]])], rows=wide)
        (keyed,) = project(keyed, [(2 + chosen, [picked[1]])], rows=wide)

    held_weights = [pltpu.VMEM(w.shape[1:], BF16) for w in weights]
    held_rows = pltpu.VMEM((rows_here, channels), BF16)
    held_slots = pltpu.VMEM((devices, pair_slots, channels), BF16)
    held_both = pltpu.VMEM((2 * rows_here, channels), BF16)
    pair_rows = channels // LANES * pair_slots + TAIL
    outgoing = pl.pallas_call(
        functools.partial(first_kernel, chips if ring else 0),
        out_shape=jax.ShapeDtypeStruct((devices, pair_rows, LANES), BF16),
        in_specs=[SMEM_SPEC] * 2 + [VMEM_SPEC] * 8 + [ANY_SPEC] * (2 + len(points_beyond)),
        out_specs=ANY_SPEC,
        scratch_shapes=[
            held_both,
            held_both,
            held_both,
            held_slots,
            pltpu.SemaphoreType.DMA((1 + SEND_PARTS, 4)),
        ],
        compiler_params=pltpu.CompilerParams(vmem_limit_bytes=FIRST_BYTES),
        name="block_first",
    )(
        pattern_first,
        pattern_beyond,
        slot_index,
        gains_kept,
        keyed,
        queries,
        queries_beyond,
        *kept,
        tail,
        points,
        *points_beyond,
    )
    incoming = lax.all_to_all(outgoing, ("grp", "seq"), split_axis=0, concat_axis=0, tiled=True)

    return pl.pallas_call(
        second_kernel,
        out_shape=(
            jax.ShapeDtypeStruct((rows_here, channels), BF16),
            jax.ShapeDtypeStruct((w_head.shape[0], rows_here), F32),
        ),
        in_specs=[SMEM_SPEC] + [ANY_SPEC] * 7,
        out_specs=(VMEM_SPEC, VMEM_SPEC),
        scratch_shapes=[
            pltpu.VMEM((rows_here, 2 * channels), BF16),
            held_rows,
            held_slots,
            pltpu.VMEM(w_qkv.shape[1:], BF16),
            *held_weights,
            pltpu.VMEM(norm_gains.shape, F32),
            pltpu.VMEM(tail.shape, BF16),
            pltpu.VMEM(w_head.shape, BF16),
            pltpu.SemaphoreType.DMA((3, 5)),
        ],
        compiler_params=pltpu.CompilerParams(vmem_limit_bytes=SECOND_BYTES),
        name="block_second",
    )(pattern_second.T, norm_gains, incoming, w_qkv, *weights, w_head)


def solution(mesh):
    groups, shards_in_group = mesh.devices.shape
    halves = Mesh(
        mesh.devices.reshape(groups, 2, shards_in_group // 2), ("grp",) + GROUP
    )
    everywhere = ("grp",) + GROUP
    placed = (
        P(everywhere, None),
        P(everywhere, None),
        P(everywhere, None),
        P(everywhere),
        P(),
        P(),
        P(),
        P(),
        P(),
        P(),
    )
    return jax.shard_map(
        shards,
        mesh=halves,
        in_specs=placed,
        out_specs=(P(everywhere, None), P(None, everywhere)),
        check_vma=False,
    )
```

```python
import functools

import jax
import jax.numpy as jnp
from jax import lax
from jax.experimental import pallas as pl
from jax.experimental.pallas import tpu as pltpu
from jax.sharding import Mesh, PartitionSpec as P

HEADS = 8
PATCH = 64
HEADS_TOGETHER = 4
GROUP = ("half", "seq")
RING_PARTS = 2
SEND_PARTS = 4
LANES = 128
TAIL = 8
DIGIT = 256
FIRST_BYTES = 28 * 1024 * 1024
SECOND_BYTES = 50 * 1024 * 1024
PROJECT_BYTES = 16 * 1024 * 1024
SPLIT_BYTES = 60 * 1024 * 1024
PREPARE_BYTES = 46 * 1024 * 1024
RING_BYTES = 16 * 1024 * 1024
F32 = jnp.float32
BF16 = jnp.bfloat16


def layer_norm(rows, gains):
    values = rows.astype(F32)
    average = jnp.mean(values, axis=-1, keepdims=True)
    spread = jnp.mean((values - average) ** 2, axis=-1, keepdims=True)
    return ((values - average) * lax.rsqrt(spread + 1e-05) * gains).astype(BF16)


def gelu(x):
    half = 0.5 * x
    return half + half * lax.erf(x * 0.5**0.5)


def head_masks(head_dim):
    lane = lax.broadcasted_iota(jnp.int32, (PATCH, HEADS_TOGETHER * head_dim), 1)
    return [
        jnp.where((lane >= h * head_dim) & (lane < (h + 1) * head_dim), 1.0, 0.0).astype(BF16)
        for h in range(HEADS_TOGETHER)
    ]


def attend(patches, head_dim):
    masks = head_masks(head_dim)
    width = HEADS_TOGETHER * head_dim
    heads_per_tile = LANES // head_dim
    lane = lax.broadcasted_iota(jnp.int32, (PATCH, LANES), 1)
    steps = [(p, g) for p in range(len(patches)) for g in range(HEADS // HEADS_TOGETHER)]

    def scores_of(step):
        p, g = step
        queries, keys, _ = patches[p]
        q = queries(g * width, width)
        stacked = jnp.concatenate([q * mask for mask in masks], axis=0)
        return lax.dot_general(
            stacked, keys(g * width, width), (((1,), (1,)), ((), ())), preferred_element_type=F32
        )

    scores = scores_of(steps[0])
    for i, (p, g) in enumerate(steps):
        later = scores_of(steps[i + 1]) if i + 1 < len(steps) else None
        grown = jnp.exp(scores - jnp.max(scores, axis=-1, keepdims=True))
        scale = 1.0 / jnp.sum(grown, axis=-1, keepdims=True)
        values = patches[p][2](g * width, width)
        mixed = jnp.dot(grown.astype(BF16), values, preferred_element_type=F32)
        tiles = []
        for t in range(width // LANES):
            tile = None
            for h in range(heads_per_tile):
                rows = slice((t * heads_per_tile + h) * PATCH, (t * heads_per_tile + h + 1) * PATCH)
                head = mixed[rows, t * LANES : (t + 1) * LANES] * scale[rows]
                tile = head if tile is None else jnp.where(lane < h * head_dim, tile, head)
            tiles.append(tile)
        yield p, g * width, jnp.concatenate(tiles, axis=1).astype(BF16)
        scores = later


def one_hot_rows(places, rows):
    row = lax.broadcasted_iota(jnp.int32, (rows, places.shape[1]), 0)
    return jnp.where(row == places, 1.0, 0.0).astype(BF16)


def started(pairs, sems):
    copies = [
        pltpu.make_async_copy(source, place, sems.at[at])
        for at, (source, place) in enumerate(pairs)
    ]
    for copy in copies:
        copy.start()
    return copies


def finish(rows, attended, gain, held, copies=()):
    w_proj, w_up, w_down = held
    for copy in copies[:1]:
        copy.wait()
    first = (
        rows.astype(F32) + jnp.dot(attended, w_proj[...], preferred_element_type=F32)
    ).astype(BF16)
    hidden = layer_norm(first, gain)
    total = first.astype(F32)
    for copy in copies[1:]:
        copy.wait()
    piece = 512
    pieces = range(0, w_up.shape[1], piece)
    upper = jnp.dot(hidden, w_up[:, :piece], preferred_element_type=F32)
    for at in pieces:
        later = None
        if at + piece < w_up.shape[1]:
            later = jnp.dot(
                hidden, w_up[:, at + piece : at + 2 * piece], preferred_element_type=F32
            )
        act = gelu(upper).astype(BF16)
        total = total + jnp.dot(act, w_down[at : at + piece, :], preferred_element_type=F32)
        upper = later
    return total.astype(BF16)


def split_kernel(points, destination, pattern, *refs):
    *parts, destination_held, pattern_held, notes, sems = refs
    rows = points.shape[0] // len(parts)
    fetches = started([(destination, destination_held), (pattern, pattern_held)], sems.at[0])
    copies = started(
        [
            (points.at[pl.ds(i * rows, rows), :], part.at[pl.ds(0, rows), :])
            for i, part in enumerate(parts)
        ],
        sems.at[1],
    )
    for fetch in fetches:
        fetch.wait()
    chosen, patches = pattern.shape
    row = lax.broadcasted_iota(jnp.int32, notes.shape, 0)
    low = destination_held[...] & (DIGIT - 1)
    high = lax.shift_right_logical(destination_held[...], DIGIT.bit_length() - 1)
    values = jnp.where(row == chosen, low, jnp.where(row == chosen + 1, high, 0))
    notes[...] = values.astype(F32)
    notes[0:chosen, 0:patches] = pattern_held[...].astype(F32)
    parts[0][rows : rows + TAIL, :] = notes[...].astype(BF16)
    for copy in copies:
        copy.wait()


def keep_kernel(*refs):
    *refs, sems = refs
    count = len(refs) // 2
    for copy in started(
        [
            (source.at[0] if len(source.shape) == 3 else source, place)
            for source, place in zip(refs[:count], refs[count:])
        ],
        sems,
    ):
        copy.wait()


def index_kernel(capacity, destination, beyond, slots, tail, pattern, held, notes, sems):
    added = beyond.at[pl.ds(beyond.shape[0] - TAIL, TAIL), :]
    for fetch in started([(destination, held.at[0]), (added, notes)], sems):
        fetch.wait()
    chosen, patches = pattern.shape
    noted = notes[...].astype(F32)
    pattern[...] = noted[0:chosen, 0:patches].astype(jnp.int32)
    low, high = noted[chosen : chosen + 1, :], noted[chosen + 1 : chosen + 2, :]
    held[1] = (low + DIGIT * high).astype(jnp.int32)
    rows = held.shape[2]
    devices = tail.shape[0]
    in_half = lax.axis_size("seq")
    seq_bits = in_half.bit_length() - 1
    index = lax.axis_index(("grp", "seq"))
    offset = lax.rem(index, LANES // (2 * capacity)) * 2 * capacity
    before = lax.broadcasted_iota(jnp.int32, (rows, rows), 0)
    before = before < lax.broadcasted_iota(jnp.int32, (rows, rows), 1)
    before = jnp.where(before, 1.0, 0.0).astype(BF16)
    lines = jnp.zeros((devices * TAIL, LANES), F32)
    for b in range(2):
        target = lax.shift_right_logical(held[b], rows.bit_length() - 1)
        place = held[b] & (rows - 1)
        half = lax.shift_right_logical(target, seq_bits) & 1
        group = lax.shift_right_logical(target, seq_bits + 1)
        target = group * in_half + (target & (in_half - 1))
        target = jnp.where(half == lax.axis_index("half"), target, -1)
        mine = lax.broadcasted_iota(jnp.int32, (devices, rows), 0) == target
        mine = jnp.where(mine, 1.0, 0.0).astype(F32)
        earlier = jnp.dot(mine.astype(BF16), before, preferred_element_type=F32)
        rank = jnp.sum(mine * earlier, axis=0, keepdims=True).astype(jnp.int32) + b * capacity
        slots[:, b * rows : (b + 1) * rows] = jnp.where(
            target >= 0, target * 2 * capacity + rank, -1
        )
        by_lane = lax.broadcasted_iota(jnp.int32, (LANES, rows), 0) == rank + offset
        by_lane = jnp.where(by_lane, 1.0, 0.0).astype(BF16)
        line = lax.broadcasted_iota(jnp.int32, (devices * TAIL, rows), 0)
        code = place + 1
        low = (code & (DIGIT - 1)).astype(F32)
        high = lax.shift_right_logical(code, DIGIT.bit_length() - 1).astype(F32)
        digit = line & (TAIL - 1)
        digits = jnp.where(digit == 0, low, jnp.where(digit == 1, high, 0.0))
        line = lax.shift_right_logical(line, TAIL.bit_length() - 1)
        digits = jnp.where(line == target, digits, 0.0)
        lines = lines + lax.dot_general(
            digits.astype(BF16), by_lane, (((1,), (1,)), ((), ())), preferred_element_type=F32
        )
    tail[...] = lines.reshape(devices, TAIL, LANES).astype(BF16)


def project_kernel(first_rows, new, ask, *refs):
    count = len(first_rows)
    parts, gains, w_qkv = refs[:count], refs[count], refs[count + 1]
    refs = refs[count + 2 if new else count + 3 :]
    whole, (held, sems) = refs[0], refs[-2:]
    channels = w_qkv.shape[0]
    rows = held.shape[1]
    copies = started(
        [(part.at[pl.ds(0, rows), :], held.at[i]) for i, part in enumerate(parts)], sems
    )
    for i, first in enumerate(first_rows):
        copies[i].wait()
        normed = layer_norm(held[i], gains[0:1, :])
        whole[first : first + rows, :] = jnp.dot(
            normed, w_qkv[:, channels:], preferred_element_type=F32
        ).astype(BF16)
        if ask and i * rows < refs[1].shape[0]:
            scale = BF16((channels // HEADS) ** (-0.5))
            query = jnp.dot(normed, w_qkv[:, :channels], preferred_element_type=F32).astype(BF16)
            refs[1][i * rows : (i + 1) * rows, :] = (query * scale).astype(BF16)


def loads(queries, p, keyed, starts):
    channels = queries.shape[1]

    def asked(at, width):
        return queries[p * PATCH : (p + 1) * PATCH, at : at + width]

    def keys(at, width):
        pieces = [keyed[pl.ds(start, PATCH), at : at + width] for start in starts]
        return jnp.concatenate(pieces, axis=0)

    return asked, keys, lambda at, width: keys(channels + at, width)


def lane_tiles(packed, rows):
    capacity, channels = rows.shape[1:]
    return [
        (
            packed.at[:, pl.ds(j * capacity, capacity), :],
            rows.at[:, :, pl.ds(j * LANES, LANES)],
        )
        for j in range(channels // LANES)
    ]


def first_kernel(
    ring_chips,
    pattern,
    pattern_beyond,
    slot_of_row,
    gains,
    keyed,
    queries,
    queries_beyond,
    w_proj,
    w_up,
    w_down,
    tail,
    points,
    *refs,
):
    *points_beyond, outgoing, attended, points_held, first_held, outgoing_held, sems = refs
    rows, channels = points.shape
    devices, capacity, _ = outgoing_held.shape
    row_tiles = channels // LANES * capacity
    patches = rows // PATCH
    chosen = pattern.shape[0]
    me = lax.axis_index(GROUP)
    part = rows // len(points_beyond)
    copies = started(
        [(tail, outgoing.at[:, pl.ds(row_tiles, TAIL), :]), (points, points_held.at[:rows])]
        + [
            (piece.at[pl.ds(0, part), :], points_held.at[pl.ds(rows + i * part, part), :])
            for i, piece in enumerate(points_beyond)
        ],
        sems.at[0],
    )
    blocks = ((pattern, queries, 0), (pattern_beyond, queries_beyond, ring_chips or 1))
    loaded = []
    for b, (picked, asking, own_slot) in enumerate(blocks):
        for p in range(patches):
            starts = [own_slot * rows + p * PATCH]
            for j in range(chosen):
                if ring_chips:
                    patch = picked[j, p]
                    owner, local = lax.div(patch, patches), lax.rem(patch, patches)
                    chip = lax.rem(lax.div(me, 2) - lax.div(owner, 2) + ring_chips, ring_chips)
                    slot = 2 * chip + jnp.where(lax.rem(me, 2) == lax.rem(owner, 2), 0, 1)
                    starts.append(pl.multiple_of((slot * patches + local) * PATCH, PATCH))
                else:
                    starts.append((2 * patches + (b * patches + p) * chosen + j) * PATCH)
            loaded.append(loads(asking, p, keyed, starts))
    for p, at, rows_done in attend(loaded, channels // HEADS):
        attended[p * PATCH : (p + 1) * PATCH, at : at + rows_done.shape[1]] = rows_done
    for copy in copies[1:]:
        copy.wait()

    @pl.loop(0, 2)
    def _(b):
        here = pl.ds(pl.multiple_of(b * rows, rows), rows)
        first_held[here, :] = finish(
            points_held[here, :], attended[here, :], gains[1:2, :], (w_proj, w_up, w_down)
        )

    copies[0].wait()
    slots = slot_of_row[...]
    targets = devices // SEND_PARTS
    piece = targets * capacity
    leaving = []
    for i in range(SEND_PARTS):
        here = pl.ds(i * targets, targets)
        send = one_hot_rows(slots - i * piece, piece)
        moved = jnp.dot(send, first_held[...], preferred_element_type=F32).astype(BF16)
        outgoing_held[here] = moved.reshape(targets, capacity, channels)
        pairs = lane_tiles(outgoing.at[here], outgoing_held.at[here])
        leaving += started([(source, place) for place, source in pairs], sems.at[1 + i])
    for copy in leaving:
        copy.wait()


def second_kernel(
    pattern,
    gains,
    incoming,
    w_qkv,
    w_proj,
    w_up,
    w_down,
    w_head,
    features,
    normals,
    kv,
    queries,
    attended,
    incoming_held,
    qkv_held,
    proj_held,
    up_held,
    down_held,
    gains_held,
    tail_held,
    head_held,
    sems,
):
    rows, channels = features.shape
    devices, capacity, _ = incoming_held.shape
    patches = rows // PATCH
    chosen = pattern.shape[0]
    tail = incoming.at[:, pl.ds(channels // LANES * capacity, TAIL), :]
    small = started(
        [(tail, tail_held), (gains, gains_held), (w_head, head_held)], sems.at[0]
    )
    landing = started(lane_tiles(incoming, incoming_held), sems.at[1])
    copies = started(
        [
            (w_qkv.at[1], qkv_held),
            (w_proj.at[1], proj_held),
            (w_up.at[1], up_held),
            (w_down.at[1], down_held),
        ],
        sems.at[2],
    )
    for copy in small:
        copy.wait()
    per_row = LANES // capacity
    digits = tail_held[...].astype(F32)
    codes = digits[:, 0:1, :] + DIGIT * digits[:, 1:2, :]
    pieces = []
    for at in range(0, devices, per_row):
        code = codes[at]
        for i in range(1, per_row):
            code = code + codes[at + i]
        pieces.append(code)
    places = jnp.concatenate(pieces, axis=1).astype(jnp.int32) - 1
    place = one_hot_rows(places, rows)
    sides = []
    for at in range(0, len(landing), 2):
        for copy in landing[at : at + 2]:
            copy.wait()
        moved = incoming_held[:, :, at * LANES : (at + 2) * LANES]
        moved = moved.reshape(devices * capacity, 2 * LANES)
        sides.append(jnp.dot(place, moved, preferred_element_type=F32).astype(BF16))
    second = jnp.concatenate(sides, axis=1)
    normed = layer_norm(second, gains_held[2:3, :])
    scale = (channels // HEADS) ** (-0.5)
    copies[0].wait()
    asked = jnp.dot(normed, qkv_held[:, :channels], preferred_element_type=F32).astype(BF16)
    queries[...] = (asked * BF16(scale)).astype(BF16)
    kv[...] = jnp.dot(normed, qkv_held[:, channels:], preferred_element_type=F32).astype(BF16)
    loaded = []
    for p in range(patches):
        starts = [pl.multiple_of(pattern[j, p] * PATCH, PATCH) for j in range(chosen)]
        loaded.append(loads(queries, p, kv, [p * PATCH] + starts))
    for p, at, rows_done in attend(loaded, channels // HEADS):
        attended[p * PATCH : (p + 1) * PATCH, at : at + rows_done.shape[1]] = rows_done
    done = finish(
        second, attended[...], gains_held[3:4, :], (proj_held, up_held, down_held), copies[1:]
    )
    features[...] = done
    normals[...] = lax.dot_general(
        head_held[...], done, (((1,), (1,)), ((), ())), preferred_element_type=F32
    )


VMEM_SPEC = pl.BlockSpec(memory_space=pltpu.VMEM)
SMEM_SPEC = pl.BlockSpec(memory_space=pltpu.SMEM)
ANY_SPEC = pl.BlockSpec(memory_space=pl.ANY)


def shards(
    points,
    pattern_first,
    pattern_second,
    destination,
    norm_gains,
    w_qkv,
    w_proj,
    w_up,
    w_down,
    w_head,
):
    rows_here, channels = points.shape
    patches, chosen = pattern_first.shape
    devices = lax.axis_size("grp") * lax.axis_size("seq")
    capacity = 2 * rows_here // (2 * devices)
    pair_slots = 2 * capacity

    shards_in_group = lax.axis_size(GROUP)
    chips = shards_in_group // 2
    onward = [(i, (i + 2) % shards_in_group) for i in range(shards_in_group)]
    swap = [(i, i ^ 1) for i in range(shards_in_group)]
    across = [(i, (i + chips) % shards_in_group) for i in range(shards_in_group)]
    ring = shards_in_group * rows_here * 2 * channels * 2 <= RING_BYTES
    kept_rows = shards_in_group * rows_here if ring else 2 * patches * (1 + chosen) * PATCH
    part = rows_here // RING_PARTS

    destination = destination.reshape(1, rows_here)
    pattern_first = pattern_first.T
    part_rows = [part + TAIL] + [part] * (RING_PARTS - 1)
    column = pl.pallas_call(
        split_kernel,
        out_shape=[jax.ShapeDtypeStruct((rows, channels), BF16) for rows in part_rows],
        in_specs=[ANY_SPEC] * 3,
        out_specs=[VMEM_SPEC] * RING_PARTS,
        scratch_shapes=[
            pltpu.VMEM((1, rows_here), jnp.int32),
            pltpu.VMEM(pattern_first.shape, jnp.int32),
            pltpu.VMEM((TAIL, channels), F32),
            pltpu.SemaphoreType.DMA((2, RING_PARTS)),
        ],
        compiler_params=pltpu.CompilerParams(vmem_limit_bytes=SPLIT_BYTES),
        name="split",
    )(points, destination, pattern_first)

    weights = (w_proj, w_up, w_down)
    kv_shape = jax.ShapeDtypeStruct((kept_rows, 2 * channels), BF16)
    own_shape = jax.ShapeDtypeStruct((rows_here, channels), BF16)

    qkv_kept, *kept, gains_kept = pl.pallas_call(
        keep_kernel,
        out_shape=[
            *[jax.ShapeDtypeStruct(w.shape[1:], BF16) for w in (w_qkv,) + weights],
            jax.ShapeDtypeStruct(norm_gains.shape, F32),
        ],
        in_specs=[ANY_SPEC] * 5,
        out_specs=[VMEM_SPEC] * 5,
        scratch_shapes=[pltpu.SemaphoreType.DMA((5,))],
        compiler_params=pltpu.CompilerParams(vmem_limit_bytes=PREPARE_BYTES),
        name="keep",
    )(w_qkv, *weights, norm_gains)
    def index(beyond):
        return pl.pallas_call(
            functools.partial(index_kernel, capacity),
            out_shape=[
                jax.ShapeDtypeStruct((1, 2 * rows_here), jnp.int32),
                jax.ShapeDtypeStruct((devices, TAIL, LANES), BF16),
                jax.ShapeDtypeStruct(pattern_first.shape, jnp.int32),
            ],
            in_specs=[ANY_SPEC] * 2,
            out_specs=[VMEM_SPEC] * 3,
            scratch_shapes=[
                pltpu.VMEM((2, 1, rows_here), jnp.int32),
                pltpu.VMEM((TAIL, channels), BF16),
                pltpu.SemaphoreType.DMA((2,)),
            ],
            compiler_params=pltpu.CompilerParams(vmem_limit_bytes=PROJECT_BYTES),
            name="index",
        )(destination, beyond)

    def project(keyed, blocks, ask=False, rows=part):
        parts = [piece for _, _, block in blocks for piece in block]
        count = len(parts)
        first_rows = [
            slot * rows_here + first + i * rows
            for slot, first, block in blocks
            for i in range(len(block))
        ]
        new = keyed is None
        return pl.pallas_call(
            functools.partial(project_kernel, first_rows, new, ask),
            out_shape=[kv_shape] + [own_shape] * ask,
            in_specs=[ANY_SPEC] * count + [VMEM_SPEC] * (2 if new else 3),
            out_specs=[VMEM_SPEC] * (1 + ask),
            scratch_shapes=[
                pltpu.VMEM((count, rows, channels), BF16),
                pltpu.SemaphoreType.DMA((count,)),
            ],
            input_output_aliases={} if new else {count + 2: 0},
            cost_estimate=pl.CostEstimate(
                flops=4 * count * rows * channels**2,
                bytes_accessed=3 * count * rows * channels * 2 + 3 * channels**2 * 2,
                transcendentals=0,
            ),
            compiler_params=pltpu.CompilerParams(vmem_limit_bytes=PROJECT_BYTES),
            name="project_own" if new else "project",
        )(*parts, gains_kept, qkv_kept, *([] if new else [keyed]))

    if ring:
        beside = [lax.ppermute(rows, GROUP, swap) for rows in column]
        waiting = [(0, 0, column), (1, 0, beside)]
        for step in range(1, chips):
            column = [lax.ppermute(rows, GROUP, onward) for rows in column]
            if step == 1:
                column[0], gains_kept = lax.optimization_barrier((column[0], gains_kept))
                keyed, queries = project(None, waiting, ask=True)
                column[1], keyed = lax.optimization_barrier((column[1], keyed))
            else:
                for i, block in enumerate(waiting):
                    if block[0] == chips:
                        keyed, queries_beyond = project(keyed, [block], ask=True)
                    else:
                        (keyed,) = project(keyed, [block])
                    column[i], keyed = lax.optimization_barrier((column[i], keyed))
            if step == chips // 2:
                points_beyond = column
                slot_index, tail, pattern_beyond = index(column[0])
            if step == chips - 1:
                column[0], slot_index = lax.optimization_barrier((column[0], slot_index))
            beside = [lax.ppermute(rows, GROUP, swap) for rows in column]
            waiting = [(2 * step, 0, column), (2 * step + 1, 0, beside)]
        for i in range(RING_PARTS):
            halves = [(slot, i * part, block[i : i + 1]) for slot, _, block in waiting]
            if i + 1 < RING_PARTS:
                (keyed,) = project(keyed, halves)
            else:
                for half in halves:
                    (keyed,) = project(keyed, [half])
    else:
        group = lax.all_gather(points, GROUP, axis=0, tiled=True)
        partner = lax.rem(lax.axis_index(GROUP) + chips, shards_in_group)
        points_beyond = [lax.dynamic_slice_in_dim(group, partner * rows_here, rows_here)]
        group = group.reshape(-1, PATCH, channels)
        slot_index, tail, pattern_beyond = index(lax.ppermute(column[0], GROUP, across))
        picked = [
            group[pattern.T].reshape(-1, channels) for pattern in (pattern_first, pattern_beyond)
        ]
        wide = picked[0].shape[0]
        keyed, queries = project(None, [(0, 0, column)], ask=True)
        keyed, queries_beyond = project(keyed, [(1, 0, points_beyond)], ask=True, rows=rows_here)
        (keyed,) = project(keyed, [(2, 0, [picked[0]])], rows=wide)
        (keyed,) = project(keyed, [(2 + chosen, 0, [picked[1]])], rows=wide)

    held_weights = [pltpu.VMEM(w.shape[1:], BF16) for w in weights]
    held_rows = pltpu.VMEM((rows_here, channels), BF16)
    held_slots = pltpu.VMEM((devices, pair_slots, channels), BF16)
    held_both = pltpu.VMEM((2 * rows_here, channels), BF16)
    pair_rows = channels // LANES * pair_slots + TAIL
    outgoing = pl.pallas_call(
        functools.partial(first_kernel, chips if ring else 0),
        out_shape=jax.ShapeDtypeStruct((devices, pair_rows, LANES), BF16),
        in_specs=[SMEM_SPEC] * 2 + [VMEM_SPEC] * 8 + [ANY_SPEC] * (2 + len(points_beyond)),
        out_specs=ANY_SPEC,
        scratch_shapes=[
            held_both,
            held_both,
            held_both,
            held_slots,
            pltpu.SemaphoreType.DMA((1 + SEND_PARTS, 4)),
        ],
        compiler_params=pltpu.CompilerParams(vmem_limit_bytes=FIRST_BYTES),
        name="block_first",
    )(
        pattern_first,
        pattern_beyond,
        slot_index,
        gains_kept,
        keyed,
        queries,
        queries_beyond,
        *kept,
        tail,
        points,
        *points_beyond,
    )
    incoming = lax.all_to_all(outgoing, ("grp", "seq"), split_axis=0, concat_axis=0, tiled=True)

    return pl.pallas_call(
        second_kernel,
        out_shape=(
            jax.ShapeDtypeStruct((rows_here, channels), BF16),
            jax.ShapeDtypeStruct((w_head.shape[0], rows_here), F32),
        ),
        in_specs=[SMEM_SPEC] + [ANY_SPEC] * 7,
        out_specs=(VMEM_SPEC, VMEM_SPEC),
        scratch_shapes=[
            pltpu.VMEM((rows_here, 2 * channels), BF16),
            held_rows,
            held_rows,
            held_slots,
            pltpu.VMEM(w_qkv.shape[1:], BF16),
            *held_weights,
            pltpu.VMEM(norm_gains.shape, F32),
            pltpu.VMEM(tail.shape, BF16),
            pltpu.VMEM(w_head.shape, BF16),
            pltpu.SemaphoreType.DMA((3, 5)),
        ],
        compiler_params=pltpu.CompilerParams(vmem_limit_bytes=SECOND_BYTES),
        name="block_second",
    )(pattern_second.T, norm_gains, incoming, w_qkv, *weights, w_head)


def solution(mesh):
    groups, shards_in_group = mesh.devices.shape
    halves = Mesh(
        mesh.devices.reshape(groups, 2, shards_in_group // 2), ("grp",) + GROUP
    )
    everywhere = ("grp",) + GROUP
    placed = (
        P(everywhere, None),
        P(everywhere, None),
        P(everywhere, None),
        P(everywhere),
        P(),
        P(),
        P(),
        P(),
        P(),
        P(),
    )
    return jax.shard_map(
        shards,
        mesh=halves,
        in_specs=placed,
        out_specs=(P(everywhere, None), P(None, everywhere)),
        check_vma=False,
    )
```

```python
import functools

import jax
import jax.numpy as jnp
from jax import lax
from jax.experimental import pallas as pl
from jax.experimental.pallas import tpu as pltpu
from jax.sharding import Mesh, PartitionSpec as P

HEADS = 8
PATCH = 64
HEADS_TOGETHER = 4
GROUP = ("half", "seq")
RING_PARTS = 2
SEND_PARTS = 4
LANES = 128
TAIL = 8
DIGIT = 256
FIRST_BYTES = 28 * 1024 * 1024
SECOND_BYTES = 50 * 1024 * 1024
PROJECT_BYTES = 16 * 1024 * 1024
SPLIT_BYTES = 60 * 1024 * 1024
PREPARE_BYTES = 46 * 1024 * 1024
RING_BYTES = 16 * 1024 * 1024
F32 = jnp.float32
BF16 = jnp.bfloat16


def layer_norm(rows, gains):
    values = rows.astype(F32)
    average = jnp.mean(values, axis=-1, keepdims=True)
    spread = jnp.mean((values - average) ** 2, axis=-1, keepdims=True)
    return ((values - average) * lax.rsqrt(spread + 1e-05) * gains).astype(BF16)


def gelu(x):
    half = 0.5 * x
    return half + half * lax.erf(x * 0.5**0.5)


def head_masks(head_dim):
    lane = lax.broadcasted_iota(jnp.int32, (PATCH, HEADS_TOGETHER * head_dim), 1)
    return [
        jnp.where((lane >= h * head_dim) & (lane < (h + 1) * head_dim), 1.0, 0.0).astype(BF16)
        for h in range(HEADS_TOGETHER)
    ]


def attend(patches, head_dim):
    masks = head_masks(head_dim)
    width = HEADS_TOGETHER * head_dim
    heads_per_tile = LANES // head_dim
    lane = lax.broadcasted_iota(jnp.int32, (PATCH, LANES), 1)
    steps = [(p, g) for p in range(len(patches)) for g in range(HEADS // HEADS_TOGETHER)]

    def scores_of(step):
        p, g = step
        queries, keys, _ = patches[p]
        q = queries(g * width, width)
        stacked = jnp.concatenate([q * mask for mask in masks], axis=0)
        return lax.dot_general(
            stacked, keys(g * width, width), (((1,), (1,)), ((), ())), preferred_element_type=F32
        )

    scores = scores_of(steps[0])
    for i, (p, g) in enumerate(steps):
        later = scores_of(steps[i + 1]) if i + 1 < len(steps) else None
        grown = jnp.exp(scores - jnp.max(scores, axis=-1, keepdims=True))
        scale = 1.0 / jnp.sum(grown, axis=-1, keepdims=True)
        values = patches[p][2](g * width, width)
        mixed = jnp.dot(grown.astype(BF16), values, preferred_element_type=F32)
        tiles = []
        for t in range(width // LANES):
            tile = None
            for h in range(heads_per_tile):
                rows = slice((t * heads_per_tile + h) * PATCH, (t * heads_per_tile + h + 1) * PATCH)
                head = mixed[rows, t * LANES : (t + 1) * LANES] * scale[rows]
                tile = head if tile is None else jnp.where(lane < h * head_dim, tile, head)
            tiles.append(tile)
        yield p, g * width, jnp.concatenate(tiles, axis=1).astype(BF16)
        scores = later


def one_hot_rows(places, rows):
    row = lax.broadcasted_iota(jnp.int32, (rows, places.shape[1]), 0)
    return jnp.where(row == places, 1.0, 0.0).astype(BF16)


def started(pairs, sems):
    copies = [
        pltpu.make_async_copy(source, place, sems.at[at])
        for at, (source, place) in enumerate(pairs)
    ]
    for copy in copies:
        copy.start()
    return copies


def finish(rows, attended, gain, held, copies=()):
    w_proj, w_up, w_down = held
    for copy in copies[:1]:
        copy.wait()
    first = (
        rows.astype(F32) + jnp.dot(attended, w_proj[...], preferred_element_type=F32)
    ).astype(BF16)
    hidden = layer_norm(first, gain)
    total = first.astype(F32)
    for copy in copies[1:]:
        copy.wait()
    piece = 512
    pieces = range(0, w_up.shape[1], piece)
    upper = jnp.dot(hidden, w_up[:, :piece], preferred_element_type=F32)
    for at in pieces:
        later = None
        if at + piece < w_up.shape[1]:
            later = jnp.dot(
                hidden, w_up[:, at + piece : at + 2 * piece], preferred_element_type=F32
            )
        act = gelu(upper).astype(BF16)
        total = total + jnp.dot(act, w_down[at : at + piece, :], preferred_element_type=F32)
        upper = later
    return total.astype(BF16)


def split_kernel(points, destination, pattern, *refs):
    *parts, destination_held, pattern_held, notes, sems = refs
    rows = points.shape[0] // len(parts)
    fetches = started([(destination, destination_held), (pattern, pattern_held)], sems.at[0])
    copies = started(
        [
            (points.at[pl.ds(i * rows, rows), :], part.at[pl.ds(0, rows), :])
            for i, part in enumerate(parts)
        ],
        sems.at[1],
    )
    for fetch in fetches:
        fetch.wait()
    chosen, patches = pattern.shape
    row = lax.broadcasted_iota(jnp.int32, notes.shape, 0)
    low = destination_held[...] & (DIGIT - 1)
    high = lax.shift_right_logical(destination_held[...], DIGIT.bit_length() - 1)
    values = jnp.where(row == chosen, low, jnp.where(row == chosen + 1, high, 0))
    notes[...] = values.astype(F32)
    notes[0:chosen, 0:patches] = pattern_held[...].astype(F32)
    parts[0][rows : rows + TAIL, :] = notes[...].astype(BF16)
    for copy in copies:
        copy.wait()


def keep_kernel(*refs):
    *refs, sems = refs
    count = len(refs) // 2
    for copy in started(
        [
            (source.at[0] if len(source.shape) == 3 else source, place)
            for source, place in zip(refs[:count], refs[count:])
        ],
        sems,
    ):
        copy.wait()


def index_kernel(capacity, destination, beyond, slots, tail, pattern, held, notes, sems):
    added = beyond.at[pl.ds(beyond.shape[0] - TAIL, TAIL), :]
    for fetch in started([(destination, held.at[0]), (added, notes)], sems):
        fetch.wait()
    chosen, patches = pattern.shape
    noted = notes[...].astype(F32)
    pattern[...] = noted[0:chosen, 0:patches].astype(jnp.int32)
    low, high = noted[chosen : chosen + 1, :], noted[chosen + 1 : chosen + 2, :]
    held[1] = (low + DIGIT * high).astype(jnp.int32)
    rows = held.shape[2]
    devices = tail.shape[0]
    in_half = lax.axis_size("seq")
    seq_bits = in_half.bit_length() - 1
    index = lax.axis_index(("grp", "seq"))
    offset = lax.rem(index, LANES // (2 * capacity)) * 2 * capacity
    before = lax.broadcasted_iota(jnp.int32, (rows, rows), 0)
    before = before < lax.broadcasted_iota(jnp.int32, (rows, rows), 1)
    before = jnp.where(before, 1.0, 0.0).astype(BF16)
    lines = jnp.zeros((devices * TAIL, LANES), F32)
    for b in range(2):
        target = lax.shift_right_logical(held[b], rows.bit_length() - 1)
        place = held[b] & (rows - 1)
        half = lax.shift_right_logical(target, seq_bits) & 1
        group = lax.shift_right_logical(target, seq_bits + 1)
        target = group * in_half + (target & (in_half - 1))
        target = jnp.where(half == lax.axis_index("half"), target, -1)
        mine = lax.broadcasted_iota(jnp.int32, (devices, rows), 0) == target
        mine = jnp.where(mine, 1.0, 0.0).astype(F32)
        earlier = jnp.dot(mine.astype(BF16), before, preferred_element_type=F32)
        rank = jnp.sum(mine * earlier, axis=0, keepdims=True).astype(jnp.int32)
        slots[:, b * rows : (b + 1) * rows] = jnp.where(target >= 0, target * capacity + rank, -1)
        rank = rank + b * capacity + offset
        by_lane = lax.broadcasted_iota(jnp.int32, (LANES, rows), 0) == rank
        by_lane = jnp.where(by_lane, 1.0, 0.0).astype(BF16)
        line = lax.broadcasted_iota(jnp.int32, (devices * TAIL, rows), 0)
        code = place + 1
        low = (code & (DIGIT - 1)).astype(F32)
        high = lax.shift_right_logical(code, DIGIT.bit_length() - 1).astype(F32)
        digit = line & (TAIL - 1)
        digits = jnp.where(digit == 0, low, jnp.where(digit == 1, high, 0.0))
        line = lax.shift_right_logical(line, TAIL.bit_length() - 1)
        digits = jnp.where(line == target, digits, 0.0)
        lines = lines + lax.dot_general(
            digits.astype(BF16), by_lane, (((1,), (1,)), ((), ())), preferred_element_type=F32
        )
    tail[...] = lines.reshape(devices, TAIL, LANES).astype(BF16)


def project_kernel(first_rows, new, ask, *refs):
    count = len(first_rows)
    parts, gains, w_qkv = refs[:count], refs[count], refs[count + 1]
    refs = refs[count + 2 if new else count + 3 :]
    whole, (held, sems) = refs[0], refs[-2:]
    channels = w_qkv.shape[0]
    rows = held.shape[1]
    copies = started(
        [(part.at[pl.ds(0, rows), :], held.at[i]) for i, part in enumerate(parts)], sems
    )
    for i, first in enumerate(first_rows):
        copies[i].wait()
        normed = layer_norm(held[i], gains[0:1, :])
        whole[first : first + rows, :] = jnp.dot(
            normed, w_qkv[:, channels:], preferred_element_type=F32
        ).astype(BF16)
        if ask and i * rows < refs[1].shape[0]:
            scale = BF16((channels // HEADS) ** (-0.5))
            query = jnp.dot(normed, w_qkv[:, :channels], preferred_element_type=F32).astype(BF16)
            refs[1][i * rows : (i + 1) * rows, :] = (query * scale).astype(BF16)


def loads(queries, p, keyed, starts):
    channels = queries.shape[1]

    def asked(at, width):
        return queries[p * PATCH : (p + 1) * PATCH, at : at + width]

    def keys(at, width):
        pieces = [keyed[pl.ds(start, PATCH), at : at + width] for start in starts]
        return jnp.concatenate(pieces, axis=0)

    return asked, keys, lambda at, width: keys(channels + at, width)


def lane_tiles(packed, rows):
    capacity, channels = rows.shape[1:]
    return [
        (
            packed.at[:, pl.ds(j * capacity, capacity), :],
            rows.at[:, :, pl.ds(j * LANES, LANES)],
        )
        for j in range(channels // LANES)
    ]


def first_kernel(
    ring_chips,
    pattern,
    pattern_beyond,
    slot_of_row,
    gains,
    keyed,
    queries,
    queries_beyond,
    w_proj,
    w_up,
    w_down,
    tail,
    points,
    *refs,
):
    *points_beyond, outgoing, attended, points_held, first_held, outgoing_held, sems = refs
    rows, channels = points.shape
    devices, capacity, _ = outgoing_held.shape
    row_tiles = channels // LANES * capacity
    patches = rows // PATCH
    chosen = pattern.shape[0]
    me = lax.axis_index(GROUP)
    part = rows // len(points_beyond)
    copies = started(
        [(tail, outgoing.at[:, pl.ds(row_tiles, TAIL), :]), (points, points_held.at[:rows])]
        + [
            (piece.at[pl.ds(0, part), :], points_held.at[pl.ds(rows + i * part, part), :])
            for i, piece in enumerate(points_beyond)
        ],
        sems.at[0],
    )
    blocks = ((pattern, queries, 0), (pattern_beyond, queries_beyond, ring_chips or 1))
    loaded = []
    for b, (picked, asking, own_slot) in enumerate(blocks):
        for p in range(patches):
            starts = [own_slot * rows + p * PATCH]
            for j in range(chosen):
                if ring_chips:
                    patch = picked[j, p]
                    owner, local = lax.div(patch, patches), lax.rem(patch, patches)
                    chip = lax.rem(lax.div(me, 2) - lax.div(owner, 2) + ring_chips, ring_chips)
                    slot = 2 * chip + jnp.where(lax.rem(me, 2) == lax.rem(owner, 2), 0, 1)
                    starts.append(pl.multiple_of((slot * patches + local) * PATCH, PATCH))
                else:
                    starts.append((2 * patches + (b * patches + p) * chosen + j) * PATCH)
            loaded.append(loads(asking, p, keyed, starts))
    for p, at, rows_done in attend(loaded, channels // HEADS):
        attended[p * PATCH : (p + 1) * PATCH, at : at + rows_done.shape[1]] = rows_done
    for copy in copies[1:]:
        copy.wait()

    first_held[...] = finish(
        points_held[...], attended[...], gains[1:2, :], (w_proj, w_up, w_down)
    )
    copies[0].wait()
    targets = devices // SEND_PARTS
    block_slots = capacity // 2
    leaving = []
    for i in range(SEND_PARTS):
        here = pl.ds(i * targets, targets)
        for b in range(2):
            mine = pl.ds(b * block_slots, block_slots)
            slots = slot_of_row[:, b * rows : (b + 1) * rows] - i * targets * block_slots
            send = one_hot_rows(slots, targets * block_slots)
            moved = jnp.dot(
                send, first_held[b * rows : (b + 1) * rows, :], preferred_element_type=F32
            )
            outgoing_held[here, mine, :] = moved.astype(BF16).reshape(
                targets, block_slots, channels
            )
        pairs = lane_tiles(outgoing.at[here], outgoing_held.at[here])
        leaving += started([(source, place) for place, source in pairs], sems.at[1 + i])
    for copy in leaving:
        copy.wait()


def second_kernel(
    pattern,
    gains,
    incoming,
    w_qkv,
    w_proj,
    w_up,
    w_down,
    w_head,
    features,
    normals,
    kv,
    queries,
    attended,
    incoming_held,
    qkv_held,
    proj_held,
    up_held,
    down_held,
    gains_held,
    tail_held,
    head_held,
    features_held,
    sems,
):
    rows, channels = features.shape
    devices, capacity, _ = incoming_held.shape
    patches = rows // PATCH
    chosen = pattern.shape[0]
    tail = incoming.at[:, pl.ds(channels // LANES * capacity, TAIL), :]
    small = started(
        [(tail, tail_held), (gains, gains_held), (w_head, head_held)], sems.at[0]
    )
    landing = started(lane_tiles(incoming, incoming_held), sems.at[1])
    copies = started(
        [
            (w_qkv.at[1], qkv_held),
            (w_proj.at[1], proj_held),
            (w_up.at[1], up_held),
            (w_down.at[1], down_held),
        ],
        sems.at[2],
    )
    for copy in small:
        copy.wait()
    per_row = LANES // capacity
    digits = tail_held[...].astype(F32)
    codes = digits[:, 0:1, :] + DIGIT * digits[:, 1:2, :]
    pieces = []
    for at in range(0, devices, per_row):
        code = codes[at]
        for i in range(1, per_row):
            code = code + codes[at + i]
        pieces.append(code)
    places = jnp.concatenate(pieces, axis=1).astype(jnp.int32) - 1
    place = one_hot_rows(places, rows)
    sides = []
    for at in range(0, len(landing), 2):
        for copy in landing[at : at + 2]:
            copy.wait()
        moved = incoming_held[:, :, at * LANES : (at + 2) * LANES]
        moved = moved.reshape(devices * capacity, 2 * LANES)
        sides.append(jnp.dot(place, moved, preferred_element_type=F32).astype(BF16))
    second = jnp.concatenate(sides, axis=1)
    normed = layer_norm(second, gains_held[2:3, :])
    scale = (channels // HEADS) ** (-0.5)
    copies[0].wait()
    asked = jnp.dot(normed, qkv_held[:, :channels], preferred_element_type=F32).astype(BF16)
    queries[...] = (asked * BF16(scale)).astype(BF16)
    kv[...] = jnp.dot(normed, qkv_held[:, channels:], preferred_element_type=F32).astype(BF16)
    loaded = []
    for p in range(patches):
        starts = [pl.multiple_of(pattern[j, p] * PATCH, PATCH) for j in range(chosen)]
        loaded.append(loads(queries, p, kv, [p * PATCH] + starts))
    for p, at, rows_done in attend(loaded, channels // HEADS):
        attended[p * PATCH : (p + 1) * PATCH, at : at + rows_done.shape[1]] = rows_done
    done = finish(
        second, attended[...], gains_held[3:4, :], (proj_held, up_held, down_held), copies[1:]
    )
    features_held[...] = done
    (leaving,) = started([(features_held, features)], sems.at[0])
    normals[...] = lax.dot_general(
        head_held[...], done, (((1,), (1,)), ((), ())), preferred_element_type=F32
    )
    leaving.wait()


VMEM_SPEC = pl.BlockSpec(memory_space=pltpu.VMEM)
SMEM_SPEC = pl.BlockSpec(memory_space=pltpu.SMEM)
ANY_SPEC = pl.BlockSpec(memory_space=pl.ANY)


def shards(
    points,
    pattern_first,
    pattern_second,
    destination,
    norm_gains,
    w_qkv,
    w_proj,
    w_up,
    w_down,
    w_head,
):
    rows_here, channels = points.shape
    patches, chosen = pattern_first.shape
    devices = lax.axis_size("grp") * lax.axis_size("seq")
    capacity = 2 * rows_here // (2 * devices)
    pair_slots = 2 * capacity

    shards_in_group = lax.axis_size(GROUP)
    chips = shards_in_group // 2
    onward = [(i, (i + 2) % shards_in_group) for i in range(shards_in_group)]
    swap = [(i, i ^ 1) for i in range(shards_in_group)]
    across = [(i, (i + chips) % shards_in_group) for i in range(shards_in_group)]
    ring = shards_in_group * rows_here * 2 * channels * 2 <= RING_BYTES
    kept_rows = shards_in_group * rows_here if ring else 2 * patches * (1 + chosen) * PATCH
    part = rows_here // RING_PARTS

    destination = destination.reshape(1, rows_here)
    pattern_first = pattern_first.T
    part_rows = [part + TAIL] + [part] * (RING_PARTS - 1)
    column = pl.pallas_call(
        split_kernel,
        out_shape=[jax.ShapeDtypeStruct((rows, channels), BF16) for rows in part_rows],
        in_specs=[ANY_SPEC] * 3,
        out_specs=[VMEM_SPEC] * RING_PARTS,
        scratch_shapes=[
            pltpu.VMEM((1, rows_here), jnp.int32),
            pltpu.VMEM(pattern_first.shape, jnp.int32),
            pltpu.VMEM((TAIL, channels), F32),
            pltpu.SemaphoreType.DMA((2, RING_PARTS)),
        ],
        compiler_params=pltpu.CompilerParams(vmem_limit_bytes=SPLIT_BYTES),
        name="split",
    )(points, destination, pattern_first)

    weights = (w_proj, w_up, w_down)
    kv_shape = jax.ShapeDtypeStruct((kept_rows, 2 * channels), BF16)
    own_shape = jax.ShapeDtypeStruct((rows_here, channels), BF16)

    qkv_kept, *kept, gains_kept = pl.pallas_call(
        keep_kernel,
        out_shape=[
            *[jax.ShapeDtypeStruct(w.shape[1:], BF16) for w in (w_qkv,) + weights],
            jax.ShapeDtypeStruct(norm_gains.shape, F32),
        ],
        in_specs=[ANY_SPEC] * 5,
        out_specs=[VMEM_SPEC] * 5,
        scratch_shapes=[pltpu.SemaphoreType.DMA((5,))],
        compiler_params=pltpu.CompilerParams(vmem_limit_bytes=PREPARE_BYTES),
        name="keep",
    )(w_qkv, *weights, norm_gains)
    def index(beyond):
        return pl.pallas_call(
            functools.partial(index_kernel, capacity),
            out_shape=[
                jax.ShapeDtypeStruct((1, 2 * rows_here), jnp.int32),
                jax.ShapeDtypeStruct((devices, TAIL, LANES), BF16),
                jax.ShapeDtypeStruct(pattern_first.shape, jnp.int32),
            ],
            in_specs=[ANY_SPEC] * 2,
            out_specs=[VMEM_SPEC] * 3,
            scratch_shapes=[
                pltpu.VMEM((2, 1, rows_here), jnp.int32),
                pltpu.VMEM((TAIL, channels), BF16),
                pltpu.SemaphoreType.DMA((2,)),
            ],
            compiler_params=pltpu.CompilerParams(vmem_limit_bytes=PROJECT_BYTES),
            name="index",
        )(destination, beyond)

    def project(keyed, blocks, ask=False, rows=part):
        parts = [piece for _, _, block in blocks for piece in block]
        count = len(parts)
        first_rows = [
            slot * rows_here + first + i * rows
            for slot, first, block in blocks
            for i in range(len(block))
        ]
        new = keyed is None
        return pl.pallas_call(
            functools.partial(project_kernel, first_rows, new, ask),
            out_shape=[kv_shape] + [own_shape] * ask,
            in_specs=[ANY_SPEC] * count + [VMEM_SPEC] * (2 if new else 3),
            out_specs=[VMEM_SPEC] * (1 + ask),
            scratch_shapes=[
                pltpu.VMEM((count, rows, channels), BF16),
                pltpu.SemaphoreType.DMA((count,)),
            ],
            input_output_aliases={} if new else {count + 2: 0},
            cost_estimate=pl.CostEstimate(
                flops=4 * count * rows * channels**2,
                bytes_accessed=3 * count * rows * channels * 2 + 3 * channels**2 * 2,
                transcendentals=0,
            ),
            compiler_params=pltpu.CompilerParams(vmem_limit_bytes=PROJECT_BYTES),
            name="project_own" if new else "project",
        )(*parts, gains_kept, qkv_kept, *([] if new else [keyed]))

    if ring:
        beside = [lax.ppermute(rows, GROUP, swap) for rows in column]
        waiting = [(0, 0, column), (1, 0, beside)]
        for step in range(1, chips):
            column = [lax.ppermute(rows, GROUP, onward) for rows in column]
            if step == 1:
                column[0], gains_kept = lax.optimization_barrier((column[0], gains_kept))
                keyed, queries = project(None, waiting, ask=True)
                column[1], keyed = lax.optimization_barrier((column[1], keyed))
            else:
                for i, block in enumerate(waiting):
                    if block[0] == chips:
                        keyed, queries_beyond = project(keyed, [block], ask=True)
                    else:
                        (keyed,) = project(keyed, [block])
                    column[i], keyed = lax.optimization_barrier((column[i], keyed))
            if step == chips // 2:
                points_beyond = column
                slot_index, tail, pattern_beyond = index(column[0])
            if step == chips - 1:
                column[0], slot_index = lax.optimization_barrier((column[0], slot_index))
            beside = [lax.ppermute(rows, GROUP, swap) for rows in column]
            waiting = [(2 * step, 0, column), (2 * step + 1, 0, beside)]
        for i in range(RING_PARTS):
            halves = [(slot, i * part, block[i : i + 1]) for slot, _, block in waiting]
            if i + 1 < RING_PARTS:
                (keyed,) = project(keyed, halves)
            else:
                for half in halves:
                    (keyed,) = project(keyed, [half])
    else:
        group = lax.all_gather(points, GROUP, axis=0, tiled=True)
        partner = lax.rem(lax.axis_index(GROUP) + chips, shards_in_group)
        points_beyond = [lax.dynamic_slice_in_dim(group, partner * rows_here, rows_here)]
        group = group.reshape(-1, PATCH, channels)
        slot_index, tail, pattern_beyond = index(lax.ppermute(column[0], GROUP, across))
        picked = [
            group[pattern.T].reshape(-1, channels) for pattern in (pattern_first, pattern_beyond)
        ]
        wide = picked[0].shape[0]
        keyed, queries = project(None, [(0, 0, column)], ask=True)
        keyed, queries_beyond = project(keyed, [(1, 0, points_beyond)], ask=True, rows=rows_here)
        (keyed,) = project(keyed, [(2, 0, [picked[0]])], rows=wide)
        (keyed,) = project(keyed, [(2 + chosen, 0, [picked[1]])], rows=wide)

    held_weights = [pltpu.VMEM(w.shape[1:], BF16) for w in weights]
    held_rows = pltpu.VMEM((rows_here, channels), BF16)
    held_slots = pltpu.VMEM((devices, pair_slots, channels), BF16)
    held_both = pltpu.VMEM((2 * rows_here, channels), BF16)
    pair_rows = channels // LANES * pair_slots + TAIL
    outgoing = pl.pallas_call(
        functools.partial(first_kernel, chips if ring else 0),
        out_shape=jax.ShapeDtypeStruct((devices, pair_rows, LANES), BF16),
        in_specs=[SMEM_SPEC] * 2 + [VMEM_SPEC] * 8 + [ANY_SPEC] * (2 + len(points_beyond)),
        out_specs=ANY_SPEC,
        scratch_shapes=[
            held_both,
            held_both,
            held_both,
            held_slots,
            pltpu.SemaphoreType.DMA((1 + SEND_PARTS, 4)),
        ],
        compiler_params=pltpu.CompilerParams(vmem_limit_bytes=FIRST_BYTES),
        name="block_first",
    )(
        pattern_first,
        pattern_beyond,
        slot_index,
        gains_kept,
        keyed,
        queries,
        queries_beyond,
        *kept,
        tail,
        points,
        *points_beyond,
    )
    incoming = lax.all_to_all(outgoing, ("grp", "seq"), split_axis=0, concat_axis=0, tiled=True)

    return pl.pallas_call(
        second_kernel,
        out_shape=(
            jax.ShapeDtypeStruct((rows_here, channels), BF16),
            jax.ShapeDtypeStruct((w_head.shape[0], rows_here), F32),
        ),
        in_specs=[SMEM_SPEC] + [ANY_SPEC] * 7,
        out_specs=(ANY_SPEC, VMEM_SPEC),
        scratch_shapes=[
            pltpu.VMEM((rows_here, 2 * channels), BF16),
            held_rows,
            held_rows,
            held_slots,
            pltpu.VMEM(w_qkv.shape[1:], BF16),
            *held_weights,
            pltpu.VMEM(norm_gains.shape, F32),
            pltpu.VMEM(tail.shape, BF16),
            pltpu.VMEM(w_head.shape, BF16),
            held_rows,
            pltpu.SemaphoreType.DMA((3, 5)),
        ],
        compiler_params=pltpu.CompilerParams(vmem_limit_bytes=SECOND_BYTES),
        name="block_second",
    )(pattern_second.T, norm_gains, incoming, w_qkv, *weights, w_head)


def solution(mesh):
    groups, shards_in_group = mesh.devices.shape
    halves = Mesh(
        mesh.devices.reshape(groups, 2, shards_in_group // 2), ("grp",) + GROUP
    )
    everywhere = ("grp",) + GROUP
    placed = (
        P(everywhere, None),
        P(everywhere, None),
        P(everywhere, None),
        P(everywhere),
        P(),
        P(),
        P(),
        P(),
        P(),
        P(),
    )
    return jax.shard_map(
        shards,
        mesh=halves,
        in_specs=placed,
        out_specs=(P(everywhere, None), P(None, everywhere)),
        check_vma=False,
    )
```

```python
import functools

import jax
import jax.numpy as jnp
from jax import lax
from jax.experimental import pallas as pl
from jax.experimental.pallas import tpu as pltpu
from jax.sharding import Mesh, PartitionSpec as P

HEADS = 8
PATCH = 64
HEADS_TOGETHER = 4
GROUP = ("half", "seq")
RING_PARTS = 2
SEND_PARTS = 4
LANES = 128
SECOND_SCRATCH = 13
PERMUTED_DEVICES = 16
TAIL = 8
DIGIT = 256
FIRST_BYTES = 28 * 1024 * 1024
SECOND_BYTES = 50 * 1024 * 1024
PROJECT_BYTES = 16 * 1024 * 1024
SPLIT_BYTES = 60 * 1024 * 1024
PREPARE_BYTES = 46 * 1024 * 1024
RING_BYTES = 16 * 1024 * 1024
F32 = jnp.float32
BF16 = jnp.bfloat16


def layer_norm(rows, gains):
    values = rows.astype(F32)
    average = jnp.mean(values, axis=-1, keepdims=True)
    spread = jnp.mean((values - average) ** 2, axis=-1, keepdims=True)
    return ((values - average) * lax.rsqrt(spread + 1e-05) * gains).astype(BF16)


def gelu(x):
    half = 0.5 * x
    return half + half * lax.erf(x * 0.5**0.5)


def head_masks(head_dim):
    lane = lax.broadcasted_iota(jnp.int32, (PATCH, HEADS_TOGETHER * head_dim), 1)
    return [
        jnp.where((lane >= h * head_dim) & (lane < (h + 1) * head_dim), 1.0, 0.0).astype(BF16)
        for h in range(HEADS_TOGETHER)
    ]


def attend(patches, head_dim):
    masks = head_masks(head_dim)
    width = HEADS_TOGETHER * head_dim
    heads_per_tile = LANES // head_dim
    lane = lax.broadcasted_iota(jnp.int32, (PATCH, LANES), 1)
    steps = [(p, g) for p in range(len(patches)) for g in range(HEADS // HEADS_TOGETHER)]

    def scores_of(step):
        p, g = step
        queries, keys, _ = patches[p]
        q = queries(g * width, width)
        stacked = jnp.concatenate([q * mask for mask in masks], axis=0)
        return lax.dot_general(
            stacked, keys(g * width, width), (((1,), (1,)), ((), ())), preferred_element_type=F32
        )

    scores = scores_of(steps[0])
    for i, (p, g) in enumerate(steps):
        later = scores_of(steps[i + 1]) if i + 1 < len(steps) else None
        grown = jnp.exp(scores - jnp.max(scores, axis=-1, keepdims=True))
        scale = 1.0 / jnp.sum(grown, axis=-1, keepdims=True)
        values = patches[p][2](g * width, width)
        mixed = jnp.dot(grown.astype(BF16), values, preferred_element_type=F32)
        tiles = []
        for t in range(width // LANES):
            tile = None
            for h in range(heads_per_tile):
                rows = slice((t * heads_per_tile + h) * PATCH, (t * heads_per_tile + h + 1) * PATCH)
                head = mixed[rows, t * LANES : (t + 1) * LANES] * scale[rows]
                tile = head if tile is None else jnp.where(lane < h * head_dim, tile, head)
            tiles.append(tile)
        yield p, g * width, jnp.concatenate(tiles, axis=1).astype(BF16)
        scores = later


def one_hot_rows(places, rows):
    row = lax.broadcasted_iota(jnp.int32, (rows, places.shape[1]), 0)
    return jnp.where(row == places, 1.0, 0.0).astype(BF16)


def started(pairs, sems):
    copies = [
        pltpu.make_async_copy(source, place, sems.at[at])
        for at, (source, place) in enumerate(pairs)
    ]
    for copy in copies:
        copy.start()
    return copies


def finish(rows, attended, gain, held, copies=()):
    w_proj, w_up, w_down = held
    for copy in copies[:1]:
        copy.wait()
    first = (
        rows.astype(F32) + jnp.dot(attended, w_proj[...], preferred_element_type=F32)
    ).astype(BF16)
    hidden = layer_norm(first, gain)
    total = first.astype(F32)
    for copy in copies[1:]:
        copy.wait()
    piece = 512
    pieces = range(0, w_up.shape[1], piece)
    upper = jnp.dot(hidden, w_up[:, :piece], preferred_element_type=F32)
    for at in pieces:
        later = None
        if at + piece < w_up.shape[1]:
            later = jnp.dot(
                hidden, w_up[:, at + piece : at + 2 * piece], preferred_element_type=F32
            )
        act = gelu(upper).astype(BF16)
        total = total + jnp.dot(act, w_down[at : at + piece, :], preferred_element_type=F32)
        upper = later
    return total.astype(BF16)


def split_kernel(points, destination, pattern, *refs):
    *parts, destination_held, pattern_held, notes, sems = refs
    rows = points.shape[0] // len(parts)
    fetches = started([(destination, destination_held), (pattern, pattern_held)], sems.at[0])
    copies = started(
        [
            (points.at[pl.ds(i * rows, rows), :], part.at[pl.ds(0, rows), :])
            for i, part in enumerate(parts)
        ],
        sems.at[1],
    )
    for fetch in fetches:
        fetch.wait()
    chosen, patches = pattern.shape
    row = lax.broadcasted_iota(jnp.int32, notes.shape, 0)
    low = destination_held[...] & (DIGIT - 1)
    high = lax.shift_right_logical(destination_held[...], DIGIT.bit_length() - 1)
    values = jnp.where(row == chosen, low, jnp.where(row == chosen + 1, high, 0))
    notes[...] = values.astype(F32)
    notes[0:chosen, 0:patches] = pattern_held[...].astype(F32)
    parts[0][rows : rows + TAIL, :] = notes[...].astype(BF16)
    for copy in copies:
        copy.wait()


def keep_kernel(*refs):
    *refs, sems = refs
    count = len(refs) // 2
    for copy in started(
        [
            (source.at[0] if len(source.shape) == 3 else source, place)
            for source, place in zip(refs[:count], refs[count:])
        ],
        sems,
    ):
        copy.wait()


def index_kernel(capacity, destination, beyond, slots, tail, pattern, held, notes, sems):
    added = beyond.at[pl.ds(beyond.shape[0] - TAIL, TAIL), :]
    for fetch in started([(destination, held.at[0]), (added, notes)], sems):
        fetch.wait()
    chosen, patches = pattern.shape
    noted = notes[...].astype(F32)
    pattern[...] = noted[0:chosen, 0:patches].astype(jnp.int32)
    low, high = noted[chosen : chosen + 1, :], noted[chosen + 1 : chosen + 2, :]
    held[1] = (low + DIGIT * high).astype(jnp.int32)
    rows = held.shape[2]
    devices = tail.shape[0]
    in_half = lax.axis_size("seq")
    seq_bits = in_half.bit_length() - 1
    index = lax.axis_index(("grp", "seq"))
    offset = lax.rem(index, LANES // (2 * capacity)) * 2 * capacity
    before = lax.broadcasted_iota(jnp.int32, (rows, rows), 0)
    before = before < lax.broadcasted_iota(jnp.int32, (rows, rows), 1)
    before = jnp.where(before, 1.0, 0.0).astype(BF16)
    lines = jnp.zeros((devices * TAIL, LANES), F32)
    for b in range(2):
        target = lax.shift_right_logical(held[b], rows.bit_length() - 1)
        place = held[b] & (rows - 1)
        half = lax.shift_right_logical(target, seq_bits) & 1
        group = lax.shift_right_logical(target, seq_bits + 1)
        target = group * in_half + (target & (in_half - 1))
        target = jnp.where(half == lax.axis_index("half"), target, -1)
        mine = lax.broadcasted_iota(jnp.int32, (devices, rows), 0) == target
        mine = jnp.where(mine, 1.0, 0.0).astype(F32)
        earlier = jnp.dot(mine.astype(BF16), before, preferred_element_type=F32)
        rank = jnp.sum(mine * earlier, axis=0, keepdims=True).astype(jnp.int32)
        slots[:, b * rows : (b + 1) * rows] = jnp.where(target >= 0, target * capacity + rank, -1)
        rank = rank + b * capacity + offset
        by_lane = lax.broadcasted_iota(jnp.int32, (LANES, rows), 0) == rank
        by_lane = jnp.where(by_lane, 1.0, 0.0).astype(BF16)
        line = lax.broadcasted_iota(jnp.int32, (devices * TAIL, rows), 0)
        code = place + 1
        low = (code & (DIGIT - 1)).astype(F32)
        high = lax.shift_right_logical(code, DIGIT.bit_length() - 1).astype(F32)
        digit = line & (TAIL - 1)
        digits = jnp.where(digit == 0, low, jnp.where(digit == 1, high, 0.0))
        line = lax.shift_right_logical(line, TAIL.bit_length() - 1)
        digits = jnp.where(line == target, digits, 0.0)
        lines = lines + lax.dot_general(
            digits.astype(BF16), by_lane, (((1,), (1,)), ((), ())), preferred_element_type=F32
        )
    tail[...] = lines.reshape(devices, TAIL, LANES).astype(BF16)


def project_kernel(first_rows, new, ask, *refs):
    count = len(first_rows)
    parts, gains, w_qkv = refs[:count], refs[count], refs[count + 1]
    refs = refs[count + 2 if new else count + 3 :]
    whole, (held, sems) = refs[0], refs[-2:]
    channels = w_qkv.shape[0]
    rows = held.shape[1]
    copies = started(
        [(part.at[pl.ds(0, rows), :], held.at[i]) for i, part in enumerate(parts)], sems
    )
    for i, first in enumerate(first_rows):
        copies[i].wait()
        normed = layer_norm(held[i], gains[0:1, :])
        whole[first : first + rows, :] = jnp.dot(
            normed, w_qkv[:, channels:], preferred_element_type=F32
        ).astype(BF16)
        if ask and i * rows < refs[1].shape[0]:
            scale = BF16((channels // HEADS) ** (-0.5))
            query = jnp.dot(normed, w_qkv[:, :channels], preferred_element_type=F32).astype(BF16)
            refs[1][i * rows : (i + 1) * rows, :] = (query * scale).astype(BF16)


def loads(queries, p, keyed, starts):
    channels = queries.shape[1]

    def asked(at, width):
        return queries[p * PATCH : (p + 1) * PATCH, at : at + width]

    def keys(at, width):
        pieces = [keyed[pl.ds(start, PATCH), at : at + width] for start in starts]
        return jnp.concatenate(pieces, axis=0)

    return asked, keys, lambda at, width: keys(channels + at, width)


def part_pairs(arrays, mask, partner, rows, tail):
    part = arrays[mask] if len(arrays) > 1 else arrays[0].at[partner]
    capacity, channels = rows.shape
    tiles = channels // LANES
    return [
        (part.at[pl.ds(j * capacity, capacity), :], rows.at[:, pl.ds(j * LANES, LANES)])
        for j in range(tiles)
    ] + [(part.at[pl.ds(tiles * capacity, TAIL), :], tail)]


def first_kernel(
    ring_chips,
    beyond_parts,
    pattern,
    pattern_beyond,
    slot_of_row,
    gains,
    keyed,
    queries,
    queries_beyond,
    w_proj,
    w_up,
    w_down,
    tail,
    points,
    *refs,
):
    points_beyond, refs = refs[:beyond_parts], refs[beyond_parts:]
    *outgoing, attended, points_held, first_held, outgoing_held, sems, part_sems = refs
    rows, channels = points.shape
    devices, capacity, _ = outgoing_held.shape
    index = lax.axis_index(("grp", "seq"))
    patches = rows // PATCH
    chosen = pattern.shape[0]
    me = lax.axis_index(GROUP)
    part = rows // len(points_beyond)
    copies = started(
        [(points, points_held.at[:rows])]
        + [
            (piece.at[pl.ds(0, part), :], points_held.at[pl.ds(rows + i * part, part), :])
            for i, piece in enumerate(points_beyond)
        ],
        sems,
    )
    blocks = ((pattern, queries, 0), (pattern_beyond, queries_beyond, ring_chips or 1))
    loaded = []
    for b, (picked, asking, own_slot) in enumerate(blocks):
        for p in range(patches):
            starts = [own_slot * rows + p * PATCH]
            for j in range(chosen):
                if ring_chips:
                    patch = picked[j, p]
                    owner, local = lax.div(patch, patches), lax.rem(patch, patches)
                    chip = lax.rem(lax.div(me, 2) - lax.div(owner, 2) + ring_chips, ring_chips)
                    slot = 2 * chip + jnp.where(lax.rem(me, 2) == lax.rem(owner, 2), 0, 1)
                    starts.append(pl.multiple_of((slot * patches + local) * PATCH, PATCH))
                else:
                    starts.append((2 * patches + (b * patches + p) * chosen + j) * PATCH)
            loaded.append(loads(asking, p, keyed, starts))
    for p, at, rows_done in attend(loaded, channels // HEADS):
        attended[p * PATCH : (p + 1) * PATCH, at : at + rows_done.shape[1]] = rows_done
    for copy in copies:
        copy.wait()
    first_held[...] = finish(
        points_held[...], attended[...], gains[1:2, :], (w_proj, w_up, w_down)
    )
    targets = devices // SEND_PARTS
    block_slots = capacity // 2
    leaving = []
    for i in range(SEND_PARTS):
        masks = range(i * targets, (i + 1) * targets)
        start = (lax.div(index, targets) ^ i) * targets * block_slots
        for b in range(2):
            mine = pl.ds(b * block_slots, block_slots)
            slots = slot_of_row[:, b * rows : (b + 1) * rows] - start
            send = one_hot_rows(slots, targets * block_slots)
            moved = jnp.dot(
                send, first_held[b * rows : (b + 1) * rows, :], preferred_element_type=F32
            )
            outgoing_held[pl.ds(i * targets, targets), mine, :] = moved.astype(BF16).reshape(
                targets, block_slots, channels
            )
        for mask in masks:
            partner = index ^ mask
            rows_out = outgoing_held.at[i * targets + lax.rem(partner, targets)]
            pairs = part_pairs(outgoing, mask, partner, rows_out, tail.at[partner])
            leaving += started([(source, place) for place, source in pairs], part_sems.at[mask])
    for copy in leaving:
        copy.wait()


def second_kernel(
    pattern,
    gains,
    w_qkv,
    w_proj,
    w_up,
    w_down,
    w_head,
    *refs,
):
    *incoming, features, normals = refs[:-SECOND_SCRATCH]
    (
        kv,
        queries,
        attended,
        incoming_held,
        qkv_held,
        proj_held,
        up_held,
        down_held,
        gains_held,
        tail_held,
        head_held,
        sems,
        part_sems,
    ) = refs[-SECOND_SCRATCH:]
    rows, channels = features.shape
    devices, capacity, _ = incoming_held.shape
    patches = rows // PATCH
    chosen = pattern.shape[0]
    small = started([(gains, gains_held), (w_head, head_held)], sems.at[0])
    per_row = LANES // capacity
    index = lax.axis_index(("grp", "seq"))
    landing = []
    for mask in range(devices):
        at = mask ^ lax.rem(index, per_row)
        pairs = part_pairs(
            incoming, mask, index ^ mask, incoming_held.at[at], tail_held.at[at]
        )
        landing.append(started(pairs, part_sems.at[mask]))
    copies = started(
        [
            (w_qkv.at[1], qkv_held),
            (w_proj.at[1], proj_held),
            (w_up.at[1], up_held),
            (w_down.at[1], down_held),
        ],
        sems.at[1],
    )
    for copy in small + [part[-1] for part in landing]:
        copy.wait()
    digits = tail_held[...].astype(F32)
    codes = digits[:, 0:1, :] + DIGIT * digits[:, 1:2, :]
    pieces = []
    for at in range(0, devices, per_row):
        code = codes[at]
        for i in range(1, per_row):
            code = code + codes[at + i]
        pieces.append(code)
    places = jnp.concatenate(pieces, axis=1).astype(jnp.int32) - 1
    place = one_hot_rows(places, rows)
    sides = []
    for at in range(0, channels // LANES, 2):
        for part in landing:
            for copy in part[at : at + 2]:
                copy.wait()
        moved = incoming_held[:, :, at * LANES : (at + 2) * LANES]
        moved = moved.reshape(devices * capacity, 2 * LANES)
        sides.append(jnp.dot(place, moved, preferred_element_type=F32).astype(BF16))
    second = jnp.concatenate(sides, axis=1)
    normed = layer_norm(second, gains_held[2:3, :])
    scale = (channels // HEADS) ** (-0.5)
    copies[0].wait()
    asked = jnp.dot(normed, qkv_held[:, :channels], preferred_element_type=F32).astype(BF16)
    queries[...] = (asked * BF16(scale)).astype(BF16)
    kv[...] = jnp.dot(normed, qkv_held[:, channels:], preferred_element_type=F32).astype(BF16)
    loaded = []
    for p in range(patches):
        starts = [pl.multiple_of(pattern[j, p] * PATCH, PATCH) for j in range(chosen)]
        loaded.append(loads(queries, p, kv, [p * PATCH] + starts))
    for p, at, rows_done in attend(loaded, channels // HEADS):
        attended[p * PATCH : (p + 1) * PATCH, at : at + rows_done.shape[1]] = rows_done
    done = finish(
        second, attended[...], gains_held[3:4, :], (proj_held, up_held, down_held), copies[1:]
    )
    features[...] = done
    normals[...] = lax.dot_general(
        head_held[...], done, (((1,), (1,)), ((), ())), preferred_element_type=F32
    )


VMEM_SPEC = pl.BlockSpec(memory_space=pltpu.VMEM)
SMEM_SPEC = pl.BlockSpec(memory_space=pltpu.SMEM)
ANY_SPEC = pl.BlockSpec(memory_space=pl.ANY)


def shards(
    points,
    pattern_first,
    pattern_second,
    destination,
    norm_gains,
    w_qkv,
    w_proj,
    w_up,
    w_down,
    w_head,
):
    rows_here, channels = points.shape
    patches, chosen = pattern_first.shape
    devices = lax.axis_size("grp") * lax.axis_size("seq")
    capacity = 2 * rows_here // (2 * devices)
    pair_slots = 2 * capacity

    shards_in_group = lax.axis_size(GROUP)
    chips = shards_in_group // 2
    onward = [(i, (i + 2) % shards_in_group) for i in range(shards_in_group)]
    swap = [(i, i ^ 1) for i in range(shards_in_group)]
    across = [(i, (i + chips) % shards_in_group) for i in range(shards_in_group)]
    ring = shards_in_group * rows_here * 2 * channels * 2 <= RING_BYTES
    kept_rows = shards_in_group * rows_here if ring else 2 * patches * (1 + chosen) * PATCH
    part = rows_here // RING_PARTS

    destination = destination.reshape(1, rows_here)
    pattern_first = pattern_first.T
    part_rows = [part + TAIL] + [part] * (RING_PARTS - 1)
    column = pl.pallas_call(
        split_kernel,
        out_shape=[jax.ShapeDtypeStruct((rows, channels), BF16) for rows in part_rows],
        in_specs=[ANY_SPEC] * 3,
        out_specs=[VMEM_SPEC] * RING_PARTS,
        scratch_shapes=[
            pltpu.VMEM((1, rows_here), jnp.int32),
            pltpu.VMEM(pattern_first.shape, jnp.int32),
            pltpu.VMEM((TAIL, channels), F32),
            pltpu.SemaphoreType.DMA((2, RING_PARTS)),
        ],
        compiler_params=pltpu.CompilerParams(vmem_limit_bytes=SPLIT_BYTES),
        name="split",
    )(points, destination, pattern_first)

    weights = (w_proj, w_up, w_down)
    kv_shape = jax.ShapeDtypeStruct((kept_rows, 2 * channels), BF16)
    own_shape = jax.ShapeDtypeStruct((rows_here, channels), BF16)

    qkv_kept, *kept, gains_kept = pl.pallas_call(
        keep_kernel,
        out_shape=[
            *[jax.ShapeDtypeStruct(w.shape[1:], BF16) for w in (w_qkv,) + weights],
            jax.ShapeDtypeStruct(norm_gains.shape, F32),
        ],
        in_specs=[ANY_SPEC] * 5,
        out_specs=[VMEM_SPEC] * 5,
        scratch_shapes=[pltpu.SemaphoreType.DMA((5,))],
        compiler_params=pltpu.CompilerParams(vmem_limit_bytes=PREPARE_BYTES),
        name="keep",
    )(w_qkv, *weights, norm_gains)
    def index(beyond):
        return pl.pallas_call(
            functools.partial(index_kernel, capacity),
            out_shape=[
                jax.ShapeDtypeStruct((1, 2 * rows_here), jnp.int32),
                jax.ShapeDtypeStruct((devices, TAIL, LANES), BF16),
                jax.ShapeDtypeStruct(pattern_first.shape, jnp.int32),
            ],
            in_specs=[ANY_SPEC] * 2,
            out_specs=[VMEM_SPEC] * 3,
            scratch_shapes=[
                pltpu.VMEM((2, 1, rows_here), jnp.int32),
                pltpu.VMEM((TAIL, channels), BF16),
                pltpu.SemaphoreType.DMA((2,)),
            ],
            compiler_params=pltpu.CompilerParams(vmem_limit_bytes=PROJECT_BYTES),
            name="index",
        )(destination, beyond)

    def project(keyed, blocks, ask=False, rows=part):
        parts = [piece for _, _, block in blocks for piece in block]
        count = len(parts)
        first_rows = [
            slot * rows_here + first + i * rows
            for slot, first, block in blocks
            for i in range(len(block))
        ]
        new = keyed is None
        return pl.pallas_call(
            functools.partial(project_kernel, first_rows, new, ask),
            out_shape=[kv_shape] + [own_shape] * ask,
            in_specs=[ANY_SPEC] * count + [VMEM_SPEC] * (2 if new else 3),
            out_specs=[VMEM_SPEC] * (1 + ask),
            scratch_shapes=[
                pltpu.VMEM((count, rows, channels), BF16),
                pltpu.SemaphoreType.DMA((count,)),
            ],
            input_output_aliases={} if new else {count + 2: 0},
            cost_estimate=pl.CostEstimate(
                flops=4 * count * rows * channels**2,
                bytes_accessed=3 * count * rows * channels * 2 + 3 * channels**2 * 2,
                transcendentals=0,
            ),
            compiler_params=pltpu.CompilerParams(vmem_limit_bytes=PROJECT_BYTES),
            name="project_own" if new else "project",
        )(*parts, gains_kept, qkv_kept, *([] if new else [keyed]))

    if ring:
        beside = [lax.ppermute(rows, GROUP, swap) for rows in column]
        waiting = [(0, 0, column), (1, 0, beside)]
        for step in range(1, chips):
            column = [lax.ppermute(rows, GROUP, onward) for rows in column]
            if step == 1:
                column[0], gains_kept = lax.optimization_barrier((column[0], gains_kept))
                keyed, queries = project(None, waiting, ask=True)
                column[1], keyed = lax.optimization_barrier((column[1], keyed))
            else:
                for i, block in enumerate(waiting):
                    if block[0] == chips:
                        keyed, queries_beyond = project(keyed, [block], ask=True)
                    else:
                        (keyed,) = project(keyed, [block])
                    column[i], keyed = lax.optimization_barrier((column[i], keyed))
            if step == chips // 2:
                points_beyond = column
                slot_index, tail, pattern_beyond = index(column[0])
            if step == chips - 1:
                column[0], slot_index = lax.optimization_barrier((column[0], slot_index))
            beside = [lax.ppermute(rows, GROUP, swap) for rows in column]
            waiting = [(2 * step, 0, column), (2 * step + 1, 0, beside)]
        for i in range(RING_PARTS):
            halves = [(slot, i * part, block[i : i + 1]) for slot, _, block in waiting]
            if i + 1 < RING_PARTS:
                (keyed,) = project(keyed, halves)
            else:
                for half in halves:
                    (keyed,) = project(keyed, [half])
    else:
        group = lax.all_gather(points, GROUP, axis=0, tiled=True)
        partner = lax.rem(lax.axis_index(GROUP) + chips, shards_in_group)
        points_beyond = [lax.dynamic_slice_in_dim(group, partner * rows_here, rows_here)]
        group = group.reshape(-1, PATCH, channels)
        slot_index, tail, pattern_beyond = index(lax.ppermute(column[0], GROUP, across))
        picked = [
            group[pattern.T].reshape(-1, channels) for pattern in (pattern_first, pattern_beyond)
        ]
        wide = picked[0].shape[0]
        keyed, queries = project(None, [(0, 0, column)], ask=True)
        keyed, queries_beyond = project(keyed, [(1, 0, points_beyond)], ask=True, rows=rows_here)
        (keyed,) = project(keyed, [(2, 0, [picked[0]])], rows=wide)
        (keyed,) = project(keyed, [(2 + chosen, 0, [picked[1]])], rows=wide)

    held_weights = [pltpu.VMEM(w.shape[1:], BF16) for w in weights]
    held_rows = pltpu.VMEM((rows_here, channels), BF16)
    held_slots = pltpu.VMEM((devices, pair_slots, channels), BF16)
    held_both = pltpu.VMEM((2 * rows_here, channels), BF16)
    pair_rows = channels // LANES * pair_slots + TAIL
    permuted = devices <= PERMUTED_DEVICES
    part_shape = jax.ShapeDtypeStruct((pair_rows, LANES), BF16)
    whole_shape = jax.ShapeDtypeStruct((devices, pair_rows, LANES), BF16)
    outgoing = pl.pallas_call(
        functools.partial(first_kernel, chips if ring else 0, len(points_beyond)),
        out_shape=[part_shape] * devices if permuted else [whole_shape],
        in_specs=[SMEM_SPEC] * 2 + [VMEM_SPEC] * 8 + [ANY_SPEC] * (2 + len(points_beyond)),
        out_specs=[ANY_SPEC] * (devices if permuted else 1),
        scratch_shapes=[
            held_both,
            held_both,
            held_both,
            held_slots,
            pltpu.SemaphoreType.DMA((1 + len(points_beyond),)),
            pltpu.SemaphoreType.DMA((devices, channels // LANES + 1)),
        ],
        compiler_params=pltpu.CompilerParams(vmem_limit_bytes=FIRST_BYTES),
        name="block_first",
    )(
        pattern_first,
        pattern_beyond,
        slot_index,
        gains_kept,
        keyed,
        queries,
        queries_beyond,
        *kept,
        tail,
        points,
        *points_beyond,
    )
    inside = ("grp", "seq")
    if permuted:
        incoming = [outgoing[0]] + [
            lax.ppermute(outgoing[mask], inside, [(i, i ^ mask) for i in range(devices)])
            for mask in range(1, devices)
        ]
    else:
        incoming = [lax.all_to_all(outgoing[0], inside, split_axis=0, concat_axis=0, tiled=True)]

    return pl.pallas_call(
        second_kernel,
        out_shape=(
            jax.ShapeDtypeStruct((rows_here, channels), BF16),
            jax.ShapeDtypeStruct((w_head.shape[0], rows_here), F32),
        ),
        in_specs=[SMEM_SPEC] + [ANY_SPEC] * (6 + len(incoming)),
        out_specs=(VMEM_SPEC, VMEM_SPEC),
        scratch_shapes=[
            pltpu.VMEM((rows_here, 2 * channels), BF16),
            held_rows,
            held_rows,
            held_slots,
            pltpu.VMEM(w_qkv.shape[1:], BF16),
            *held_weights,
            pltpu.VMEM(norm_gains.shape, F32),
            pltpu.VMEM(tail.shape, BF16),
            pltpu.VMEM(w_head.shape, BF16),
            pltpu.SemaphoreType.DMA((2, 5)),
            pltpu.SemaphoreType.DMA((devices, channels // LANES + 1)),
        ],
        compiler_params=pltpu.CompilerParams(vmem_limit_bytes=SECOND_BYTES),
        name="block_second",
    )(pattern_second.T, norm_gains, w_qkv, *weights, w_head, *incoming)


def solution(mesh):
    groups, shards_in_group = mesh.devices.shape
    halves = Mesh(
        mesh.devices.reshape(groups, 2, shards_in_group // 2), ("grp",) + GROUP
    )
    everywhere = ("grp",) + GROUP
    placed = (
        P(everywhere, None),
        P(everywhere, None),
        P(everywhere, None),
        P(everywhere),
        P(),
        P(),
        P(),
        P(),
        P(),
        P(),
    )
    return jax.shard_map(
        shards,
        mesh=halves,
        in_specs=placed,
        out_specs=(P(everywhere, None), P(None, everywhere)),
        check_vma=False,
    )
```

```python
import functools

import jax
import jax.numpy as jnp
from jax import lax
from jax.experimental import pallas as pl
from jax.experimental.pallas import tpu as pltpu
from jax.sharding import Mesh, PartitionSpec as P

HEADS = 8
PATCH = 64
HEADS_TOGETHER = 4
GROUP = ("half", "seq")
RING_PARTS = 2
SEND_PARTS = 4
LANES = 128
TAIL = 8
DIGIT = 256
FIRST_BYTES = 28 * 1024 * 1024
SECOND_BYTES = 50 * 1024 * 1024
PROJECT_BYTES = 16 * 1024 * 1024
SPLIT_BYTES = 60 * 1024 * 1024
PREPARE_BYTES = 46 * 1024 * 1024
RING_BYTES = 16 * 1024 * 1024
F32 = jnp.float32
BF16 = jnp.bfloat16


def layer_norm(rows, gains):
    values = rows.astype(F32)
    average = jnp.mean(values, axis=-1, keepdims=True)
    spread = jnp.mean((values - average) ** 2, axis=-1, keepdims=True)
    return ((values - average) * lax.rsqrt(spread + 1e-05) * gains).astype(BF16)


def gelu(x):
    half = 0.5 * x
    return half + half * lax.erf(x * 0.5**0.5)


def head_masks(head_dim):
    lane = lax.broadcasted_iota(jnp.int32, (PATCH, HEADS_TOGETHER * head_dim), 1)
    return [
        jnp.where((lane >= h * head_dim) & (lane < (h + 1) * head_dim), 1.0, 0.0).astype(BF16)
        for h in range(HEADS_TOGETHER)
    ]


def attend(patches, head_dim):
    masks = head_masks(head_dim)
    width = HEADS_TOGETHER * head_dim
    heads_per_tile = LANES // head_dim
    lane = lax.broadcasted_iota(jnp.int32, (PATCH, LANES), 1)
    steps = [(p, g) for p in range(len(patches)) for g in range(HEADS // HEADS_TOGETHER)]

    def scores_of(step):
        p, g = step
        queries, keys, _ = patches[p]
        q = queries(g * width, width)
        stacked = jnp.concatenate([q * mask for mask in masks], axis=0)
        return lax.dot_general(
            stacked, keys(g * width, width), (((1,), (1,)), ((), ())), preferred_element_type=F32
        )

    scores = scores_of(steps[0])
    for i, (p, g) in enumerate(steps):
        later = scores_of(steps[i + 1]) if i + 1 < len(steps) else None
        grown = jnp.exp(scores - jnp.max(scores, axis=-1, keepdims=True))
        scale = 1.0 / jnp.sum(grown, axis=-1, keepdims=True)
        values = patches[p][2](g * width, width)
        mixed = jnp.dot(grown.astype(BF16), values, preferred_element_type=F32)
        tiles = []
        for t in range(width // LANES):
            tile = None
            for h in range(heads_per_tile):
                rows = slice((t * heads_per_tile + h) * PATCH, (t * heads_per_tile + h + 1) * PATCH)
                head = mixed[rows, t * LANES : (t + 1) * LANES] * scale[rows]
                tile = head if tile is None else jnp.where(lane < h * head_dim, tile, head)
            tiles.append(tile)
        yield p, g * width, jnp.concatenate(tiles, axis=1).astype(BF16)
        scores = later


def one_hot_rows(places, rows):
    row = lax.broadcasted_iota(jnp.int32, (rows, places.shape[1]), 0)
    return jnp.where(row == places, 1.0, 0.0).astype(BF16)


def started(pairs, sems):
    copies = [
        pltpu.make_async_copy(source, place, sems.at[at])
        for at, (source, place) in enumerate(pairs)
    ]
    for copy in copies:
        copy.start()
    return copies


def mix(rows, attended, w_proj):
    mixed = jnp.dot(attended, w_proj[...], preferred_element_type=F32)
    return (rows.astype(F32) + mixed).astype(BF16)


def feed(first, gain, w_up, w_down, copies=()):
    hidden = layer_norm(first, gain)
    total = first.astype(F32)
    for copy in copies:
        copy.wait()
    piece = 512
    pieces = range(0, w_up.shape[1], piece)
    upper = jnp.dot(hidden, w_up[:, :piece], preferred_element_type=F32)
    for at in pieces:
        later = None
        if at + piece < w_up.shape[1]:
            later = jnp.dot(
                hidden, w_up[:, at + piece : at + 2 * piece], preferred_element_type=F32
            )
        act = gelu(upper).astype(BF16)
        total = total + jnp.dot(act, w_down[at : at + piece, :], preferred_element_type=F32)
        upper = later
    return total.astype(BF16)


def split_kernel(points, destination, pattern, *refs):
    *parts, destination_held, pattern_held, notes, sems = refs
    rows = points.shape[0] // len(parts)
    fetches = started([(destination, destination_held), (pattern, pattern_held)], sems.at[0])
    copies = started(
        [
            (points.at[pl.ds(i * rows, rows), :], part.at[pl.ds(0, rows), :])
            for i, part in enumerate(parts)
        ],
        sems.at[1],
    )
    for fetch in fetches:
        fetch.wait()
    chosen, patches = pattern.shape
    row = lax.broadcasted_iota(jnp.int32, notes.shape, 0)
    low = destination_held[...] & (DIGIT - 1)
    high = lax.shift_right_logical(destination_held[...], DIGIT.bit_length() - 1)
    values = jnp.where(row == chosen, low, jnp.where(row == chosen + 1, high, 0))
    notes[...] = values.astype(F32)
    notes[0:chosen, 0:patches] = pattern_held[...].astype(F32)
    parts[0][rows : rows + TAIL, :] = notes[...].astype(BF16)
    for copy in copies:
        copy.wait()


def keep_kernel(*refs):
    *refs, sems = refs
    count = len(refs) // 2
    for copy in started(
        [
            (source.at[0] if len(source.shape) == 3 else source, place)
            for source, place in zip(refs[:count], refs[count:])
        ],
        sems,
    ):
        copy.wait()


def index_kernel(capacity, destination, beyond, slots, tail, pattern, held, notes, sems):
    added = beyond.at[pl.ds(beyond.shape[0] - TAIL, TAIL), :]
    for fetch in started([(destination, held.at[0]), (added, notes)], sems):
        fetch.wait()
    chosen, patches = pattern.shape
    noted = notes[...].astype(F32)
    pattern[...] = noted[0:chosen, 0:patches].astype(jnp.int32)
    low, high = noted[chosen : chosen + 1, :], noted[chosen + 1 : chosen + 2, :]
    held[1] = (low + DIGIT * high).astype(jnp.int32)
    rows = held.shape[2]
    devices = tail.shape[0]
    in_half = lax.axis_size("seq")
    seq_bits = in_half.bit_length() - 1
    index = lax.axis_index(("grp", "seq"))
    offset = lax.rem(index, LANES // (2 * capacity)) * 2 * capacity
    before = lax.broadcasted_iota(jnp.int32, (rows, rows), 0)
    before = before < lax.broadcasted_iota(jnp.int32, (rows, rows), 1)
    before = jnp.where(before, 1.0, 0.0).astype(BF16)
    lines = jnp.zeros((devices * TAIL, LANES), F32)
    for b in range(2):
        target = lax.shift_right_logical(held[b], rows.bit_length() - 1)
        place = held[b] & (rows - 1)
        half = lax.shift_right_logical(target, seq_bits) & 1
        group = lax.shift_right_logical(target, seq_bits + 1)
        target = group * in_half + (target & (in_half - 1))
        target = jnp.where(half == lax.axis_index("half"), target, -1)
        mine = lax.broadcasted_iota(jnp.int32, (devices, rows), 0) == target
        mine = jnp.where(mine, 1.0, 0.0).astype(F32)
        earlier = jnp.dot(mine.astype(BF16), before, preferred_element_type=F32)
        rank = jnp.sum(mine * earlier, axis=0, keepdims=True).astype(jnp.int32)
        slots[:, b * rows : (b + 1) * rows] = jnp.where(target >= 0, target * capacity + rank, -1)
        rank = rank + b * capacity + offset
        by_lane = lax.broadcasted_iota(jnp.int32, (LANES, rows), 0) == rank
        by_lane = jnp.where(by_lane, 1.0, 0.0).astype(BF16)
        line = lax.broadcasted_iota(jnp.int32, (devices * TAIL, rows), 0)
        code = place + 1
        low = (code & (DIGIT - 1)).astype(F32)
        high = lax.shift_right_logical(code, DIGIT.bit_length() - 1).astype(F32)
        digit = line & (TAIL - 1)
        digits = jnp.where(digit == 0, low, jnp.where(digit == 1, high, 0.0))
        line = lax.shift_right_logical(line, TAIL.bit_length() - 1)
        digits = jnp.where(line == target, digits, 0.0)
        lines = lines + lax.dot_general(
            digits.astype(BF16), by_lane, (((1,), (1,)), ((), ())), preferred_element_type=F32
        )
    tail[...] = lines.reshape(devices, TAIL, LANES).astype(BF16)


def project_kernel(first_rows, new, ask, *refs):
    count = len(first_rows)
    parts, gains, w_qkv = refs[:count], refs[count], refs[count + 1]
    refs = refs[count + 2 if new else count + 3 :]
    whole, (held, sems) = refs[0], refs[-2:]
    channels = w_qkv.shape[0]
    rows = held.shape[1]
    copies = started(
        [(part.at[pl.ds(0, rows), :], held.at[i]) for i, part in enumerate(parts)], sems
    )
    for i, first in enumerate(first_rows):
        copies[i].wait()
        normed = layer_norm(held[i], gains[0:1, :])
        whole[first : first + rows, :] = jnp.dot(
            normed, w_qkv[:, channels:], preferred_element_type=F32
        ).astype(BF16)
        if ask and i * rows < refs[1].shape[0]:
            scale = BF16((channels // HEADS) ** (-0.5))
            query = jnp.dot(normed, w_qkv[:, :channels], preferred_element_type=F32).astype(BF16)
            refs[1][i * rows : (i + 1) * rows, :] = (query * scale).astype(BF16)


def loads(queries, p, keyed, starts):
    channels = queries.shape[1]

    def asked(at, width):
        return queries[p * PATCH : (p + 1) * PATCH, at : at + width]

    def keys(at, width):
        pieces = [keyed[pl.ds(start, PATCH), at : at + width] for start in starts]
        return jnp.concatenate(pieces, axis=0)

    return asked, keys, lambda at, width: keys(channels + at, width)


def lane_tiles(packed, rows):
    capacity, channels = rows.shape[1:]
    return [
        (
            packed.at[:, pl.ds(j * capacity, capacity), :],
            rows.at[:, :, pl.ds(j * LANES, LANES)],
        )
        for j in range(channels // LANES)
    ]


def first_kernel(
    ring_chips,
    pattern,
    pattern_beyond,
    slot_of_row,
    keyed,
    queries,
    queries_beyond,
    w_proj,
    tail,
    points,
    *refs,
):
    *points_beyond, outgoing, attended, points_held, first_held, outgoing_held, sems = refs
    rows, channels = points.shape
    devices, capacity, _ = outgoing_held.shape
    row_tiles = channels // LANES * capacity
    patches = rows // PATCH
    chosen = pattern.shape[0]
    me = lax.axis_index(GROUP)
    part = rows // len(points_beyond)
    copies = started(
        [(tail, outgoing.at[:, pl.ds(row_tiles, TAIL), :]), (points, points_held.at[:rows])]
        + [
            (piece.at[pl.ds(0, part), :], points_held.at[pl.ds(rows + i * part, part), :])
            for i, piece in enumerate(points_beyond)
        ],
        sems.at[0],
    )
    blocks = ((pattern, queries, 0), (pattern_beyond, queries_beyond, ring_chips or 1))
    loaded = []
    for b, (picked, asking, own_slot) in enumerate(blocks):
        for p in range(patches):
            starts = [own_slot * rows + p * PATCH]
            for j in range(chosen):
                if ring_chips:
                    patch = picked[j, p]
                    owner, local = lax.div(patch, patches), lax.rem(patch, patches)
                    chip = lax.rem(lax.div(me, 2) - lax.div(owner, 2) + ring_chips, ring_chips)
                    slot = 2 * chip + jnp.where(lax.rem(me, 2) == lax.rem(owner, 2), 0, 1)
                    starts.append(pl.multiple_of((slot * patches + local) * PATCH, PATCH))
                else:
                    starts.append((2 * patches + (b * patches + p) * chosen + j) * PATCH)
            loaded.append(loads(asking, p, keyed, starts))
    for p, at, rows_done in attend(loaded, channels // HEADS):
        attended[p * PATCH : (p + 1) * PATCH, at : at + rows_done.shape[1]] = rows_done
    for copy in copies[1:]:
        copy.wait()

    first_held[...] = mix(points_held[...], attended[...], w_proj)
    copies[0].wait()
    targets = devices // SEND_PARTS
    block_slots = capacity // 2
    leaving = []
    for i in range(SEND_PARTS):
        here = pl.ds(i * targets, targets)
        for b in range(2):
            mine = pl.ds(b * block_slots, block_slots)
            slots = slot_of_row[:, b * rows : (b + 1) * rows] - i * targets * block_slots
            send = one_hot_rows(slots, targets * block_slots)
            moved = jnp.dot(
                send, first_held[b * rows : (b + 1) * rows, :], preferred_element_type=F32
            )
            outgoing_held[here, mine, :] = moved.astype(BF16).reshape(
                targets, block_slots, channels
            )
        pairs = lane_tiles(outgoing.at[here], outgoing_held.at[here])
        leaving += started([(source, place) for place, source in pairs], sems.at[1 + i])
    for copy in leaving:
        copy.wait()


def second_kernel(
    pattern,
    gains,
    incoming,
    w_qkv,
    w_proj,
    w_up,
    w_down,
    w_head,
    features,
    normals,
    kv,
    queries,
    attended,
    incoming_held,
    first_up_held,
    first_down_held,
    qkv_held,
    proj_held,
    up_held,
    down_held,
    gains_held,
    tail_held,
    head_held,
    sems,
):
    rows, channels = features.shape
    devices, capacity, _ = incoming_held.shape
    patches = rows // PATCH
    chosen = pattern.shape[0]
    tail = incoming.at[:, pl.ds(channels // LANES * capacity, TAIL), :]
    small = started(
        [(tail, tail_held), (gains, gains_held), (w_head, head_held)], sems.at[0]
    )
    landing = started(lane_tiles(incoming, incoming_held), sems.at[1])
    copies = started(
        [
            (w_up.at[0], first_up_held),
            (w_down.at[0], first_down_held),
            (w_qkv.at[1], qkv_held),
            (w_proj.at[1], proj_held),
            (w_up.at[1], up_held),
            (w_down.at[1], down_held),
        ],
        sems.at[2],
    )
    for copy in small:
        copy.wait()
    per_row = LANES // capacity
    digits = tail_held[...].astype(F32)
    codes = digits[:, 0:1, :] + DIGIT * digits[:, 1:2, :]
    pieces = []
    for at in range(0, devices, per_row):
        code = codes[at]
        for i in range(1, per_row):
            code = code + codes[at + i]
        pieces.append(code)
    places = jnp.concatenate(pieces, axis=1).astype(jnp.int32) - 1
    place = one_hot_rows(places, rows)
    sides = []
    for at in range(0, len(landing), 2):
        for copy in landing[at : at + 2]:
            copy.wait()
        moved = incoming_held[:, :, at * LANES : (at + 2) * LANES]
        moved = moved.reshape(devices * capacity, 2 * LANES)
        sides.append(jnp.dot(place, moved, preferred_element_type=F32).astype(BF16))
    first = jnp.concatenate(sides, axis=1)
    second = feed(first, gains_held[1:2, :], first_up_held, first_down_held, copies[:2])
    normed = layer_norm(second, gains_held[2:3, :])
    scale = (channels // HEADS) ** (-0.5)
    copies[2].wait()
    asked = jnp.dot(normed, qkv_held[:, :channels], preferred_element_type=F32).astype(BF16)
    queries[...] = (asked * BF16(scale)).astype(BF16)
    kv[...] = jnp.dot(normed, qkv_held[:, channels:], preferred_element_type=F32).astype(BF16)
    loaded = []
    for p in range(patches):
        starts = [pl.multiple_of(pattern[j, p] * PATCH, PATCH) for j in range(chosen)]
        loaded.append(loads(queries, p, kv, [p * PATCH] + starts))
    for p, at, rows_done in attend(loaded, channels // HEADS):
        attended[p * PATCH : (p + 1) * PATCH, at : at + rows_done.shape[1]] = rows_done
    copies[3].wait()
    mixed = mix(second, attended[...], proj_held)
    done = feed(mixed, gains_held[3:4, :], up_held, down_held, copies[4:])
    features[...] = done
    normals[...] = lax.dot_general(
        head_held[...], done, (((1,), (1,)), ((), ())), preferred_element_type=F32
    )


VMEM_SPEC = pl.BlockSpec(memory_space=pltpu.VMEM)
SMEM_SPEC = pl.BlockSpec(memory_space=pltpu.SMEM)
ANY_SPEC = pl.BlockSpec(memory_space=pl.ANY)


def shards(
    points,
    pattern_first,
    pattern_second,
    destination,
    norm_gains,
    w_qkv,
    w_proj,
    w_up,
    w_down,
    w_head,
):
    rows_here, channels = points.shape
    patches, chosen = pattern_first.shape
    devices = lax.axis_size("grp") * lax.axis_size("seq")
    capacity = 2 * rows_here // (2 * devices)
    pair_slots = 2 * capacity

    shards_in_group = lax.axis_size(GROUP)
    chips = shards_in_group // 2
    onward = [(i, (i + 2) % shards_in_group) for i in range(shards_in_group)]
    swap = [(i, i ^ 1) for i in range(shards_in_group)]
    across = [(i, (i + chips) % shards_in_group) for i in range(shards_in_group)]
    ring = shards_in_group * rows_here * 2 * channels * 2 <= RING_BYTES
    kept_rows = shards_in_group * rows_here if ring else 2 * patches * (1 + chosen) * PATCH
    part = rows_here // RING_PARTS

    destination = destination.reshape(1, rows_here)
    pattern_first = pattern_first.T
    part_rows = [part + TAIL] + [part] * (RING_PARTS - 1)
    column = pl.pallas_call(
        split_kernel,
        out_shape=[jax.ShapeDtypeStruct((rows, channels), BF16) for rows in part_rows],
        in_specs=[ANY_SPEC] * 3,
        out_specs=[VMEM_SPEC] * RING_PARTS,
        scratch_shapes=[
            pltpu.VMEM((1, rows_here), jnp.int32),
            pltpu.VMEM(pattern_first.shape, jnp.int32),
            pltpu.VMEM((TAIL, channels), F32),
            pltpu.SemaphoreType.DMA((2, RING_PARTS)),
        ],
        compiler_params=pltpu.CompilerParams(vmem_limit_bytes=SPLIT_BYTES),
        name="split",
    )(points, destination, pattern_first)

    weights = (w_proj, w_up, w_down)
    kv_shape = jax.ShapeDtypeStruct((kept_rows, 2 * channels), BF16)
    own_shape = jax.ShapeDtypeStruct((rows_here, channels), BF16)

    qkv_kept, proj_kept, gains_kept = pl.pallas_call(
        keep_kernel,
        out_shape=[
            *[jax.ShapeDtypeStruct(w.shape[1:], BF16) for w in (w_qkv, w_proj)],
            jax.ShapeDtypeStruct(norm_gains.shape, F32),
        ],
        in_specs=[ANY_SPEC] * 3,
        out_specs=[VMEM_SPEC] * 3,
        scratch_shapes=[pltpu.SemaphoreType.DMA((3,))],
        compiler_params=pltpu.CompilerParams(vmem_limit_bytes=PREPARE_BYTES),
        name="keep",
    )(w_qkv, w_proj, norm_gains)
    def index(beyond):
        return pl.pallas_call(
            functools.partial(index_kernel, capacity),
            out_shape=[
                jax.ShapeDtypeStruct((1, 2 * rows_here), jnp.int32),
                jax.ShapeDtypeStruct((devices, TAIL, LANES), BF16),
                jax.ShapeDtypeStruct(pattern_first.shape, jnp.int32),
            ],
            in_specs=[ANY_SPEC] * 2,
            out_specs=[VMEM_SPEC] * 3,
            scratch_shapes=[
                pltpu.VMEM((2, 1, rows_here), jnp.int32),
                pltpu.VMEM((TAIL, channels), BF16),
                pltpu.SemaphoreType.DMA((2,)),
            ],
            compiler_params=pltpu.CompilerParams(vmem_limit_bytes=PROJECT_BYTES),
            name="index",
        )(destination, beyond)

    def project(keyed, blocks, ask=False, rows=part):
        parts = [piece for _, _, block in blocks for piece in block]
        count = len(parts)
        first_rows = [
            slot * rows_here + first + i * rows
            for slot, first, block in blocks
            for i in range(len(block))
        ]
        new = keyed is None
        return pl.pallas_call(
            functools.partial(project_kernel, first_rows, new, ask),
            out_shape=[kv_shape] + [own_shape] * ask,
            in_specs=[ANY_SPEC] * count + [VMEM_SPEC] * (2 if new else 3),
            out_specs=[VMEM_SPEC] * (1 + ask),
            scratch_shapes=[
                pltpu.VMEM((count, rows, channels), BF16),
                pltpu.SemaphoreType.DMA((count,)),
            ],
            input_output_aliases={} if new else {count + 2: 0},
            cost_estimate=pl.CostEstimate(
                flops=4 * count * rows * channels**2,
                bytes_accessed=3 * count * rows * channels * 2 + 3 * channels**2 * 2,
                transcendentals=0,
            ),
            compiler_params=pltpu.CompilerParams(vmem_limit_bytes=PROJECT_BYTES),
            name="project_own" if new else "project",
        )(*parts, gains_kept, qkv_kept, *([] if new else [keyed]))

    if ring:
        beside = [lax.ppermute(rows, GROUP, swap) for rows in column]
        waiting = [(0, 0, column), (1, 0, beside)]
        for step in range(1, chips):
            column = [lax.ppermute(rows, GROUP, onward) for rows in column]
            if step == 1:
                column[0], gains_kept = lax.optimization_barrier((column[0], gains_kept))
                keyed, queries = project(None, waiting, ask=True)
                column[1], keyed = lax.optimization_barrier((column[1], keyed))
            else:
                for i, block in enumerate(waiting):
                    if block[0] == chips:
                        keyed, queries_beyond = project(keyed, [block], ask=True)
                    else:
                        (keyed,) = project(keyed, [block])
                    column[i], keyed = lax.optimization_barrier((column[i], keyed))
            if step == chips // 2:
                points_beyond = column
                slot_index, tail, pattern_beyond = index(column[0])
            if step == chips - 1:
                column[0], slot_index = lax.optimization_barrier((column[0], slot_index))
            beside = [lax.ppermute(rows, GROUP, swap) for rows in column]
            waiting = [(2 * step, 0, column), (2 * step + 1, 0, beside)]
        for i in range(RING_PARTS):
            halves = [(slot, i * part, block[i : i + 1]) for slot, _, block in waiting]
            if i + 1 < RING_PARTS:
                (keyed,) = project(keyed, halves)
            else:
                for half in halves:
                    (keyed,) = project(keyed, [half])
    else:
        group = lax.all_gather(points, GROUP, axis=0, tiled=True)
        partner = lax.rem(lax.axis_index(GROUP) + chips, shards_in_group)
        points_beyond = [lax.dynamic_slice_in_dim(group, partner * rows_here, rows_here)]
        group = group.reshape(-1, PATCH, channels)
        slot_index, tail, pattern_beyond = index(lax.ppermute(column[0], GROUP, across))
        picked = [
            group[pattern.T].reshape(-1, channels) for pattern in (pattern_first, pattern_beyond)
        ]
        wide = picked[0].shape[0]
        keyed, queries = project(None, [(0, 0, column)], ask=True)
        keyed, queries_beyond = project(keyed, [(1, 0, points_beyond)], ask=True, rows=rows_here)
        (keyed,) = project(keyed, [(2, 0, [picked[0]])], rows=wide)
        (keyed,) = project(keyed, [(2 + chosen, 0, [picked[1]])], rows=wide)

    held_weights = [pltpu.VMEM(w.shape[1:], BF16) for w in weights]
    held_rows = pltpu.VMEM((rows_here, channels), BF16)
    held_slots = pltpu.VMEM((devices, pair_slots, channels), BF16)
    held_both = pltpu.VMEM((2 * rows_here, channels), BF16)
    pair_rows = channels // LANES * pair_slots + TAIL
    outgoing = pl.pallas_call(
        functools.partial(first_kernel, chips if ring else 0),
        out_shape=jax.ShapeDtypeStruct((devices, pair_rows, LANES), BF16),
        in_specs=[SMEM_SPEC] * 2 + [VMEM_SPEC] * 5 + [ANY_SPEC] * (2 + len(points_beyond)),
        out_specs=ANY_SPEC,
        scratch_shapes=[
            held_both,
            held_both,
            held_both,
            held_slots,
            pltpu.SemaphoreType.DMA((1 + SEND_PARTS, 4)),
        ],
        compiler_params=pltpu.CompilerParams(vmem_limit_bytes=FIRST_BYTES),
        name="block_first",
    )(
        pattern_first,
        pattern_beyond,
        slot_index,
        keyed,
        queries,
        queries_beyond,
        proj_kept,
        tail,
        points,
        *points_beyond,
    )
    incoming = lax.all_to_all(outgoing, ("grp", "seq"), split_axis=0, concat_axis=0, tiled=True)

    return pl.pallas_call(
        second_kernel,
        out_shape=(
            jax.ShapeDtypeStruct((rows_here, channels), BF16),
            jax.ShapeDtypeStruct((w_head.shape[0], rows_here), F32),
        ),
        in_specs=[SMEM_SPEC] + [ANY_SPEC] * 7,
        out_specs=(VMEM_SPEC, VMEM_SPEC),
        scratch_shapes=[
            pltpu.VMEM((rows_here, 2 * channels), BF16),
            held_rows,
            held_rows,
            held_slots,
            *held_weights[1:],
            pltpu.VMEM(w_qkv.shape[1:], BF16),
            *held_weights,
            pltpu.VMEM(norm_gains.shape, F32),
            pltpu.VMEM(tail.shape, BF16),
            pltpu.VMEM(w_head.shape, BF16),
            pltpu.SemaphoreType.DMA((3, 6)),
        ],
        compiler_params=pltpu.CompilerParams(vmem_limit_bytes=SECOND_BYTES),
        name="block_second",
    )(pattern_second.T, norm_gains, incoming, w_qkv, *weights, w_head)


def solution(mesh):
    groups, shards_in_group = mesh.devices.shape
    halves = Mesh(
        mesh.devices.reshape(groups, 2, shards_in_group // 2), ("grp",) + GROUP
    )
    everywhere = ("grp",) + GROUP
    placed = (
        P(everywhere, None),
        P(everywhere, None),
        P(everywhere, None),
        P(everywhere),
        P(),
        P(),
        P(),
        P(),
        P(),
        P(),
    )
    return jax.shard_map(
        shards,
        mesh=halves,
        in_specs=placed,
        out_specs=(P(everywhere, None), P(None, everywhere)),
        check_vma=False,
    )
```

```python
import functools

import jax
import jax.numpy as jnp
from jax import lax
from jax.experimental import pallas as pl
from jax.experimental.pallas import tpu as pltpu
from jax.sharding import Mesh, PartitionSpec as P

HEADS = 8
PATCH = 64
HEADS_TOGETHER = 4
GROUP = ("half", "seq")
RING_PARTS = 2
SEND_PARTS = 4
LANES = 128
TAIL = 8
DIGIT = 256
FIRST_BYTES = 28 * 1024 * 1024
SECOND_BYTES = 50 * 1024 * 1024
PROJECT_BYTES = 16 * 1024 * 1024
SPLIT_BYTES = 60 * 1024 * 1024
PREPARE_BYTES = 46 * 1024 * 1024
RING_BYTES = 16 * 1024 * 1024
F32 = jnp.float32
BF16 = jnp.bfloat16


def layer_norm(rows, gains):
    values = rows.astype(F32)
    average = jnp.mean(values, axis=-1, keepdims=True)
    spread = jnp.mean((values - average) ** 2, axis=-1, keepdims=True)
    return ((values - average) * lax.rsqrt(spread + 1e-05) * gains).astype(BF16)


def gelu(x):
    half = 0.5 * x
    return half + half * lax.erf(x * 0.5**0.5)


def head_masks(head_dim):
    lane = lax.broadcasted_iota(jnp.int32, (PATCH, HEADS_TOGETHER * head_dim), 1)
    return [
        jnp.where((lane >= h * head_dim) & (lane < (h + 1) * head_dim), 1.0, 0.0).astype(BF16)
        for h in range(HEADS_TOGETHER)
    ]


def attend(patches, head_dim):
    masks = head_masks(head_dim)
    width = HEADS_TOGETHER * head_dim
    heads_per_tile = LANES // head_dim
    lane = lax.broadcasted_iota(jnp.int32, (PATCH, LANES), 1)
    steps = [(p, g) for p in range(len(patches)) for g in range(HEADS // HEADS_TOGETHER)]

    def scores_of(step):
        p, g = step
        queries, keys, _ = patches[p]
        q = queries(g * width, width)
        stacked = jnp.concatenate([q * mask for mask in masks], axis=0)
        return lax.dot_general(
            stacked, keys(g * width, width), (((1,), (1,)), ((), ())), preferred_element_type=F32
        )

    scores = scores_of(steps[0])
    for i, (p, g) in enumerate(steps):
        later = scores_of(steps[i + 1]) if i + 1 < len(steps) else None
        grown = jnp.exp(scores - jnp.max(scores, axis=-1, keepdims=True))
        scale = 1.0 / jnp.sum(grown, axis=-1, keepdims=True)
        values = patches[p][2](g * width, width)
        mixed = jnp.dot(grown.astype(BF16), values, preferred_element_type=F32)
        tiles = []
        for t in range(width // LANES):
            tile = None
            for h in range(heads_per_tile):
                rows = slice((t * heads_per_tile + h) * PATCH, (t * heads_per_tile + h + 1) * PATCH)
                head = mixed[rows, t * LANES : (t + 1) * LANES] * scale[rows]
                tile = head if tile is None else jnp.where(lane < h * head_dim, tile, head)
            tiles.append(tile)
        yield p, g * width, jnp.concatenate(tiles, axis=1).astype(BF16)
        scores = later


def one_hot_rows(places, rows):
    row = lax.broadcasted_iota(jnp.int32, (rows, places.shape[1]), 0)
    return jnp.where(row == places, 1.0, 0.0).astype(BF16)


def started(pairs, sems):
    copies = [
        pltpu.make_async_copy(source, place, sems.at[at])
        for at, (source, place) in enumerate(pairs)
    ]
    for copy in copies:
        copy.start()
    return copies


def mix(rows, attended, w_proj):
    mixed = jnp.dot(attended, w_proj[...], preferred_element_type=F32)
    return (rows.astype(F32) + mixed).astype(BF16)


def feed(first, gain, w_up, w_down, copies=()):
    hidden = layer_norm(first, gain)
    total = first.astype(F32)
    for copy in copies[:1]:
        copy.wait()
    piece = 512
    pieces = range(0, w_up.shape[1], piece)
    upper = jnp.dot(hidden, w_up[:, :piece], preferred_element_type=F32)
    for at in pieces:
        later = None
        if at + piece < w_up.shape[1]:
            later = jnp.dot(
                hidden, w_up[:, at + piece : at + 2 * piece], preferred_element_type=F32
            )
        act = gelu(upper).astype(BF16)
        if at == 0:
            for copy in copies[1:]:
                copy.wait()
        total = total + jnp.dot(act, w_down[at : at + piece, :], preferred_element_type=F32)
        upper = later
    return total.astype(BF16)


def split_kernel(points, destination, pattern, *refs):
    *parts, destination_held, pattern_held, notes, sems = refs
    rows = points.shape[0] // len(parts)
    fetches = started([(destination, destination_held), (pattern, pattern_held)], sems.at[0])
    copies = started(
        [
            (points.at[pl.ds(i * rows, rows), :], part.at[pl.ds(0, rows), :])
            for i, part in enumerate(parts)
        ],
        sems.at[1],
    )
    for fetch in fetches:
        fetch.wait()
    chosen, patches = pattern.shape
    row = lax.broadcasted_iota(jnp.int32, notes.shape, 0)
    low = destination_held[...] & (DIGIT - 1)
    high = lax.shift_right_logical(destination_held[...], DIGIT.bit_length() - 1)
    values = jnp.where(row == chosen, low, jnp.where(row == chosen + 1, high, 0))
    notes[...] = values.astype(F32)
    notes[0:chosen, 0:patches] = pattern_held[...].astype(F32)
    parts[0][rows : rows + TAIL, :] = notes[...].astype(BF16)
    for copy in copies:
        copy.wait()


def keep_kernel(*refs):
    *refs, sems = refs
    count = len(refs) // 2
    for copy in started(
        [
            (source.at[0] if len(source.shape) == 3 else source, place)
            for source, place in zip(refs[:count], refs[count:])
        ],
        sems,
    ):
        copy.wait()


def index_kernel(capacity, destination, beyond, slots, tail, pattern, held, notes, sems):
    added = beyond.at[pl.ds(beyond.shape[0] - TAIL, TAIL), :]
    for fetch in started([(destination, held.at[0]), (added, notes)], sems):
        fetch.wait()
    chosen, patches = pattern.shape
    noted = notes[...].astype(F32)
    pattern[...] = noted[0:chosen, 0:patches].astype(jnp.int32)
    low, high = noted[chosen : chosen + 1, :], noted[chosen + 1 : chosen + 2, :]
    held[1] = (low + DIGIT * high).astype(jnp.int32)
    rows = held.shape[2]
    devices = tail.shape[0]
    in_half = lax.axis_size("seq")
    seq_bits = in_half.bit_length() - 1
    index = lax.axis_index(("grp", "seq"))
    offset = lax.rem(index, LANES // (2 * capacity)) * 2 * capacity
    before = lax.broadcasted_iota(jnp.int32, (rows, rows), 0)
    before = before < lax.broadcasted_iota(jnp.int32, (rows, rows), 1)
    before = jnp.where(before, 1.0, 0.0).astype(BF16)
    lines = jnp.zeros((devices * TAIL, LANES), F32)
    for b in range(2):
        target = lax.shift_right_logical(held[b], rows.bit_length() - 1)
        place = held[b] & (rows - 1)
        half = lax.shift_right_logical(target, seq_bits) & 1
        group = lax.shift_right_logical(target, seq_bits + 1)
        target = group * in_half + (target & (in_half - 1))
        target = jnp.where(half == lax.axis_index("half"), target, -1)
        mine = lax.broadcasted_iota(jnp.int32, (devices, rows), 0) == target
        mine = jnp.where(mine, 1.0, 0.0).astype(F32)
        earlier = jnp.dot(mine.astype(BF16), before, preferred_element_type=F32)
        rank = jnp.sum(mine * earlier, axis=0, keepdims=True).astype(jnp.int32)
        slots[:, b * rows : (b + 1) * rows] = jnp.where(target >= 0, target * capacity + rank, -1)
        rank = rank + b * capacity + offset
        by_lane = lax.broadcasted_iota(jnp.int32, (LANES, rows), 0) == rank
        by_lane = jnp.where(by_lane, 1.0, 0.0).astype(BF16)
        line = lax.broadcasted_iota(jnp.int32, (devices * TAIL, rows), 0)
        code = place + 1
        low = (code & (DIGIT - 1)).astype(F32)
        high = lax.shift_right_logical(code, DIGIT.bit_length() - 1).astype(F32)
        digit = line & (TAIL - 1)
        digits = jnp.where(digit == 0, low, jnp.where(digit == 1, high, 0.0))
        line = lax.shift_right_logical(line, TAIL.bit_length() - 1)
        digits = jnp.where(line == target, digits, 0.0)
        lines = lines + lax.dot_general(
            digits.astype(BF16), by_lane, (((1,), (1,)), ((), ())), preferred_element_type=F32
        )
    tail[...] = lines.reshape(devices, TAIL, LANES).astype(BF16)


def project_kernel(first_rows, new, ask, *refs):
    count = len(first_rows)
    parts, gains, w_qkv = refs[:count], refs[count], refs[count + 1]
    refs = refs[count + 2 if new else count + 3 :]
    whole, (held, sems) = refs[0], refs[-2:]
    channels = w_qkv.shape[0]
    rows = held.shape[1]
    copies = started(
        [(part.at[pl.ds(0, rows), :], held.at[i]) for i, part in enumerate(parts)], sems
    )
    for i, first in enumerate(first_rows):
        copies[i].wait()
        normed = layer_norm(held[i], gains[0:1, :])
        whole[first : first + rows, :] = jnp.dot(
            normed, w_qkv[:, channels:], preferred_element_type=F32
        ).astype(BF16)
        if ask and i * rows < refs[1].shape[0]:
            scale = BF16((channels // HEADS) ** (-0.5))
            query = jnp.dot(normed, w_qkv[:, :channels], preferred_element_type=F32).astype(BF16)
            refs[1][i * rows : (i + 1) * rows, :] = (query * scale).astype(BF16)


def loads(queries, p, keyed, starts):
    channels = queries.shape[1]

    def asked(at, width):
        return queries[p * PATCH : (p + 1) * PATCH, at : at + width]

    def keys(at, width):
        pieces = [keyed[pl.ds(start, PATCH), at : at + width] for start in starts]
        return jnp.concatenate(pieces, axis=0)

    return asked, keys, lambda at, width: keys(channels + at, width)


def lane_tiles(packed, rows):
    capacity, channels = rows.shape[1:]
    return [
        (
            packed.at[:, pl.ds(j * capacity, capacity), :],
            rows.at[:, :, pl.ds(j * LANES, LANES)],
        )
        for j in range(channels // LANES)
    ]


def first_kernel(
    ring_chips,
    late_rows,
    pattern,
    pattern_beyond,
    slot_of_row,
    kept_rows,
    gains,
    w_qkv,
    queries,
    queries_beyond,
    w_proj,
    tail,
    points,
    *refs,
):
    late, refs = refs[: len(late_rows)], refs[len(late_rows) :]
    *points_beyond, outgoing, keyed, attended, points_held, first_held, outgoing_held = refs[:-3]
    late_held, sems, late_sems = refs[-3:]
    rows, channels = points.shape
    devices, capacity, _ = outgoing_held.shape
    row_tiles = channels // LANES * capacity
    patches = rows // PATCH
    chosen = pattern.shape[0]
    me = lax.axis_index(GROUP)
    part = rows // len(points_beyond)
    late_part = late_held.shape[1]
    landing = started(
        [(piece.at[pl.ds(0, late_part), :], late_held.at[i]) for i, piece in enumerate(late)],
        late_sems,
    )
    copies = started(
        [(tail, outgoing.at[:, pl.ds(row_tiles, TAIL), :]), (points, points_held.at[:rows])]
        + [
            (piece.at[pl.ds(0, part), :], points_held.at[pl.ds(rows + i * part, part), :])
            for i, piece in enumerate(points_beyond)
        ],
        sems.at[0],
    )
    for i, first in enumerate(late_rows):
        landing[i].wait()
        keyed[first : first + late_part, :] = jnp.dot(
            layer_norm(late_held[i], gains[0:1, :]),
            w_qkv[:, channels:],
            preferred_element_type=F32,
        ).astype(BF16)
    blocks = ((pattern, queries, 0), (pattern_beyond, queries_beyond, ring_chips or 1))
    loaded = []
    for b, (picked, asking, own_slot) in enumerate(blocks):
        for p in range(patches):
            starts = [own_slot * rows + p * PATCH]
            for j in range(chosen):
                if ring_chips:
                    patch = picked[j, p]
                    owner, local = lax.div(patch, patches), lax.rem(patch, patches)
                    chip = lax.rem(lax.div(me, 2) - lax.div(owner, 2) + ring_chips, ring_chips)
                    slot = 2 * chip + jnp.where(lax.rem(me, 2) == lax.rem(owner, 2), 0, 1)
                    starts.append(pl.multiple_of((slot * patches + local) * PATCH, PATCH))
                else:
                    starts.append((2 * patches + (b * patches + p) * chosen + j) * PATCH)
            loaded.append(loads(asking, p, keyed, starts))
    for p, at, rows_done in attend(loaded, channels // HEADS):
        attended[p * PATCH : (p + 1) * PATCH, at : at + rows_done.shape[1]] = rows_done
    for copy in copies[1:]:
        copy.wait()

    first_held[...] = mix(points_held[...], attended[...], w_proj)
    copies[0].wait()
    targets = devices // SEND_PARTS
    block_slots = capacity // 2
    leaving = []
    for i in range(SEND_PARTS):
        here = pl.ds(i * targets, targets)
        for b in range(2):
            mine = pl.ds(b * block_slots, block_slots)
            slots = slot_of_row[:, b * rows : (b + 1) * rows] - i * targets * block_slots
            send = one_hot_rows(slots, targets * block_slots)
            moved = jnp.dot(
                send, first_held[b * rows : (b + 1) * rows, :], preferred_element_type=F32
            )
            outgoing_held[here, mine, :] = moved.astype(BF16).reshape(
                targets, block_slots, channels
            )
        pairs = lane_tiles(outgoing.at[here], outgoing_held.at[here])
        leaving += started([(source, place) for place, source in pairs], sems.at[1 + i])
    for copy in leaving:
        copy.wait()


def second_kernel(
    pattern,
    gains,
    incoming,
    w_qkv,
    w_proj,
    w_up,
    w_down,
    w_head,
    features,
    normals,
    kv,
    queries,
    attended,
    incoming_held,
    first_up_held,
    first_down_held,
    qkv_held,
    proj_held,
    up_held,
    down_held,
    gains_held,
    tail_held,
    head_held,
    sems,
):
    rows, channels = features.shape
    devices, capacity, _ = incoming_held.shape
    patches = rows // PATCH
    chosen = pattern.shape[0]
    tail = incoming.at[:, pl.ds(channels // LANES * capacity, TAIL), :]
    small = started(
        [(tail, tail_held), (gains, gains_held), (w_head, head_held)], sems.at[0]
    )
    landing = started(lane_tiles(incoming, incoming_held), sems.at[1])
    copies = started([(w_up.at[0], first_up_held)], sems.at[2])
    for copy in small:
        copy.wait()
    per_row = LANES // capacity
    digits = tail_held[...].astype(F32)
    codes = digits[:, 0:1, :] + DIGIT * digits[:, 1:2, :]
    pieces = []
    for at in range(0, devices, per_row):
        code = codes[at]
        for i in range(1, per_row):
            code = code + codes[at + i]
        pieces.append(code)
    places = jnp.concatenate(pieces, axis=1).astype(jnp.int32) - 1
    place = one_hot_rows(places, rows)
    sides = []
    later = (
        [(w_down.at[0], first_down_held), (w_qkv.at[1], qkv_held)],
        [(w_proj.at[1], proj_held), (w_up.at[1], up_held), (w_down.at[1], down_held)],
    )
    for at in range(0, len(landing), 2):
        for copy in landing[at : at + 2]:
            copy.wait()
        moved = incoming_held[:, :, at * LANES : (at + 2) * LANES]
        moved = moved.reshape(devices * capacity, 2 * LANES)
        sides.append(jnp.dot(place, moved, preferred_element_type=F32).astype(BF16))
        copies += started(later[at // 2], sems.at[3 + at // 2])
    first = jnp.concatenate(sides, axis=1)
    second = feed(first, gains_held[1:2, :], first_up_held, first_down_held, copies[:2])
    normed = layer_norm(second, gains_held[2:3, :])
    scale = (channels // HEADS) ** (-0.5)
    copies[2].wait()
    asked = jnp.dot(normed, qkv_held[:, :channels], preferred_element_type=F32).astype(BF16)
    queries[...] = (asked * BF16(scale)).astype(BF16)
    kv[...] = jnp.dot(normed, qkv_held[:, channels:], preferred_element_type=F32).astype(BF16)
    loaded = []
    for p in range(patches):
        starts = [pl.multiple_of(pattern[j, p] * PATCH, PATCH) for j in range(chosen)]
        loaded.append(loads(queries, p, kv, [p * PATCH] + starts))
    for p, at, rows_done in attend(loaded, channels // HEADS):
        attended[p * PATCH : (p + 1) * PATCH, at : at + rows_done.shape[1]] = rows_done
    copies[3].wait()
    mixed = mix(second, attended[...], proj_held)
    done = feed(mixed, gains_held[3:4, :], up_held, down_held, copies[4:])
    features[...] = done
    normals[...] = lax.dot_general(
        head_held[...], done, (((1,), (1,)), ((), ())), preferred_element_type=F32
    )


VMEM_SPEC = pl.BlockSpec(memory_space=pltpu.VMEM)
SMEM_SPEC = pl.BlockSpec(memory_space=pltpu.SMEM)
ANY_SPEC = pl.BlockSpec(memory_space=pl.ANY)


def shards(
    points,
    pattern_first,
    pattern_second,
    destination,
    norm_gains,
    w_qkv,
    w_proj,
    w_up,
    w_down,
    w_head,
):
    rows_here, channels = points.shape
    patches, chosen = pattern_first.shape
    devices = lax.axis_size("grp") * lax.axis_size("seq")
    capacity = 2 * rows_here // (2 * devices)
    pair_slots = 2 * capacity

    shards_in_group = lax.axis_size(GROUP)
    chips = shards_in_group // 2
    onward = [(i, (i + 2) % shards_in_group) for i in range(shards_in_group)]
    swap = [(i, i ^ 1) for i in range(shards_in_group)]
    across = [(i, (i + chips) % shards_in_group) for i in range(shards_in_group)]
    ring = shards_in_group * rows_here * 2 * channels * 2 <= RING_BYTES
    kept_rows = shards_in_group * rows_here if ring else 2 * patches * (1 + chosen) * PATCH
    part = rows_here // RING_PARTS

    destination = destination.reshape(1, rows_here)
    pattern_first = pattern_first.T
    part_rows = [part + TAIL] + [part] * (RING_PARTS - 1)
    column = pl.pallas_call(
        split_kernel,
        out_shape=[jax.ShapeDtypeStruct((rows, channels), BF16) for rows in part_rows],
        in_specs=[ANY_SPEC] * 3,
        out_specs=[VMEM_SPEC] * RING_PARTS,
        scratch_shapes=[
            pltpu.VMEM((1, rows_here), jnp.int32),
            pltpu.VMEM(pattern_first.shape, jnp.int32),
            pltpu.VMEM((TAIL, channels), F32),
            pltpu.SemaphoreType.DMA((2, RING_PARTS)),
        ],
        compiler_params=pltpu.CompilerParams(vmem_limit_bytes=SPLIT_BYTES),
        name="split",
    )(points, destination, pattern_first)

    weights = (w_proj, w_up, w_down)
    kv_shape = jax.ShapeDtypeStruct((kept_rows, 2 * channels), BF16)
    own_shape = jax.ShapeDtypeStruct((rows_here, channels), BF16)

    qkv_kept, proj_kept, gains_kept = pl.pallas_call(
        keep_kernel,
        out_shape=[
            *[jax.ShapeDtypeStruct(w.shape[1:], BF16) for w in (w_qkv, w_proj)],
            jax.ShapeDtypeStruct(norm_gains.shape, F32),
        ],
        in_specs=[ANY_SPEC] * 3,
        out_specs=[VMEM_SPEC] * 3,
        scratch_shapes=[pltpu.SemaphoreType.DMA((3,))],
        compiler_params=pltpu.CompilerParams(vmem_limit_bytes=PREPARE_BYTES),
        name="keep",
    )(w_qkv, w_proj, norm_gains)
    def index(beyond):
        return pl.pallas_call(
            functools.partial(index_kernel, capacity),
            out_shape=[
                jax.ShapeDtypeStruct((1, 2 * rows_here), jnp.int32),
                jax.ShapeDtypeStruct((devices, TAIL, LANES), BF16),
                jax.ShapeDtypeStruct(pattern_first.shape, jnp.int32),
            ],
            in_specs=[ANY_SPEC] * 2,
            out_specs=[VMEM_SPEC] * 3,
            scratch_shapes=[
                pltpu.VMEM((2, 1, rows_here), jnp.int32),
                pltpu.VMEM((TAIL, channels), BF16),
                pltpu.SemaphoreType.DMA((2,)),
            ],
            compiler_params=pltpu.CompilerParams(vmem_limit_bytes=PROJECT_BYTES),
            name="index",
        )(destination, beyond)

    def project(keyed, blocks, ask=False, rows=part):
        parts = [piece for _, _, block in blocks for piece in block]
        count = len(parts)
        first_rows = [
            slot * rows_here + first + i * rows
            for slot, first, block in blocks
            for i in range(len(block))
        ]
        new = keyed is None
        return pl.pallas_call(
            functools.partial(project_kernel, first_rows, new, ask),
            out_shape=[kv_shape] + [own_shape] * ask,
            in_specs=[ANY_SPEC] * count + [VMEM_SPEC] * (2 if new else 3),
            out_specs=[VMEM_SPEC] * (1 + ask),
            scratch_shapes=[
                pltpu.VMEM((count, rows, channels), BF16),
                pltpu.SemaphoreType.DMA((count,)),
            ],
            input_output_aliases={} if new else {count + 2: 0},
            cost_estimate=pl.CostEstimate(
                flops=4 * count * rows * channels**2,
                bytes_accessed=3 * count * rows * channels * 2 + 3 * channels**2 * 2,
                transcendentals=0,
            ),
            compiler_params=pltpu.CompilerParams(vmem_limit_bytes=PROJECT_BYTES),
            name="project_own" if new else "project",
        )(*parts, gains_kept, qkv_kept, *([] if new else [keyed]))

    if ring:
        beside = [lax.ppermute(rows, GROUP, swap) for rows in column]
        waiting = [(0, 0, column), (1, 0, beside)]
        for step in range(1, chips):
            column = [lax.ppermute(rows, GROUP, onward) for rows in column]
            if step == 1:
                column[0], gains_kept = lax.optimization_barrier((column[0], gains_kept))
                keyed, queries = project(None, waiting, ask=True)
                column[1], keyed = lax.optimization_barrier((column[1], keyed))
            else:
                for i, block in enumerate(waiting):
                    if block[0] == chips:
                        keyed, queries_beyond = project(keyed, [block], ask=True)
                    else:
                        (keyed,) = project(keyed, [block])
                    column[i], keyed = lax.optimization_barrier((column[i], keyed))
            if step == chips // 2:
                points_beyond = column
                slot_index, tail, pattern_beyond = index(column[0])
            if step == chips - 1:
                column[0], slot_index = lax.optimization_barrier((column[0], slot_index))
            beside = [lax.ppermute(rows, GROUP, swap) for rows in column]
            waiting = [(2 * step, 0, column), (2 * step + 1, 0, beside)]
        early = [(slot, 0, block[:-1]) for slot, _, block in waiting]
        (keyed,) = project(keyed, early)
        late_rows = [(slot + 1) * rows_here - part for slot, _, _ in waiting]
        late = [block[-1] for _, _, block in waiting]
    else:
        group = lax.all_gather(points, GROUP, axis=0, tiled=True)
        partner = lax.rem(lax.axis_index(GROUP) + chips, shards_in_group)
        points_beyond = [lax.dynamic_slice_in_dim(group, partner * rows_here, rows_here)]
        group = group.reshape(-1, PATCH, channels)
        slot_index, tail, pattern_beyond = index(lax.ppermute(column[0], GROUP, across))
        picked = [
            group[pattern.T].reshape(-1, channels) for pattern in (pattern_first, pattern_beyond)
        ]
        wide = picked[0].shape[0]
        keyed, queries = project(None, [(0, 0, column)], ask=True)
        keyed, queries_beyond = project(keyed, [(1, 0, points_beyond)], ask=True, rows=rows_here)
        (keyed,) = project(keyed, [(2, 0, [picked[0]])], rows=wide)
        (keyed,) = project(keyed, [(2 + chosen, 0, [picked[1]])], rows=wide)
        late_rows, late = [], []

    held_weights = [pltpu.VMEM(w.shape[1:], BF16) for w in weights]
    held_rows = pltpu.VMEM((rows_here, channels), BF16)
    held_slots = pltpu.VMEM((devices, pair_slots, channels), BF16)
    held_both = pltpu.VMEM((2 * rows_here, channels), BF16)
    pair_rows = channels // LANES * pair_slots + TAIL
    outgoing, _ = pl.pallas_call(
        functools.partial(first_kernel, chips if ring else 0, late_rows),
        out_shape=[jax.ShapeDtypeStruct((devices, pair_rows, LANES), BF16), kv_shape],
        in_specs=[SMEM_SPEC] * 2
        + [VMEM_SPEC] * 7
        + [ANY_SPEC] * (2 + len(late) + len(points_beyond)),
        out_specs=[ANY_SPEC, VMEM_SPEC],
        scratch_shapes=[
            held_both,
            held_both,
            held_both,
            held_slots,
            pltpu.VMEM((max(len(late), 1), part, channels), BF16),
            pltpu.SemaphoreType.DMA((1 + SEND_PARTS, 4)),
            pltpu.SemaphoreType.DMA((max(len(late), 1),)),
        ],
        input_output_aliases={3: 1},
        compiler_params=pltpu.CompilerParams(vmem_limit_bytes=FIRST_BYTES),
        name="block_first",
    )(
        pattern_first,
        pattern_beyond,
        slot_index,
        keyed,
        gains_kept,
        qkv_kept,
        queries,
        queries_beyond,
        proj_kept,
        tail,
        points,
        *late,
        *points_beyond,
    )
    incoming = lax.all_to_all(outgoing, ("grp", "seq"), split_axis=0, concat_axis=0, tiled=True)

    return pl.pallas_call(
        second_kernel,
        out_shape=(
            jax.ShapeDtypeStruct((rows_here, channels), BF16),
            jax.ShapeDtypeStruct((w_head.shape[0], rows_here), F32),
        ),
        in_specs=[SMEM_SPEC] + [ANY_SPEC] * 7,
        out_specs=(VMEM_SPEC, VMEM_SPEC),
        scratch_shapes=[
            pltpu.VMEM((rows_here, 2 * channels), BF16),
            held_rows,
            held_rows,
            held_slots,
            *held_weights[1:],
            pltpu.VMEM(w_qkv.shape[1:], BF16),
            *held_weights,
            pltpu.VMEM(norm_gains.shape, F32),
            pltpu.VMEM(tail.shape, BF16),
            pltpu.VMEM(w_head.shape, BF16),
            pltpu.SemaphoreType.DMA((5, 4)),
        ],
        compiler_params=pltpu.CompilerParams(vmem_limit_bytes=SECOND_BYTES),
        name="block_second",
    )(pattern_second.T, norm_gains, incoming, w_qkv, *weights, w_head)


def solution(mesh):
    groups, shards_in_group = mesh.devices.shape
    halves = Mesh(
        mesh.devices.reshape(groups, 2, shards_in_group // 2), ("grp",) + GROUP
    )
    everywhere = ("grp",) + GROUP
    placed = (
        P(everywhere, None),
        P(everywhere, None),
        P(everywhere, None),
        P(everywhere),
        P(),
        P(),
        P(),
        P(),
        P(),
        P(),
    )
    return jax.shard_map(
        shards,
        mesh=halves,
        in_specs=placed,
        out_specs=(P(everywhere, None), P(None, everywhere)),
        check_vma=False,
    )
```

```python
import functools

import jax
import jax.numpy as jnp
from jax import lax
from jax.experimental import pallas as pl
from jax.experimental.pallas import tpu as pltpu
from jax.sharding import Mesh, PartitionSpec as P

HEADS = 8
PATCH = 64
HEADS_TOGETHER = 4
GROUP = ("half", "seq")
RING_PARTS = 2
SEND_PARTS = 4
LANES = 128
TAIL = 8
DIGIT = 256
FIRST_BYTES = 28 * 1024 * 1024
SECOND_BYTES = 50 * 1024 * 1024
PROJECT_BYTES = 16 * 1024 * 1024
SPLIT_BYTES = 60 * 1024 * 1024
PREPARE_BYTES = 46 * 1024 * 1024
RING_BYTES = 16 * 1024 * 1024
F32 = jnp.float32
BF16 = jnp.bfloat16


def layer_norm(rows, gains):
    values = rows.astype(F32)
    average = jnp.mean(values, axis=-1, keepdims=True)
    spread = jnp.mean((values - average) ** 2, axis=-1, keepdims=True)
    return ((values - average) * lax.rsqrt(spread + 1e-05) * gains).astype(BF16)


def gelu(x):
    half = 0.5 * x
    return half + half * lax.erf(x * 0.5**0.5)


def head_masks(head_dim):
    lane = lax.broadcasted_iota(jnp.int32, (PATCH, HEADS_TOGETHER * head_dim), 1)
    return [
        jnp.where((lane >= h * head_dim) & (lane < (h + 1) * head_dim), 1.0, 0.0).astype(BF16)
        for h in range(HEADS_TOGETHER)
    ]


def attend(patches, head_dim):
    masks = head_masks(head_dim)
    width = HEADS_TOGETHER * head_dim
    heads_per_tile = LANES // head_dim
    lane = lax.broadcasted_iota(jnp.int32, (PATCH, LANES), 1)
    firsts = range(0, HEADS * head_dim, width)

    def scores_of(patch):
        queries, keys, _ = patch
        every = []
        for at in firsts:
            q = queries(at, width)
            stacked = jnp.concatenate([q * mask for mask in masks], axis=0)
            every.append(
                lax.dot_general(
                    stacked, keys(at, width), (((1,), (1,)), ((), ())), preferred_element_type=F32
                )
            )
        return every

    every = scores_of(patches[0])
    for p, (_, _, values) in enumerate(patches):
        later = scores_of(patches[p + 1]) if p + 1 < len(patches) else None
        grown = [jnp.exp(scores - jnp.max(scores, axis=-1, keepdims=True)) for scores in every]
        sides = []
        for at, weights in zip(firsts, grown):
            mixed = jnp.dot(
                weights.astype(BF16), values(at, width), preferred_element_type=F32
            )
            scale = 1.0 / jnp.sum(weights, axis=-1, keepdims=True)
            tiles = []
            for t in range(width // LANES):
                tile = None
                for h in range(heads_per_tile):
                    head = t * heads_per_tile + h
                    rows = slice(head * PATCH, (head + 1) * PATCH)
                    side = mixed[rows, t * LANES : (t + 1) * LANES] * scale[rows]
                    tile = side if tile is None else jnp.where(lane < h * head_dim, tile, side)
                tiles.append(tile)
            sides += tiles
        yield p, jnp.concatenate(sides, axis=1).astype(BF16)
        every = later


def one_hot_rows(places, rows):
    row = lax.broadcasted_iota(jnp.int32, (rows, places.shape[1]), 0)
    return jnp.where(row == places, 1.0, 0.0).astype(BF16)


def started(pairs, sems):
    copies = [
        pltpu.make_async_copy(source, place, sems.at[at])
        for at, (source, place) in enumerate(pairs)
    ]
    for copy in copies:
        copy.start()
    return copies


def mix(rows, attended, w_proj):
    mixed = jnp.dot(attended, w_proj[...], preferred_element_type=F32)
    return (rows.astype(F32) + mixed).astype(BF16)


def feed(first, gain, w_up, w_down, copies=()):
    hidden = layer_norm(first, gain)
    total = first.astype(F32)
    for copy in copies[:1]:
        copy.wait()
    piece = 512
    pieces = range(0, w_up.shape[1], piece)
    upper = jnp.dot(hidden, w_up[:, :piece], preferred_element_type=F32)
    for at in pieces:
        later = None
        if at + piece < w_up.shape[1]:
            later = jnp.dot(
                hidden, w_up[:, at + piece : at + 2 * piece], preferred_element_type=F32
            )
        act = gelu(upper).astype(BF16)
        if at == 0:
            for copy in copies[1:]:
                copy.wait()
        total = total + jnp.dot(act, w_down[at : at + piece, :], preferred_element_type=F32)
        upper = later
    return total.astype(BF16)


def split_kernel(points, destination, pattern, *refs):
    *parts, destination_held, pattern_held, notes, sems = refs
    rows = points.shape[0] // len(parts)
    fetches = started([(destination, destination_held), (pattern, pattern_held)], sems.at[0])
    copies = started(
        [
            (points.at[pl.ds(i * rows, rows), :], part.at[pl.ds(0, rows), :])
            for i, part in enumerate(parts)
        ],
        sems.at[1],
    )
    for fetch in fetches:
        fetch.wait()
    chosen, patches = pattern.shape
    row = lax.broadcasted_iota(jnp.int32, notes.shape, 0)
    low = destination_held[...] & (DIGIT - 1)
    high = lax.shift_right_logical(destination_held[...], DIGIT.bit_length() - 1)
    values = jnp.where(row == chosen, low, jnp.where(row == chosen + 1, high, 0))
    notes[...] = values.astype(F32)
    notes[0:chosen, 0:patches] = pattern_held[...].astype(F32)
    parts[0][rows : rows + TAIL, :] = notes[...].astype(BF16)
    for copy in copies:
        copy.wait()


def keep_kernel(*refs):
    *refs, sems = refs
    count = len(refs) // 2
    for copy in started(
        [
            (source.at[0] if len(source.shape) == 3 else source, place)
            for source, place in zip(refs[:count], refs[count:])
        ],
        sems,
    ):
        copy.wait()


def index_kernel(capacity, destination, beyond, slots, tail, pattern, held, notes, sems):
    added = beyond.at[pl.ds(beyond.shape[0] - TAIL, TAIL), :]
    for fetch in started([(destination, held.at[0]), (added, notes)], sems):
        fetch.wait()
    chosen, patches = pattern.shape
    noted = notes[...].astype(F32)
    pattern[...] = noted[0:chosen, 0:patches].astype(jnp.int32)
    low, high = noted[chosen : chosen + 1, :], noted[chosen + 1 : chosen + 2, :]
    held[1] = (low + DIGIT * high).astype(jnp.int32)
    rows = held.shape[2]
    devices = tail.shape[0]
    in_half = lax.axis_size("seq")
    seq_bits = in_half.bit_length() - 1
    index = lax.axis_index(("grp", "seq"))
    offset = lax.rem(index, LANES // (2 * capacity)) * 2 * capacity
    before = lax.broadcasted_iota(jnp.int32, (rows, rows), 0)
    before = before < lax.broadcasted_iota(jnp.int32, (rows, rows), 1)
    before = jnp.where(before, 1.0, 0.0).astype(BF16)
    lines = jnp.zeros((devices * TAIL, LANES), F32)
    for b in range(2):
        target = lax.shift_right_logical(held[b], rows.bit_length() - 1)
        place = held[b] & (rows - 1)
        half = lax.shift_right_logical(target, seq_bits) & 1
        group = lax.shift_right_logical(target, seq_bits + 1)
        target = group * in_half + (target & (in_half - 1))
        target = jnp.where(half == lax.axis_index("half"), target, -1)
        mine = lax.broadcasted_iota(jnp.int32, (devices, rows), 0) == target
        mine = jnp.where(mine, 1.0, 0.0).astype(F32)
        earlier = jnp.dot(mine.astype(BF16), before, preferred_element_type=F32)
        rank = jnp.sum(mine * earlier, axis=0, keepdims=True).astype(jnp.int32)
        slots[:, b * rows : (b + 1) * rows] = jnp.where(target >= 0, target * capacity + rank, -1)
        rank = rank + b * capacity + offset
        by_lane = lax.broadcasted_iota(jnp.int32, (LANES, rows), 0) == rank
        by_lane = jnp.where(by_lane, 1.0, 0.0).astype(BF16)
        line = lax.broadcasted_iota(jnp.int32, (devices * TAIL, rows), 0)
        code = place + 1
        low = (code & (DIGIT - 1)).astype(F32)
        high = lax.shift_right_logical(code, DIGIT.bit_length() - 1).astype(F32)
        digit = line & (TAIL - 1)
        digits = jnp.where(digit == 0, low, jnp.where(digit == 1, high, 0.0))
        line = lax.shift_right_logical(line, TAIL.bit_length() - 1)
        digits = jnp.where(line == target, digits, 0.0)
        lines = lines + lax.dot_general(
            digits.astype(BF16), by_lane, (((1,), (1,)), ((), ())), preferred_element_type=F32
        )
    tail[...] = lines.reshape(devices, TAIL, LANES).astype(BF16)


def project_kernel(first_rows, new, ask, *refs):
    count = len(first_rows)
    parts, gains, w_qkv = refs[:count], refs[count], refs[count + 1]
    refs = refs[count + 2 if new else count + 3 :]
    whole, (held, sems) = refs[0], refs[-2:]
    channels = w_qkv.shape[0]
    rows = held.shape[1]
    copies = started(
        [(part.at[pl.ds(0, rows), :], held.at[i]) for i, part in enumerate(parts)], sems
    )
    for i, first in enumerate(first_rows):
        copies[i].wait()
        normed = layer_norm(held[i], gains[0:1, :])
        whole[first : first + rows, :] = jnp.dot(
            normed, w_qkv[:, channels:], preferred_element_type=F32
        ).astype(BF16)
        if ask and i * rows < refs[1].shape[0]:
            scale = BF16((channels // HEADS) ** (-0.5))
            query = jnp.dot(normed, w_qkv[:, :channels], preferred_element_type=F32).astype(BF16)
            refs[1][i * rows : (i + 1) * rows, :] = (query * scale).astype(BF16)


def loads(queries, p, keyed, starts):
    channels = queries.shape[1]

    def asked(at, width):
        return queries[p * PATCH : (p + 1) * PATCH, at : at + width]

    def keys(at, width):
        pieces = [keyed[pl.ds(start, PATCH), at : at + width] for start in starts]
        return jnp.concatenate(pieces, axis=0)

    return asked, keys, lambda at, width: keys(channels + at, width)


def lane_tiles(packed, rows):
    capacity, channels = rows.shape[1:]
    return [
        (
            packed.at[:, pl.ds(j * capacity, capacity), :],
            rows.at[:, :, pl.ds(j * LANES, LANES)],
        )
        for j in range(channels // LANES)
    ]


def first_kernel(
    ring_chips,
    late_rows,
    pattern,
    pattern_beyond,
    slot_of_row,
    kept_rows,
    gains,
    w_qkv,
    queries,
    queries_beyond,
    w_proj,
    tail,
    points,
    *refs,
):
    late, refs = refs[: len(late_rows)], refs[len(late_rows) :]
    *points_beyond, outgoing, keyed, attended, points_held, first_held, outgoing_held = refs[:-3]
    late_held, sems, late_sems = refs[-3:]
    rows, channels = points.shape
    devices, capacity, _ = outgoing_held.shape
    row_tiles = channels // LANES * capacity
    patches = rows // PATCH
    chosen = pattern.shape[0]
    me = lax.axis_index(GROUP)
    part = rows // len(points_beyond)
    late_part = late_held.shape[1]
    landing = started(
        [(piece.at[pl.ds(0, late_part), :], late_held.at[i]) for i, piece in enumerate(late)],
        late_sems,
    )
    copies = started(
        [(tail, outgoing.at[:, pl.ds(row_tiles, TAIL), :]), (points, points_held.at[:rows])]
        + [
            (piece.at[pl.ds(0, part), :], points_held.at[pl.ds(rows + i * part, part), :])
            for i, piece in enumerate(points_beyond)
        ],
        sems.at[0],
    )
    for i, first in enumerate(late_rows):
        landing[i].wait()
        keyed[first : first + late_part, :] = jnp.dot(
            layer_norm(late_held[i], gains[0:1, :]),
            w_qkv[:, channels:],
            preferred_element_type=F32,
        ).astype(BF16)
    blocks = ((pattern, queries, 0), (pattern_beyond, queries_beyond, ring_chips or 1))
    loaded = []
    for b, (picked, asking, own_slot) in enumerate(blocks):
        for p in range(patches):
            starts = [own_slot * rows + p * PATCH]
            for j in range(chosen):
                if ring_chips:
                    patch = picked[j, p]
                    owner, local = lax.div(patch, patches), lax.rem(patch, patches)
                    chip = lax.rem(lax.div(me, 2) - lax.div(owner, 2) + ring_chips, ring_chips)
                    slot = 2 * chip + jnp.where(lax.rem(me, 2) == lax.rem(owner, 2), 0, 1)
                    starts.append(pl.multiple_of((slot * patches + local) * PATCH, PATCH))
                else:
                    starts.append((2 * patches + (b * patches + p) * chosen + j) * PATCH)
            loaded.append(loads(asking, p, keyed, starts))
    for p, done in attend(loaded, channels // HEADS):
        attended[p * PATCH : (p + 1) * PATCH, :] = done
    for copy in copies[1:]:
        copy.wait()

    first_held[...] = mix(points_held[...], attended[...], w_proj)
    copies[0].wait()
    targets = devices // SEND_PARTS
    block_slots = capacity // 2
    leaving = []
    for i in range(SEND_PARTS):
        here = pl.ds(i * targets, targets)
        for b in range(2):
            mine = pl.ds(b * block_slots, block_slots)
            slots = slot_of_row[:, b * rows : (b + 1) * rows] - i * targets * block_slots
            send = one_hot_rows(slots, targets * block_slots)
            moved = jnp.dot(
                send, first_held[b * rows : (b + 1) * rows, :], preferred_element_type=F32
            )
            outgoing_held[here, mine, :] = moved.astype(BF16).reshape(
                targets, block_slots, channels
            )
        pairs = lane_tiles(outgoing.at[here], outgoing_held.at[here])
        leaving += started([(source, place) for place, source in pairs], sems.at[1 + i])
    for copy in leaving:
        copy.wait()


def second_kernel(
    pattern,
    gains,
    incoming,
    w_qkv,
    w_proj,
    w_up,
    w_down,
    w_head,
    features,
    normals,
    kv,
    queries,
    attended,
    incoming_held,
    first_up_held,
    first_down_held,
    qkv_held,
    proj_held,
    up_held,
    down_held,
    gains_held,
    tail_held,
    head_held,
    sems,
):
    rows, channels = features.shape
    devices, capacity, _ = incoming_held.shape
    patches = rows // PATCH
    chosen = pattern.shape[0]
    tail = incoming.at[:, pl.ds(channels // LANES * capacity, TAIL), :]
    small = started(
        [(tail, tail_held), (gains, gains_held), (w_head, head_held)], sems.at[0]
    )
    landing = started(lane_tiles(incoming, incoming_held), sems.at[1])
    copies = started(
        [
            (w_up.at[0], first_up_held),
            (w_down.at[0], first_down_held),
            (w_qkv.at[1], qkv_held),
            (w_proj.at[1], proj_held),
            (w_up.at[1], up_held),
            (w_down.at[1], down_held),
        ],
        sems.at[2],
    )
    for copy in small:
        copy.wait()
    per_row = LANES // capacity
    digits = tail_held[...].astype(F32)
    codes = digits[:, 0:1, :] + DIGIT * digits[:, 1:2, :]
    pieces = []
    for at in range(0, devices, per_row):
        code = codes[at]
        for i in range(1, per_row):
            code = code + codes[at + i]
        pieces.append(code)
    places = jnp.concatenate(pieces, axis=1).astype(jnp.int32) - 1
    place = one_hot_rows(places, rows)
    sides = []
    for at in range(0, len(landing), 2):
        for copy in landing[at : at + 2]:
            copy.wait()
        moved = incoming_held[:, :, at * LANES : (at + 2) * LANES]
        moved = moved.reshape(devices * capacity, 2 * LANES)
        sides.append(jnp.dot(place, moved, preferred_element_type=F32).astype(BF16))
    first = jnp.concatenate(sides, axis=1)
    second = feed(first, gains_held[1:2, :], first_up_held, first_down_held, copies[:2])
    normed = layer_norm(second, gains_held[2:3, :])
    scale = (channels // HEADS) ** (-0.5)
    copies[2].wait()
    asked = jnp.dot(normed, qkv_held[:, :channels], preferred_element_type=F32).astype(BF16)
    queries[...] = (asked * BF16(scale)).astype(BF16)
    kv[...] = jnp.dot(normed, qkv_held[:, channels:], preferred_element_type=F32).astype(BF16)
    loaded = []
    for p in range(patches):
        starts = [pl.multiple_of(pattern[j, p] * PATCH, PATCH) for j in range(chosen)]
        loaded.append(loads(queries, p, kv, [p * PATCH] + starts))
    for p, done in attend(loaded, channels // HEADS):
        attended[p * PATCH : (p + 1) * PATCH, :] = done
    copies[3].wait()
    mixed = mix(second, attended[...], proj_held)
    done = feed(mixed, gains_held[3:4, :], up_held, down_held, copies[4:])
    features[...] = done
    normals[...] = lax.dot_general(
        head_held[...], done, (((1,), (1,)), ((), ())), preferred_element_type=F32
    )


VMEM_SPEC = pl.BlockSpec(memory_space=pltpu.VMEM)
SMEM_SPEC = pl.BlockSpec(memory_space=pltpu.SMEM)
ANY_SPEC = pl.BlockSpec(memory_space=pl.ANY)


def shards(
    points,
    pattern_first,
    pattern_second,
    destination,
    norm_gains,
    w_qkv,
    w_proj,
    w_up,
    w_down,
    w_head,
):
    rows_here, channels = points.shape
    patches, chosen = pattern_first.shape
    devices = lax.axis_size("grp") * lax.axis_size("seq")
    capacity = 2 * rows_here // (2 * devices)
    pair_slots = 2 * capacity

    shards_in_group = lax.axis_size(GROUP)
    chips = shards_in_group // 2
    onward = [(i, (i + 2) % shards_in_group) for i in range(shards_in_group)]
    swap = [(i, i ^ 1) for i in range(shards_in_group)]
    across = [(i, (i + chips) % shards_in_group) for i in range(shards_in_group)]
    ring = shards_in_group * rows_here * 2 * channels * 2 <= RING_BYTES
    kept_rows = shards_in_group * rows_here if ring else 2 * patches * (1 + chosen) * PATCH
    part = rows_here // RING_PARTS

    destination = destination.reshape(1, rows_here)
    pattern_first = pattern_first.T
    part_rows = [part + TAIL] + [part] * (RING_PARTS - 1)
    column = pl.pallas_call(
        split_kernel,
        out_shape=[jax.ShapeDtypeStruct((rows, channels), BF16) for rows in part_rows],
        in_specs=[ANY_SPEC] * 3,
        out_specs=[VMEM_SPEC] * RING_PARTS,
        scratch_shapes=[
            pltpu.VMEM((1, rows_here), jnp.int32),
            pltpu.VMEM(pattern_first.shape, jnp.int32),
            pltpu.VMEM((TAIL, channels), F32),
            pltpu.SemaphoreType.DMA((2, RING_PARTS)),
        ],
        compiler_params=pltpu.CompilerParams(vmem_limit_bytes=SPLIT_BYTES),
        name="split",
    )(points, destination, pattern_first)

    weights = (w_proj, w_up, w_down)
    kv_shape = jax.ShapeDtypeStruct((kept_rows, 2 * channels), BF16)
    own_shape = jax.ShapeDtypeStruct((rows_here, channels), BF16)

    qkv_kept, proj_kept, gains_kept = pl.pallas_call(
        keep_kernel,
        out_shape=[
            *[jax.ShapeDtypeStruct(w.shape[1:], BF16) for w in (w_qkv, w_proj)],
            jax.ShapeDtypeStruct(norm_gains.shape, F32),
        ],
        in_specs=[ANY_SPEC] * 3,
        out_specs=[VMEM_SPEC] * 3,
        scratch_shapes=[pltpu.SemaphoreType.DMA((3,))],
        compiler_params=pltpu.CompilerParams(vmem_limit_bytes=PREPARE_BYTES),
        name="keep",
    )(w_qkv, w_proj, norm_gains)
    def index(beyond):
        return pl.pallas_call(
            functools.partial(index_kernel, capacity),
            out_shape=[
                jax.ShapeDtypeStruct((1, 2 * rows_here), jnp.int32),
                jax.ShapeDtypeStruct((devices, TAIL, LANES), BF16),
                jax.ShapeDtypeStruct(pattern_first.shape, jnp.int32),
            ],
            in_specs=[ANY_SPEC] * 2,
            out_specs=[VMEM_SPEC] * 3,
            scratch_shapes=[
                pltpu.VMEM((2, 1, rows_here), jnp.int32),
                pltpu.VMEM((TAIL, channels), BF16),
                pltpu.SemaphoreType.DMA((2,)),
            ],
            compiler_params=pltpu.CompilerParams(vmem_limit_bytes=PROJECT_BYTES),
            name="index",
        )(destination, beyond)

    def project(keyed, blocks, ask=False, rows=part):
        parts = [piece for _, _, block in blocks for piece in block]
        count = len(parts)
        first_rows = [
            slot * rows_here + first + i * rows
            for slot, first, block in blocks
            for i in range(len(block))
        ]
        new = keyed is None
        return pl.pallas_call(
            functools.partial(project_kernel, first_rows, new, ask),
            out_shape=[kv_shape] + [own_shape] * ask,
            in_specs=[ANY_SPEC] * count + [VMEM_SPEC] * (2 if new else 3),
            out_specs=[VMEM_SPEC] * (1 + ask),
            scratch_shapes=[
                pltpu.VMEM((count, rows, channels), BF16),
                pltpu.SemaphoreType.DMA((count,)),
            ],
            input_output_aliases={} if new else {count + 2: 0},
            cost_estimate=pl.CostEstimate(
                flops=4 * count * rows * channels**2,
                bytes_accessed=3 * count * rows * channels * 2 + 3 * channels**2 * 2,
                transcendentals=0,
            ),
            compiler_params=pltpu.CompilerParams(vmem_limit_bytes=PROJECT_BYTES),
            name="project_own" if new else "project",
        )(*parts, gains_kept, qkv_kept, *([] if new else [keyed]))

    if ring:
        beside = [lax.ppermute(rows, GROUP, swap) for rows in column]
        waiting = [(0, 0, column), (1, 0, beside)]
        for step in range(1, chips):
            column = [lax.ppermute(rows, GROUP, onward) for rows in column]
            if step == 1:
                column[0], gains_kept = lax.optimization_barrier((column[0], gains_kept))
                keyed, queries = project(None, waiting, ask=True)
                column[1], keyed = lax.optimization_barrier((column[1], keyed))
            else:
                for i, block in enumerate(waiting):
                    if block[0] == chips:
                        keyed, queries_beyond = project(keyed, [block], ask=True)
                    else:
                        (keyed,) = project(keyed, [block])
                    column[i], keyed = lax.optimization_barrier((column[i], keyed))
            if step == chips // 2:
                points_beyond = column
                slot_index, tail, pattern_beyond = index(column[0])
            if step == chips - 1:
                column[0], slot_index = lax.optimization_barrier((column[0], slot_index))
            beside = [lax.ppermute(rows, GROUP, swap) for rows in column]
            waiting = [(2 * step, 0, column), (2 * step + 1, 0, beside)]
        early = [(slot, 0, block[:-1]) for slot, _, block in waiting]
        (keyed,) = project(keyed, early)
        late_rows = [(slot + 1) * rows_here - part for slot, _, _ in waiting]
        late = [block[-1] for _, _, block in waiting]
    else:
        group = lax.all_gather(points, GROUP, axis=0, tiled=True)
        partner = lax.rem(lax.axis_index(GROUP) + chips, shards_in_group)
        points_beyond = [lax.dynamic_slice_in_dim(group, partner * rows_here, rows_here)]
        group = group.reshape(-1, PATCH, channels)
        slot_index, tail, pattern_beyond = index(lax.ppermute(column[0], GROUP, across))
        picked = [
            group[pattern.T].reshape(-1, channels) for pattern in (pattern_first, pattern_beyond)
        ]
        wide = picked[0].shape[0]
        keyed, queries = project(None, [(0, 0, column)], ask=True)
        keyed, queries_beyond = project(keyed, [(1, 0, points_beyond)], ask=True, rows=rows_here)
        (keyed,) = project(keyed, [(2, 0, [picked[0]])], rows=wide)
        (keyed,) = project(keyed, [(2 + chosen, 0, [picked[1]])], rows=wide)
        late_rows, late = [], []

    held_weights = [pltpu.VMEM(w.shape[1:], BF16) for w in weights]
    held_rows = pltpu.VMEM((rows_here, channels), BF16)
    held_slots = pltpu.VMEM((devices, pair_slots, channels), BF16)
    held_both = pltpu.VMEM((2 * rows_here, channels), BF16)
    pair_rows = channels // LANES * pair_slots + TAIL
    outgoing, _ = pl.pallas_call(
        functools.partial(first_kernel, chips if ring else 0, late_rows),
        out_shape=[jax.ShapeDtypeStruct((devices, pair_rows, LANES), BF16), kv_shape],
        in_specs=[SMEM_SPEC] * 2
        + [VMEM_SPEC] * 7
        + [ANY_SPEC] * (2 + len(late) + len(points_beyond)),
        out_specs=[ANY_SPEC, VMEM_SPEC],
        scratch_shapes=[
            held_both,
            held_both,
            held_both,
            held_slots,
            pltpu.VMEM((max(len(late), 1), part, channels), BF16),
            pltpu.SemaphoreType.DMA((1 + SEND_PARTS, 4)),
            pltpu.SemaphoreType.DMA((max(len(late), 1),)),
        ],
        input_output_aliases={3: 1},
        compiler_params=pltpu.CompilerParams(vmem_limit_bytes=FIRST_BYTES),
        name="block_first",
    )(
        pattern_first,
        pattern_beyond,
        slot_index,
        keyed,
        gains_kept,
        qkv_kept,
        queries,
        queries_beyond,
        proj_kept,
        tail,
        points,
        *late,
        *points_beyond,
    )
    incoming = lax.all_to_all(outgoing, ("grp", "seq"), split_axis=0, concat_axis=0, tiled=True)

    return pl.pallas_call(
        second_kernel,
        out_shape=(
            jax.ShapeDtypeStruct((rows_here, channels), BF16),
            jax.ShapeDtypeStruct((w_head.shape[0], rows_here), F32),
        ),
        in_specs=[SMEM_SPEC] + [ANY_SPEC] * 7,
        out_specs=(VMEM_SPEC, VMEM_SPEC),
        scratch_shapes=[
            pltpu.VMEM((rows_here, 2 * channels), BF16),
            held_rows,
            held_rows,
            held_slots,
            *held_weights[1:],
            pltpu.VMEM(w_qkv.shape[1:], BF16),
            *held_weights,
            pltpu.VMEM(norm_gains.shape, F32),
            pltpu.VMEM(tail.shape, BF16),
            pltpu.VMEM(w_head.shape, BF16),
            pltpu.SemaphoreType.DMA((3, 6)),
        ],
        compiler_params=pltpu.CompilerParams(vmem_limit_bytes=SECOND_BYTES),
        name="block_second",
    )(pattern_second.T, norm_gains, incoming, w_qkv, *weights, w_head)


def solution(mesh):
    groups, shards_in_group = mesh.devices.shape
    halves = Mesh(
        mesh.devices.reshape(groups, 2, shards_in_group // 2), ("grp",) + GROUP
    )
    everywhere = ("grp",) + GROUP
    placed = (
        P(everywhere, None),
        P(everywhere, None),
        P(everywhere, None),
        P(everywhere),
        P(),
        P(),
        P(),
        P(),
        P(),
        P(),
    )
    return jax.shard_map(
        shards,
        mesh=halves,
        in_specs=placed,
        out_specs=(P(everywhere, None), P(None, everywhere)),
        check_vma=False,
    )
```

```python
import functools

import jax
import jax.numpy as jnp
from jax import lax
from jax.experimental import pallas as pl
from jax.experimental.pallas import tpu as pltpu
from jax.sharding import Mesh, PartitionSpec as P

HEADS = 8
PATCH = 64
HEADS_TOGETHER = 4
GROUP = ("half", "seq")
RING_PARTS = 2
SEND_PARTS = 4
LANES = 128
TAIL = 8
DIGIT = 256
FIRST_BYTES = 28 * 1024 * 1024
SECOND_BYTES = 50 * 1024 * 1024
PROJECT_BYTES = 16 * 1024 * 1024
SPLIT_BYTES = 60 * 1024 * 1024
PREPARE_BYTES = 46 * 1024 * 1024
RING_BYTES = 16 * 1024 * 1024
F32 = jnp.float32
BF16 = jnp.bfloat16


def layer_norm(rows, gains):
    values = rows.astype(F32)
    average = jnp.mean(values, axis=-1, keepdims=True)
    spread = jnp.mean((values - average) ** 2, axis=-1, keepdims=True)
    return ((values - average) * lax.rsqrt(spread + 1e-05) * gains).astype(BF16)


def gelu(x):
    half = 0.5 * x
    return half + half * lax.erf(x * 0.5**0.5)


def head_masks(head_dim):
    lane = lax.broadcasted_iota(jnp.int32, (PATCH, HEADS_TOGETHER * head_dim), 1)
    return [
        jnp.where((lane >= h * head_dim) & (lane < (h + 1) * head_dim), 1.0, 0.0).astype(BF16)
        for h in range(HEADS_TOGETHER)
    ]


def attend(patches, head_dim):
    masks = head_masks(head_dim)
    width = HEADS_TOGETHER * head_dim
    heads_per_tile = LANES // head_dim
    lane = lax.broadcasted_iota(jnp.int32, (PATCH, LANES), 1)
    steps = [(p, g) for p in range(len(patches)) for g in range(HEADS // HEADS_TOGETHER)]

    def scores_of(step):
        p, g = step
        queries, keys, _ = patches[p]
        q = queries(g * width, width)
        stacked = jnp.concatenate([q * mask for mask in masks], axis=0)
        return lax.dot_general(
            stacked, keys(g * width, width), (((1,), (1,)), ((), ())), preferred_element_type=F32
        )

    scores = scores_of(steps[0])
    for i, (p, g) in enumerate(steps):
        later = scores_of(steps[i + 1]) if i + 1 < len(steps) else None
        grown = jnp.exp(scores - jnp.max(scores, axis=-1, keepdims=True))
        scale = 1.0 / jnp.sum(grown, axis=-1, keepdims=True)
        values = patches[p][2](g * width, width)
        mixed = jnp.dot(grown.astype(BF16), values, preferred_element_type=F32)
        tiles = []
        for t in range(width // LANES):
            tile = None
            for h in range(heads_per_tile):
                rows = slice((t * heads_per_tile + h) * PATCH, (t * heads_per_tile + h + 1) * PATCH)
                head = mixed[rows, t * LANES : (t + 1) * LANES] * scale[rows]
                tile = head if tile is None else jnp.where(lane < h * head_dim, tile, head)
            tiles.append(tile)
        yield p, g * width, jnp.concatenate(tiles, axis=1).astype(BF16)
        scores = later


def one_hot_rows(places, rows):
    row = lax.broadcasted_iota(jnp.int32, (rows, places.shape[1]), 0)
    return jnp.where(row == places, 1.0, 0.0).astype(BF16)


def started(pairs, sems):
    copies = [
        pltpu.make_async_copy(source, place, sems.at[at])
        for at, (source, place) in enumerate(pairs)
    ]
    for copy in copies:
        copy.start()
    return copies


def mix(rows, attended, w_proj):
    mixed = jnp.dot(attended, w_proj[...], preferred_element_type=F32)
    return (rows.astype(F32) + mixed).astype(BF16)


def feed(first, gain, w_up, w_down, copies=()):
    hidden = layer_norm(first, gain)
    total = first.astype(F32)
    for copy in copies[:1]:
        copy.wait()
    piece = 512
    pieces = range(0, w_up.shape[1], piece)
    upper = jnp.dot(hidden, w_up[:, :piece], preferred_element_type=F32)
    for at in pieces:
        later = None
        if at + piece < w_up.shape[1]:
            later = jnp.dot(
                hidden, w_up[:, at + piece : at + 2 * piece], preferred_element_type=F32
            )
        act = gelu(upper).astype(BF16)
        if at == 0:
            for copy in copies[1:]:
                copy.wait()
        total = total + jnp.dot(act, w_down[at : at + piece, :], preferred_element_type=F32)
        upper = later
    return total.astype(BF16)


def split_kernel(points, destination, pattern, *refs):
    *parts, destination_held, pattern_held, notes, sems = refs
    rows = points.shape[0] // len(parts)
    fetches = started([(destination, destination_held), (pattern, pattern_held)], sems.at[0])
    copies = started(
        [
            (points.at[pl.ds(i * rows, rows), :], part.at[pl.ds(0, rows), :])
            for i, part in enumerate(parts)
        ],
        sems.at[1],
    )
    for fetch in fetches:
        fetch.wait()
    chosen, patches = pattern.shape
    row = lax.broadcasted_iota(jnp.int32, notes.shape, 0)
    low = destination_held[...] & (DIGIT - 1)
    high = lax.shift_right_logical(destination_held[...], DIGIT.bit_length() - 1)
    values = jnp.where(row == chosen, low, jnp.where(row == chosen + 1, high, 0))
    notes[...] = values.astype(F32)
    notes[0:chosen, 0:patches] = pattern_held[...].astype(F32)
    parts[0][rows : rows + TAIL, :] = notes[...].astype(BF16)
    for copy in copies:
        copy.wait()


def keep_kernel(*refs):
    *refs, sems = refs
    count = len(refs) // 2
    for copy in started(
        [
            (source.at[0] if len(source.shape) == 3 else source, place)
            for source, place in zip(refs[:count], refs[count:])
        ],
        sems,
    ):
        copy.wait()


def index_kernel(capacity, destination, beyond, slots, tail, pattern, held, notes, sems):
    added = beyond.at[pl.ds(beyond.shape[0] - TAIL, TAIL), :]
    for fetch in started([(destination, held.at[0]), (added, notes)], sems):
        fetch.wait()
    chosen, patches = pattern.shape
    noted = notes[...].astype(F32)
    pattern[...] = noted[0:chosen, 0:patches].astype(jnp.int32)
    low, high = noted[chosen : chosen + 1, :], noted[chosen + 1 : chosen + 2, :]
    held[1] = (low + DIGIT * high).astype(jnp.int32)
    rows = held.shape[2]
    devices = tail.shape[0]
    in_half = lax.axis_size("seq")
    seq_bits = in_half.bit_length() - 1
    index = lax.axis_index(("grp", "seq"))
    offset = lax.rem(index, LANES // (2 * capacity)) * 2 * capacity
    before = lax.broadcasted_iota(jnp.int32, (rows, rows), 0)
    before = before < lax.broadcasted_iota(jnp.int32, (rows, rows), 1)
    before = jnp.where(before, 1.0, 0.0).astype(BF16)
    lines = jnp.zeros((devices * TAIL, LANES), F32)
    for b in range(2):
        target = lax.shift_right_logical(held[b], rows.bit_length() - 1)
        place = held[b] & (rows - 1)
        half = lax.shift_right_logical(target, seq_bits) & 1
        group = lax.shift_right_logical(target, seq_bits + 1)
        target = group * in_half + (target & (in_half - 1))
        target = jnp.where(half == lax.axis_index("half"), target, -1)
        mine = lax.broadcasted_iota(jnp.int32, (devices, rows), 0) == target
        mine = jnp.where(mine, 1.0, 0.0).astype(F32)
        earlier = jnp.dot(mine.astype(BF16), before, preferred_element_type=F32)
        rank = jnp.sum(mine * earlier, axis=0, keepdims=True).astype(jnp.int32)
        slots[:, b * rows : (b + 1) * rows] = jnp.where(target >= 0, target * capacity + rank, -1)
        rank = rank + b * capacity + offset
        by_lane = lax.broadcasted_iota(jnp.int32, (LANES, rows), 0) == rank
        by_lane = jnp.where(by_lane, 1.0, 0.0).astype(BF16)
        line = lax.broadcasted_iota(jnp.int32, (devices * TAIL, rows), 0)
        code = place + 1
        low = (code & (DIGIT - 1)).astype(F32)
        high = lax.shift_right_logical(code, DIGIT.bit_length() - 1).astype(F32)
        digit = line & (TAIL - 1)
        digits = jnp.where(digit == 0, low, jnp.where(digit == 1, high, 0.0))
        line = lax.shift_right_logical(line, TAIL.bit_length() - 1)
        digits = jnp.where(line == target, digits, 0.0)
        lines = lines + lax.dot_general(
            digits.astype(BF16), by_lane, (((1,), (1,)), ((), ())), preferred_element_type=F32
        )
    tail[...] = lines.reshape(devices, TAIL, LANES).astype(BF16)


def project_kernel(first_rows, new, ask, *refs):
    count = len(first_rows)
    parts, gains, w_qkv = refs[:count], refs[count], refs[count + 1]
    refs = refs[count + 2 if new else count + 3 :]
    whole, (held, sems) = refs[0], refs[-2:]
    channels = w_qkv.shape[0]
    rows = held.shape[1]
    copies = started(
        [(part.at[pl.ds(0, rows), :], held.at[i]) for i, part in enumerate(parts)], sems
    )
    for i, first in enumerate(first_rows):
        copies[i].wait()
        normed = layer_norm(held[i], gains[0:1, :])
        whole[first : first + rows, :] = jnp.dot(
            normed, w_qkv[:, channels:], preferred_element_type=F32
        ).astype(BF16)
        if ask and i * rows < refs[1].shape[0]:
            scale = BF16((channels // HEADS) ** (-0.5))
            query = jnp.dot(normed, w_qkv[:, :channels], preferred_element_type=F32).astype(BF16)
            refs[1][i * rows : (i + 1) * rows, :] = (query * scale).astype(BF16)


def loads(queries, p, keyed, starts):
    channels = queries.shape[1]

    def asked(at, width):
        return queries[p * PATCH : (p + 1) * PATCH, at : at + width]

    def keys(at, width):
        pieces = [keyed[pl.ds(start, PATCH), at : at + width] for start in starts]
        return jnp.concatenate(pieces, axis=0)

    return asked, keys, lambda at, width: keys(channels + at, width)


def lane_tiles(packed, rows):
    capacity, channels = rows.shape[1:]
    return [
        (
            packed.at[:, pl.ds(j * capacity, capacity), :],
            rows.at[:, :, pl.ds(j * LANES, LANES)],
        )
        for j in range(channels // LANES)
    ]


def first_kernel(
    ring_chips,
    late_rows,
    pattern,
    pattern_beyond,
    slot_of_row,
    kept_rows,
    gains,
    w_qkv,
    queries,
    queries_beyond,
    w_proj,
    tail,
    points,
    *refs,
):
    late, refs = refs[: len(late_rows)], refs[len(late_rows) :]
    *points_beyond, outgoing, keyed, attended, points_held, first_held, outgoing_held = refs[:-3]
    late_held, sems, late_sems = refs[-3:]
    rows, channels = points.shape
    devices, capacity, _ = outgoing_held.shape
    row_tiles = channels // LANES * capacity
    patches = rows // PATCH
    chosen = pattern.shape[0]
    me = lax.axis_index(GROUP)
    part = rows // len(points_beyond)
    late_part = late_held.shape[1]
    landing = started(
        [(piece.at[pl.ds(0, late_part), :], late_held.at[i]) for i, piece in enumerate(late)],
        late_sems,
    )
    copies = started(
        [(tail, outgoing.at[:, pl.ds(row_tiles, TAIL), :]), (points, points_held.at[:rows])]
        + [
            (piece.at[pl.ds(0, part), :], points_held.at[pl.ds(rows + i * part, part), :])
            for i, piece in enumerate(points_beyond)
        ],
        sems.at[0],
    )
    for i, first in enumerate(late_rows):
        landing[i].wait()
        keyed[first : first + late_part, :] = jnp.dot(
            layer_norm(late_held[i], gains[0:1, :]),
            w_qkv[:, channels:],
            preferred_element_type=F32,
        ).astype(BF16)
    blocks = ((pattern, queries, 0), (pattern_beyond, queries_beyond, ring_chips or 1))
    loaded = []
    for b, (picked, asking, own_slot) in enumerate(blocks):
        for p in range(patches):
            starts = [own_slot * rows + p * PATCH]
            for j in range(chosen):
                if ring_chips:
                    patch = picked[j, p]
                    owner, local = lax.div(patch, patches), lax.rem(patch, patches)
                    chip = lax.div(me, 2) - lax.div(owner, 2)
                    chip = jnp.where(local * RING_PARTS < patches, chip, -chip)
                    chip = lax.rem(chip + ring_chips, ring_chips)
                    slot = 2 * chip + jnp.where(lax.rem(me, 2) == lax.rem(owner, 2), 0, 1)
                    starts.append(pl.multiple_of((slot * patches + local) * PATCH, PATCH))
                else:
                    starts.append((2 * patches + (b * patches + p) * chosen + j) * PATCH)
            loaded.append(loads(asking, p, keyed, starts))
    for p, at, rows_done in attend(loaded, channels // HEADS):
        attended[p * PATCH : (p + 1) * PATCH, at : at + rows_done.shape[1]] = rows_done
    for copy in copies[1:]:
        copy.wait()

    first_held[...] = mix(points_held[...], attended[...], w_proj)
    copies[0].wait()
    targets = devices // SEND_PARTS
    block_slots = capacity // 2
    leaving = []
    for i in range(SEND_PARTS):
        here = pl.ds(i * targets, targets)
        for b in range(2):
            mine = pl.ds(b * block_slots, block_slots)
            slots = slot_of_row[:, b * rows : (b + 1) * rows] - i * targets * block_slots
            send = one_hot_rows(slots, targets * block_slots)
            moved = jnp.dot(
                send, first_held[b * rows : (b + 1) * rows, :], preferred_element_type=F32
            )
            outgoing_held[here, mine, :] = moved.astype(BF16).reshape(
                targets, block_slots, channels
            )
        pairs = lane_tiles(outgoing.at[here], outgoing_held.at[here])
        leaving += started([(source, place) for place, source in pairs], sems.at[1 + i])
    for copy in leaving:
        copy.wait()


def second_kernel(
    pattern,
    gains,
    incoming,
    w_qkv,
    w_proj,
    w_up,
    w_down,
    w_head,
    features,
    normals,
    kv,
    queries,
    attended,
    incoming_held,
    first_up_held,
    first_down_held,
    qkv_held,
    proj_held,
    up_held,
    down_held,
    gains_held,
    tail_held,
    head_held,
    sems,
):
    rows, channels = features.shape
    devices, capacity, _ = incoming_held.shape
    patches = rows // PATCH
    chosen = pattern.shape[0]
    tail = incoming.at[:, pl.ds(channels // LANES * capacity, TAIL), :]
    small = started(
        [(tail, tail_held), (gains, gains_held), (w_head, head_held)], sems.at[0]
    )
    landing = started(lane_tiles(incoming, incoming_held), sems.at[1])
    copies = started(
        [
            (w_up.at[0], first_up_held),
            (w_down.at[0], first_down_held),
            (w_qkv.at[1], qkv_held),
            (w_proj.at[1], proj_held),
            (w_up.at[1], up_held),
            (w_down.at[1], down_held),
        ],
        sems.at[2],
    )
    for copy in small:
        copy.wait()
    per_row = LANES // capacity
    digits = tail_held[...].astype(F32)
    codes = digits[:, 0:1, :] + DIGIT * digits[:, 1:2, :]
    pieces = []
    for at in range(0, devices, per_row):
        code = codes[at]
        for i in range(1, per_row):
            code = code + codes[at + i]
        pieces.append(code)
    places = jnp.concatenate(pieces, axis=1).astype(jnp.int32) - 1
    place = one_hot_rows(places, rows)
    sides = []
    for at in range(0, len(landing), 2):
        for copy in landing[at : at + 2]:
            copy.wait()
        moved = incoming_held[:, :, at * LANES : (at + 2) * LANES]
        moved = moved.reshape(devices * capacity, 2 * LANES)
        sides.append(jnp.dot(place, moved, preferred_element_type=F32).astype(BF16))
    first = jnp.concatenate(sides, axis=1)
    second = feed(first, gains_held[1:2, :], first_up_held, first_down_held, copies[:2])
    normed = layer_norm(second, gains_held[2:3, :])
    scale = (channels // HEADS) ** (-0.5)
    copies[2].wait()
    asked = jnp.dot(normed, qkv_held[:, :channels], preferred_element_type=F32).astype(BF16)
    queries[...] = (asked * BF16(scale)).astype(BF16)
    kv[...] = jnp.dot(normed, qkv_held[:, channels:], preferred_element_type=F32).astype(BF16)
    loaded = []
    for p in range(patches):
        starts = [pl.multiple_of(pattern[j, p] * PATCH, PATCH) for j in range(chosen)]
        loaded.append(loads(queries, p, kv, [p * PATCH] + starts))
    for p, at, rows_done in attend(loaded, channels // HEADS):
        attended[p * PATCH : (p + 1) * PATCH, at : at + rows_done.shape[1]] = rows_done
    copies[3].wait()
    mixed = mix(second, attended[...], proj_held)
    done = feed(mixed, gains_held[3:4, :], up_held, down_held, copies[4:])
    features[...] = done
    normals[...] = lax.dot_general(
        head_held[...], done, (((1,), (1,)), ((), ())), preferred_element_type=F32
    )


VMEM_SPEC = pl.BlockSpec(memory_space=pltpu.VMEM)
SMEM_SPEC = pl.BlockSpec(memory_space=pltpu.SMEM)
ANY_SPEC = pl.BlockSpec(memory_space=pl.ANY)


def shards(
    points,
    pattern_first,
    pattern_second,
    destination,
    norm_gains,
    w_qkv,
    w_proj,
    w_up,
    w_down,
    w_head,
):
    rows_here, channels = points.shape
    patches, chosen = pattern_first.shape
    devices = lax.axis_size("grp") * lax.axis_size("seq")
    capacity = 2 * rows_here // (2 * devices)
    pair_slots = 2 * capacity

    shards_in_group = lax.axis_size(GROUP)
    chips = shards_in_group // 2
    ways = [[(i, (i + by) % shards_in_group) for i in range(shards_in_group)] for by in (2, -2)]
    swap = [(i, i ^ 1) for i in range(shards_in_group)]
    across = [(i, (i + chips) % shards_in_group) for i in range(shards_in_group)]
    ring = shards_in_group * rows_here * 2 * channels * 2 <= RING_BYTES
    kept_rows = shards_in_group * rows_here if ring else 2 * patches * (1 + chosen) * PATCH
    part = rows_here // RING_PARTS

    destination = destination.reshape(1, rows_here)
    pattern_first = pattern_first.T
    part_rows = [part + TAIL] + [part] * (RING_PARTS - 1)
    column = pl.pallas_call(
        split_kernel,
        out_shape=[jax.ShapeDtypeStruct((rows, channels), BF16) for rows in part_rows],
        in_specs=[ANY_SPEC] * 3,
        out_specs=[VMEM_SPEC] * RING_PARTS,
        scratch_shapes=[
            pltpu.VMEM((1, rows_here), jnp.int32),
            pltpu.VMEM(pattern_first.shape, jnp.int32),
            pltpu.VMEM((TAIL, channels), F32),
            pltpu.SemaphoreType.DMA((2, RING_PARTS)),
        ],
        compiler_params=pltpu.CompilerParams(vmem_limit_bytes=SPLIT_BYTES),
        name="split",
    )(points, destination, pattern_first)

    weights = (w_proj, w_up, w_down)
    kv_shape = jax.ShapeDtypeStruct((kept_rows, 2 * channels), BF16)
    own_shape = jax.ShapeDtypeStruct((rows_here, channels), BF16)

    qkv_kept, proj_kept, gains_kept = pl.pallas_call(
        keep_kernel,
        out_shape=[
            *[jax.ShapeDtypeStruct(w.shape[1:], BF16) for w in (w_qkv, w_proj)],
            jax.ShapeDtypeStruct(norm_gains.shape, F32),
        ],
        in_specs=[ANY_SPEC] * 3,
        out_specs=[VMEM_SPEC] * 3,
        scratch_shapes=[pltpu.SemaphoreType.DMA((3,))],
        compiler_params=pltpu.CompilerParams(vmem_limit_bytes=PREPARE_BYTES),
        name="keep",
    )(w_qkv, w_proj, norm_gains)
    def index(beyond):
        return pl.pallas_call(
            functools.partial(index_kernel, capacity),
            out_shape=[
                jax.ShapeDtypeStruct((1, 2 * rows_here), jnp.int32),
                jax.ShapeDtypeStruct((devices, TAIL, LANES), BF16),
                jax.ShapeDtypeStruct(pattern_first.shape, jnp.int32),
            ],
            in_specs=[ANY_SPEC] * 2,
            out_specs=[VMEM_SPEC] * 3,
            scratch_shapes=[
                pltpu.VMEM((2, 1, rows_here), jnp.int32),
                pltpu.VMEM((TAIL, channels), BF16),
                pltpu.SemaphoreType.DMA((2,)),
            ],
            compiler_params=pltpu.CompilerParams(vmem_limit_bytes=PROJECT_BYTES),
            name="index",
        )(destination, beyond)

    def project(keyed, blocks, ask=False, rows=part):
        parts = [piece for _, _, block in blocks for piece in block]
        count = len(parts)
        first_rows = [
            slot * rows_here + first + i * rows
            for slot, first, block in blocks
            for i in range(len(block))
        ]
        new = keyed is None
        return pl.pallas_call(
            functools.partial(project_kernel, first_rows, new, ask),
            out_shape=[kv_shape] + [own_shape] * ask,
            in_specs=[ANY_SPEC] * count + [VMEM_SPEC] * (2 if new else 3),
            out_specs=[VMEM_SPEC] * (1 + ask),
            scratch_shapes=[
                pltpu.VMEM((count, rows, channels), BF16),
                pltpu.SemaphoreType.DMA((count,)),
            ],
            input_output_aliases={} if new else {count + 2: 0},
            cost_estimate=pl.CostEstimate(
                flops=4 * count * rows * channels**2,
                bytes_accessed=3 * count * rows * channels * 2 + 3 * channels**2 * 2,
                transcendentals=0,
            ),
            compiler_params=pltpu.CompilerParams(vmem_limit_bytes=PROJECT_BYTES),
            name="project_own" if new else "project",
        )(*parts, gains_kept, qkv_kept, *([] if new else [keyed]))

    if ring:
        beside = [lax.ppermute(rows, GROUP, swap) for rows in column]
        waiting = [(0, 0, column), (1, 0, beside)]
        for step in range(1, chips):
            column = [lax.ppermute(rows, GROUP, way) for rows, way in zip(column, ways)]
            if step == 1:
                column[0], gains_kept = lax.optimization_barrier((column[0], gains_kept))
                keyed, queries = project(None, waiting, ask=True)
                column[1], keyed = lax.optimization_barrier((column[1], keyed))
            else:
                for i, block in enumerate(waiting):
                    if block[0] == chips:
                        keyed, queries_beyond = project(keyed, [block], ask=True)
                    else:
                        (keyed,) = project(keyed, [block])
                    column[i], keyed = lax.optimization_barrier((column[i], keyed))
            if step == chips // 2:
                points_beyond = column
                slot_index, tail, pattern_beyond = index(column[0])
            if step == chips - 1:
                column[0], slot_index = lax.optimization_barrier((column[0], slot_index))
            beside = [lax.ppermute(rows, GROUP, swap) for rows in column]
            waiting = [(2 * step, 0, column), (2 * step + 1, 0, beside)]
        early = [(slot, 0, block[:-1]) for slot, _, block in waiting]
        (keyed,) = project(keyed, early)
        late_rows = [(slot + 1) * rows_here - part for slot, _, _ in waiting]
        late = [block[-1] for _, _, block in waiting]
    else:
        group = lax.all_gather(points, GROUP, axis=0, tiled=True)
        partner = lax.rem(lax.axis_index(GROUP) + chips, shards_in_group)
        points_beyond = [lax.dynamic_slice_in_dim(group, partner * rows_here, rows_here)]
        group = group.reshape(-1, PATCH, channels)
        slot_index, tail, pattern_beyond = index(lax.ppermute(column[0], GROUP, across))
        picked = [
            group[pattern.T].reshape(-1, channels) for pattern in (pattern_first, pattern_beyond)
        ]
        wide = picked[0].shape[0]
        keyed, queries = project(None, [(0, 0, column)], ask=True)
        keyed, queries_beyond = project(keyed, [(1, 0, points_beyond)], ask=True, rows=rows_here)
        (keyed,) = project(keyed, [(2, 0, [picked[0]])], rows=wide)
        (keyed,) = project(keyed, [(2 + chosen, 0, [picked[1]])], rows=wide)
        late_rows, late = [], []

    held_weights = [pltpu.VMEM(w.shape[1:], BF16) for w in weights]
    held_rows = pltpu.VMEM((rows_here, channels), BF16)
    held_slots = pltpu.VMEM((devices, pair_slots, channels), BF16)
    held_both = pltpu.VMEM((2 * rows_here, channels), BF16)
    pair_rows = channels // LANES * pair_slots + TAIL
    outgoing, _ = pl.pallas_call(
        functools.partial(first_kernel, chips if ring else 0, late_rows),
        out_shape=[jax.ShapeDtypeStruct((devices, pair_rows, LANES), BF16), kv_shape],
        in_specs=[SMEM_SPEC] * 2
        + [VMEM_SPEC] * 7
        + [ANY_SPEC] * (2 + len(late) + len(points_beyond)),
        out_specs=[ANY_SPEC, VMEM_SPEC],
        scratch_shapes=[
            held_both,
            held_both,
            held_both,
            held_slots,
            pltpu.VMEM((max(len(late), 1), part, channels), BF16),
            pltpu.SemaphoreType.DMA((1 + SEND_PARTS, 4)),
            pltpu.SemaphoreType.DMA((max(len(late), 1),)),
        ],
        input_output_aliases={3: 1},
        compiler_params=pltpu.CompilerParams(vmem_limit_bytes=FIRST_BYTES),
        name="block_first",
    )(
        pattern_first,
        pattern_beyond,
        slot_index,
        keyed,
        gains_kept,
        qkv_kept,
        queries,
        queries_beyond,
        proj_kept,
        tail,
        points,
        *late,
        *points_beyond,
    )
    incoming = lax.all_to_all(outgoing, ("grp", "seq"), split_axis=0, concat_axis=0, tiled=True)

    return pl.pallas_call(
        second_kernel,
        out_shape=(
            jax.ShapeDtypeStruct((rows_here, channels), BF16),
            jax.ShapeDtypeStruct((w_head.shape[0], rows_here), F32),
        ),
        in_specs=[SMEM_SPEC] + [ANY_SPEC] * 7,
        out_specs=(VMEM_SPEC, VMEM_SPEC),
        scratch_shapes=[
            pltpu.VMEM((rows_here, 2 * channels), BF16),
            held_rows,
            held_rows,
            held_slots,
            *held_weights[1:],
            pltpu.VMEM(w_qkv.shape[1:], BF16),
            *held_weights,
            pltpu.VMEM(norm_gains.shape, F32),
            pltpu.VMEM(tail.shape, BF16),
            pltpu.VMEM(w_head.shape, BF16),
            pltpu.SemaphoreType.DMA((3, 6)),
        ],
        compiler_params=pltpu.CompilerParams(vmem_limit_bytes=SECOND_BYTES),
        name="block_second",
    )(pattern_second.T, norm_gains, incoming, w_qkv, *weights, w_head)


def solution(mesh):
    groups, shards_in_group = mesh.devices.shape
    halves = Mesh(
        mesh.devices.reshape(groups, 2, shards_in_group // 2), ("grp",) + GROUP
    )
    everywhere = ("grp",) + GROUP
    placed = (
        P(everywhere, None),
        P(everywhere, None),
        P(everywhere, None),
        P(everywhere),
        P(),
        P(),
        P(),
        P(),
        P(),
        P(),
    )
    return jax.shard_map(
        shards,
        mesh=halves,
        in_specs=placed,
        out_specs=(P(everywhere, None), P(None, everywhere)),
        check_vma=False,
    )
```

```python
import functools

import jax
import jax.numpy as jnp
from jax import lax
from jax.experimental import pallas as pl
from jax.experimental.pallas import tpu as pltpu
from jax.sharding import Mesh, PartitionSpec as P

HEADS = 8
PATCH = 64
HEADS_TOGETHER = 4
GROUP = ("half", "seq")
RING_PARTS = 2
SEND_PARTS = 4
LANES = 128
TAIL = 8
DIGIT = 256
FIRST_BYTES = 28 * 1024 * 1024
SECOND_BYTES = 50 * 1024 * 1024
PROJECT_BYTES = 16 * 1024 * 1024
SPLIT_BYTES = 60 * 1024 * 1024
PREPARE_BYTES = 46 * 1024 * 1024
RING_BYTES = 16 * 1024 * 1024
F32 = jnp.float32
BF16 = jnp.bfloat16


def layer_norm(rows, gains):
    values = rows.astype(F32)
    average = jnp.mean(values, axis=-1, keepdims=True)
    spread = jnp.mean((values - average) ** 2, axis=-1, keepdims=True)
    return ((values - average) * lax.rsqrt(spread + 1e-05) * gains).astype(BF16)


def gelu(x):
    half = 0.5 * x
    return half + half * lax.erf(x * 0.5**0.5)


def head_masks(head_dim):
    lane = lax.broadcasted_iota(jnp.int32, (PATCH, HEADS_TOGETHER * head_dim), 1)
    return [
        jnp.where((lane >= h * head_dim) & (lane < (h + 1) * head_dim), 1.0, 0.0).astype(BF16)
        for h in range(HEADS_TOGETHER)
    ]


def attend(patches, head_dim):
    masks = head_masks(head_dim)
    width = HEADS_TOGETHER * head_dim
    heads_per_tile = LANES // head_dim
    lane = lax.broadcasted_iota(jnp.int32, (PATCH, LANES), 1)
    steps = [(p, g) for p in range(len(patches)) for g in range(HEADS // HEADS_TOGETHER)]

    def scores_of(step):
        p, g = step
        queries, keys, _ = patches[p]
        q = queries(g * width, width)
        stacked = jnp.concatenate([q * mask for mask in masks], axis=0)
        return lax.dot_general(
            stacked, keys(g * width, width), (((1,), (1,)), ((), ())), preferred_element_type=F32
        )

    scores = scores_of(steps[0])
    for i, (p, g) in enumerate(steps):
        later = scores_of(steps[i + 1]) if i + 1 < len(steps) else None
        grown = jnp.exp(scores - jnp.max(scores, axis=-1, keepdims=True))
        scale = 1.0 / jnp.sum(grown, axis=-1, keepdims=True)
        values = patches[p][2](g * width, width)
        mixed = jnp.dot(grown.astype(BF16), values, preferred_element_type=F32)
        tiles = []
        for t in range(width // LANES):
            tile = None
            for h in range(heads_per_tile):
                rows = slice((t * heads_per_tile + h) * PATCH, (t * heads_per_tile + h + 1) * PATCH)
                head = mixed[rows, t * LANES : (t + 1) * LANES] * scale[rows]
                tile = head if tile is None else jnp.where(lane < h * head_dim, tile, head)
            tiles.append(tile)
        yield p, g * width, jnp.concatenate(tiles, axis=1).astype(BF16)
        scores = later


def one_hot_rows(places, rows):
    row = lax.broadcasted_iota(jnp.int32, (rows, places.shape[1]), 0)
    return jnp.where(row == places, 1.0, 0.0).astype(BF16)


def started(pairs, sems):
    copies = [
        pltpu.make_async_copy(source, place, sems.at[at])
        for at, (source, place) in enumerate(pairs)
    ]
    for copy in copies:
        copy.start()
    return copies


def mix(rows, attended, w_proj):
    mixed = jnp.dot(attended, w_proj[...], preferred_element_type=F32)
    return (rows.astype(F32) + mixed).astype(BF16)


def feed(first, gain, w_up, w_down):
    hidden = layer_norm(first, gain)
    total = first.astype(F32)
    piece = 512
    pieces = range(0, w_up.shape[1], piece)
    upper = jnp.dot(hidden, w_up[:, :piece], preferred_element_type=F32)
    for at in pieces:
        later = None
        if at + piece < w_up.shape[1]:
            later = jnp.dot(
                hidden, w_up[:, at + piece : at + 2 * piece], preferred_element_type=F32
            )
        act = gelu(upper).astype(BF16)
        total = total + jnp.dot(act, w_down[at : at + piece, :], preferred_element_type=F32)
        upper = later
    return total.astype(BF16)


def split_kernel(points, destination, pattern, *refs):
    *parts, destination_held, pattern_held, notes, sems = refs
    rows = points.shape[0] // len(parts)
    fetches = started([(destination, destination_held), (pattern, pattern_held)], sems.at[0])
    copies = started(
        [
            (points.at[pl.ds(i * rows, rows), :], part.at[pl.ds(0, rows), :])
            for i, part in enumerate(parts)
        ],
        sems.at[1],
    )
    for fetch in fetches:
        fetch.wait()
    chosen, patches = pattern.shape
    row = lax.broadcasted_iota(jnp.int32, notes.shape, 0)
    low = destination_held[...] & (DIGIT - 1)
    high = lax.shift_right_logical(destination_held[...], DIGIT.bit_length() - 1)
    values = jnp.where(row == chosen, low, jnp.where(row == chosen + 1, high, 0))
    notes[...] = values.astype(F32)
    notes[0:chosen, 0:patches] = pattern_held[...].astype(F32)
    parts[0][rows : rows + TAIL, :] = notes[...].astype(BF16)
    for copy in copies:
        copy.wait()


def keep_kernel(*refs):
    *refs, sems = refs
    count = len(refs) // 2
    for copy in started(
        [
            (source.at[0] if len(source.shape) == 3 else source, place)
            for source, place in zip(refs[:count], refs[count:])
        ],
        sems,
    ):
        copy.wait()


def index_kernel(capacity, destination, beyond, slots, tail, pattern, held, notes, sems):
    added = beyond.at[pl.ds(beyond.shape[0] - TAIL, TAIL), :]
    for fetch in started([(destination, held.at[0]), (added, notes)], sems):
        fetch.wait()
    chosen, patches = pattern.shape
    noted = notes[...].astype(F32)
    pattern[...] = noted[0:chosen, 0:patches].astype(jnp.int32)
    low, high = noted[chosen : chosen + 1, :], noted[chosen + 1 : chosen + 2, :]
    held[1] = (low + DIGIT * high).astype(jnp.int32)
    rows = held.shape[2]
    devices = tail.shape[0]
    in_half = lax.axis_size("seq")
    seq_bits = in_half.bit_length() - 1
    index = lax.axis_index(("grp", "seq"))
    offset = lax.rem(index, LANES // (2 * capacity)) * 2 * capacity
    before = lax.broadcasted_iota(jnp.int32, (rows, rows), 0)
    before = before < lax.broadcasted_iota(jnp.int32, (rows, rows), 1)
    before = jnp.where(before, 1.0, 0.0).astype(BF16)
    lines = jnp.zeros((devices * TAIL, LANES), F32)
    for b in range(2):
        target = lax.shift_right_logical(held[b], rows.bit_length() - 1)
        place = held[b] & (rows - 1)
        half = lax.shift_right_logical(target, seq_bits) & 1
        group = lax.shift_right_logical(target, seq_bits + 1)
        target = group * in_half + (target & (in_half - 1))
        target = jnp.where(half == lax.axis_index("half"), target, -1)
        mine = lax.broadcasted_iota(jnp.int32, (devices, rows), 0) == target
        mine = jnp.where(mine, 1.0, 0.0).astype(F32)
        earlier = jnp.dot(mine.astype(BF16), before, preferred_element_type=F32)
        rank = jnp.sum(mine * earlier, axis=0, keepdims=True).astype(jnp.int32)
        slots[:, b * rows : (b + 1) * rows] = jnp.where(target >= 0, target * capacity + rank, -1)
        rank = rank + b * capacity + offset
        by_lane = lax.broadcasted_iota(jnp.int32, (LANES, rows), 0) == rank
        by_lane = jnp.where(by_lane, 1.0, 0.0).astype(BF16)
        line = lax.broadcasted_iota(jnp.int32, (devices * TAIL, rows), 0)
        code = place + 1
        low = (code & (DIGIT - 1)).astype(F32)
        high = lax.shift_right_logical(code, DIGIT.bit_length() - 1).astype(F32)
        digit = line & (TAIL - 1)
        digits = jnp.where(digit == 0, low, jnp.where(digit == 1, high, 0.0))
        line = lax.shift_right_logical(line, TAIL.bit_length() - 1)
        digits = jnp.where(line == target, digits, 0.0)
        lines = lines + lax.dot_general(
            digits.astype(BF16), by_lane, (((1,), (1,)), ((), ())), preferred_element_type=F32
        )
    tail[...] = lines.reshape(devices, TAIL, LANES).astype(BF16)


def project_kernel(first_rows, new, ask, *refs):
    count = len(first_rows)
    parts, gains, w_qkv = refs[:count], refs[count], refs[count + 1]
    refs = refs[count + 2 if new else count + 3 :]
    whole, (held, sems) = refs[0], refs[-2:]
    channels = w_qkv.shape[0]
    rows = held.shape[1]
    copies = started(
        [(part.at[pl.ds(0, rows), :], held.at[i]) for i, part in enumerate(parts)], sems
    )
    for i, first in enumerate(first_rows):
        copies[i].wait()
        normed = layer_norm(held[i], gains[0:1, :])
        whole[first : first + rows, :] = jnp.dot(
            normed, w_qkv[:, channels:], preferred_element_type=F32
        ).astype(BF16)
        if ask and i * rows < refs[1].shape[0]:
            scale = BF16((channels // HEADS) ** (-0.5))
            query = jnp.dot(normed, w_qkv[:, :channels], preferred_element_type=F32).astype(BF16)
            refs[1][i * rows : (i + 1) * rows, :] = (query * scale).astype(BF16)


def loads(queries, p, keyed, starts):
    channels = queries.shape[1]

    def asked(at, width):
        return queries[p * PATCH : (p + 1) * PATCH, at : at + width]

    def keys(at, width):
        pieces = [keyed[pl.ds(start, PATCH), at : at + width] for start in starts]
        return jnp.concatenate(pieces, axis=0)

    return asked, keys, lambda at, width: keys(channels + at, width)


def lane_tiles(packed, rows):
    capacity, channels = rows.shape[1:]
    return [
        (
            packed.at[:, pl.ds(j * capacity, capacity), :],
            rows.at[:, :, pl.ds(j * LANES, LANES)],
        )
        for j in range(channels // LANES)
    ]


def first_kernel(
    ring_chips,
    late_rows,
    pattern,
    pattern_beyond,
    slot_of_row,
    kept_rows,
    gains,
    w_qkv,
    queries,
    queries_beyond,
    w_proj,
    tail,
    points,
    *refs,
):
    late, refs = refs[: len(late_rows)], refs[len(late_rows) :]
    *points_beyond, outgoing, keyed, attended, points_held, first_held, outgoing_held = refs[:-3]
    late_held, sems, late_sems = refs[-3:]
    rows, channels = points.shape
    devices, capacity, _ = outgoing_held.shape
    row_tiles = channels // LANES * capacity
    patches = rows // PATCH
    chosen = pattern.shape[0]
    me = lax.axis_index(GROUP)
    part = rows // len(points_beyond)
    late_part = late_held.shape[1]
    landing = started(
        [(piece.at[pl.ds(0, late_part), :], late_held.at[i]) for i, piece in enumerate(late)],
        late_sems,
    )
    copies = started(
        [(tail, outgoing.at[:, pl.ds(row_tiles, TAIL), :]), (points, points_held.at[:rows])]
        + [
            (piece.at[pl.ds(0, part), :], points_held.at[pl.ds(rows + i * part, part), :])
            for i, piece in enumerate(points_beyond)
        ],
        sems.at[0],
    )
    for copy in landing + copies[1:]:
        copy.wait()
    for i, first in enumerate(late_rows):
        keyed[first : first + late_part, :] = jnp.dot(
            layer_norm(late_held[i], gains[0:1, :]),
            w_qkv[:, channels:],
            preferred_element_type=F32,
        ).astype(BF16)
    blocks = ((pattern, queries, 0), (pattern_beyond, queries_beyond, ring_chips or 1))
    loaded = []
    for b, (picked, asking, own_slot) in enumerate(blocks):
        for p in range(patches):
            starts = [own_slot * rows + p * PATCH]
            for j in range(chosen):
                if ring_chips:
                    patch = picked[j, p]
                    owner, local = lax.div(patch, patches), lax.rem(patch, patches)
                    chip = lax.rem(lax.div(me, 2) - lax.div(owner, 2) + ring_chips, ring_chips)
                    slot = 2 * chip + jnp.where(lax.rem(me, 2) == lax.rem(owner, 2), 0, 1)
                    starts.append(pl.multiple_of((slot * patches + local) * PATCH, PATCH))
                else:
                    starts.append((2 * patches + (b * patches + p) * chosen + j) * PATCH)
            loaded.append(loads(asking, p, keyed, starts))
    for p, at, rows_done in attend(loaded, channels // HEADS):
        attended[p * PATCH : (p + 1) * PATCH, at : at + rows_done.shape[1]] = rows_done

    first_held[...] = mix(points_held[...], attended[...], w_proj)
    targets = devices // SEND_PARTS
    block_slots = capacity // 2
    leaving = []
    for i in range(SEND_PARTS):
        here = pl.ds(i * targets, targets)
        for b in range(2):
            mine = pl.ds(b * block_slots, block_slots)
            slots = slot_of_row[:, b * rows : (b + 1) * rows] - i * targets * block_slots
            send = one_hot_rows(slots, targets * block_slots)
            moved = jnp.dot(
                send, first_held[b * rows : (b + 1) * rows, :], preferred_element_type=F32
            )
            outgoing_held[here, mine, :] = moved.astype(BF16).reshape(
                targets, block_slots, channels
            )
        pairs = lane_tiles(outgoing.at[here], outgoing_held.at[here])
        leaving += started([(source, place) for place, source in pairs], sems.at[1 + i])
    for copy in copies[:1] + leaving:
        copy.wait()


def second_kernel(
    pattern,
    gains,
    incoming,
    w_qkv,
    w_proj,
    w_up,
    w_down,
    w_head,
    features,
    normals,
    kv,
    queries,
    attended,
    incoming_held,
    first_up_held,
    first_down_held,
    qkv_held,
    proj_held,
    up_held,
    down_held,
    gains_held,
    tail_held,
    head_held,
    sems,
):
    rows, channels = features.shape
    devices, capacity, _ = incoming_held.shape
    patches = rows // PATCH
    chosen = pattern.shape[0]
    tail = incoming.at[:, pl.ds(channels // LANES * capacity, TAIL), :]
    small = started(
        [(tail, tail_held), (gains, gains_held), (w_head, head_held)], sems.at[0]
    )
    landing = started(lane_tiles(incoming, incoming_held), sems.at[1])
    copies = started(
        [
            (w_up.at[0], first_up_held),
            (w_down.at[0], first_down_held),
            (w_qkv.at[1], qkv_held),
            (w_proj.at[1], proj_held),
            (w_up.at[1], up_held),
            (w_down.at[1], down_held),
        ],
        sems.at[2],
    )
    for copy in small:
        copy.wait()
    per_row = LANES // capacity
    digits = tail_held[...].astype(F32)
    codes = digits[:, 0:1, :] + DIGIT * digits[:, 1:2, :]
    pieces = []
    for at in range(0, devices, per_row):
        code = codes[at]
        for i in range(1, per_row):
            code = code + codes[at + i]
        pieces.append(code)
    places = jnp.concatenate(pieces, axis=1).astype(jnp.int32) - 1
    place = one_hot_rows(places, rows)
    sides = []
    for at in range(0, len(landing), 2):
        for copy in landing[at : at + 2]:
            copy.wait()
        moved = incoming_held[:, :, at * LANES : (at + 2) * LANES]
        moved = moved.reshape(devices * capacity, 2 * LANES)
        sides.append(jnp.dot(place, moved, preferred_element_type=F32).astype(BF16))
    first = jnp.concatenate(sides, axis=1)
    for copy in copies[:2]:
        copy.wait()
    second = feed(first, gains_held[1:2, :], first_up_held, first_down_held)
    for copy in copies[2:]:
        copy.wait()
    normed = layer_norm(second, gains_held[2:3, :])
    scale = (channels // HEADS) ** (-0.5)
    asked = jnp.dot(normed, qkv_held[:, :channels], preferred_element_type=F32).astype(BF16)
    queries[...] = (asked * BF16(scale)).astype(BF16)
    kv[...] = jnp.dot(normed, qkv_held[:, channels:], preferred_element_type=F32).astype(BF16)
    loaded = []
    for p in range(patches):
        starts = [pl.multiple_of(pattern[j, p] * PATCH, PATCH) for j in range(chosen)]
        loaded.append(loads(queries, p, kv, [p * PATCH] + starts))
    for p, at, rows_done in attend(loaded, channels // HEADS):
        attended[p * PATCH : (p + 1) * PATCH, at : at + rows_done.shape[1]] = rows_done
    mixed = mix(second, attended[...], proj_held)
    done = feed(mixed, gains_held[3:4, :], up_held, down_held)
    features[...] = done
    normals[...] = lax.dot_general(
        head_held[...], done, (((1,), (1,)), ((), ())), preferred_element_type=F32
    )


VMEM_SPEC = pl.BlockSpec(memory_space=pltpu.VMEM)
SMEM_SPEC = pl.BlockSpec(memory_space=pltpu.SMEM)
ANY_SPEC = pl.BlockSpec(memory_space=pl.ANY)


def shards(
    points,
    pattern_first,
    pattern_second,
    destination,
    norm_gains,
    w_qkv,
    w_proj,
    w_up,
    w_down,
    w_head,
):
    rows_here, channels = points.shape
    patches, chosen = pattern_first.shape
    devices = lax.axis_size("grp") * lax.axis_size("seq")
    capacity = 2 * rows_here // (2 * devices)
    pair_slots = 2 * capacity

    shards_in_group = lax.axis_size(GROUP)
    chips = shards_in_group // 2
    onward = [(i, (i + 2) % shards_in_group) for i in range(shards_in_group)]
    swap = [(i, i ^ 1) for i in range(shards_in_group)]
    across = [(i, (i + chips) % shards_in_group) for i in range(shards_in_group)]
    ring = shards_in_group * rows_here * 2 * channels * 2 <= RING_BYTES
    kept_rows = shards_in_group * rows_here if ring else 2 * patches * (1 + chosen) * PATCH
    part = rows_here // RING_PARTS

    destination = destination.reshape(1, rows_here)
    pattern_first = pattern_first.T
    part_rows = [part + TAIL] + [part] * (RING_PARTS - 1)
    column = pl.pallas_call(
        split_kernel,
        out_shape=[jax.ShapeDtypeStruct((rows, channels), BF16) for rows in part_rows],
        in_specs=[ANY_SPEC] * 3,
        out_specs=[VMEM_SPEC] * RING_PARTS,
        scratch_shapes=[
            pltpu.VMEM((1, rows_here), jnp.int32),
            pltpu.VMEM(pattern_first.shape, jnp.int32),
            pltpu.VMEM((TAIL, channels), F32),
            pltpu.SemaphoreType.DMA((2, RING_PARTS)),
        ],
        compiler_params=pltpu.CompilerParams(vmem_limit_bytes=SPLIT_BYTES),
        name="split",
    )(points, destination, pattern_first)

    weights = (w_proj, w_up, w_down)
    kv_shape = jax.ShapeDtypeStruct((kept_rows, 2 * channels), BF16)
    own_shape = jax.ShapeDtypeStruct((rows_here, channels), BF16)

    qkv_kept, proj_kept, gains_kept = pl.pallas_call(
        keep_kernel,
        out_shape=[
            *[jax.ShapeDtypeStruct(w.shape[1:], BF16) for w in (w_qkv, w_proj)],
            jax.ShapeDtypeStruct(norm_gains.shape, F32),
        ],
        in_specs=[ANY_SPEC] * 3,
        out_specs=[VMEM_SPEC] * 3,
        scratch_shapes=[pltpu.SemaphoreType.DMA((3,))],
        compiler_params=pltpu.CompilerParams(vmem_limit_bytes=PREPARE_BYTES),
        name="keep",
    )(w_qkv, w_proj, norm_gains)
    def index(beyond):
        return pl.pallas_call(
            functools.partial(index_kernel, capacity),
            out_shape=[
                jax.ShapeDtypeStruct((1, 2 * rows_here), jnp.int32),
                jax.ShapeDtypeStruct((devices, TAIL, LANES), BF16),
                jax.ShapeDtypeStruct(pattern_first.shape, jnp.int32),
            ],
            in_specs=[ANY_SPEC] * 2,
            out_specs=[VMEM_SPEC] * 3,
            scratch_shapes=[
                pltpu.VMEM((2, 1, rows_here), jnp.int32),
                pltpu.VMEM((TAIL, channels), BF16),
                pltpu.SemaphoreType.DMA((2,)),
            ],
            compiler_params=pltpu.CompilerParams(vmem_limit_bytes=PROJECT_BYTES),
            name="index",
        )(destination, beyond)

    def project(keyed, blocks, ask=False, rows=part):
        parts = [piece for _, _, block in blocks for piece in block]
        count = len(parts)
        first_rows = [
            slot * rows_here + first + i * rows
            for slot, first, block in blocks
            for i in range(len(block))
        ]
        new = keyed is None
        return pl.pallas_call(
            functools.partial(project_kernel, first_rows, new, ask),
            out_shape=[kv_shape] + [own_shape] * ask,
            in_specs=[ANY_SPEC] * count + [VMEM_SPEC] * (2 if new else 3),
            out_specs=[VMEM_SPEC] * (1 + ask),
            scratch_shapes=[
                pltpu.VMEM((count, rows, channels), BF16),
                pltpu.SemaphoreType.DMA((count,)),
            ],
            input_output_aliases={} if new else {count + 2: 0},
            cost_estimate=pl.CostEstimate(
                flops=4 * count * rows * channels**2,
                bytes_accessed=3 * count * rows * channels * 2 + 3 * channels**2 * 2,
                transcendentals=0,
            ),
            compiler_params=pltpu.CompilerParams(vmem_limit_bytes=PROJECT_BYTES),
            name="project_own" if new else "project",
        )(*parts, gains_kept, qkv_kept, *([] if new else [keyed]))

    if ring:
        beside = [lax.ppermute(rows, GROUP, swap) for rows in column]
        waiting = [(0, 0, column), (1, 0, beside)]
        for step in range(1, chips):
            column = [lax.ppermute(rows, GROUP, onward) for rows in column]
            if step == 1:
                column[0], gains_kept = lax.optimization_barrier((column[0], gains_kept))
                keyed, queries = project(None, waiting, ask=True)
                column[1], keyed = lax.optimization_barrier((column[1], keyed))
            else:
                for i, block in enumerate(waiting):
                    if block[0] == chips:
                        keyed, queries_beyond = project(keyed, [block], ask=True)
                    else:
                        (keyed,) = project(keyed, [block])
                    column[i], keyed = lax.optimization_barrier((column[i], keyed))
            if step == chips // 2:
                points_beyond = column
                slot_index, tail, pattern_beyond = index(column[0])
            if step == chips - 1:
                column[0], slot_index = lax.optimization_barrier((column[0], slot_index))
            beside = [lax.ppermute(rows, GROUP, swap) for rows in column]
            waiting = [(2 * step, 0, column), (2 * step + 1, 0, beside)]
        early = [(slot, 0, block[:-1]) for slot, _, block in waiting]
        (keyed,) = project(keyed, early)
        late_rows = [(slot + 1) * rows_here - part for slot, _, _ in waiting]
        late = [block[-1] for _, _, block in waiting]
    else:
        group = lax.all_gather(points, GROUP, axis=0, tiled=True)
        partner = lax.rem(lax.axis_index(GROUP) + chips, shards_in_group)
        points_beyond = [lax.dynamic_slice_in_dim(group, partner * rows_here, rows_here)]
        group = group.reshape(-1, PATCH, channels)
        slot_index, tail, pattern_beyond = index(lax.ppermute(column[0], GROUP, across))
        picked = [
            group[pattern.T].reshape(-1, channels) for pattern in (pattern_first, pattern_beyond)
        ]
        wide = picked[0].shape[0]
        keyed, queries = project(None, [(0, 0, column)], ask=True)
        keyed, queries_beyond = project(keyed, [(1, 0, points_beyond)], ask=True, rows=rows_here)
        (keyed,) = project(keyed, [(2, 0, [picked[0]])], rows=wide)
        (keyed,) = project(keyed, [(2 + chosen, 0, [picked[1]])], rows=wide)
        late_rows, late = [], []

    held_weights = [pltpu.VMEM(w.shape[1:], BF16) for w in weights]
    held_rows = pltpu.VMEM((rows_here, channels), BF16)
    held_slots = pltpu.VMEM((devices, pair_slots, channels), BF16)
    held_both = pltpu.VMEM((2 * rows_here, channels), BF16)
    pair_rows = channels // LANES * pair_slots + TAIL
    outgoing, _ = pl.pallas_call(
        functools.partial(first_kernel, chips if ring else 0, late_rows),
        out_shape=[jax.ShapeDtypeStruct((devices, pair_rows, LANES), BF16), kv_shape],
        in_specs=[SMEM_SPEC] * 2
        + [VMEM_SPEC] * 7
        + [ANY_SPEC] * (2 + len(late) + len(points_beyond)),
        out_specs=[ANY_SPEC, VMEM_SPEC],
        scratch_shapes=[
            held_both,
            held_both,
            held_both,
            held_slots,
            pltpu.VMEM((max(len(late), 1), part, channels), BF16),
            pltpu.SemaphoreType.DMA((1 + SEND_PARTS, 4)),
            pltpu.SemaphoreType.DMA((max(len(late), 1),)),
        ],
        input_output_aliases={3: 1},
        compiler_params=pltpu.CompilerParams(vmem_limit_bytes=FIRST_BYTES),
        name="block_first",
    )(
        pattern_first,
        pattern_beyond,
        slot_index,
        keyed,
        gains_kept,
        qkv_kept,
        queries,
        queries_beyond,
        proj_kept,
        tail,
        points,
        *late,
        *points_beyond,
    )
    incoming = lax.all_to_all(outgoing, ("grp", "seq"), split_axis=0, concat_axis=0, tiled=True)

    return pl.pallas_call(
        second_kernel,
        out_shape=(
            jax.ShapeDtypeStruct((rows_here, channels), BF16),
            jax.ShapeDtypeStruct((w_head.shape[0], rows_here), F32),
        ),
        in_specs=[SMEM_SPEC] + [ANY_SPEC] * 7,
        out_specs=(VMEM_SPEC, VMEM_SPEC),
        scratch_shapes=[
            pltpu.VMEM((rows_here, 2 * channels), BF16),
            held_rows,
            held_rows,
            held_slots,
            *held_weights[1:],
            pltpu.VMEM(w_qkv.shape[1:], BF16),
            *held_weights,
            pltpu.VMEM(norm_gains.shape, F32),
            pltpu.VMEM(tail.shape, BF16),
            pltpu.VMEM(w_head.shape, BF16),
            pltpu.SemaphoreType.DMA((3, 6)),
        ],
        compiler_params=pltpu.CompilerParams(vmem_limit_bytes=SECOND_BYTES),
        name="block_second",
    )(pattern_second.T, norm_gains, incoming, w_qkv, *weights, w_head)


def solution(mesh):
    groups, shards_in_group = mesh.devices.shape
    halves = Mesh(
        mesh.devices.reshape(groups, 2, shards_in_group // 2), ("grp",) + GROUP
    )
    everywhere = ("grp",) + GROUP
    placed = (
        P(everywhere, None),
        P(everywhere, None),
        P(everywhere, None),
        P(everywhere),
        P(),
        P(),
        P(),
        P(),
        P(),
        P(),
    )
    return jax.shard_map(
        shards,
        mesh=halves,
        in_specs=placed,
        out_specs=(P(everywhere, None), P(None, everywhere)),
        check_vma=False,
    )
```

```python
import functools

import jax
import jax.numpy as jnp
from jax import lax
from jax.experimental import pallas as pl
from jax.experimental.pallas import tpu as pltpu
from jax.sharding import Mesh, PartitionSpec as P

HEADS = 8
PATCH = 64
HEADS_TOGETHER = 4
GROUP = ("half", "seq")
RING_PARTS = 2
SEND_PARTS = 2
LANES = 128
TAIL = 8
DIGIT = 256
FIRST_BYTES = 28 * 1024 * 1024
SECOND_BYTES = 50 * 1024 * 1024
PROJECT_BYTES = 16 * 1024 * 1024
SPLIT_BYTES = 60 * 1024 * 1024
PREPARE_BYTES = 46 * 1024 * 1024
RING_BYTES = 16 * 1024 * 1024
F32 = jnp.float32
BF16 = jnp.bfloat16


def layer_norm(rows, gains):
    values = rows.astype(F32)
    average = jnp.mean(values, axis=-1, keepdims=True)
    spread = jnp.mean((values - average) ** 2, axis=-1, keepdims=True)
    return ((values - average) * lax.rsqrt(spread + 1e-05) * gains).astype(BF16)


def gelu(x):
    half = 0.5 * x
    return half + half * lax.erf(x * 0.5**0.5)


def head_masks(head_dim):
    lane = lax.broadcasted_iota(jnp.int32, (PATCH, HEADS_TOGETHER * head_dim), 1)
    return [
        jnp.where((lane >= h * head_dim) & (lane < (h + 1) * head_dim), 1.0, 0.0).astype(BF16)
        for h in range(HEADS_TOGETHER)
    ]


def attend(patches, head_dim):
    masks = head_masks(head_dim)
    width = HEADS_TOGETHER * head_dim
    heads_per_tile = LANES // head_dim
    lane = lax.broadcasted_iota(jnp.int32, (PATCH, LANES), 1)
    steps = [(p, g) for p in range(len(patches)) for g in range(HEADS // HEADS_TOGETHER)]

    def scores_of(step):
        p, g = step
        queries, keys, _ = patches[p]
        q = queries(g * width, width)
        stacked = jnp.concatenate([q * mask for mask in masks], axis=0)
        return lax.dot_general(
            stacked, keys(g * width, width), (((1,), (1,)), ((), ())), preferred_element_type=F32
        )

    scores = scores_of(steps[0])
    for i, (p, g) in enumerate(steps):
        later = scores_of(steps[i + 1]) if i + 1 < len(steps) else None
        grown = jnp.exp(scores - jnp.max(scores, axis=-1, keepdims=True))
        scale = 1.0 / jnp.sum(grown, axis=-1, keepdims=True)
        values = patches[p][2](g * width, width)
        mixed = jnp.dot(grown.astype(BF16), values, preferred_element_type=F32)
        tiles = []
        for t in range(width // LANES):
            tile = None
            for h in range(heads_per_tile):
                rows = slice((t * heads_per_tile + h) * PATCH, (t * heads_per_tile + h + 1) * PATCH)
                head = mixed[rows, t * LANES : (t + 1) * LANES] * scale[rows]
                tile = head if tile is None else jnp.where(lane < h * head_dim, tile, head)
            tiles.append(tile)
        yield p, g * width, jnp.concatenate(tiles, axis=1).astype(BF16)
        scores = later


def one_hot_rows(places, rows):
    row = lax.broadcasted_iota(jnp.int32, (rows, places.shape[1]), 0)
    return jnp.where(row == places, 1.0, 0.0).astype(BF16)


def started(pairs, sems):
    copies = [
        pltpu.make_async_copy(source, place, sems.at[at])
        for at, (source, place) in enumerate(pairs)
    ]
    for copy in copies:
        copy.start()
    return copies


def mix(rows, attended, w_proj):
    mixed = jnp.dot(attended, w_proj[...], preferred_element_type=F32)
    return (rows.astype(F32) + mixed).astype(BF16)


def feed(first, gain, w_up, w_down):
    hidden = layer_norm(first, gain)
    total = first.astype(F32)
    piece = 1024
    pieces = range(0, w_up.shape[1], piece)
    upper = jnp.dot(hidden, w_up[:, :piece], preferred_element_type=F32)
    for at in pieces:
        later = None
        if at + piece < w_up.shape[1]:
            later = jnp.dot(
                hidden, w_up[:, at + piece : at + 2 * piece], preferred_element_type=F32
            )
        act = gelu(upper).astype(BF16)
        total = total + jnp.dot(act, w_down[at : at + piece, :], preferred_element_type=F32)
        upper = later
    return total.astype(BF16)


def split_kernel(points, destination, pattern, *refs):
    *parts, destination_held, pattern_held, notes, sems = refs
    rows = points.shape[0] // len(parts)
    fetches = started([(destination, destination_held), (pattern, pattern_held)], sems.at[0])
    copies = started(
        [
            (points.at[pl.ds(i * rows, rows), :], part.at[pl.ds(0, rows), :])
            for i, part in enumerate(parts)
        ],
        sems.at[1],
    )
    for fetch in fetches:
        fetch.wait()
    chosen, patches = pattern.shape
    row = lax.broadcasted_iota(jnp.int32, notes.shape, 0)
    low = destination_held[...] & (DIGIT - 1)
    high = lax.shift_right_logical(destination_held[...], DIGIT.bit_length() - 1)
    values = jnp.where(row == chosen, low, jnp.where(row == chosen + 1, high, 0))
    notes[...] = values.astype(F32)
    notes[0:chosen, 0:patches] = pattern_held[...].astype(F32)
    parts[0][rows : rows + TAIL, :] = notes[...].astype(BF16)
    for copy in copies:
        copy.wait()


def keep_kernel(*refs):
    *refs, sems = refs
    count = len(refs) // 2
    for copy in started(
        [
            (source.at[0] if len(source.shape) == 3 else source, place)
            for source, place in zip(refs[:count], refs[count:])
        ],
        sems,
    ):
        copy.wait()


def index_kernel(capacity, destination, beyond, slots, tail, pattern, held, notes, sems):
    added = beyond.at[pl.ds(beyond.shape[0] - TAIL, TAIL), :]
    for fetch in started([(destination, held.at[0]), (added, notes)], sems):
        fetch.wait()
    chosen, patches = pattern.shape
    noted = notes[...].astype(F32)
    pattern[...] = noted[0:chosen, 0:patches].astype(jnp.int32)
    low, high = noted[chosen : chosen + 1, :], noted[chosen + 1 : chosen + 2, :]
    held[1] = (low + DIGIT * high).astype(jnp.int32)
    rows = held.shape[2]
    devices = tail.shape[0]
    in_half = lax.axis_size("seq")
    seq_bits = in_half.bit_length() - 1
    index = lax.axis_index(("grp", "seq"))
    offset = lax.rem(index, LANES // (2 * capacity)) * 2 * capacity
    before = lax.broadcasted_iota(jnp.int32, (rows, rows), 0)
    before = before < lax.broadcasted_iota(jnp.int32, (rows, rows), 1)
    before = jnp.where(before, 1.0, 0.0).astype(BF16)
    lines = jnp.zeros((devices * TAIL, LANES), F32)
    for b in range(2):
        target = lax.shift_right_logical(held[b], rows.bit_length() - 1)
        place = held[b] & (rows - 1)
        half = lax.shift_right_logical(target, seq_bits) & 1
        group = lax.shift_right_logical(target, seq_bits + 1)
        target = group * in_half + (target & (in_half - 1))
        target = jnp.where(half == lax.axis_index("half"), target, -1)
        mine = lax.broadcasted_iota(jnp.int32, (devices, rows), 0) == target
        mine = jnp.where(mine, 1.0, 0.0).astype(F32)
        earlier = jnp.dot(mine.astype(BF16), before, preferred_element_type=F32)
        rank = jnp.sum(mine * earlier, axis=0, keepdims=True).astype(jnp.int32)
        slots[:, b * rows : (b + 1) * rows] = jnp.where(target >= 0, target * capacity + rank, -1)
        rank = rank + b * capacity + offset
        by_lane = lax.broadcasted_iota(jnp.int32, (LANES, rows), 0) == rank
        by_lane = jnp.where(by_lane, 1.0, 0.0).astype(BF16)
        line = lax.broadcasted_iota(jnp.int32, (devices * TAIL, rows), 0)
        code = place + 1
        low = (code & (DIGIT - 1)).astype(F32)
        high = lax.shift_right_logical(code, DIGIT.bit_length() - 1).astype(F32)
        digit = line & (TAIL - 1)
        digits = jnp.where(digit == 0, low, jnp.where(digit == 1, high, 0.0))
        line = lax.shift_right_logical(line, TAIL.bit_length() - 1)
        digits = jnp.where(line == target, digits, 0.0)
        lines = lines + lax.dot_general(
            digits.astype(BF16), by_lane, (((1,), (1,)), ((), ())), preferred_element_type=F32
        )
    tail[...] = lines.reshape(devices, TAIL, LANES).astype(BF16)


def project_kernel(first_rows, new, ask, *refs):
    count = len(first_rows)
    parts, gains, w_qkv = refs[:count], refs[count], refs[count + 1]
    refs = refs[count + 2 if new else count + 3 :]
    whole, (held, sems) = refs[0], refs[-2:]
    channels = w_qkv.shape[0]
    rows = held.shape[1]
    copies = started(
        [(part.at[pl.ds(0, rows), :], held.at[i]) for i, part in enumerate(parts)], sems
    )
    for i, first in enumerate(first_rows):
        copies[i].wait()
        normed = layer_norm(held[i], gains[0:1, :])
        whole[first : first + rows, :] = jnp.dot(
            normed, w_qkv[:, channels:], preferred_element_type=F32
        ).astype(BF16)
        if ask and i * rows < refs[1].shape[0]:
            scale = BF16((channels // HEADS) ** (-0.5))
            query = jnp.dot(normed, w_qkv[:, :channels], preferred_element_type=F32).astype(BF16)
            refs[1][i * rows : (i + 1) * rows, :] = (query * scale).astype(BF16)


def loads(queries, p, keyed, starts):
    channels = queries.shape[1]

    def asked(at, width):
        return queries[p * PATCH : (p + 1) * PATCH, at : at + width]

    def keys(at, width):
        pieces = [keyed[pl.ds(start, PATCH), at : at + width] for start in starts]
        return jnp.concatenate(pieces, axis=0)

    return asked, keys, lambda at, width: keys(channels + at, width)


def lane_tiles(packed, rows):
    capacity, channels = rows.shape[1:]
    return [
        (
            packed.at[:, pl.ds(j * capacity, capacity), :],
            rows.at[:, :, pl.ds(j * LANES, LANES)],
        )
        for j in range(channels // LANES)
    ]


def first_kernel(
    ring_chips,
    late_rows,
    pattern,
    pattern_beyond,
    slot_of_row,
    kept_rows,
    gains,
    w_qkv,
    queries,
    queries_beyond,
    w_proj,
    tail,
    points,
    *refs,
):
    late, refs = refs[: len(late_rows)], refs[len(late_rows) :]
    *points_beyond, outgoing, keyed, attended, points_held, first_held, outgoing_held = refs[:-3]
    late_held, sems, late_sems = refs[-3:]
    rows, channels = points.shape
    devices, capacity, _ = outgoing_held.shape
    row_tiles = channels // LANES * capacity
    patches = rows // PATCH
    chosen = pattern.shape[0]
    me = lax.axis_index(GROUP)
    part = rows // len(points_beyond)
    late_part = late_held.shape[1]
    landing = started(
        [(piece.at[pl.ds(0, late_part), :], late_held.at[i]) for i, piece in enumerate(late)],
        late_sems,
    )
    copies = started(
        [(tail, outgoing.at[:, pl.ds(row_tiles, TAIL), :]), (points, points_held.at[:rows])]
        + [
            (piece.at[pl.ds(0, part), :], points_held.at[pl.ds(rows + i * part, part), :])
            for i, piece in enumerate(points_beyond)
        ],
        sems.at[0],
    )
    for copy in landing + copies[1:]:
        copy.wait()
    for i, first in enumerate(late_rows):
        keyed[first : first + late_part, :] = jnp.dot(
            layer_norm(late_held[i], gains[0:1, :]),
            w_qkv[:, channels:],
            preferred_element_type=F32,
        ).astype(BF16)
    blocks = ((pattern, queries, 0), (pattern_beyond, queries_beyond, ring_chips or 1))
    loaded = []
    for b, (picked, asking, own_slot) in enumerate(blocks):
        for p in range(patches):
            starts = [own_slot * rows + p * PATCH]
            for j in range(chosen):
                if ring_chips:
                    patch = picked[j, p]
                    owner, local = lax.div(patch, patches), lax.rem(patch, patches)
                    chip = lax.rem(lax.div(me, 2) - lax.div(owner, 2) + ring_chips, ring_chips)
                    slot = 2 * chip + jnp.where(lax.rem(me, 2) == lax.rem(owner, 2), 0, 1)
                    starts.append(pl.multiple_of((slot * patches + local) * PATCH, PATCH))
                else:
                    starts.append((2 * patches + (b * patches + p) * chosen + j) * PATCH)
            loaded.append(loads(asking, p, keyed, starts))
    for p, at, rows_done in attend(loaded, channels // HEADS):
        attended[p * PATCH : (p + 1) * PATCH, at : at + rows_done.shape[1]] = rows_done

    first_held[...] = mix(points_held[...], attended[...], w_proj)
    targets = devices // SEND_PARTS
    block_slots = capacity // 2
    leaving = []
    for i in range(SEND_PARTS):
        here = pl.ds(i * targets, targets)
        for b in range(2):
            mine = pl.ds(b * block_slots, block_slots)
            slots = slot_of_row[:, b * rows : (b + 1) * rows] - i * targets * block_slots
            send = one_hot_rows(slots, targets * block_slots)
            moved = jnp.dot(
                send, first_held[b * rows : (b + 1) * rows, :], preferred_element_type=F32
            )
            outgoing_held[here, mine, :] = moved.astype(BF16).reshape(
                targets, block_slots, channels
            )
        pairs = lane_tiles(outgoing.at[here], outgoing_held.at[here])
        leaving += started([(source, place) for place, source in pairs], sems.at[1 + i])
    for copy in copies[:1] + leaving:
        copy.wait()


def second_kernel(
    pattern,
    gains,
    incoming,
    w_qkv,
    w_proj,
    w_up,
    w_down,
    w_head,
    features,
    normals,
    kv,
    queries,
    attended,
    incoming_held,
    first_up_held,
    first_down_held,
    qkv_held,
    proj_held,
    up_held,
    down_held,
    gains_held,
    tail_held,
    head_held,
    sems,
):
    rows, channels = features.shape
    devices, capacity, _ = incoming_held.shape
    patches = rows // PATCH
    chosen = pattern.shape[0]
    tail = incoming.at[:, pl.ds(channels // LANES * capacity, TAIL), :]
    small = started(
        [(tail, tail_held), (gains, gains_held), (w_head, head_held)], sems.at[0]
    )
    landing = started(lane_tiles(incoming, incoming_held), sems.at[1])
    copies = started(
        [
            (w_up.at[0], first_up_held),
            (w_down.at[0], first_down_held),
            (w_qkv.at[1], qkv_held),
            (w_proj.at[1], proj_held),
            (w_up.at[1], up_held),
            (w_down.at[1], down_held),
        ],
        sems.at[2],
    )
    for copy in small:
        copy.wait()
    per_row = LANES // capacity
    digits = tail_held[...].astype(F32)
    codes = digits[:, 0:1, :] + DIGIT * digits[:, 1:2, :]
    pieces = []
    for at in range(0, devices, per_row):
        code = codes[at]
        for i in range(1, per_row):
            code = code + codes[at + i]
        pieces.append(code)
    places = jnp.concatenate(pieces, axis=1).astype(jnp.int32) - 1
    place = one_hot_rows(places, rows)
    sides = []
    for at in range(0, len(landing), 2):
        for copy in landing[at : at + 2]:
            copy.wait()
        moved = incoming_held[:, :, at * LANES : (at + 2) * LANES]
        moved = moved.reshape(devices * capacity, 2 * LANES)
        sides.append(jnp.dot(place, moved, preferred_element_type=F32).astype(BF16))
    first = jnp.concatenate(sides, axis=1)
    for copy in copies[:2]:
        copy.wait()
    second = feed(first, gains_held[1:2, :], first_up_held, first_down_held)
    for copy in copies[2:]:
        copy.wait()
    normed = layer_norm(second, gains_held[2:3, :])
    scale = (channels // HEADS) ** (-0.5)
    asked = jnp.dot(normed, qkv_held[:, :channels], preferred_element_type=F32).astype(BF16)
    queries[...] = (asked * BF16(scale)).astype(BF16)
    kv[...] = jnp.dot(normed, qkv_held[:, channels:], preferred_element_type=F32).astype(BF16)
    loaded = []
    for p in range(patches):
        starts = [pl.multiple_of(pattern[j, p] * PATCH, PATCH) for j in range(chosen)]
        loaded.append(loads(queries, p, kv, [p * PATCH] + starts))
    for p, at, rows_done in attend(loaded, channels // HEADS):
        attended[p * PATCH : (p + 1) * PATCH, at : at + rows_done.shape[1]] = rows_done
    mixed = mix(second, attended[...], proj_held)
    done = feed(mixed, gains_held[3:4, :], up_held, down_held)
    features[...] = done
    normals[...] = lax.dot_general(
        head_held[...], done, (((1,), (1,)), ((), ())), preferred_element_type=F32
    )


VMEM_SPEC = pl.BlockSpec(memory_space=pltpu.VMEM)
SMEM_SPEC = pl.BlockSpec(memory_space=pltpu.SMEM)
ANY_SPEC = pl.BlockSpec(memory_space=pl.ANY)


def shards(
    points,
    pattern_first,
    pattern_second,
    destination,
    norm_gains,
    w_qkv,
    w_proj,
    w_up,
    w_down,
    w_head,
):
    rows_here, channels = points.shape
    patches, chosen = pattern_first.shape
    devices = lax.axis_size("grp") * lax.axis_size("seq")
    capacity = 2 * rows_here // (2 * devices)
    pair_slots = 2 * capacity

    shards_in_group = lax.axis_size(GROUP)
    chips = shards_in_group // 2
    onward = [(i, (i + 2) % shards_in_group) for i in range(shards_in_group)]
    swap = [(i, i ^ 1) for i in range(shards_in_group)]
    across = [(i, (i + chips) % shards_in_group) for i in range(shards_in_group)]
    ring = shards_in_group * rows_here * 2 * channels * 2 <= RING_BYTES
    kept_rows = shards_in_group * rows_here if ring else 2 * patches * (1 + chosen) * PATCH
    part = rows_here // RING_PARTS

    destination = destination.reshape(1, rows_here)
    pattern_first = pattern_first.T
    part_rows = [part + TAIL] + [part] * (RING_PARTS - 1)
    column = pl.pallas_call(
        split_kernel,
        out_shape=[jax.ShapeDtypeStruct((rows, channels), BF16) for rows in part_rows],
        in_specs=[ANY_SPEC] * 3,
        out_specs=[VMEM_SPEC] * RING_PARTS,
        scratch_shapes=[
            pltpu.VMEM((1, rows_here), jnp.int32),
            pltpu.VMEM(pattern_first.shape, jnp.int32),
            pltpu.VMEM((TAIL, channels), F32),
            pltpu.SemaphoreType.DMA((2, RING_PARTS)),
        ],
        compiler_params=pltpu.CompilerParams(vmem_limit_bytes=SPLIT_BYTES),
        name="split",
    )(points, destination, pattern_first)

    weights = (w_proj, w_up, w_down)
    kv_shape = jax.ShapeDtypeStruct((kept_rows, 2 * channels), BF16)
    own_shape = jax.ShapeDtypeStruct((rows_here, channels), BF16)

    qkv_kept, proj_kept, gains_kept = pl.pallas_call(
        keep_kernel,
        out_shape=[
            *[jax.ShapeDtypeStruct(w.shape[1:], BF16) for w in (w_qkv, w_proj)],
            jax.ShapeDtypeStruct(norm_gains.shape, F32),
        ],
        in_specs=[ANY_SPEC] * 3,
        out_specs=[VMEM_SPEC] * 3,
        scratch_shapes=[pltpu.SemaphoreType.DMA((3,))],
        compiler_params=pltpu.CompilerParams(vmem_limit_bytes=PREPARE_BYTES),
        name="keep",
    )(w_qkv, w_proj, norm_gains)
    def index(beyond):
        return pl.pallas_call(
            functools.partial(index_kernel, capacity),
            out_shape=[
                jax.ShapeDtypeStruct((1, 2 * rows_here), jnp.int32),
                jax.ShapeDtypeStruct((devices, TAIL, LANES), BF16),
                jax.ShapeDtypeStruct(pattern_first.shape, jnp.int32),
            ],
            in_specs=[ANY_SPEC] * 2,
            out_specs=[VMEM_SPEC] * 3,
            scratch_shapes=[
                pltpu.VMEM((2, 1, rows_here), jnp.int32),
                pltpu.VMEM((TAIL, channels), BF16),
                pltpu.SemaphoreType.DMA((2,)),
            ],
            compiler_params=pltpu.CompilerParams(vmem_limit_bytes=PROJECT_BYTES),
            name="index",
        )(destination, beyond)

    def project(keyed, blocks, ask=False, rows=part):
        parts = [piece for _, _, block in blocks for piece in block]
        count = len(parts)
        first_rows = [
            slot * rows_here + first + i * rows
            for slot, first, block in blocks
            for i in range(len(block))
        ]
        new = keyed is None
        return pl.pallas_call(
            functools.partial(project_kernel, first_rows, new, ask),
            out_shape=[kv_shape] + [own_shape] * ask,
            in_specs=[ANY_SPEC] * count + [VMEM_SPEC] * (2 if new else 3),
            out_specs=[VMEM_SPEC] * (1 + ask),
            scratch_shapes=[
                pltpu.VMEM((count, rows, channels), BF16),
                pltpu.SemaphoreType.DMA((count,)),
            ],
            input_output_aliases={} if new else {count + 2: 0},
            cost_estimate=pl.CostEstimate(
                flops=4 * count * rows * channels**2,
                bytes_accessed=3 * count * rows * channels * 2 + 3 * channels**2 * 2,
                transcendentals=0,
            ),
            compiler_params=pltpu.CompilerParams(vmem_limit_bytes=PROJECT_BYTES),
            name="project_own" if new else "project",
        )(*parts, gains_kept, qkv_kept, *([] if new else [keyed]))

    if ring:
        beside = [lax.ppermute(rows, GROUP, swap) for rows in column]
        waiting = [(0, 0, column), (1, 0, beside)]
        for step in range(1, chips):
            column = [lax.ppermute(rows, GROUP, onward) for rows in column]
            if step == 1:
                column[0], gains_kept = lax.optimization_barrier((column[0], gains_kept))
                keyed, queries = project(None, waiting, ask=True)
                column[1], keyed = lax.optimization_barrier((column[1], keyed))
            else:
                for i, block in enumerate(waiting):
                    if block[0] == chips:
                        keyed, queries_beyond = project(keyed, [block], ask=True)
                    else:
                        (keyed,) = project(keyed, [block])
                    column[i], keyed = lax.optimization_barrier((column[i], keyed))
            if step == chips // 2:
                points_beyond = column
                slot_index, tail, pattern_beyond = index(column[0])
            if step == chips - 1:
                column[0], slot_index = lax.optimization_barrier((column[0], slot_index))
            beside = [lax.ppermute(rows, GROUP, swap) for rows in column]
            waiting = [(2 * step, 0, column), (2 * step + 1, 0, beside)]
        early = [(slot, 0, block[:-1]) for slot, _, block in waiting]
        (keyed,) = project(keyed, early)
        late_rows = [(slot + 1) * rows_here - part for slot, _, _ in waiting]
        late = [block[-1] for _, _, block in waiting]
    else:
        group = lax.all_gather(points, GROUP, axis=0, tiled=True)
        partner = lax.rem(lax.axis_index(GROUP) + chips, shards_in_group)
        points_beyond = [lax.dynamic_slice_in_dim(group, partner * rows_here, rows_here)]
        group = group.reshape(-1, PATCH, channels)
        slot_index, tail, pattern_beyond = index(lax.ppermute(column[0], GROUP, across))
        picked = [
            group[pattern.T].reshape(-1, channels) for pattern in (pattern_first, pattern_beyond)
        ]
        wide = picked[0].shape[0]
        keyed, queries = project(None, [(0, 0, column)], ask=True)
        keyed, queries_beyond = project(keyed, [(1, 0, points_beyond)], ask=True, rows=rows_here)
        (keyed,) = project(keyed, [(2, 0, [picked[0]])], rows=wide)
        (keyed,) = project(keyed, [(2 + chosen, 0, [picked[1]])], rows=wide)
        late_rows, late = [], []

    held_weights = [pltpu.VMEM(w.shape[1:], BF16) for w in weights]
    held_rows = pltpu.VMEM((rows_here, channels), BF16)
    held_slots = pltpu.VMEM((devices, pair_slots, channels), BF16)
    held_both = pltpu.VMEM((2 * rows_here, channels), BF16)
    pair_rows = channels // LANES * pair_slots + TAIL
    outgoing, _ = pl.pallas_call(
        functools.partial(first_kernel, chips if ring else 0, late_rows),
        out_shape=[jax.ShapeDtypeStruct((devices, pair_rows, LANES), BF16), kv_shape],
        in_specs=[SMEM_SPEC] * 2
        + [VMEM_SPEC] * 7
        + [ANY_SPEC] * (2 + len(late) + len(points_beyond)),
        out_specs=[ANY_SPEC, VMEM_SPEC],
        scratch_shapes=[
            held_both,
            held_both,
            held_both,
            held_slots,
            pltpu.VMEM((max(len(late), 1), part, channels), BF16),
            pltpu.SemaphoreType.DMA((1 + SEND_PARTS, 4)),
            pltpu.SemaphoreType.DMA((max(len(late), 1),)),
        ],
        input_output_aliases={3: 1},
        compiler_params=pltpu.CompilerParams(vmem_limit_bytes=FIRST_BYTES),
        name="block_first",
    )(
        pattern_first,
        pattern_beyond,
        slot_index,
        keyed,
        gains_kept,
        qkv_kept,
        queries,
        queries_beyond,
        proj_kept,
        tail,
        points,
        *late,
        *points_beyond,
    )
    incoming = lax.all_to_all(outgoing, ("grp", "seq"), split_axis=0, concat_axis=0, tiled=True)

    return pl.pallas_call(
        second_kernel,
        out_shape=(
            jax.ShapeDtypeStruct((rows_here, channels), BF16),
            jax.ShapeDtypeStruct((w_head.shape[0], rows_here), F32),
        ),
        in_specs=[SMEM_SPEC] + [ANY_SPEC] * 7,
        out_specs=(VMEM_SPEC, VMEM_SPEC),
        scratch_shapes=[
            pltpu.VMEM((rows_here, 2 * channels), BF16),
            held_rows,
            held_rows,
            held_slots,
            *held_weights[1:],
            pltpu.VMEM(w_qkv.shape[1:], BF16),
            *held_weights,
            pltpu.VMEM(norm_gains.shape, F32),
            pltpu.VMEM(tail.shape, BF16),
            pltpu.VMEM(w_head.shape, BF16),
            pltpu.SemaphoreType.DMA((3, 6)),
        ],
        compiler_params=pltpu.CompilerParams(vmem_limit_bytes=SECOND_BYTES),
        name="block_second",
    )(pattern_second.T, norm_gains, incoming, w_qkv, *weights, w_head)


def solution(mesh):
    groups, shards_in_group = mesh.devices.shape
    halves = Mesh(
        mesh.devices.reshape(groups, 2, shards_in_group // 2), ("grp",) + GROUP
    )
    everywhere = ("grp",) + GROUP
    placed = (
        P(everywhere, None),
        P(everywhere, None),
        P(everywhere, None),
        P(everywhere),
        P(),
        P(),
        P(),
        P(),
        P(),
        P(),
    )
    return jax.shard_map(
        shards,
        mesh=halves,
        in_specs=placed,
        out_specs=(P(everywhere, None), P(None, everywhere)),
        check_vma=False,
    )
```

```python
import functools

import jax
import jax.numpy as jnp
from jax import lax
from jax.experimental import pallas as pl
from jax.experimental.pallas import tpu as pltpu
from jax.sharding import Mesh, PartitionSpec as P

HEADS = 8
PATCH = 64
HEADS_TOGETHER = 4
GROUP = ("half", "seq")
RING_PARTS = 2
SEND_PARTS = 1
LANES = 128
TAIL = 8
DIGIT = 256
FIRST_BYTES = 28 * 1024 * 1024
SECOND_BYTES = 50 * 1024 * 1024
PROJECT_BYTES = 16 * 1024 * 1024
SPLIT_BYTES = 60 * 1024 * 1024
PREPARE_BYTES = 46 * 1024 * 1024
RING_BYTES = 16 * 1024 * 1024
F32 = jnp.float32
BF16 = jnp.bfloat16


def layer_norm(rows, gains):
    values = rows.astype(F32)
    average = jnp.mean(values, axis=-1, keepdims=True)
    spread = jnp.mean((values - average) ** 2, axis=-1, keepdims=True)
    return ((values - average) * lax.rsqrt(spread + 1e-05) * gains).astype(BF16)


def gelu(x):
    half = 0.5 * x
    return half + half * lax.erf(x * 0.5**0.5)


def head_masks(head_dim):
    lane = lax.broadcasted_iota(jnp.int32, (PATCH, HEADS_TOGETHER * head_dim), 1)
    return [
        jnp.where((lane >= h * head_dim) & (lane < (h + 1) * head_dim), 1.0, 0.0).astype(BF16)
        for h in range(HEADS_TOGETHER)
    ]


def attend(patches, head_dim):
    masks = head_masks(head_dim)
    width = HEADS_TOGETHER * head_dim
    heads_per_tile = LANES // head_dim
    lane = lax.broadcasted_iota(jnp.int32, (PATCH, LANES), 1)
    steps = [(p, g) for p in range(len(patches)) for g in range(HEADS // HEADS_TOGETHER)]

    def scores_of(step):
        p, g = step
        queries, keys, _ = patches[p]
        q = queries(g * width, width)
        stacked = jnp.concatenate([q * mask for mask in masks], axis=0)
        return lax.dot_general(
            stacked, keys(g * width, width), (((1,), (1,)), ((), ())), preferred_element_type=F32
        )

    scores = scores_of(steps[0])
    for i, (p, g) in enumerate(steps):
        later = scores_of(steps[i + 1]) if i + 1 < len(steps) else None
        grown = jnp.exp(scores - jnp.max(scores, axis=-1, keepdims=True))
        scale = 1.0 / jnp.sum(grown, axis=-1, keepdims=True)
        values = patches[p][2](g * width, width)
        mixed = jnp.dot(grown.astype(BF16), values, preferred_element_type=F32)
        tiles = []
        for t in range(width // LANES):
            tile = None
            for h in range(heads_per_tile):
                rows = slice((t * heads_per_tile + h) * PATCH, (t * heads_per_tile + h + 1) * PATCH)
                head = mixed[rows, t * LANES : (t + 1) * LANES] * scale[rows]
                tile = head if tile is None else jnp.where(lane < h * head_dim, tile, head)
            tiles.append(tile)
        yield p, g * width, jnp.concatenate(tiles, axis=1).astype(BF16)
        scores = later


def one_hot_rows(places, rows):
    row = lax.broadcasted_iota(jnp.int32, (rows, places.shape[1]), 0)
    return jnp.where(row == places, 1.0, 0.0).astype(BF16)


def started(pairs, sems):
    copies = [
        pltpu.make_async_copy(source, place, sems.at[at])
        for at, (source, place) in enumerate(pairs)
    ]
    for copy in copies:
        copy.start()
    return copies


def mix(rows, attended, w_proj):
    mixed = jnp.dot(attended, w_proj[...], preferred_element_type=F32)
    return (rows.astype(F32) + mixed).astype(BF16)


def feed(first, gain, w_up, w_down):
    hidden = layer_norm(first, gain)
    total = first.astype(F32)
    piece = 1024
    pieces = range(0, w_up.shape[1], piece)
    upper = jnp.dot(hidden, w_up[:, :piece], preferred_element_type=F32)
    for at in pieces:
        later = None
        if at + piece < w_up.shape[1]:
            later = jnp.dot(
                hidden, w_up[:, at + piece : at + 2 * piece], preferred_element_type=F32
            )
        act = gelu(upper).astype(BF16)
        total = total + jnp.dot(act, w_down[at : at + piece, :], preferred_element_type=F32)
        upper = later
    return total.astype(BF16)


def split_kernel(points, destination, pattern, *refs):
    *parts, destination_held, pattern_held, notes, sems = refs
    rows = points.shape[0] // len(parts)
    fetches = started([(destination, destination_held), (pattern, pattern_held)], sems.at[0])
    copies = started(
        [
            (points.at[pl.ds(i * rows, rows), :], part.at[pl.ds(0, rows), :])
            for i, part in enumerate(parts)
        ],
        sems.at[1],
    )
    for fetch in fetches:
        fetch.wait()
    chosen, patches = pattern.shape
    row = lax.broadcasted_iota(jnp.int32, notes.shape, 0)
    low = destination_held[...] & (DIGIT - 1)
    high = lax.shift_right_logical(destination_held[...], DIGIT.bit_length() - 1)
    values = jnp.where(row == chosen, low, jnp.where(row == chosen + 1, high, 0))
    notes[...] = values.astype(F32)
    notes[0:chosen, 0:patches] = pattern_held[...].astype(F32)
    parts[0][rows : rows + TAIL, :] = notes[...].astype(BF16)
    for copy in copies:
        copy.wait()


def keep_kernel(*refs):
    *refs, sems = refs
    count = len(refs) // 2
    for copy in started(
        [
            (source.at[0] if len(source.shape) == 3 else source, place)
            for source, place in zip(refs[:count], refs[count:])
        ],
        sems,
    ):
        copy.wait()


def index_kernel(capacity, destination, beyond, slots, tail, pattern, held, notes, sems):
    added = beyond.at[pl.ds(beyond.shape[0] - TAIL, TAIL), :]
    for fetch in started([(destination, held.at[0]), (added, notes)], sems):
        fetch.wait()
    chosen, patches = pattern.shape
    noted = notes[...].astype(F32)
    pattern[...] = noted[0:chosen, 0:patches].astype(jnp.int32)
    low, high = noted[chosen : chosen + 1, :], noted[chosen + 1 : chosen + 2, :]
    held[1] = (low + DIGIT * high).astype(jnp.int32)
    rows = held.shape[2]
    devices = tail.shape[0]
    in_half = lax.axis_size("seq")
    seq_bits = in_half.bit_length() - 1
    index = lax.axis_index(("grp", "seq"))
    offset = lax.rem(index, LANES // (2 * capacity)) * 2 * capacity
    before = lax.broadcasted_iota(jnp.int32, (rows, rows), 0)
    before = before < lax.broadcasted_iota(jnp.int32, (rows, rows), 1)
    before = jnp.where(before, 1.0, 0.0).astype(BF16)
    lines = jnp.zeros((devices * TAIL, LANES), F32)
    for b in range(2):
        target = lax.shift_right_logical(held[b], rows.bit_length() - 1)
        place = held[b] & (rows - 1)
        half = lax.shift_right_logical(target, seq_bits) & 1
        group = lax.shift_right_logical(target, seq_bits + 1)
        target = group * in_half + (target & (in_half - 1))
        target = jnp.where(half == lax.axis_index("half"), target, -1)
        mine = lax.broadcasted_iota(jnp.int32, (devices, rows), 0) == target
        mine = jnp.where(mine, 1.0, 0.0).astype(F32)
        earlier = jnp.dot(mine.astype(BF16), before, preferred_element_type=F32)
        rank = jnp.sum(mine * earlier, axis=0, keepdims=True).astype(jnp.int32)
        slots[:, b * rows : (b + 1) * rows] = jnp.where(target >= 0, target * capacity + rank, -1)
        rank = rank + b * capacity + offset
        by_lane = lax.broadcasted_iota(jnp.int32, (LANES, rows), 0) == rank
        by_lane = jnp.where(by_lane, 1.0, 0.0).astype(BF16)
        line = lax.broadcasted_iota(jnp.int32, (devices * TAIL, rows), 0)
        code = place + 1
        low = (code & (DIGIT - 1)).astype(F32)
        high = lax.shift_right_logical(code, DIGIT.bit_length() - 1).astype(F32)
        digit = line & (TAIL - 1)
        digits = jnp.where(digit == 0, low, jnp.where(digit == 1, high, 0.0))
        line = lax.shift_right_logical(line, TAIL.bit_length() - 1)
        digits = jnp.where(line == target, digits, 0.0)
        lines = lines + lax.dot_general(
            digits.astype(BF16), by_lane, (((1,), (1,)), ((), ())), preferred_element_type=F32
        )
    tail[...] = lines.reshape(devices, TAIL, LANES).astype(BF16)


def project_kernel(first_rows, new, ask, *refs):
    count = len(first_rows)
    parts, gains, w_qkv = refs[:count], refs[count], refs[count + 1]
    refs = refs[count + 2 if new else count + 3 :]
    whole, (held, sems) = refs[0], refs[-2:]
    channels = w_qkv.shape[0]
    rows = held.shape[1]
    copies = started(
        [(part.at[pl.ds(0, rows), :], held.at[i]) for i, part in enumerate(parts)], sems
    )
    for i, first in enumerate(first_rows):
        copies[i].wait()
        normed = layer_norm(held[i], gains[0:1, :])
        whole[first : first + rows, :] = jnp.dot(
            normed, w_qkv[:, channels:], preferred_element_type=F32
        ).astype(BF16)
        if ask and i * rows < refs[1].shape[0]:
            scale = BF16((channels // HEADS) ** (-0.5))
            query = jnp.dot(normed, w_qkv[:, :channels], preferred_element_type=F32).astype(BF16)
            refs[1][i * rows : (i + 1) * rows, :] = (query * scale).astype(BF16)


def loads(queries, p, keyed, starts):
    channels = queries.shape[1]

    def asked(at, width):
        return queries[p * PATCH : (p + 1) * PATCH, at : at + width]

    def keys(at, width):
        pieces = [keyed[pl.ds(start, PATCH), at : at + width] for start in starts]
        return jnp.concatenate(pieces, axis=0)

    return asked, keys, lambda at, width: keys(channels + at, width)


def lane_tiles(packed, rows):
    capacity, channels = rows.shape[1:]
    return [
        (
            packed.at[:, pl.ds(j * capacity, capacity), :],
            rows.at[:, :, pl.ds(j * LANES, LANES)],
        )
        for j in range(channels // LANES)
    ]


def first_kernel(
    ring_chips,
    late_rows,
    pattern,
    pattern_beyond,
    slot_of_row,
    kept_rows,
    gains,
    w_qkv,
    queries,
    queries_beyond,
    w_proj,
    tail,
    points,
    *refs,
):
    late, refs = refs[: len(late_rows)], refs[len(late_rows) :]
    *points_beyond, outgoing, keyed, attended, points_held, first_held, outgoing_held = refs[:-3]
    late_held, sems, late_sems = refs[-3:]
    rows, channels = points.shape
    devices, capacity, _ = outgoing_held.shape
    row_tiles = channels // LANES * capacity
    patches = rows // PATCH
    chosen = pattern.shape[0]
    me = lax.axis_index(GROUP)
    part = rows // len(points_beyond)
    late_part = late_held.shape[1]
    landing = started(
        [(piece.at[pl.ds(0, late_part), :], late_held.at[i]) for i, piece in enumerate(late)],
        late_sems,
    )
    copies = started(
        [(tail, outgoing.at[:, pl.ds(row_tiles, TAIL), :]), (points, points_held.at[:rows])]
        + [
            (piece.at[pl.ds(0, part), :], points_held.at[pl.ds(rows + i * part, part), :])
            for i, piece in enumerate(points_beyond)
        ],
        sems.at[0],
    )
    for copy in landing + copies[1:]:
        copy.wait()
    for i, first in enumerate(late_rows):
        keyed[first : first + late_part, :] = jnp.dot(
            layer_norm(late_held[i], gains[0:1, :]),
            w_qkv[:, channels:],
            preferred_element_type=F32,
        ).astype(BF16)
    blocks = ((pattern, queries, 0), (pattern_beyond, queries_beyond, ring_chips or 1))
    loaded = []
    for b, (picked, asking, own_slot) in enumerate(blocks):
        for p in range(patches):
            starts = [own_slot * rows + p * PATCH]
            for j in range(chosen):
                if ring_chips:
                    patch = picked[j, p]
                    owner, local = lax.div(patch, patches), lax.rem(patch, patches)
                    chip = lax.rem(lax.div(me, 2) - lax.div(owner, 2) + ring_chips, ring_chips)
                    slot = 2 * chip + jnp.where(lax.rem(me, 2) == lax.rem(owner, 2), 0, 1)
                    starts.append(pl.multiple_of((slot * patches + local) * PATCH, PATCH))
                else:
                    starts.append((2 * patches + (b * patches + p) * chosen + j) * PATCH)
            loaded.append(loads(asking, p, keyed, starts))
    for p, at, rows_done in attend(loaded, channels // HEADS):
        attended[p * PATCH : (p + 1) * PATCH, at : at + rows_done.shape[1]] = rows_done

    first_held[...] = mix(points_held[...], attended[...], w_proj)
    targets = devices // SEND_PARTS
    block_slots = capacity // 2
    leaving = []
    for i in range(SEND_PARTS):
        here = pl.ds(i * targets, targets)
        for b in range(2):
            mine = pl.ds(b * block_slots, block_slots)
            slots = slot_of_row[:, b * rows : (b + 1) * rows] - i * targets * block_slots
            send = one_hot_rows(slots, targets * block_slots)
            moved = jnp.dot(
                send, first_held[b * rows : (b + 1) * rows, :], preferred_element_type=F32
            )
            outgoing_held[here, mine, :] = moved.astype(BF16).reshape(
                targets, block_slots, channels
            )
        pairs = lane_tiles(outgoing.at[here], outgoing_held.at[here])
        leaving += started([(source, place) for place, source in pairs], sems.at[1 + i])
    for copy in copies[:1] + leaving:
        copy.wait()


def second_kernel(
    pattern,
    gains,
    incoming,
    w_qkv,
    w_proj,
    w_up,
    w_down,
    w_head,
    features,
    normals,
    kv,
    queries,
    attended,
    incoming_held,
    first_up_held,
    first_down_held,
    qkv_held,
    proj_held,
    up_held,
    down_held,
    gains_held,
    tail_held,
    head_held,
    sems,
):
    rows, channels = features.shape
    devices, capacity, _ = incoming_held.shape
    patches = rows // PATCH
    chosen = pattern.shape[0]
    tail = incoming.at[:, pl.ds(channels // LANES * capacity, TAIL), :]
    small = started(
        [(tail, tail_held), (gains, gains_held), (w_head, head_held)], sems.at[0]
    )
    landing = started(lane_tiles(incoming, incoming_held), sems.at[1])
    copies = started(
        [
            (w_up.at[0], first_up_held),
            (w_down.at[0], first_down_held),
            (w_qkv.at[1], qkv_held),
            (w_proj.at[1], proj_held),
            (w_up.at[1], up_held),
            (w_down.at[1], down_held),
        ],
        sems.at[2],
    )
    for copy in small:
        copy.wait()
    per_row = LANES // capacity
    digits = tail_held[...].astype(F32)
    codes = digits[:, 0:1, :] + DIGIT * digits[:, 1:2, :]
    pieces = []
    for at in range(0, devices, per_row):
        code = codes[at]
        for i in range(1, per_row):
            code = code + codes[at + i]
        pieces.append(code)
    places = jnp.concatenate(pieces, axis=1).astype(jnp.int32) - 1
    place = one_hot_rows(places, rows)
    for copy in landing:
        copy.wait()
    moved = incoming_held[...].reshape(devices * capacity, channels)
    first = jnp.dot(place, moved, preferred_element_type=F32).astype(BF16)
    for copy in copies[:2]:
        copy.wait()
    second = feed(first, gains_held[1:2, :], first_up_held, first_down_held)
    for copy in copies[2:]:
        copy.wait()
    normed = layer_norm(second, gains_held[2:3, :])
    scale = (channels // HEADS) ** (-0.5)
    asked = jnp.dot(normed, qkv_held[:, :channels], preferred_element_type=F32).astype(BF16)
    queries[...] = (asked * BF16(scale)).astype(BF16)
    kv[...] = jnp.dot(normed, qkv_held[:, channels:], preferred_element_type=F32).astype(BF16)
    loaded = []
    for p in range(patches):
        starts = [pl.multiple_of(pattern[j, p] * PATCH, PATCH) for j in range(chosen)]
        loaded.append(loads(queries, p, kv, [p * PATCH] + starts))
    for p, at, rows_done in attend(loaded, channels // HEADS):
        attended[p * PATCH : (p + 1) * PATCH, at : at + rows_done.shape[1]] = rows_done
    mixed = mix(second, attended[...], proj_held)
    done = feed(mixed, gains_held[3:4, :], up_held, down_held)
    features[...] = done
    normals[...] = lax.dot_general(
        head_held[...], done, (((1,), (1,)), ((), ())), preferred_element_type=F32
    )


VMEM_SPEC = pl.BlockSpec(memory_space=pltpu.VMEM)
SMEM_SPEC = pl.BlockSpec(memory_space=pltpu.SMEM)
ANY_SPEC = pl.BlockSpec(memory_space=pl.ANY)


def shards(
    points,
    pattern_first,
    pattern_second,
    destination,
    norm_gains,
    w_qkv,
    w_proj,
    w_up,
    w_down,
    w_head,
):
    rows_here, channels = points.shape
    patches, chosen = pattern_first.shape
    devices = lax.axis_size("grp") * lax.axis_size("seq")
    capacity = 2 * rows_here // (2 * devices)
    pair_slots = 2 * capacity

    shards_in_group = lax.axis_size(GROUP)
    chips = shards_in_group // 2
    onward = [(i, (i + 2) % shards_in_group) for i in range(shards_in_group)]
    swap = [(i, i ^ 1) for i in range(shards_in_group)]
    across = [(i, (i + chips) % shards_in_group) for i in range(shards_in_group)]
    ring = shards_in_group * rows_here * 2 * channels * 2 <= RING_BYTES
    kept_rows = shards_in_group * rows_here if ring else 2 * patches * (1 + chosen) * PATCH
    part = rows_here // RING_PARTS

    destination = destination.reshape(1, rows_here)
    pattern_first = pattern_first.T
    part_rows = [part + TAIL] + [part] * (RING_PARTS - 1)
    column = pl.pallas_call(
        split_kernel,
        out_shape=[jax.ShapeDtypeStruct((rows, channels), BF16) for rows in part_rows],
        in_specs=[ANY_SPEC] * 3,
        out_specs=[VMEM_SPEC] * RING_PARTS,
        scratch_shapes=[
            pltpu.VMEM((1, rows_here), jnp.int32),
            pltpu.VMEM(pattern_first.shape, jnp.int32),
            pltpu.VMEM((TAIL, channels), F32),
            pltpu.SemaphoreType.DMA((2, RING_PARTS)),
        ],
        compiler_params=pltpu.CompilerParams(vmem_limit_bytes=SPLIT_BYTES),
        name="split",
    )(points, destination, pattern_first)

    weights = (w_proj, w_up, w_down)
    kv_shape = jax.ShapeDtypeStruct((kept_rows, 2 * channels), BF16)
    own_shape = jax.ShapeDtypeStruct((rows_here, channels), BF16)

    qkv_kept, proj_kept, gains_kept = pl.pallas_call(
        keep_kernel,
        out_shape=[
            *[jax.ShapeDtypeStruct(w.shape[1:], BF16) for w in (w_qkv, w_proj)],
            jax.ShapeDtypeStruct(norm_gains.shape, F32),
        ],
        in_specs=[ANY_SPEC] * 3,
        out_specs=[VMEM_SPEC] * 3,
        scratch_shapes=[pltpu.SemaphoreType.DMA((3,))],
        compiler_params=pltpu.CompilerParams(vmem_limit_bytes=PREPARE_BYTES),
        name="keep",
    )(w_qkv, w_proj, norm_gains)
    def index(beyond):
        return pl.pallas_call(
            functools.partial(index_kernel, capacity),
            out_shape=[
                jax.ShapeDtypeStruct((1, 2 * rows_here), jnp.int32),
                jax.ShapeDtypeStruct((devices, TAIL, LANES), BF16),
                jax.ShapeDtypeStruct(pattern_first.shape, jnp.int32),
            ],
            in_specs=[ANY_SPEC] * 2,
            out_specs=[VMEM_SPEC] * 3,
            scratch_shapes=[
                pltpu.VMEM((2, 1, rows_here), jnp.int32),
                pltpu.VMEM((TAIL, channels), BF16),
                pltpu.SemaphoreType.DMA((2,)),
            ],
            compiler_params=pltpu.CompilerParams(vmem_limit_bytes=PROJECT_BYTES),
            name="index",
        )(destination, beyond)

    def project(keyed, blocks, ask=False, rows=part):
        parts = [piece for _, _, block in blocks for piece in block]
        count = len(parts)
        first_rows = [
            slot * rows_here + first + i * rows
            for slot, first, block in blocks
            for i in range(len(block))
        ]
        new = keyed is None
        return pl.pallas_call(
            functools.partial(project_kernel, first_rows, new, ask),
            out_shape=[kv_shape] + [own_shape] * ask,
            in_specs=[ANY_SPEC] * count + [VMEM_SPEC] * (2 if new else 3),
            out_specs=[VMEM_SPEC] * (1 + ask),
            scratch_shapes=[
                pltpu.VMEM((count, rows, channels), BF16),
                pltpu.SemaphoreType.DMA((count,)),
            ],
            input_output_aliases={} if new else {count + 2: 0},
            cost_estimate=pl.CostEstimate(
                flops=4 * count * rows * channels**2,
                bytes_accessed=3 * count * rows * channels * 2 + 3 * channels**2 * 2,
                transcendentals=0,
            ),
            compiler_params=pltpu.CompilerParams(vmem_limit_bytes=PROJECT_BYTES),
            name="project_own" if new else "project",
        )(*parts, gains_kept, qkv_kept, *([] if new else [keyed]))

    if ring:
        beside = [lax.ppermute(rows, GROUP, swap) for rows in column]
        waiting = [(0, 0, column), (1, 0, beside)]
        for step in range(1, chips):
            column = [lax.ppermute(rows, GROUP, onward) for rows in column]
            if step == 1:
                column[0], gains_kept = lax.optimization_barrier((column[0], gains_kept))
                keyed, queries = project(None, waiting, ask=True)
                column[1], keyed = lax.optimization_barrier((column[1], keyed))
            else:
                for i, block in enumerate(waiting):
                    if block[0] == chips:
                        keyed, queries_beyond = project(keyed, [block], ask=True)
                    else:
                        (keyed,) = project(keyed, [block])
                    column[i], keyed = lax.optimization_barrier((column[i], keyed))
            if step == chips // 2:
                points_beyond = column
                slot_index, tail, pattern_beyond = index(column[0])
            if step == chips - 1:
                column[0], slot_index = lax.optimization_barrier((column[0], slot_index))
            beside = [lax.ppermute(rows, GROUP, swap) for rows in column]
            waiting = [(2 * step, 0, column), (2 * step + 1, 0, beside)]
        early = [(slot, 0, block[:-1]) for slot, _, block in waiting]
        (keyed,) = project(keyed, early)
        late_rows = [(slot + 1) * rows_here - part for slot, _, _ in waiting]
        late = [block[-1] for _, _, block in waiting]
    else:
        group = lax.all_gather(points, GROUP, axis=0, tiled=True)
        partner = lax.rem(lax.axis_index(GROUP) + chips, shards_in_group)
        points_beyond = [lax.dynamic_slice_in_dim(group, partner * rows_here, rows_here)]
        group = group.reshape(-1, PATCH, channels)
        slot_index, tail, pattern_beyond = index(lax.ppermute(column[0], GROUP, across))
        picked = [
            group[pattern.T].reshape(-1, channels) for pattern in (pattern_first, pattern_beyond)
        ]
        wide = picked[0].shape[0]
        keyed, queries = project(None, [(0, 0, column)], ask=True)
        keyed, queries_beyond = project(keyed, [(1, 0, points_beyond)], ask=True, rows=rows_here)
        (keyed,) = project(keyed, [(2, 0, [picked[0]])], rows=wide)
        (keyed,) = project(keyed, [(2 + chosen, 0, [picked[1]])], rows=wide)
        late_rows, late = [], []

    held_weights = [pltpu.VMEM(w.shape[1:], BF16) for w in weights]
    held_rows = pltpu.VMEM((rows_here, channels), BF16)
    held_slots = pltpu.VMEM((devices, pair_slots, channels), BF16)
    held_both = pltpu.VMEM((2 * rows_here, channels), BF16)
    pair_rows = channels // LANES * pair_slots + TAIL
    outgoing, _ = pl.pallas_call(
        functools.partial(first_kernel, chips if ring else 0, late_rows),
        out_shape=[jax.ShapeDtypeStruct((devices, pair_rows, LANES), BF16), kv_shape],
        in_specs=[SMEM_SPEC] * 2
        + [VMEM_SPEC] * 7
        + [ANY_SPEC] * (2 + len(late) + len(points_beyond)),
        out_specs=[ANY_SPEC, VMEM_SPEC],
        scratch_shapes=[
            held_both,
            held_both,
            held_both,
            held_slots,
            pltpu.VMEM((max(len(late), 1), part, channels), BF16),
            pltpu.SemaphoreType.DMA((1 + SEND_PARTS, 4)),
            pltpu.SemaphoreType.DMA((max(len(late), 1),)),
        ],
        input_output_aliases={3: 1},
        compiler_params=pltpu.CompilerParams(vmem_limit_bytes=FIRST_BYTES),
        name="block_first",
    )(
        pattern_first,
        pattern_beyond,
        slot_index,
        keyed,
        gains_kept,
        qkv_kept,
        queries,
        queries_beyond,
        proj_kept,
        tail,
        points,
        *late,
        *points_beyond,
    )
    incoming = lax.all_to_all(outgoing, ("grp", "seq"), split_axis=0, concat_axis=0, tiled=True)

    return pl.pallas_call(
        second_kernel,
        out_shape=(
            jax.ShapeDtypeStruct((rows_here, channels), BF16),
            jax.ShapeDtypeStruct((w_head.shape[0], rows_here), F32),
        ),
        in_specs=[SMEM_SPEC] + [ANY_SPEC] * 7,
        out_specs=(VMEM_SPEC, VMEM_SPEC),
        scratch_shapes=[
            pltpu.VMEM((rows_here, 2 * channels), BF16),
            held_rows,
            held_rows,
            held_slots,
            *held_weights[1:],
            pltpu.VMEM(w_qkv.shape[1:], BF16),
            *held_weights,
            pltpu.VMEM(norm_gains.shape, F32),
            pltpu.VMEM(tail.shape, BF16),
            pltpu.VMEM(w_head.shape, BF16),
            pltpu.SemaphoreType.DMA((3, 6)),
        ],
        compiler_params=pltpu.CompilerParams(vmem_limit_bytes=SECOND_BYTES),
        name="block_second",
    )(pattern_second.T, norm_gains, incoming, w_qkv, *weights, w_head)


def solution(mesh):
    groups, shards_in_group = mesh.devices.shape
    halves = Mesh(
        mesh.devices.reshape(groups, 2, shards_in_group // 2), ("grp",) + GROUP
    )
    everywhere = ("grp",) + GROUP
    placed = (
        P(everywhere, None),
        P(everywhere, None),
        P(everywhere, None),
        P(everywhere),
        P(),
        P(),
        P(),
        P(),
        P(),
        P(),
    )
    return jax.shard_map(
        shards,
        mesh=halves,
        in_specs=placed,
        out_specs=(P(everywhere, None), P(None, everywhere)),
        check_vma=False,
    )
```

```python
import functools

import jax
import jax.numpy as jnp
from jax import lax
from jax.experimental import pallas as pl
from jax.experimental.pallas import tpu as pltpu
from jax.sharding import Mesh, PartitionSpec as P

HEADS = 8
PATCH = 64
HEADS_TOGETHER = 4
GROUP = ("half", "seq")
RING_PARTS = 2
SEND_PARTS = 1
LANES = 128
TAIL = 8
DIGIT = 256
FIRST_BYTES = 28 * 1024 * 1024
SECOND_BYTES = 50 * 1024 * 1024
PROJECT_BYTES = 16 * 1024 * 1024
SPLIT_BYTES = 60 * 1024 * 1024
PREPARE_BYTES = 46 * 1024 * 1024
RING_BYTES = 16 * 1024 * 1024
F32 = jnp.float32
BF16 = jnp.bfloat16


def layer_norm(rows, gains):
    values = rows.astype(F32)
    average = jnp.mean(values, axis=-1, keepdims=True)
    spread = jnp.mean((values - average) ** 2, axis=-1, keepdims=True)
    return ((values - average) * lax.rsqrt(spread + 1e-05) * gains).astype(BF16)


def gelu(x):
    half = 0.5 * x
    return half + half * lax.erf(x * 0.5**0.5)


def head_masks(head_dim):
    lane = lax.broadcasted_iota(jnp.int32, (PATCH, HEADS_TOGETHER * head_dim), 1)
    return [
        jnp.where((lane >= h * head_dim) & (lane < (h + 1) * head_dim), 1.0, 0.0).astype(BF16)
        for h in range(HEADS_TOGETHER)
    ]


def attend(patches, head_dim):
    masks = head_masks(head_dim)
    width = HEADS_TOGETHER * head_dim
    heads_per_tile = LANES // head_dim
    lane = lax.broadcasted_iota(jnp.int32, (PATCH, LANES), 1)
    steps = [(p, g) for p in range(len(patches)) for g in range(HEADS // HEADS_TOGETHER)]

    def scores_of(step):
        p, g = step
        queries, keys, _ = patches[p]
        q = queries(g * width, width)
        stacked = jnp.concatenate([q * mask for mask in masks], axis=0)
        return lax.dot_general(
            stacked, keys(g * width, width), (((1,), (1,)), ((), ())), preferred_element_type=F32
        )

    scores = scores_of(steps[0])
    for i, (p, g) in enumerate(steps):
        later = scores_of(steps[i + 1]) if i + 1 < len(steps) else None
        grown = jnp.exp(scores - jnp.max(scores, axis=-1, keepdims=True))
        scale = 1.0 / jnp.sum(grown, axis=-1, keepdims=True)
        values = patches[p][2](g * width, width)
        mixed = jnp.dot(grown.astype(BF16), values, preferred_element_type=F32)
        tiles = []
        for t in range(width // LANES):
            tile = None
            for h in range(heads_per_tile):
                rows = slice((t * heads_per_tile + h) * PATCH, (t * heads_per_tile + h + 1) * PATCH)
                head = mixed[rows, t * LANES : (t + 1) * LANES] * scale[rows]
                tile = head if tile is None else jnp.where(lane < h * head_dim, tile, head)
            tiles.append(tile)
        yield p, g * width, jnp.concatenate(tiles, axis=1).astype(BF16)
        scores = later


def one_hot_rows(places, rows):
    row = lax.broadcasted_iota(jnp.int32, (rows, places.shape[1]), 0)
    return jnp.where(row == places, 1.0, 0.0).astype(BF16)


def started(pairs, sems):
    copies = [
        pltpu.make_async_copy(source, place, sems.at[at])
        for at, (source, place) in enumerate(pairs)
    ]
    for copy in copies:
        copy.start()
    return copies


def mix(rows, attended, w_proj):
    mixed = jnp.dot(attended, w_proj[...], preferred_element_type=F32)
    return (rows.astype(F32) + mixed).astype(BF16)


def feed(first, gain, w_up, w_down):
    hidden = layer_norm(first, gain)
    total = first.astype(F32)
    piece = 1024
    pieces = range(0, w_up.shape[1], piece)
    upper = jnp.dot(hidden, w_up[:, :piece], preferred_element_type=F32)
    for at in pieces:
        later = None
        if at + piece < w_up.shape[1]:
            later = jnp.dot(
                hidden, w_up[:, at + piece : at + 2 * piece], preferred_element_type=F32
            )
        act = gelu(upper).astype(BF16)
        total = total + jnp.dot(act, w_down[at : at + piece, :], preferred_element_type=F32)
        upper = later
    return total.astype(BF16)


def split_kernel(points, destination, pattern, *refs):
    *parts, held, destination_held, pattern_held, notes, sems = refs
    rows = points.shape[0] // len(parts)
    fetches = started([(destination, destination_held), (pattern, pattern_held)], sems.at[0])
    copies = started(
        [
            (points.at[pl.ds(i * rows, rows), :], held.at[i, pl.ds(0, rows), :])
            for i in range(len(parts))
        ],
        sems.at[1],
    )
    for fetch in fetches:
        fetch.wait()
    chosen, patches = pattern.shape
    row = lax.broadcasted_iota(jnp.int32, notes.shape, 0)
    low = destination_held[...] & (DIGIT - 1)
    high = lax.shift_right_logical(destination_held[...], DIGIT.bit_length() - 1)
    values = jnp.where(row == chosen, low, jnp.where(row == chosen + 1, high, 0))
    notes[...] = values.astype(F32)
    notes[0:chosen, 0:patches] = pattern_held[...].astype(F32)
    held[0, rows : rows + TAIL, :] = notes[...].astype(BF16)
    leaving = []
    for i, part in enumerate(parts):
        copies[i].wait()
        leaving += started([(held.at[i, pl.ds(0, part.shape[0]), :], part)], sems.at[2 + i])
    for copy in leaving:
        copy.wait()


def keep_kernel(*refs):
    *refs, sems = refs
    count = len(refs) // 2
    for copy in started(
        [
            (source.at[0] if len(source.shape) == 3 else source, place)
            for source, place in zip(refs[:count], refs[count:])
        ],
        sems,
    ):
        copy.wait()


def index_kernel(capacity, destination, beyond, slots, tail, pattern, held, notes, sems):
    added = beyond.at[pl.ds(beyond.shape[0] - TAIL, TAIL), :]
    for fetch in started([(destination, held.at[0]), (added, notes)], sems):
        fetch.wait()
    chosen, patches = pattern.shape
    noted = notes[...].astype(F32)
    pattern[...] = noted[0:chosen, 0:patches].astype(jnp.int32)
    low, high = noted[chosen : chosen + 1, :], noted[chosen + 1 : chosen + 2, :]
    held[1] = (low + DIGIT * high).astype(jnp.int32)
    rows = held.shape[2]
    devices = tail.shape[0]
    in_half = lax.axis_size("seq")
    seq_bits = in_half.bit_length() - 1
    index = lax.axis_index(("grp", "seq"))
    offset = lax.rem(index, LANES // (2 * capacity)) * 2 * capacity
    before = lax.broadcasted_iota(jnp.int32, (rows, rows), 0)
    before = before < lax.broadcasted_iota(jnp.int32, (rows, rows), 1)
    before = jnp.where(before, 1.0, 0.0).astype(BF16)
    lines = jnp.zeros((devices * TAIL, LANES), F32)
    for b in range(2):
        target = lax.shift_right_logical(held[b], rows.bit_length() - 1)
        place = held[b] & (rows - 1)
        half = lax.shift_right_logical(target, seq_bits) & 1
        group = lax.shift_right_logical(target, seq_bits + 1)
        target = group * in_half + (target & (in_half - 1))
        target = jnp.where(half == lax.axis_index("half"), target, -1)
        mine = lax.broadcasted_iota(jnp.int32, (devices, rows), 0) == target
        mine = jnp.where(mine, 1.0, 0.0).astype(F32)
        earlier = jnp.dot(mine.astype(BF16), before, preferred_element_type=F32)
        rank = jnp.sum(mine * earlier, axis=0, keepdims=True).astype(jnp.int32)
        slots[:, b * rows : (b + 1) * rows] = jnp.where(target >= 0, target * capacity + rank, -1)
        rank = rank + b * capacity + offset
        by_lane = lax.broadcasted_iota(jnp.int32, (LANES, rows), 0) == rank
        by_lane = jnp.where(by_lane, 1.0, 0.0).astype(BF16)
        line = lax.broadcasted_iota(jnp.int32, (devices * TAIL, rows), 0)
        code = place + 1
        low = (code & (DIGIT - 1)).astype(F32)
        high = lax.shift_right_logical(code, DIGIT.bit_length() - 1).astype(F32)
        digit = line & (TAIL - 1)
        digits = jnp.where(digit == 0, low, jnp.where(digit == 1, high, 0.0))
        line = lax.shift_right_logical(line, TAIL.bit_length() - 1)
        digits = jnp.where(line == target, digits, 0.0)
        lines = lines + lax.dot_general(
            digits.astype(BF16), by_lane, (((1,), (1,)), ((), ())), preferred_element_type=F32
        )
    tail[...] = lines.reshape(devices, TAIL, LANES).astype(BF16)


def project_kernel(first_rows, new, ask, *refs):
    count = len(first_rows)
    parts, gains, w_qkv = refs[:count], refs[count], refs[count + 1]
    refs = refs[count + 2 if new else count + 3 :]
    whole, (held, sems) = refs[0], refs[-2:]
    channels = w_qkv.shape[0]
    rows = held.shape[1]
    copies = started(
        [(part.at[pl.ds(0, rows), :], held.at[i]) for i, part in enumerate(parts)], sems
    )
    for i, first in enumerate(first_rows):
        copies[i].wait()
        normed = layer_norm(held[i], gains[0:1, :])
        whole[first : first + rows, :] = jnp.dot(
            normed, w_qkv[:, channels:], preferred_element_type=F32
        ).astype(BF16)
        if ask and i * rows < refs[1].shape[0]:
            scale = BF16((channels // HEADS) ** (-0.5))
            query = jnp.dot(normed, w_qkv[:, :channels], preferred_element_type=F32).astype(BF16)
            refs[1][i * rows : (i + 1) * rows, :] = (query * scale).astype(BF16)


def loads(queries, p, keyed, starts):
    channels = queries.shape[1]

    def asked(at, width):
        return queries[p * PATCH : (p + 1) * PATCH, at : at + width]

    def keys(at, width):
        pieces = [keyed[pl.ds(start, PATCH), at : at + width] for start in starts]
        return jnp.concatenate(pieces, axis=0)

    return asked, keys, lambda at, width: keys(channels + at, width)


def lane_tiles(packed, rows):
    capacity, channels = rows.shape[1:]
    return [
        (
            packed.at[:, pl.ds(j * capacity, capacity), :],
            rows.at[:, :, pl.ds(j * LANES, LANES)],
        )
        for j in range(channels // LANES)
    ]


def first_kernel(
    ring_chips,
    late_rows,
    pattern,
    pattern_beyond,
    slot_of_row,
    kept_rows,
    gains,
    w_qkv,
    queries,
    queries_beyond,
    w_proj,
    tail,
    points,
    *refs,
):
    late, refs = refs[: len(late_rows)], refs[len(late_rows) :]
    *points_beyond, outgoing, keyed, attended, points_held, first_held, outgoing_held = refs[:-3]
    late_held, sems, late_sems = refs[-3:]
    rows, channels = points.shape
    devices, capacity, _ = outgoing_held.shape
    row_tiles = channels // LANES * capacity
    patches = rows // PATCH
    chosen = pattern.shape[0]
    me = lax.axis_index(GROUP)
    part = rows // len(points_beyond)
    late_part = late_held.shape[1]
    landing = started(
        [(piece.at[pl.ds(0, late_part), :], late_held.at[i]) for i, piece in enumerate(late)],
        late_sems,
    )
    copies = started(
        [(tail, outgoing.at[:, pl.ds(row_tiles, TAIL), :]), (points, points_held.at[:rows])]
        + [
            (piece.at[pl.ds(0, part), :], points_held.at[pl.ds(rows + i * part, part), :])
            for i, piece in enumerate(points_beyond)
        ],
        sems.at[0],
    )
    for copy in landing + copies[1:]:
        copy.wait()
    for i, first in enumerate(late_rows):
        keyed[first : first + late_part, :] = jnp.dot(
            layer_norm(late_held[i], gains[0:1, :]),
            w_qkv[:, channels:],
            preferred_element_type=F32,
        ).astype(BF16)
    blocks = ((pattern, queries, 0), (pattern_beyond, queries_beyond, ring_chips or 1))
    loaded = []
    for b, (picked, asking, own_slot) in enumerate(blocks):
        for p in range(patches):
            starts = [own_slot * rows + p * PATCH]
            for j in range(chosen):
                if ring_chips:
                    patch = picked[j, p]
                    owner, local = lax.div(patch, patches), lax.rem(patch, patches)
                    chip = lax.rem(lax.div(me, 2) - lax.div(owner, 2) + ring_chips, ring_chips)
                    slot = 2 * chip + jnp.where(lax.rem(me, 2) == lax.rem(owner, 2), 0, 1)
                    starts.append(pl.multiple_of((slot * patches + local) * PATCH, PATCH))
                else:
                    starts.append((2 * patches + (b * patches + p) * chosen + j) * PATCH)
            loaded.append(loads(asking, p, keyed, starts))
    for p, at, rows_done in attend(loaded, channels // HEADS):
        attended[p * PATCH : (p + 1) * PATCH, at : at + rows_done.shape[1]] = rows_done

    first_held[...] = mix(points_held[...], attended[...], w_proj)
    targets = devices // SEND_PARTS
    block_slots = capacity // 2
    leaving = []
    for i in range(SEND_PARTS):
        here = pl.ds(i * targets, targets)
        for b in range(2):
            mine = pl.ds(b * block_slots, block_slots)
            slots = slot_of_row[:, b * rows : (b + 1) * rows] - i * targets * block_slots
            send = one_hot_rows(slots, targets * block_slots)
            moved = jnp.dot(
                send, first_held[b * rows : (b + 1) * rows, :], preferred_element_type=F32
            )
            outgoing_held[here, mine, :] = moved.astype(BF16).reshape(
                targets, block_slots, channels
            )
        pairs = lane_tiles(outgoing.at[here], outgoing_held.at[here])
        leaving += started([(source, place) for place, source in pairs], sems.at[1 + i])
    for copy in copies[:1] + leaving:
        copy.wait()


def second_kernel(
    pattern,
    gains,
    incoming,
    w_qkv,
    w_proj,
    w_up,
    w_down,
    w_head,
    features,
    normals,
    kv,
    queries,
    attended,
    incoming_held,
    first_up_held,
    first_down_held,
    qkv_held,
    proj_held,
    up_held,
    down_held,
    gains_held,
    tail_held,
    head_held,
    sems,
):
    rows, channels = features.shape
    devices, capacity, _ = incoming_held.shape
    patches = rows // PATCH
    chosen = pattern.shape[0]
    tail = incoming.at[:, pl.ds(channels // LANES * capacity, TAIL), :]
    small = started(
        [(tail, tail_held), (gains, gains_held), (w_head, head_held)], sems.at[0]
    )
    landing = started(lane_tiles(incoming, incoming_held), sems.at[1])
    copies = started(
        [
            (w_up.at[0], first_up_held),
            (w_down.at[0], first_down_held),
            (w_qkv.at[1], qkv_held),
            (w_proj.at[1], proj_held),
            (w_up.at[1], up_held),
            (w_down.at[1], down_held),
        ],
        sems.at[2],
    )
    for copy in small:
        copy.wait()
    per_row = LANES // capacity
    digits = tail_held[...].astype(F32)
    codes = digits[:, 0:1, :] + DIGIT * digits[:, 1:2, :]
    pieces = []
    for at in range(0, devices, per_row):
        code = codes[at]
        for i in range(1, per_row):
            code = code + codes[at + i]
        pieces.append(code)
    places = jnp.concatenate(pieces, axis=1).astype(jnp.int32) - 1
    place = one_hot_rows(places, rows)
    for copy in landing:
        copy.wait()
    moved = incoming_held[...].reshape(devices * capacity, channels)
    first = jnp.dot(place, moved, preferred_element_type=F32).astype(BF16)
    for copy in copies[:2]:
        copy.wait()
    second = feed(first, gains_held[1:2, :], first_up_held, first_down_held)
    for copy in copies[2:]:
        copy.wait()
    normed = layer_norm(second, gains_held[2:3, :])
    scale = (channels // HEADS) ** (-0.5)
    asked = jnp.dot(normed, qkv_held[:, :channels], preferred_element_type=F32).astype(BF16)
    queries[...] = (asked * BF16(scale)).astype(BF16)
    kv[...] = jnp.dot(normed, qkv_held[:, channels:], preferred_element_type=F32).astype(BF16)
    loaded = []
    for p in range(patches):
        starts = [pl.multiple_of(pattern[j, p] * PATCH, PATCH) for j in range(chosen)]
        loaded.append(loads(queries, p, kv, [p * PATCH] + starts))
    for p, at, rows_done in attend(loaded, channels // HEADS):
        attended[p * PATCH : (p + 1) * PATCH, at : at + rows_done.shape[1]] = rows_done
    mixed = mix(second, attended[...], proj_held)
    done = feed(mixed, gains_held[3:4, :], up_held, down_held)
    features[...] = done
    normals[...] = lax.dot_general(
        head_held[...], done, (((1,), (1,)), ((), ())), preferred_element_type=F32
    )


VMEM_SPEC = pl.BlockSpec(memory_space=pltpu.VMEM)
SMEM_SPEC = pl.BlockSpec(memory_space=pltpu.SMEM)
ANY_SPEC = pl.BlockSpec(memory_space=pl.ANY)


def shards(
    points,
    pattern_first,
    pattern_second,
    destination,
    norm_gains,
    w_qkv,
    w_proj,
    w_up,
    w_down,
    w_head,
):
    rows_here, channels = points.shape
    patches, chosen = pattern_first.shape
    devices = lax.axis_size("grp") * lax.axis_size("seq")
    capacity = 2 * rows_here // (2 * devices)
    pair_slots = 2 * capacity

    shards_in_group = lax.axis_size(GROUP)
    chips = shards_in_group // 2
    onward = [(i, (i + 2) % shards_in_group) for i in range(shards_in_group)]
    swap = [(i, i ^ 1) for i in range(shards_in_group)]
    across = [(i, (i + chips) % shards_in_group) for i in range(shards_in_group)]
    ring = shards_in_group * rows_here * 2 * channels * 2 <= RING_BYTES
    kept_rows = shards_in_group * rows_here if ring else 2 * patches * (1 + chosen) * PATCH
    part = rows_here // RING_PARTS

    destination = destination.reshape(1, rows_here)
    pattern_first = pattern_first.T
    part_rows = [part + TAIL] + [part] * (RING_PARTS - 1)
    column = pl.pallas_call(
        split_kernel,
        out_shape=[jax.ShapeDtypeStruct((rows, channels), BF16) for rows in part_rows],
        in_specs=[ANY_SPEC] * 3,
        out_specs=[ANY_SPEC] * RING_PARTS,
        scratch_shapes=[
            pltpu.VMEM((RING_PARTS, part + TAIL, channels), BF16),
            pltpu.VMEM((1, rows_here), jnp.int32),
            pltpu.VMEM(pattern_first.shape, jnp.int32),
            pltpu.VMEM((TAIL, channels), F32),
            pltpu.SemaphoreType.DMA((2 + RING_PARTS, 2)),
        ],
        compiler_params=pltpu.CompilerParams(vmem_limit_bytes=SPLIT_BYTES),
        name="split",
    )(points, destination, pattern_first)

    weights = (w_proj, w_up, w_down)
    kv_shape = jax.ShapeDtypeStruct((kept_rows, 2 * channels), BF16)
    own_shape = jax.ShapeDtypeStruct((rows_here, channels), BF16)

    qkv_kept, proj_kept, gains_kept = pl.pallas_call(
        keep_kernel,
        out_shape=[
            *[jax.ShapeDtypeStruct(w.shape[1:], BF16) for w in (w_qkv, w_proj)],
            jax.ShapeDtypeStruct(norm_gains.shape, F32),
        ],
        in_specs=[ANY_SPEC] * 3,
        out_specs=[VMEM_SPEC] * 3,
        scratch_shapes=[pltpu.SemaphoreType.DMA((3,))],
        compiler_params=pltpu.CompilerParams(vmem_limit_bytes=PREPARE_BYTES),
        name="keep",
    )(w_qkv, w_proj, norm_gains)
    def index(beyond):
        return pl.pallas_call(
            functools.partial(index_kernel, capacity),
            out_shape=[
                jax.ShapeDtypeStruct((1, 2 * rows_here), jnp.int32),
                jax.ShapeDtypeStruct((devices, TAIL, LANES), BF16),
                jax.ShapeDtypeStruct(pattern_first.shape, jnp.int32),
            ],
            in_specs=[ANY_SPEC] * 2,
            out_specs=[VMEM_SPEC] * 3,
            scratch_shapes=[
                pltpu.VMEM((2, 1, rows_here), jnp.int32),
                pltpu.VMEM((TAIL, channels), BF16),
                pltpu.SemaphoreType.DMA((2,)),
            ],
            compiler_params=pltpu.CompilerParams(vmem_limit_bytes=PROJECT_BYTES),
            name="index",
        )(destination, beyond)

    def project(keyed, blocks, ask=False, rows=part):
        parts = [piece for _, _, block in blocks for piece in block]
        count = len(parts)
        first_rows = [
            slot * rows_here + first + i * rows
            for slot, first, block in blocks
            for i in range(len(block))
        ]
        new = keyed is None
        return pl.pallas_call(
            functools.partial(project_kernel, first_rows, new, ask),
            out_shape=[kv_shape] + [own_shape] * ask,
            in_specs=[ANY_SPEC] * count + [VMEM_SPEC] * (2 if new else 3),
            out_specs=[VMEM_SPEC] * (1 + ask),
            scratch_shapes=[
                pltpu.VMEM((count, rows, channels), BF16),
                pltpu.SemaphoreType.DMA((count,)),
            ],
            input_output_aliases={} if new else {count + 2: 0},
            cost_estimate=pl.CostEstimate(
                flops=4 * count * rows * channels**2,
                bytes_accessed=3 * count * rows * channels * 2 + 3 * channels**2 * 2,
                transcendentals=0,
            ),
            compiler_params=pltpu.CompilerParams(vmem_limit_bytes=PROJECT_BYTES),
            name="project_own" if new else "project",
        )(*parts, gains_kept, qkv_kept, *([] if new else [keyed]))

    if ring:
        beside = [lax.ppermute(rows, GROUP, swap) for rows in column]
        waiting = [(0, 0, column), (1, 0, beside)]
        for step in range(1, chips):
            column = [lax.ppermute(rows, GROUP, onward) for rows in column]
            if step == 1:
                column[0], gains_kept = lax.optimization_barrier((column[0], gains_kept))
                keyed, queries = project(None, waiting, ask=True)
                column[1], keyed = lax.optimization_barrier((column[1], keyed))
            else:
                for i, block in enumerate(waiting):
                    if block[0] == chips:
                        keyed, queries_beyond = project(keyed, [block], ask=True)
                    else:
                        (keyed,) = project(keyed, [block])
                    column[i], keyed = lax.optimization_barrier((column[i], keyed))
            if step == chips // 2:
                points_beyond = column
                slot_index, tail, pattern_beyond = index(column[0])
            if step == chips - 1:
                column[0], slot_index = lax.optimization_barrier((column[0], slot_index))
            beside = [lax.ppermute(rows, GROUP, swap) for rows in column]
            waiting = [(2 * step, 0, column), (2 * step + 1, 0, beside)]
        early = [(slot, 0, block[:-1]) for slot, _, block in waiting]
        (keyed,) = project(keyed, early)
        late_rows = [(slot + 1) * rows_here - part for slot, _, _ in waiting]
        late = [block[-1] for _, _, block in waiting]
    else:
        group = lax.all_gather(points, GROUP, axis=0, tiled=True)
        partner = lax.rem(lax.axis_index(GROUP) + chips, shards_in_group)
        points_beyond = [lax.dynamic_slice_in_dim(group, partner * rows_here, rows_here)]
        group = group.reshape(-1, PATCH, channels)
        slot_index, tail, pattern_beyond = index(lax.ppermute(column[0], GROUP, across))
        picked = [
            group[pattern.T].reshape(-1, channels) for pattern in (pattern_first, pattern_beyond)
        ]
        wide = picked[0].shape[0]
        keyed, queries = project(None, [(0, 0, column)], ask=True)
        keyed, queries_beyond = project(keyed, [(1, 0, points_beyond)], ask=True, rows=rows_here)
        (keyed,) = project(keyed, [(2, 0, [picked[0]])], rows=wide)
        (keyed,) = project(keyed, [(2 + chosen, 0, [picked[1]])], rows=wide)
        late_rows, late = [], []

    held_weights = [pltpu.VMEM(w.shape[1:], BF16) for w in weights]
    held_rows = pltpu.VMEM((rows_here, channels), BF16)
    held_slots = pltpu.VMEM((devices, pair_slots, channels), BF16)
    held_both = pltpu.VMEM((2 * rows_here, channels), BF16)
    pair_rows = channels // LANES * pair_slots + TAIL
    outgoing, _ = pl.pallas_call(
        functools.partial(first_kernel, chips if ring else 0, late_rows),
        out_shape=[jax.ShapeDtypeStruct((devices, pair_rows, LANES), BF16), kv_shape],
        in_specs=[SMEM_SPEC] * 2
        + [VMEM_SPEC] * 7
        + [ANY_SPEC] * (2 + len(late) + len(points_beyond)),
        out_specs=[ANY_SPEC, VMEM_SPEC],
        scratch_shapes=[
            held_both,
            held_both,
            held_both,
            held_slots,
            pltpu.VMEM((max(len(late), 1), part, channels), BF16),
            pltpu.SemaphoreType.DMA((1 + SEND_PARTS, 4)),
            pltpu.SemaphoreType.DMA((max(len(late), 1),)),
        ],
        input_output_aliases={3: 1},
        compiler_params=pltpu.CompilerParams(vmem_limit_bytes=FIRST_BYTES),
        name="block_first",
    )(
        pattern_first,
        pattern_beyond,
        slot_index,
        keyed,
        gains_kept,
        qkv_kept,
        queries,
        queries_beyond,
        proj_kept,
        tail,
        points,
        *late,
        *points_beyond,
    )
    incoming = lax.all_to_all(outgoing, ("grp", "seq"), split_axis=0, concat_axis=0, tiled=True)

    return pl.pallas_call(
        second_kernel,
        out_shape=(
            jax.ShapeDtypeStruct((rows_here, channels), BF16),
            jax.ShapeDtypeStruct((w_head.shape[0], rows_here), F32),
        ),
        in_specs=[SMEM_SPEC] + [ANY_SPEC] * 7,
        out_specs=(VMEM_SPEC, VMEM_SPEC),
        scratch_shapes=[
            pltpu.VMEM((rows_here, 2 * channels), BF16),
            held_rows,
            held_rows,
            held_slots,
            *held_weights[1:],
            pltpu.VMEM(w_qkv.shape[1:], BF16),
            *held_weights,
            pltpu.VMEM(norm_gains.shape, F32),
            pltpu.VMEM(tail.shape, BF16),
            pltpu.VMEM(w_head.shape, BF16),
            pltpu.SemaphoreType.DMA((3, 6)),
        ],
        compiler_params=pltpu.CompilerParams(vmem_limit_bytes=SECOND_BYTES),
        name="block_second",
    )(pattern_second.T, norm_gains, incoming, w_qkv, *weights, w_head)


def solution(mesh):
    groups, shards_in_group = mesh.devices.shape
    halves = Mesh(
        mesh.devices.reshape(groups, 2, shards_in_group // 2), ("grp",) + GROUP
    )
    everywhere = ("grp",) + GROUP
    placed = (
        P(everywhere, None),
        P(everywhere, None),
        P(everywhere, None),
        P(everywhere),
        P(),
        P(),
        P(),
        P(),
        P(),
        P(),
    )
    return jax.shard_map(
        shards,
        mesh=halves,
        in_specs=placed,
        out_specs=(P(everywhere, None), P(None, everywhere)),
        check_vma=False,
    )
```

```python
import functools

import jax
import jax.numpy as jnp
from jax import lax
from jax.experimental import pallas as pl
from jax.experimental.pallas import tpu as pltpu
from jax.sharding import Mesh, PartitionSpec as P

HEADS = 8
PATCH = 64
HEADS_TOGETHER = 4
GROUP = ("half", "seq")
RING_PARTS = 2
SEND_PARTS = 1
LANES = 128
TAIL = 8
DIGIT = 256
FIRST_BYTES = 28 * 1024 * 1024
SECOND_BYTES = 50 * 1024 * 1024
PROJECT_BYTES = 16 * 1024 * 1024
SPLIT_BYTES = 60 * 1024 * 1024
PREPARE_BYTES = 46 * 1024 * 1024
RING_BYTES = 16 * 1024 * 1024
F32 = jnp.float32
BF16 = jnp.bfloat16


def layer_norm(rows, gains):
    values = rows.astype(F32)
    average = jnp.mean(values, axis=-1, keepdims=True)
    spread = jnp.mean((values - average) ** 2, axis=-1, keepdims=True)
    return ((values - average) * lax.rsqrt(spread + 1e-05) * gains).astype(BF16)


def gelu(x):
    half = 0.5 * x
    return half + half * lax.erf(x * 0.5**0.5)


def head_masks(head_dim):
    lane = lax.broadcasted_iota(jnp.int32, (PATCH, HEADS_TOGETHER * head_dim), 1)
    return [
        jnp.where((lane >= h * head_dim) & (lane < (h + 1) * head_dim), 1.0, 0.0).astype(BF16)
        for h in range(HEADS_TOGETHER)
    ]


def attend(patches, head_dim):
    masks = head_masks(head_dim)
    width = HEADS_TOGETHER * head_dim
    heads_per_tile = LANES // head_dim
    lane = lax.broadcasted_iota(jnp.int32, (PATCH, LANES), 1)
    steps = [(p, g) for p in range(len(patches)) for g in range(HEADS // HEADS_TOGETHER)]

    def scores_of(step):
        p, g = step
        queries, keys, _ = patches[p]
        q = queries(g * width, width)
        stacked = jnp.concatenate([q * mask for mask in masks], axis=0)
        return lax.dot_general(
            stacked, keys(g * width, width), (((1,), (1,)), ((), ())), preferred_element_type=F32
        )

    scores = scores_of(steps[0])
    for i, (p, g) in enumerate(steps):
        later = scores_of(steps[i + 1]) if i + 1 < len(steps) else None
        grown = jnp.exp(scores - jnp.max(scores, axis=-1, keepdims=True))
        scale = 1.0 / jnp.sum(grown, axis=-1, keepdims=True)
        values = patches[p][2](g * width, width)
        mixed = jnp.dot(grown.astype(BF16), values, preferred_element_type=F32)
        tiles = []
        for t in range(width // LANES):
            tile = None
            for h in range(heads_per_tile):
                rows = slice((t * heads_per_tile + h) * PATCH, (t * heads_per_tile + h + 1) * PATCH)
                head = mixed[rows, t * LANES : (t + 1) * LANES] * scale[rows]
                tile = head if tile is None else jnp.where(lane < h * head_dim, tile, head)
            tiles.append(tile)
        yield p, g * width, jnp.concatenate(tiles, axis=1).astype(BF16)
        scores = later


def one_hot_rows(places, rows):
    row = lax.broadcasted_iota(jnp.int32, (rows, places.shape[1]), 0)
    return jnp.where(row == places, 1.0, 0.0).astype(BF16)


def started(pairs, sems):
    copies = [
        pltpu.make_async_copy(source, place, sems.at[at])
        for at, (source, place) in enumerate(pairs)
    ]
    for copy in copies:
        copy.start()
    return copies


def mix(rows, attended, w_proj):
    mixed = jnp.dot(attended, w_proj[...], preferred_element_type=F32)
    return (rows.astype(F32) + mixed).astype(BF16)


def feed(first, gain, w_up, w_down):
    hidden = layer_norm(first, gain)
    total = first.astype(F32)
    piece = 1024
    pieces = range(0, w_up.shape[1], piece)
    upper = jnp.dot(hidden, w_up[:, :piece], preferred_element_type=F32)
    for at in pieces:
        later = None
        if at + piece < w_up.shape[1]:
            later = jnp.dot(
                hidden, w_up[:, at + piece : at + 2 * piece], preferred_element_type=F32
            )
        act = gelu(upper).astype(BF16)
        total = total + jnp.dot(act, w_down[at : at + piece, :], preferred_element_type=F32)
        upper = later
    return total.astype(BF16)


def split_kernel(points, destination, pattern, *refs):
    *parts, destination_held, pattern_held, notes, sems = refs
    rows = points.shape[0] // len(parts)
    fetches = started([(destination, destination_held), (pattern, pattern_held)], sems.at[0])
    copies = started(
        [
            (points.at[pl.ds(i * rows, rows), :], part.at[pl.ds(0, rows), :])
            for i, part in enumerate(parts)
        ],
        sems.at[1],
    )
    for fetch in fetches:
        fetch.wait()
    chosen, patches = pattern.shape
    row = lax.broadcasted_iota(jnp.int32, notes.shape, 0)
    low = destination_held[...] & (DIGIT - 1)
    high = lax.shift_right_logical(destination_held[...], DIGIT.bit_length() - 1)
    values = jnp.where(row == chosen, low, jnp.where(row == chosen + 1, high, 0))
    notes[...] = values.astype(F32)
    notes[0:chosen, 0:patches] = pattern_held[...].astype(F32)
    parts[0][rows : rows + TAIL, :] = notes[...].astype(BF16)
    for copy in copies:
        copy.wait()


def keep_kernel(*refs):
    *refs, sems = refs
    count = len(refs) // 2
    for copy in started(
        [
            (source.at[0] if len(source.shape) == 3 else source, place)
            for source, place in zip(refs[:count], refs[count:])
        ],
        sems,
    ):
        copy.wait()


def index_kernel(capacity, destination, beyond, slots, tail, pattern, held, notes, sems):
    added = beyond.at[pl.ds(beyond.shape[0] - TAIL, TAIL), :]
    for fetch in started([(destination, held.at[0]), (added, notes)], sems):
        fetch.wait()
    chosen, patches = pattern.shape
    noted = notes[...].astype(F32)
    pattern[...] = noted[0:chosen, 0:patches].astype(jnp.int32)
    low, high = noted[chosen : chosen + 1, :], noted[chosen + 1 : chosen + 2, :]
    held[1] = (low + DIGIT * high).astype(jnp.int32)
    rows = held.shape[2]
    devices = tail.shape[0]
    in_half = lax.axis_size("seq")
    seq_bits = in_half.bit_length() - 1
    index = lax.axis_index(("grp", "seq"))
    offset = lax.rem(index, LANES // (2 * capacity)) * 2 * capacity
    before = lax.broadcasted_iota(jnp.int32, (rows, rows), 0)
    before = before < lax.broadcasted_iota(jnp.int32, (rows, rows), 1)
    before = jnp.where(before, 1.0, 0.0).astype(BF16)
    lines = jnp.zeros((devices * TAIL, LANES), F32)
    for b in range(2):
        target = lax.shift_right_logical(held[b], rows.bit_length() - 1)
        place = held[b] & (rows - 1)
        half = lax.shift_right_logical(target, seq_bits) & 1
        group = lax.shift_right_logical(target, seq_bits + 1)
        target = group * in_half + (target & (in_half - 1))
        target = jnp.where(half == lax.axis_index("half"), target, -1)
        mine = lax.broadcasted_iota(jnp.int32, (devices, rows), 0) == target
        mine = jnp.where(mine, 1.0, 0.0).astype(F32)
        earlier = jnp.dot(mine.astype(BF16), before, preferred_element_type=F32)
        rank = jnp.sum(mine * earlier, axis=0, keepdims=True).astype(jnp.int32)
        slots[:, b * rows : (b + 1) * rows] = jnp.where(target >= 0, target * capacity + rank, -1)
        rank = rank + b * capacity + offset
        by_lane = lax.broadcasted_iota(jnp.int32, (LANES, rows), 0) == rank
        by_lane = jnp.where(by_lane, 1.0, 0.0).astype(BF16)
        line = lax.broadcasted_iota(jnp.int32, (devices * TAIL, rows), 0)
        code = place + 1
        low = (code & (DIGIT - 1)).astype(F32)
        high = lax.shift_right_logical(code, DIGIT.bit_length() - 1).astype(F32)
        digit = line & (TAIL - 1)
        digits = jnp.where(digit == 0, low, jnp.where(digit == 1, high, 0.0))
        line = lax.shift_right_logical(line, TAIL.bit_length() - 1)
        digits = jnp.where(line == target, digits, 0.0)
        lines = lines + lax.dot_general(
            digits.astype(BF16), by_lane, (((1,), (1,)), ((), ())), preferred_element_type=F32
        )
    tail[...] = lines.reshape(devices, TAIL, LANES).astype(BF16)


def project_kernel(first_rows, new, ask, *refs):
    count = len(first_rows)
    parts, gains, w_qkv = refs[:count], refs[count], refs[count + 1]
    refs = refs[count + 2 if new else count + 3 :]
    whole, (held, sems) = refs[0], refs[-2:]
    channels = w_qkv.shape[0]
    rows = held.shape[1]
    copies = started(
        [(part.at[pl.ds(0, rows), :], held.at[i]) for i, part in enumerate(parts)], sems
    )
    for i, first in enumerate(first_rows):
        copies[i].wait()
        normed = layer_norm(held[i], gains[0:1, :])
        whole[first : first + rows, :] = jnp.dot(
            normed, w_qkv[:, channels:], preferred_element_type=F32
        ).astype(BF16)
        if ask and i * rows < refs[1].shape[0]:
            scale = BF16((channels // HEADS) ** (-0.5))
            query = jnp.dot(normed, w_qkv[:, :channels], preferred_element_type=F32).astype(BF16)
            refs[1][i * rows : (i + 1) * rows, :] = (query * scale).astype(BF16)


def loads(queries, p, keyed, starts):
    channels = queries.shape[1]

    def asked(at, width):
        return queries[p * PATCH : (p + 1) * PATCH, at : at + width]

    def keys(at, width):
        pieces = [keyed[pl.ds(start, PATCH), at : at + width] for start in starts]
        return jnp.concatenate(pieces, axis=0)

    return asked, keys, lambda at, width: keys(channels + at, width)


def lane_tiles(packed, rows):
    capacity, channels = rows.shape[1:]
    return [
        (
            packed.at[:, pl.ds(j * capacity, capacity), :],
            rows.at[:, :, pl.ds(j * LANES, LANES)],
        )
        for j in range(channels // LANES)
    ]


def first_kernel(
    ring_chips,
    late_rows,
    pattern,
    pattern_beyond,
    slot_of_row,
    kept_rows,
    gains,
    w_qkv,
    queries,
    queries_beyond,
    w_proj,
    tail,
    points,
    *refs,
):
    late, refs = refs[: len(late_rows)], refs[len(late_rows) :]
    *points_beyond, outgoing, keyed, attended, points_held, first_held, outgoing_held = refs[:-3]
    late_held, sems, late_sems = refs[-3:]
    rows, channels = points.shape
    devices, capacity, _ = outgoing_held.shape
    row_tiles = channels // LANES * capacity
    patches = rows // PATCH
    chosen = pattern.shape[0]
    me = lax.axis_index(GROUP)
    part = rows // len(points_beyond)
    late_part = late_held.shape[1]
    landing = started(
        [(piece.at[pl.ds(0, late_part), :], late_held.at[i]) for i, piece in enumerate(late)],
        late_sems,
    )
    copies = started(
        [(tail, outgoing.at[:, pl.ds(row_tiles, TAIL), :]), (points, points_held.at[:rows])]
        + [
            (piece.at[pl.ds(0, part), :], points_held.at[pl.ds(rows + i * part, part), :])
            for i, piece in enumerate(points_beyond)
        ],
        sems.at[0],
    )
    for copy in landing + copies[1:]:
        copy.wait()
    for i, first in enumerate(late_rows):
        keyed[first : first + late_part, :] = jnp.dot(
            layer_norm(late_held[i], gains[0:1, :]),
            w_qkv[:, channels:],
            preferred_element_type=F32,
        ).astype(BF16)
    blocks = ((pattern, queries, 0), (pattern_beyond, queries_beyond, ring_chips or 1))
    loaded = []
    for b, (picked, asking, own_slot) in enumerate(blocks):
        for p in range(patches):
            starts = [own_slot * rows + p * PATCH]
            for j in range(chosen):
                if ring_chips:
                    patch = picked[j, p]
                    owner, local = lax.div(patch, patches), lax.rem(patch, patches)
                    chip = lax.rem(lax.div(me, 2) - lax.div(owner, 2) + ring_chips, ring_chips)
                    slot = 2 * chip + jnp.where(lax.rem(me, 2) == lax.rem(owner, 2), 0, 1)
                    starts.append(pl.multiple_of((slot * patches + local) * PATCH, PATCH))
                else:
                    starts.append((2 * patches + (b * patches + p) * chosen + j) * PATCH)
            loaded.append(loads(asking, p, keyed, starts))
    for p, at, rows_done in attend(loaded, channels // HEADS):
        attended[p * PATCH : (p + 1) * PATCH, at : at + rows_done.shape[1]] = rows_done

    first_held[...] = mix(points_held[...], attended[...], w_proj)
    targets = devices // SEND_PARTS
    block_slots = capacity // 2
    leaving = []
    for i in range(SEND_PARTS):
        here = pl.ds(i * targets, targets)
        for b in range(2):
            mine = pl.ds(b * block_slots, block_slots)
            slots = slot_of_row[:, b * rows : (b + 1) * rows] - i * targets * block_slots
            send = one_hot_rows(slots, targets * block_slots)
            moved = jnp.dot(
                send, first_held[b * rows : (b + 1) * rows, :], preferred_element_type=F32
            )
            outgoing_held[here, mine, :] = moved.astype(BF16).reshape(
                targets, block_slots, channels
            )
        pairs = lane_tiles(outgoing.at[here], outgoing_held.at[here])
        leaving += started([(source, place) for place, source in pairs], sems.at[1 + i])
    for copy in copies[:1] + leaving:
        copy.wait()


def second_kernel(
    pattern,
    gains,
    incoming,
    w_qkv,
    w_proj,
    w_up,
    w_down,
    w_head,
    features,
    normals,
    kv,
    queries,
    attended,
    incoming_held,
    first_up_held,
    first_down_held,
    qkv_held,
    proj_held,
    up_held,
    down_held,
    gains_held,
    tail_held,
    head_held,
    sems,
):
    rows, channels = features.shape
    devices, capacity, _ = incoming_held.shape
    patches = rows // PATCH
    chosen = pattern.shape[0]
    tail = incoming.at[:, pl.ds(channels // LANES * capacity, TAIL), :]
    small = started(
        [(tail, tail_held), (gains, gains_held), (w_head, head_held)], sems.at[0]
    )
    landing = started(lane_tiles(incoming, incoming_held), sems.at[1])
    copies = started(
        [
            (w_up.at[0], first_up_held),
            (w_down.at[0], first_down_held),
            (w_qkv.at[1], qkv_held),
            (w_proj.at[1], proj_held),
            (w_up.at[1], up_held),
            (w_down.at[1], down_held),
        ],
        sems.at[2],
    )
    for copy in small:
        copy.wait()
    per_row = LANES // capacity
    digits = tail_held[...].astype(F32)
    codes = digits[:, 0:1, :] + DIGIT * digits[:, 1:2, :]
    pieces = []
    for at in range(0, devices, per_row):
        code = codes[at]
        for i in range(1, per_row):
            code = code + codes[at + i]
        pieces.append(code)
    places = jnp.concatenate(pieces, axis=1).astype(jnp.int32) - 1
    place = one_hot_rows(places, rows)
    for copy in landing:
        copy.wait()
    moved = incoming_held[...].reshape(devices * capacity, channels)
    first = jnp.dot(place, moved, preferred_element_type=F32).astype(BF16)
    for copy in copies[:2]:
        copy.wait()
    second = feed(first, gains_held[1:2, :], first_up_held, first_down_held)
    for copy in copies[2:]:
        copy.wait()
    normed = layer_norm(second, gains_held[2:3, :])
    scale = (channels // HEADS) ** (-0.5)
    every = jnp.dot(normed, qkv_held[...], preferred_element_type=F32).astype(BF16)
    queries[...] = (every[:, :channels] * BF16(scale)).astype(BF16)
    kv[...] = every[:, channels:]
    loaded = []
    for p in range(patches):
        starts = [pl.multiple_of(pattern[j, p] * PATCH, PATCH) for j in range(chosen)]
        loaded.append(loads(queries, p, kv, [p * PATCH] + starts))
    for p, at, rows_done in attend(loaded, channels // HEADS):
        attended[p * PATCH : (p + 1) * PATCH, at : at + rows_done.shape[1]] = rows_done
    mixed = mix(second, attended[...], proj_held)
    done = feed(mixed, gains_held[3:4, :], up_held, down_held)
    features[...] = done
    normals[...] = lax.dot_general(
        head_held[...], done, (((1,), (1,)), ((), ())), preferred_element_type=F32
    )


VMEM_SPEC = pl.BlockSpec(memory_space=pltpu.VMEM)
SMEM_SPEC = pl.BlockSpec(memory_space=pltpu.SMEM)
ANY_SPEC = pl.BlockSpec(memory_space=pl.ANY)


def shards(
    points,
    pattern_first,
    pattern_second,
    destination,
    norm_gains,
    w_qkv,
    w_proj,
    w_up,
    w_down,
    w_head,
):
    rows_here, channels = points.shape
    patches, chosen = pattern_first.shape
    devices = lax.axis_size("grp") * lax.axis_size("seq")
    capacity = 2 * rows_here // (2 * devices)
    pair_slots = 2 * capacity

    shards_in_group = lax.axis_size(GROUP)
    chips = shards_in_group // 2
    onward = [(i, (i + 2) % shards_in_group) for i in range(shards_in_group)]
    swap = [(i, i ^ 1) for i in range(shards_in_group)]
    across = [(i, (i + chips) % shards_in_group) for i in range(shards_in_group)]
    ring = shards_in_group * rows_here * 2 * channels * 2 <= RING_BYTES
    kept_rows = shards_in_group * rows_here if ring else 2 * patches * (1 + chosen) * PATCH
    part = rows_here // RING_PARTS

    destination = destination.reshape(1, rows_here)
    pattern_first = pattern_first.T
    part_rows = [part + TAIL] + [part] * (RING_PARTS - 1)
    column = pl.pallas_call(
        split_kernel,
        out_shape=[jax.ShapeDtypeStruct((rows, channels), BF16) for rows in part_rows],
        in_specs=[ANY_SPEC] * 3,
        out_specs=[VMEM_SPEC] * RING_PARTS,
        scratch_shapes=[
            pltpu.VMEM((1, rows_here), jnp.int32),
            pltpu.VMEM(pattern_first.shape, jnp.int32),
            pltpu.VMEM((TAIL, channels), F32),
            pltpu.SemaphoreType.DMA((2, RING_PARTS)),
        ],
        compiler_params=pltpu.CompilerParams(vmem_limit_bytes=SPLIT_BYTES),
        name="split",
    )(points, destination, pattern_first)

    weights = (w_proj, w_up, w_down)
    kv_shape = jax.ShapeDtypeStruct((kept_rows, 2 * channels), BF16)
    own_shape = jax.ShapeDtypeStruct((rows_here, channels), BF16)

    qkv_kept, proj_kept, gains_kept = pl.pallas_call(
        keep_kernel,
        out_shape=[
            *[jax.ShapeDtypeStruct(w.shape[1:], BF16) for w in (w_qkv, w_proj)],
            jax.ShapeDtypeStruct(norm_gains.shape, F32),
        ],
        in_specs=[ANY_SPEC] * 3,
        out_specs=[VMEM_SPEC] * 3,
        scratch_shapes=[pltpu.SemaphoreType.DMA((3,))],
        compiler_params=pltpu.CompilerParams(vmem_limit_bytes=PREPARE_BYTES),
        name="keep",
    )(w_qkv, w_proj, norm_gains)
    def index(beyond):
        return pl.pallas_call(
            functools.partial(index_kernel, capacity),
            out_shape=[
                jax.ShapeDtypeStruct((1, 2 * rows_here), jnp.int32),
                jax.ShapeDtypeStruct((devices, TAIL, LANES), BF16),
                jax.ShapeDtypeStruct(pattern_first.shape, jnp.int32),
            ],
            in_specs=[ANY_SPEC] * 2,
            out_specs=[VMEM_SPEC] * 3,
            scratch_shapes=[
                pltpu.VMEM((2, 1, rows_here), jnp.int32),
                pltpu.VMEM((TAIL, channels), BF16),
                pltpu.SemaphoreType.DMA((2,)),
            ],
            compiler_params=pltpu.CompilerParams(vmem_limit_bytes=PROJECT_BYTES),
            name="index",
        )(destination, beyond)

    def project(keyed, blocks, ask=False, rows=part):
        parts = [piece for _, _, block in blocks for piece in block]
        count = len(parts)
        first_rows = [
            slot * rows_here + first + i * rows
            for slot, first, block in blocks
            for i in range(len(block))
        ]
        new = keyed is None
        return pl.pallas_call(
            functools.partial(project_kernel, first_rows, new, ask),
            out_shape=[kv_shape] + [own_shape] * ask,
            in_specs=[ANY_SPEC] * count + [VMEM_SPEC] * (2 if new else 3),
            out_specs=[VMEM_SPEC] * (1 + ask),
            scratch_shapes=[
                pltpu.VMEM((count, rows, channels), BF16),
                pltpu.SemaphoreType.DMA((count,)),
            ],
            input_output_aliases={} if new else {count + 2: 0},
            cost_estimate=pl.CostEstimate(
                flops=4 * count * rows * channels**2,
                bytes_accessed=3 * count * rows * channels * 2 + 3 * channels**2 * 2,
                transcendentals=0,
            ),
            compiler_params=pltpu.CompilerParams(vmem_limit_bytes=PROJECT_BYTES),
            name="project_own" if new else "project",
        )(*parts, gains_kept, qkv_kept, *([] if new else [keyed]))

    if ring:
        beside = [lax.ppermute(rows, GROUP, swap) for rows in column]
        waiting = [(0, 0, column), (1, 0, beside)]
        for step in range(1, chips):
            column = [lax.ppermute(rows, GROUP, onward) for rows in column]
            if step == 1:
                column[0], gains_kept = lax.optimization_barrier((column[0], gains_kept))
                keyed, queries = project(None, waiting, ask=True)
                column[1], keyed = lax.optimization_barrier((column[1], keyed))
            else:
                for i, block in enumerate(waiting):
                    if block[0] == chips:
                        keyed, queries_beyond = project(keyed, [block], ask=True)
                    else:
                        (keyed,) = project(keyed, [block])
                    column[i], keyed = lax.optimization_barrier((column[i], keyed))
            if step == chips // 2:
                points_beyond = column
                slot_index, tail, pattern_beyond = index(column[0])
            if step == chips - 1:
                column[0], slot_index = lax.optimization_barrier((column[0], slot_index))
            beside = [lax.ppermute(rows, GROUP, swap) for rows in column]
            waiting = [(2 * step, 0, column), (2 * step + 1, 0, beside)]
        early = [(slot, 0, block[:-1]) for slot, _, block in waiting]
        (keyed,) = project(keyed, early)
        late_rows = [(slot + 1) * rows_here - part for slot, _, _ in waiting]
        late = [block[-1] for _, _, block in waiting]
    else:
        group = lax.all_gather(points, GROUP, axis=0, tiled=True)
        partner = lax.rem(lax.axis_index(GROUP) + chips, shards_in_group)
        points_beyond = [lax.dynamic_slice_in_dim(group, partner * rows_here, rows_here)]
        group = group.reshape(-1, PATCH, channels)
        slot_index, tail, pattern_beyond = index(lax.ppermute(column[0], GROUP, across))
        picked = [
            group[pattern.T].reshape(-1, channels) for pattern in (pattern_first, pattern_beyond)
        ]
        wide = picked[0].shape[0]
        keyed, queries = project(None, [(0, 0, column)], ask=True)
        keyed, queries_beyond = project(keyed, [(1, 0, points_beyond)], ask=True, rows=rows_here)
        (keyed,) = project(keyed, [(2, 0, [picked[0]])], rows=wide)
        (keyed,) = project(keyed, [(2 + chosen, 0, [picked[1]])], rows=wide)
        late_rows, late = [], []

    held_weights = [pltpu.VMEM(w.shape[1:], BF16) for w in weights]
    held_rows = pltpu.VMEM((rows_here, channels), BF16)
    held_slots = pltpu.VMEM((devices, pair_slots, channels), BF16)
    held_both = pltpu.VMEM((2 * rows_here, channels), BF16)
    pair_rows = channels // LANES * pair_slots + TAIL
    outgoing, _ = pl.pallas_call(
        functools.partial(first_kernel, chips if ring else 0, late_rows),
        out_shape=[jax.ShapeDtypeStruct((devices, pair_rows, LANES), BF16), kv_shape],
        in_specs=[SMEM_SPEC] * 2
        + [VMEM_SPEC] * 7
        + [ANY_SPEC] * (2 + len(late) + len(points_beyond)),
        out_specs=[ANY_SPEC, VMEM_SPEC],
        scratch_shapes=[
            held_both,
            held_both,
            held_both,
            held_slots,
            pltpu.VMEM((max(len(late), 1), part, channels), BF16),
            pltpu.SemaphoreType.DMA((1 + SEND_PARTS, 4)),
            pltpu.SemaphoreType.DMA((max(len(late), 1),)),
        ],
        input_output_aliases={3: 1},
        compiler_params=pltpu.CompilerParams(vmem_limit_bytes=FIRST_BYTES),
        name="block_first",
    )(
        pattern_first,
        pattern_beyond,
        slot_index,
        keyed,
        gains_kept,
        qkv_kept,
        queries,
        queries_beyond,
        proj_kept,
        tail,
        points,
        *late,
        *points_beyond,
    )
    incoming = lax.all_to_all(outgoing, ("grp", "seq"), split_axis=0, concat_axis=0, tiled=True)

    return pl.pallas_call(
        second_kernel,
        out_shape=(
            jax.ShapeDtypeStruct((rows_here, channels), BF16),
            jax.ShapeDtypeStruct((w_head.shape[0], rows_here), F32),
        ),
        in_specs=[SMEM_SPEC] + [ANY_SPEC] * 7,
        out_specs=(VMEM_SPEC, VMEM_SPEC),
        scratch_shapes=[
            pltpu.VMEM((rows_here, 2 * channels), BF16),
            held_rows,
            held_rows,
            held_slots,
            *held_weights[1:],
            pltpu.VMEM(w_qkv.shape[1:], BF16),
            *held_weights,
            pltpu.VMEM(norm_gains.shape, F32),
            pltpu.VMEM(tail.shape, BF16),
            pltpu.VMEM(w_head.shape, BF16),
            pltpu.SemaphoreType.DMA((3, 6)),
        ],
        compiler_params=pltpu.CompilerParams(vmem_limit_bytes=SECOND_BYTES),
        name="block_second",
    )(pattern_second.T, norm_gains, incoming, w_qkv, *weights, w_head)


def solution(mesh):
    groups, shards_in_group = mesh.devices.shape
    halves = Mesh(
        mesh.devices.reshape(groups, 2, shards_in_group // 2), ("grp",) + GROUP
    )
    everywhere = ("grp",) + GROUP
    placed = (
        P(everywhere, None),
        P(everywhere, None),
        P(everywhere, None),
        P(everywhere),
        P(),
        P(),
        P(),
        P(),
        P(),
        P(),
    )
    return jax.shard_map(
        shards,
        mesh=halves,
        in_specs=placed,
        out_specs=(P(everywhere, None), P(None, everywhere)),
        check_vma=False,
    )
```
